32 devices in a mesh: narrow: 4 (over y, x), wide: 8 (over z, core).
Axes of the slice: x: 2, y: 2, z: 4, core: 2. Of those that a mesh axis runs over, the one named last changes fastest.
Arguments:
- tokens_in: bfloat16 [16384, 2048], P(('narrow', 'wide')), may hold values from -6 to 6
- out_grad: bfloat16 [16384, 2048], P(('narrow', 'wide')), may hold values from -15 to 15
- positions: int32 [16384], P('narrow'), may hold values from 0 to 12285, as said below
- query_weight: float32 [2048, 2048], P('narrow', 'wide'), may hold values from -0.125 to 0.125
- query_first: float32 [2048, 2048], P('narrow', 'wide'), may hold values from -160 to 160
- query_second: float32 [2048, 2048], P('narrow', 'wide'), may hold values from 3440.64 to 13762.56
- key_weight: float32 [2048, 512], P('narrow'), may hold values from -0.125 to 0.125
- key_first: float32 [2048, 512], P('narrow'), may hold values from -320 to 320
- key_second: float32 [2048, 512], P('narrow'), may hold values from 13926.4 to 55705.6
- value_weight: float32 [2048, 512], P('narrow'), may hold values from -0.125 to 0.125
- value_first: float32 [2048, 512], P('narrow'), may hold values from -256 to 256
- value_second: float32 [2048, 512], P('narrow'), may hold values from 7864.32 to 31129.6
- output_weight: float32 [2048, 2048], P('wide', 'narrow'), may hold values from -0.875 to 0.875
- output_first: float32 [2048, 2048], P('wide', 'narrow'), may hold values from -32 to 32
- output_second: float32 [2048, 2048], P('wide', 'narrow'), may hold values from 139.264 to 557.056
- gate_weight: float32 [2048, 8192], P('narrow', 'wide'), may hold values from -0.125 to 0.125
- gate_first: float32 [2048, 8192], P('narrow', 'wide'), may hold values from -48 to 48
- gate_second: float32 [2048, 8192], P('narrow', 'wide'), may hold values from 311.296 to 1245.184
- up_weight: float32 [2048, 8192], P('narrow', 'wide'), may hold values from -0.125 to 0.125
- up_first: float32 [2048, 8192], P('narrow', 'wide'), may hold values from -48 to 48
- up_second: float32 [2048, 8192], P('narrow', 'wide'), may hold values from 311.296 to 1245.184
- down_weight: float32 [8192, 2048], P('wide', 'narrow'), may hold values from -0.0625 to 0.0625
- down_first: float32 [8192, 2048], P('wide', 'narrow'), may hold values from -112 to 112
- down_second: float32 [8192, 2048], P('wide', 'narrow'), may hold values from 1474.56 to 5898.24
- norm_gains: float32 [2, 2048], replicated, may hold values from 0.5 to 1.5
- norm_first: float32 [2, 2048], replicated, may hold values from -160 to 160
- norm_second: float32 [2, 2048], replicated, may hold values from 3440.64 to 13762.56
- head_gains: float32 [2, 64], replicated, may hold values from 1 to 1.8
- head_first: float32 [2, 64], replicated, may hold values from -896 to 896
- head_second: float32 [2, 64], replicated, may hold values from 86835.2 to 344064
Outputs:
- block_out: bfloat16 [16384, 2048], P(('narrow', 'wide'))
- input_grad: float32 [16384, 2048], P(('narrow', 'wide'))
- query_new: float32 [2048, 2048], P('narrow', 'wide')
- query_first_new: float32 [2048, 2048], P('narrow', 'wide')
- query_second_new: float32 [2048, 2048], P('narrow', 'wide')
- key_new: float32 [2048, 512], P('narrow')
- key_first_new: float32 [2048, 512], P('narrow')
- key_second_new: float32 [2048, 512], P('narrow')
- value_new: float32 [2048, 512], P('narrow')
- value_first_new: float32 [2048, 512], P('narrow')
- value_second_new: float32 [2048, 512], P('narrow')
- output_new: float32 [2048, 2048], P('wide', 'narrow')
- output_first_new: float32 [2048, 2048], P('wide', 'narrow')
- output_second_new: float32 [2048, 2048], P('wide', 'narrow')
- gate_new: float32 [2048, 8192], P('narrow', 'wide')
- gate_first_new: float32 [2048, 8192], P('narrow', 'wide')
- gate_second_new: float32 [2048, 8192], P('narrow', 'wide')
- up_new: float32 [2048, 8192], P('narrow', 'wide')
- up_first_new: float32 [2048, 8192], P('narrow', 'wide')
- up_second_new: float32 [2048, 8192], P('narrow', 'wide')
- down_new: float32 [8192, 2048], P('wide', 'narrow')
- down_first_new: float32 [8192, 2048], P('wide', 'narrow')
- down_second_new: float32 [8192, 2048], P('wide', 'narrow')
- norm_new: float32 [2, 2048], replicated
- norm_first_new: float32 [2, 2048], replicated
- norm_second_new: float32 [2, 2048], replicated
- head_new: float32 [2, 64], replicated
- head_first_new: float32 [2, 64], replicated
- head_second_new: float32 [2, 64], replicated
The draws below stay inside these ranges and needn't reach their ends.
Inputs may be any that keep to these rules, and one draw needn't show every extreme that they name: `positions`: within each sequence of 4096 tokens the ids rise by 1 or 2 from token to token; the steps and each sequence's first id differ from seed to seed.
All inputs are finite; a program needn't handle non-finite values.
Results may differ from the reference program's by a relative error of at most 0.028.
Values may be sent and summed in bfloat16 or wider, within the bound.
A program may use at most 384 MiB of HBM per device.

```python
import math
from functools import partial
import jax
import jax.numpy as jnp
from jax import lax

D = 2048
QH = 32
KVH = 8
HD = 64
FF = 8192
SEQ_LEN = 4096
STEP = 10
TOKENS = 16384
O_FAN = 50
N_WIDE = 8


def draw_positions(key, part):
    key = jax.random.fold_in(key, 11)
    start_key, pick_key, step_key = jax.random.split(key, 3)
    sequences = TOKENS // SEQ_LEN
    increments = jax.random.randint(step_key, (sequences, SEQ_LEN - 1), 1, 3).astype(jnp.int32)
    within = jnp.concatenate([jnp.zeros((sequences, 1), jnp.int32), jnp.cumsum(increments, axis=1).astype(jnp.int32)], axis=1)
    starts = jax.random.randint(start_key, (sequences,), 0, SEQ_LEN).astype(jnp.int32)
    shuffled = jax.random.permutation(pick_key, sequences)
    top_start = (3 * SEQ_LEN - 3 - within[shuffled[1], SEQ_LEN - 1]).astype(jnp.int32)
    starts = starts.at[shuffled[0]].set(0).at[shuffled[1]].set(top_start)
    return (starts[:, None] + within).reshape(TOKENS).astype(jnp.int32)


def draw_out_grad(key, part):
    key = jax.random.fold_in(key, 23)
    rising = jnp.arange(TOKENS, dtype=jnp.float32) / TOKENS
    samples = jnp.clip(jax.random.normal(key, (TOKENS, D), jnp.float32), -5.0, 5.0)
    return (samples * (1.0 + 2.0 * rising)[:, None]).astype(jnp.bfloat16)


def block_levels(key, dims, cuts, least, high):
    def one(position, blocks):
        steps = jax.random.uniform(jax.random.fold_in(jax.random.fold_in(key, 6), position), (blocks,), jnp.float32, least / len(cuts), high / len(cuts))
        return jnp.repeat(jnp.exp(steps), dims[position] // blocks).reshape((-1,) + (1,) * (len(dims) - position - 1))

    factor_of = one(*cuts[0])
    for cut in cuts[1:]:
        factor_of = factor_of * one(*cut)
    return factor_of


def scatter_about(own_key, dims, scale, reach, cuts=(), held_as=jnp.bfloat16):
    drawn = scale * jax.random.normal(own_key, dims, jnp.float32)
    if cuts:
        drawn = drawn * block_levels(own_key, dims, cuts, -0.22, 0.18)
    return jnp.clip(drawn, -reach, reach).astype(held_as)


def setup_inputs(seed: int = 0) -> dict:
    key_list = jax.random.split(jax.random.key(seed), 31)
    tokens_in = scatter_about(key_list[0], (TOKENS, D), 1.0, 6.0, ((0, 32),))
    out_grad = draw_out_grad(jax.random.fold_in(key_list[30], 71), 0)
    positions = draw_positions(jax.random.fold_in(key_list[30], 71), 0)
    query_weight = scatter_about(key_list[3], (D, QH * HD), D ** -0.5, 0.125, ((0, 4), (1, 8)), jnp.float32)
    query_first = scatter_about(key_list[4], (D, QH * HD), (0.22 * TOKENS ** 0.5), 160.0, ((0, 4), (1, 8)), jnp.float32)
    query_second = jnp.clip(jnp.exp(math.log(13762.56) - 1.3862944 * jax.random.uniform(key_list[5], (D, QH * HD), jnp.float32) ** block_levels(key_list[5], (D, QH * HD), ((0, 4), (1, 8)), -0.2, 0.2)), 3440.64, 13762.56)
    key_weight = scatter_about(key_list[6], (D, KVH * HD), D ** -0.5, 0.125, ((0, 4),), jnp.float32)
    key_first = scatter_about(key_list[7], (D, KVH * HD), (0.44 * TOKENS ** 0.5), 320.0, ((0, 4),), jnp.float32)
    key_second = jnp.clip(jnp.exp(math.log(55705.6) - 1.3862944 * jax.random.uniform(key_list[8], (D, KVH * HD), jnp.float32) ** block_levels(key_list[8], (D, KVH * HD), ((0, 4),), -0.2, 0.2)), 13926.4, 55705.6)
    value_weight = scatter_about(key_list[9], (D, KVH * HD), D ** -0.5, 0.125, ((0, 4),), jnp.float32)
    value_first = scatter_about(key_list[10], (D, KVH * HD), (0.33 * TOKENS ** 0.5), 256.0, ((0, 4),), jnp.float32)
    value_second = jnp.clip(jnp.exp(math.log(31129.6) - 1.375823 * jax.random.uniform(key_list[11], (D, KVH * HD), jnp.float32) ** block_levels(key_list[11], (D, KVH * HD), ((0, 4),), -0.2, 0.2)), 7864.32, 31129.6)
    output_weight = scatter_about(key_list[12], (QH * HD, D), O_FAN ** -0.5, 0.875, ((0, 8), (1, 4)), jnp.float32)
    output_first = scatter_about(key_list[13], (QH * HD, D), (0.044 * TOKENS ** 0.5), 32.0, ((0, 8), (1, 4)), jnp.float32)
    output_second = jnp.clip(jnp.exp(math.log(557.056) - 1.3862944 * jax.random.uniform(key_list[14], (QH * HD, D), jnp.float32) ** block_levels(key_list[14], (QH * HD, D), ((0, 8), (1, 4)), -0.2, 0.2)), 139.264, 557.056)
    gate_weight = scatter_about(key_list[15], (D, FF), D ** -0.5, 0.125, ((0, 4), (1, 8)), jnp.float32)
    gate_first = scatter_about(key_list[16], (D, FF), (0.066 * TOKENS ** 0.5), 48.0, ((0, 4), (1, 8)), jnp.float32)
    gate_second = jnp.clip(jnp.exp(math.log(1245.184) - 1.3862944 * jax.random.uniform(key_list[17], (D, FF), jnp.float32) ** block_levels(key_list[17], (D, FF), ((0, 4), (1, 8)), -0.2, 0.2)), 311.296, 1245.184)
    up_weight = scatter_about(key_list[18], (D, FF), D ** -0.5, 0.125, ((0, 4), (1, 8)), jnp.float32)
    up_first = scatter_about(key_list[19], (D, FF), (0.066 * TOKENS ** 0.5), 48.0, ((0, 4), (1, 8)), jnp.float32)
    up_second = jnp.clip(jnp.exp(math.log(1245.184) - 1.3862944 * jax.random.uniform(key_list[20], (D, FF), jnp.float32) ** block_levels(key_list[20], (D, FF), ((0, 4), (1, 8)), -0.2, 0.2)), 311.296, 1245.184)
    down_weight = scatter_about(key_list[21], (FF, D), FF ** -0.5, 0.0625, ((0, 8), (1, 4)), jnp.float32)
    down_first = scatter_about(key_list[22], (FF, D), (0.14 * TOKENS ** 0.5), 112.0, ((0, 8), (1, 4)), jnp.float32)
    down_second = jnp.clip(jnp.exp(math.log(5898.24) - 1.3862944 * jax.random.uniform(key_list[23], (FF, D), jnp.float32) ** block_levels(key_list[23], (FF, D), ((0, 8), (1, 4)), -0.2, 0.2)), 1474.56, 5898.24)
    norm_gains = jnp.clip(1.0 + 0.1 * jax.random.normal(key_list[24], (2, D), jnp.float32), 0.5, 1.5)
    norm_first = scatter_about(key_list[25], (2, D), (0.22 * TOKENS ** 0.5), 160.0, (), jnp.float32)
    norm_second = jnp.clip(jnp.exp(jax.random.uniform(key_list[26], (2, D), jnp.float32, math.log(3440.64), math.log(13762.56))), 3440.64, 13762.56)
    head_gains = jnp.clip(jax.random.uniform(key_list[27], (2, HD), jnp.float32, 1.0, 1.8), 1.0, 1.8)
    head_first = scatter_about(key_list[28], (2, HD), (1.1 * TOKENS ** 0.5), 896.0, (), jnp.float32)
    head_second = jnp.clip(jnp.exp(jax.random.uniform(key_list[29], (2, HD), jnp.float32, math.log(86835.2), math.log(344064.0))), 86835.2, 344064.0)
    return {"tokens_in": tokens_in, "out_grad": out_grad, "positions": positions, "query_weight": query_weight, "query_first": query_first, "query_second": query_second, "key_weight": key_weight, "key_first": key_first, "key_second": key_second, "value_weight": value_weight, "value_first": value_first, "value_second": value_second, "output_weight": output_weight, "output_first": output_first, "output_second": output_second, "gate_weight": gate_weight, "gate_first": gate_first, "gate_second": gate_second, "up_weight": up_weight, "up_first": up_first, "up_second": up_second, "down_weight": down_weight, "down_first": down_first, "down_second": down_second, "norm_gains": norm_gains, "norm_first": norm_first, "norm_second": norm_second, "head_gains": head_gains, "head_first": head_first, "head_second": head_second}


EPSILON = 1e-06
BETA_ONE = 0.9
BETA_TWO = 0.95
ADAM_EPSILON = 1e-08
WEIGHT_DECAY = 0.1
GAIN_RATE = 1.0
ROTARY_BASE = 10000.0
MASKED_SCORE = -1e+30

@jax.custom_vjp
def low(v):
    return lax.optimization_barrier(v.astype(jnp.bfloat16)).astype(jnp.float32)

@jax.custom_vjp
def low_back(v):
    return v

def low_keep(v):
    return (low(v), None)

def low_pass(kept, grad):
    return (grad,)

def back_keep(v):
    return (v, None)

def back_low(kept, grad):
    return (low(grad),)
low.defvjp(low_keep, low_pass)
low_back.defvjp(back_keep, back_low)

def matmul(left, right):
    return jnp.dot(left, right, precision=lax.Precision.HIGHEST, preferred_element_type=jnp.float32)

def rms_scale(inputs, gain):
    return inputs * lax.rsqrt(lax.optimization_barrier(jnp.mean(inputs * inputs, axis=-1, keepdims=True)) + EPSILON) * gain

def rotate(inputs, cosine, sine_part):
    half_width = inputs.shape[-1] // 2
    first_half = inputs[..., :half_width]
    second_half = inputs[..., half_width:]
    return jnp.concatenate([first_half * cosine - second_half * sine_part, second_half * cosine + first_half * sine_part], axis=-1)

def adam_update(weight, first_moment, second_moment, gradient, rate, decay):
    first_new = BETA_ONE * first_moment + (1.0 - BETA_ONE) * gradient
    second_new = BETA_TWO * second_moment + (1.0 - BETA_TWO) * gradient * gradient
    ratio = first_new / (1.0 - BETA_ONE ** STEP) / (jnp.sqrt(second_new / (1.0 - BETA_TWO ** STEP)) + ADAM_EPSILON)
    return (weight - rate * (ratio + decay * weight), first_new, second_new)

def one_head(allowed, head_inputs):
    queries, key_states, value_states = head_inputs
    products = low_back(matmul(queries, key_states.T))
    scores = jnp.where(allowed, products * HD ** (-0.5), MASKED_SCORE)
    row_top = jnp.floor(lax.optimization_barrier(jnp.max(scores, axis=-1, keepdims=True)))
    exponent = jnp.exp(scores - row_top)
    weight_sum = lax.optimization_barrier(jnp.sum(exponent, axis=-1, keepdims=True))
    summed = low_back(matmul(low(exponent), value_states))
    return summed / weight_sum

def layer(tokens, query_weight, key_weight, value_weight, output_weight, gate_weight, up_weight, down_weight, norm_gains, head_gains, cosine, sine_part):
    length = tokens.shape[0]
    copies = N_WIDE // KVH
    group_heads = QH // N_WIDE
    normed = low(rms_scale(tokens, norm_gains[0]))
    queries = low_back(matmul(normed, low(query_weight))).reshape(length, QH, HD).transpose(1, 0, 2)
    key_states = matmul(normed, low(key_weight)).reshape(length, KVH, HD).transpose(1, 0, 2)
    key_states = low_back(jnp.repeat(key_states, copies, axis=0))
    value_states = matmul(normed, low(value_weight)).reshape(length, KVH, HD).transpose(1, 0, 2)
    value_states = low(low_back(jnp.repeat(value_states, copies, axis=0)))
    queries = low(rotate(rms_scale(queries, head_gains[0]), cosine, sine_part))
    key_states = low(rotate(rms_scale(key_states, head_gains[1]), cosine, sine_part))
    key_states = jnp.repeat(key_states, group_heads, axis=0)
    value_states = jnp.repeat(value_states, group_heads, axis=0)
    row_numbers = jnp.arange(length)
    allowed = row_numbers[:, None] >= row_numbers[None, :]
    attended = lax.map(jax.checkpoint(partial(one_head, allowed)), (queries, key_states, value_states))
    attended = low(low_back(attended.transpose(1, 0, 2).reshape(length, QH * HD)))
    middle = tokens + low_back(matmul(attended, low(output_weight)))
    normed_mid = low(rms_scale(middle, norm_gains[1]))
    gate_pre = low_back(matmul(normed_mid, low(gate_weight)))
    upward = low_back(matmul(normed_mid, low(up_weight)))
    hidden = low(low_back(jax.nn.silu(gate_pre) * upward))
    return middle + matmul(hidden, low(down_weight))

def reference(tokens_in, out_grad, positions, query_weight, query_first, query_second, key_weight, key_first, key_second, value_weight, value_first, value_second, output_weight, output_first, output_second, gate_weight, gate_first, gate_second, up_weight, up_first, up_second, down_weight, down_first, down_second, norm_gains, norm_first, norm_second, head_gains, head_first, head_second):
    sequences = TOKENS // SEQ_LEN
    inverse = jnp.power(ROTARY_BASE, -2.0 * jnp.arange(HD // 2, dtype=jnp.float32) / HD)
    angles = positions.reshape(sequences, SEQ_LEN).astype(jnp.float32)[:, :, None] * inverse
    weights = (query_weight, key_weight, value_weight, output_weight, gate_weight, up_weight, down_weight, norm_gains, head_gains)

    def one_sequence(totals, inputs):
        tokens_seq, cotangent, angle_seq = inputs
        cosine = jnp.cos(angle_seq)
        sine_part = jnp.sin(angle_seq)
        result, pullback = jax.vjp(lambda tokens_part, *params: layer(tokens_part, *params, cosine, sine_part), tokens_seq.astype(jnp.float32), *weights)
        gradients = pullback(cotangent.astype(jnp.float32))
        totals = jax.tree.map(jnp.add, totals, tuple(gradients[1:]))
        return (totals, (result.astype(jnp.bfloat16), gradients[0]))
    zeros_start = jax.tree.map(jnp.zeros_like, weights)
    totals, (outputs, input_grads) = lax.scan(one_sequence, zeros_start, (tokens_in.reshape(sequences, SEQ_LEN, D), out_grad.reshape(sequences, SEQ_LEN, D), angles))
    wide_rate = D ** (-0.5)
    query_new = adam_update(query_weight, query_first, query_second, totals[0], wide_rate, WEIGHT_DECAY)
    key_new = adam_update(key_weight, key_first, key_second, totals[1], wide_rate, WEIGHT_DECAY)
    value_new = adam_update(value_weight, value_first, value_second, totals[2], wide_rate, WEIGHT_DECAY)
    output_new = adam_update(output_weight, output_first, output_second, totals[3], O_FAN ** (-0.5), WEIGHT_DECAY)
    gate_new = adam_update(gate_weight, gate_first, gate_second, totals[4], wide_rate, WEIGHT_DECAY)
    up_new = adam_update(up_weight, up_first, up_second, totals[5], wide_rate, WEIGHT_DECAY)
    down_new = adam_update(down_weight, down_first, down_second, totals[6], FF ** (-0.5), WEIGHT_DECAY)
    norm_new = adam_update(norm_gains, norm_first, norm_second, totals[7], GAIN_RATE, 0.0)
    head_new = adam_update(head_gains, head_first, head_second, totals[8], GAIN_RATE, 0.0)
    return (outputs.reshape(TOKENS, D), input_grads.reshape(TOKENS, D), query_new[0], query_new[1], query_new[2], key_new[0], key_new[1], key_new[2], value_new[0], value_new[1], value_new[2], output_new[0], output_new[1], output_new[2], gate_new[0], gate_new[1], gate_new[2], up_new[0], up_new[1], up_new[2], down_new[0], down_new[1], down_new[2], norm_new[0], norm_new[1], norm_new[2], head_new[0], head_new[1], head_new[2])
```

```python
import functools
import math

import jax
import jax.numpy as jnp
from jax import lax
from jax.experimental import pallas as pl
from jax.experimental.pallas import tpu as pltpu
from jax.sharding import PartitionSpec as P

D = 2048
FF = 8192
SEQ_LEN = 4096
STEP = 10
O_FAN = 50


EPSILON = 1e-06
BETA_ONE = 0.9
BETA_TWO = 0.95
ADAM_EPSILON = 1e-08
WEIGHT_DECAY = 0.1
GAIN_RATE = 1.0
ROTARY_BASE = 10000.0
MASKED_SCORE = -1e30


def rms_scale(inputs, gain):
    return inputs * lax.rsqrt(jnp.mean(inputs * inputs, axis=-1, keepdims=True) + EPSILON) * gain


def rotate(inputs, cosine, sine_part):
    half_width = inputs.shape[-1] // 2
    first_half = inputs[..., :half_width]
    second_half = inputs[..., half_width:]
    return jnp.concatenate(
        [
            first_half * cosine - second_half * sine_part,
            second_half * cosine + first_half * sine_part,
        ],
        axis=-1,
    )


def adam_update(weight, first_moment, second_moment, gradient, rate, decay):
    first_new = BETA_ONE * first_moment + (1.0 - BETA_ONE) * gradient
    second_new = BETA_TWO * second_moment + (1.0 - BETA_TWO) * gradient * gradient
    ratio = (
        first_new
        / (1.0 - BETA_ONE**STEP)
        / (jnp.sqrt(second_new / (1.0 - BETA_TWO**STEP)) + ADAM_EPSILON)
    )
    return (weight - rate * (ratio + decay * weight), first_new, second_new)


def dot_last(left, right):
    return jnp.dot(left, right, preferred_element_type=jnp.float32)


def dot_first(left, right):
    return lax.dot_general(
        left, right, (((0,), (0,)), ((), ())), preferred_element_type=jnp.float32
    )


def dot_back(left, right):
    return lax.dot_general(
        left, right, (((1,), (1,)), ((), ())), preferred_element_type=jnp.float32
    )


LOG2E = math.log2(math.e)

def nt(a, b):
    return lax.dot_general(a, b, (((1,), (1,)), ((), ())), preferred_element_type=jnp.float32)
def tn(a, b):
    return lax.dot_general(a, b, (((0,), (0,)), ((), ())), preferred_element_type=jnp.float32)
def nn(a, b):
    return jnp.dot(a, b, preferred_element_type=jnp.float32)

def low_lanes(rows):
    return lax.broadcasted_iota(jnp.int32, (rows, 128), 1) < 64

def attend_kernel(block, heads, q_ref, kv_ref, o_ref, s_ref, kk_ref, va_ref, vb_ref, acc_ref):
    total = q_ref.shape[0]
    low = low_lanes(block)

    @pl.loop(0, total // block)
    def _(j):
        rows = pl.ds(pl.multiple_of(j * block, block), block)
        kv = kv_ref[rows, :]
        vk = jnp.concatenate([kv[:, 64:], kv[:, :64]], axis=1)
        one = jnp.ones_like(kv)
        kk_ref[rows, :] = jnp.where(low, kv, vk)
        va_ref[rows, :] = jnp.where(low, vk, one)
        vb_ref[rows, :] = jnp.where(low, one, kv)

    causal = lax.broadcasted_iota(jnp.int32, (block, block), 0) >= lax.broadcasted_iota(
        jnp.int32, (block, block), 1
    )

    @pl.loop(0, total // block)
    def _(i):
        rows = pl.ds(pl.multiple_of(i * block, block), block)
        for pair in range(heads // 2):
            lanes = pl.ds(pair * 128, 128)
            both = q_ref[rows, lanes]
            zero = jnp.zeros_like(both)
            sides = (jnp.where(low, both, zero), jnp.where(low, zero, both))

            def step(j, diagonal):
                keys = pl.ds(pl.multiple_of(j * block, block), block)
                kk = kk_ref[keys, :]
                for side in range(2):
                    weights = jnp.exp2(nt(sides[side], kk))
                    if diagonal:
                        weights = jnp.where(causal, weights, 0.0)
                    part = nn(weights.astype(jnp.bfloat16), (va_ref, vb_ref)[side][keys, :])
                    if diagonal:
                        acc_ref[side] = part
                    else:
                        acc_ref[side] += part

            step(i, True)

            @pl.loop(0, i)
            def _(j):
                step(j, False)

            first, second = acc_ref[0], acc_ref[1]
            summed = jnp.where(low, first, second)
            sums = jnp.where(low, second, first)
            sums = jnp.concatenate([sums[:, 64:], sums[:, :64]], axis=1)
            o_ref[rows, lanes] = summed / sums
            s_ref[rows, lanes] = sums

def attend(q, kv, heads, block=512):
    total = q.shape[0]
    cost = heads * total * total // 2
    return pl.pallas_call(
        functools.partial(attend_kernel, block, heads),
        out_shape=[jax.ShapeDtypeStruct(q.shape, jnp.float32), jax.ShapeDtypeStruct(q.shape, jnp.float32)],
        in_specs=[pl.BlockSpec(memory_space=pltpu.VMEM)] * 2,
        out_specs=[pl.BlockSpec(memory_space=pltpu.VMEM)] * 2,
        scratch_shapes=[pltpu.VMEM((total, 128), jnp.bfloat16)] * 3 + [pltpu.VMEM((2, block, 128), jnp.float32)],
        compiler_params=pltpu.CompilerParams(vmem_limit_bytes=56 << 20),
        cost_estimate=pl.CostEstimate(flops=4 * cost * 256, bytes_accessed=12 * q.size, transcendentals=cost),
        name="attend",
    )(q, kv)

def back_kernel(block, heads, q_ref, g_ref, d_ref, kv_ref, dq_ref, dkv_ref, kk_ref, vv_ref, ka_ref, kb_ref):
    total = q_ref.shape[0]
    low = low_lanes(block)
    count = total // block

    @pl.loop(0, count)
    def _(j):
        rows = pl.ds(pl.multiple_of(j * block, block), block)
        kv = kv_ref[rows, :]
        vk = jnp.concatenate([kv[:, 64:], kv[:, :64]], axis=1)
        zero = jnp.zeros_like(kv)
        kk_ref[rows, :] = jnp.where(low, kv, vk)
        vv_ref[rows, :] = jnp.where(low, vk, kv)
        ka_ref[rows, :] = jnp.where(low, kv, zero)
        kb_ref[rows, :] = jnp.where(low, zero, vk)
        dkv_ref[0, rows, :] = jnp.zeros((block, 128), jnp.float32)
        dkv_ref[1, rows, :] = jnp.zeros((block, 128), jnp.float32)

    causal = lax.broadcasted_iota(jnp.int32, (block, block), 0) <= lax.broadcasted_iota(
        jnp.int32, (block, block), 1
    )

    @pl.loop(0, count)
    def _(i):
        rows = pl.ds(pl.multiple_of(i * block, block), block)
        for pair in range(heads // 2):
            lanes = pl.ds(pair * 128, 128)
            qboth = q_ref[rows, lanes]
            gboth = g_ref[rows, lanes]
            zero = jnp.zeros_like(qboth)
            qs = (jnp.where(low, qboth, zero), jnp.where(low, zero, qboth))
            gs = (jnp.where(low, gboth, zero), jnp.where(low, zero, gboth))

            def step(j, diagonal):
                keys = pl.ds(pl.multiple_of(j * block, block), block)
                kk = kk_ref[keys, :]
                vv = vv_ref[keys, :]
                for side in range(2):
                    weights = jnp.exp2(nt(kk, qs[side]))
                    if diagonal:
                        weights = jnp.where(causal, weights, 0.0)
                    dots = d_ref[pl.ds(pair * 2 + side, 1), rows]
                    grads = (weights * (nt(vv, gs[side]) - dots)).astype(jnp.bfloat16)
                    dkv_ref[1, keys, :] += nn(weights.astype(jnp.bfloat16), gs[side])
                    dkv_ref[0, keys, :] += nn(grads, qs[side])
                    part = tn(grads, (ka_ref, kb_ref)[side][keys, :])
                    if diagonal and side == 0:
                        dq_ref[rows, lanes] = part
                    else:
                        dq_ref[rows, lanes] += part

            step(i, True)

            @pl.loop(0, i)
            def _(j):
                step(j, False)

def attend_back(q, g, dots, kv, heads, block=512):
    total = q.shape[0]
    cost = heads * total * total // 2
    return pl.pallas_call(
        functools.partial(back_kernel, block, heads),
        out_shape=[jax.ShapeDtypeStruct(q.shape, jnp.float32), jax.ShapeDtypeStruct((2, total, 128), jnp.float32)],
        in_specs=[pl.BlockSpec(memory_space=pltpu.VMEM)] * 4,
        out_specs=[pl.BlockSpec(memory_space=pltpu.VMEM)] * 2,
        scratch_shapes=[pltpu.VMEM((total, 128), jnp.bfloat16)] * 4,
        compiler_params=pltpu.CompilerParams(vmem_limit_bytes=56 << 20),
        cost_estimate=pl.CostEstimate(flops=10 * cost * 256, bytes_accessed=12 * q.size, transcendentals=cost),
        name="attend_back",
    )(q, g, dots, kv)


def gather_rows(shard):
    return lax.all_gather(shard, "wide", axis=0, tiled=True)


def sum_back(pairs, row_count):
    summed = jnp.zeros((row_count * lax.axis_size("wide"), pairs[0][1].shape[0]), jnp.float32)
    for gradient, weight in pairs:
        summed = summed + dot_back(gradient, weight)
    return lax.psum_scatter(
        summed.astype(jnp.bfloat16), "wide", scatter_dimension=0, tiled=True
    ).astype(jnp.float32)


def shards(
    tokens_in,
    out_grad,
    positions,
    query_weight,
    query_first,
    query_second,
    key_weight,
    key_first,
    key_second,
    value_weight,
    value_first,
    value_second,
    output_weight,
    output_first,
    output_second,
    gate_weight,
    gate_first,
    gate_second,
    up_weight,
    up_first,
    up_second,
    down_weight,
    down_first,
    down_second,
    norm_gains,
    norm_first,
    norm_second,
    head_gains,
    head_first,
    head_second,
):
    wide_count = lax.axis_size("wide")
    wide_rank = lax.axis_index("wide")
    head_dim = head_gains.shape[1]
    key_heads = key_weight.shape[1] // head_dim
    local_heads = query_weight.shape[1] // head_dim
    shard_rows = tokens_in.shape[0]
    copies = wide_count // key_heads
    key_slot = wide_rank // copies
    key_own = lax.dynamic_slice_in_dim(key_weight, key_slot * head_dim, head_dim, 1)
    value_own = lax.dynamic_slice_in_dim(value_weight, key_slot * head_dim, head_dim, 1)
    query_columns = query_weight.shape[1]
    input_full = lax.all_gather(
        jnp.concatenate([query_weight, key_own, value_own], axis=1).astype(jnp.bfloat16),
        "narrow", axis=0, tiled=True,
    )
    output_local, gate_local, up_local, down_local = (
        lax.all_gather(output_weight.astype(jnp.bfloat16), "narrow", axis=1, tiled=True),
        lax.all_gather(gate_weight.astype(jnp.bfloat16), "narrow", axis=0, tiled=True),
        lax.all_gather(up_weight.astype(jnp.bfloat16), "narrow", axis=0, tiled=True),
        lax.all_gather(down_weight.astype(jnp.bfloat16), "narrow", axis=1, tiled=True),
    )
    inverse = jnp.power(ROTARY_BASE, -2.0 * jnp.arange(head_dim // 2, dtype=jnp.float32) / head_dim)
    angles = positions.astype(jnp.float32)[:, None] * inverse[None, :]
    cosine = jnp.cos(angles)
    sine_part = jnp.sin(angles)
    residual = tokens_in.astype(jnp.float32)
    normed_in, norm_in_back = jax.vjp(rms_scale, residual, norm_gains[0])
    rows_in = gather_rows(normed_in.astype(jnp.bfloat16))
    total_rows = rows_in.shape[0]
    model_width = rows_in.shape[1]
    input_raw = dot_last(rows_in, input_full)
    query_raw = input_raw[:, :query_columns].reshape(total_rows, local_heads, head_dim)
    key_raw = input_raw[:, query_columns : query_columns + head_dim]
    value_rows = input_raw[:, query_columns + head_dim :].astype(jnp.bfloat16)

    def query_turn(raw_heads, gain):
        return rotate(rms_scale(raw_heads, gain), cosine[:, None, :], sine_part[:, None, :])

    def key_turn(raw_heads, gain):
        return rotate(rms_scale(raw_heads, gain), cosine, sine_part)

    query_rot, query_back = jax.vjp(query_turn, query_raw, head_gains[0])
    key_rot, key_back = jax.vjp(key_turn, key_raw, head_gains[1])
    score_scale = head_dim ** (-0.5)
    query_rot = (
        (query_rot * (score_scale * LOG2E))
        .reshape(total_rows, local_heads * head_dim)
        .astype(jnp.bfloat16)
    )
    key_values = jnp.concatenate([key_rot.astype(jnp.bfloat16), value_rows], axis=1)
    attended, weight_sums = attend(query_rot, key_values, local_heads)
    attended_low = attended.astype(jnp.bfloat16)
    branch = lax.psum_scatter(
        dot_last(attended_low, output_local).astype(jnp.bfloat16),
        "wide",
        scatter_dimension=0,
        tiled=True,
    ).astype(jnp.float32)
    middle = residual + branch
    normed_mid, norm_mid_back = jax.vjp(rms_scale, middle, norm_gains[1])
    rows_mid = gather_rows(normed_mid.astype(jnp.bfloat16))
    gate_pre = dot_last(rows_mid, gate_local)
    up_pre = dot_last(rows_mid, up_local)
    hidden, hidden_back = jax.vjp(
        lambda gate_in, up_in: jax.nn.silu(gate_in) * up_in, gate_pre, up_pre
    )
    hidden_low = hidden.astype(jnp.bfloat16)
    block_out = (
        middle
        + lax.psum_scatter(
            dot_last(hidden_low, down_local).astype(jnp.bfloat16),
            "wide",
            scatter_dimension=0,
            tiled=True,
        ).astype(jnp.float32)
    ).astype(jnp.bfloat16)
    grad_rows = lax.all_gather(out_grad, "wide", axis=0, tiled=True)
    hidden_grad = dot_back(grad_rows, down_local).astype(jnp.bfloat16)
    down_grad = dot_first(hidden_low, grad_rows)
    gate_grad, up_grad = hidden_back(hidden_grad.astype(jnp.float32))
    gate_grad = gate_grad.astype(jnp.bfloat16)
    up_grad = up_grad.astype(jnp.bfloat16)
    gate_wgrad = dot_first(rows_mid, gate_grad)
    up_wgrad = dot_first(rows_mid, up_grad)
    mid_back = sum_back(((gate_grad, gate_local), (up_grad, up_local)), shard_rows)
    middle_part, mid_gain_grad = norm_mid_back(mid_back)
    middle_grad = out_grad.astype(jnp.float32) + middle_part
    branch_grad = middle_grad.astype(jnp.bfloat16)
    branch_rows = lax.all_gather(branch_grad, "wide", axis=0, tiled=True)
    attended_grad = dot_back(branch_rows, output_local).astype(jnp.bfloat16)
    output_wgrad = dot_first(attended_low, branch_rows)
    head_grad = attended_grad.astype(jnp.float32) / weight_sums
    scaled_grad = head_grad.astype(jnp.bfloat16)
    grad_dot = jnp.sum(
        (head_grad * attended).reshape(total_rows, local_heads, head_dim), axis=-1
    ).T
    query_rot_grad, key_value_grad = attend_back(
        query_rot, scaled_grad, grad_dot, key_values, local_heads
    )
    query_rot_grad = query_rot_grad.reshape(total_rows, local_heads, head_dim) * score_scale
    key_value_grad = key_value_grad[:, :, :head_dim] + key_value_grad[:, :, head_dim:]
    key_rot_grad = key_value_grad[0] * (1.0 / LOG2E)
    value_grad = key_value_grad[1]
    query_raw_grad, query_gain_grad = query_back(query_rot_grad)
    key_raw_grad, key_gain_grad = key_back(key_rot_grad)
    input_low = jnp.concatenate(
        [
            query_raw_grad.reshape(total_rows, local_heads * head_dim).astype(jnp.bfloat16),
            key_raw_grad.astype(jnp.bfloat16),
            value_grad.astype(jnp.bfloat16),
        ],
        axis=1,
    )
    input_wgrad = dot_first(rows_in, input_low)
    input_back = sum_back(((input_low, input_full),), shard_rows)
    input_part, in_gain_grad = norm_in_back(input_back)
    input_grad = middle_grad + input_part
    gain_stack = jnp.stack([in_gain_grad, mid_gain_grad])
    head_stack = jnp.stack([query_gain_grad, key_gain_grad])
    gain_total, head_total = lax.psum((gain_stack, head_stack), ("narrow", "wide"))
    input_total = lax.psum_scatter(
        input_wgrad.astype(jnp.bfloat16), "narrow", scatter_dimension=0, tiled=True
    )
    query_total = input_total[:, :query_columns].astype(jnp.float32)
    spread = lax.all_gather(input_total[:, query_columns:], "wide", axis=0)
    spread = jnp.sum(
        spread.reshape(key_heads, copies, -1, 2, head_dim).astype(jnp.float32), axis=1
    ).transpose(2, 1, 0, 3)
    key_total = spread[0].reshape(key_weight.shape)
    value_total = spread[1].reshape(value_weight.shape)
    output_total, gate_total, up_total, down_total = (
        lax.psum_scatter(
            output_wgrad.astype(jnp.bfloat16), "narrow", scatter_dimension=1, tiled=True
        ).astype(jnp.float32),
        lax.psum_scatter(
            gate_wgrad.astype(jnp.bfloat16), "narrow", scatter_dimension=0, tiled=True
        ).astype(jnp.float32),
        lax.psum_scatter(
            up_wgrad.astype(jnp.bfloat16), "narrow", scatter_dimension=0, tiled=True
        ).astype(jnp.float32),
        lax.psum_scatter(
            down_grad.astype(jnp.bfloat16), "narrow", scatter_dimension=1, tiled=True
        ).astype(jnp.float32),
    )
    wide_rate = D ** (-0.5)
    query_new = adam_update(
        query_weight, query_first, query_second, query_total, wide_rate, WEIGHT_DECAY
    )
    key_new = adam_update(key_weight, key_first, key_second, key_total, wide_rate, WEIGHT_DECAY)
    value_new = adam_update(
        value_weight, value_first, value_second, value_total, wide_rate, WEIGHT_DECAY
    )
    output_new = adam_update(
        output_weight, output_first, output_second, output_total, O_FAN ** (-0.5), WEIGHT_DECAY
    )
    gate_new = adam_update(
        gate_weight, gate_first, gate_second, gate_total, wide_rate, WEIGHT_DECAY
    )
    up_new = adam_update(up_weight, up_first, up_second, up_total, wide_rate, WEIGHT_DECAY)
    down_new = adam_update(
        down_weight, down_first, down_second, down_total, FF ** (-0.5), WEIGHT_DECAY
    )
    norm_new = adam_update(norm_gains, norm_first, norm_second, gain_total, GAIN_RATE, 0.0)
    head_new = adam_update(head_gains, head_first, head_second, head_total, GAIN_RATE, 0.0)
    return (
        block_out,
        input_grad,
        query_new[0],
        query_new[1],
        query_new[2],
        key_new[0],
        key_new[1],
        key_new[2],
        value_new[0],
        value_new[1],
        value_new[2],
        output_new[0],
        output_new[1],
        output_new[2],
        gate_new[0],
        gate_new[1],
        gate_new[2],
        up_new[0],
        up_new[1],
        up_new[2],
        down_new[0],
        down_new[1],
        down_new[2],
        norm_new[0],
        norm_new[1],
        norm_new[2],
        head_new[0],
        head_new[1],
        head_new[2],
    )


def solution(mesh):
    return jax.shard_map(
        shards,
        mesh=mesh,
        in_specs=(
            P(("narrow", "wide"), None),
            P(("narrow", "wide"), None),
            P("narrow"),
            P("narrow", "wide"),
            P("narrow", "wide"),
            P("narrow", "wide"),
            P("narrow", None),
            P("narrow", None),
            P("narrow", None),
            P("narrow", None),
            P("narrow", None),
            P("narrow", None),
            P("wide", "narrow"),
            P("wide", "narrow"),
            P("wide", "narrow"),
            P("narrow", "wide"),
            P("narrow", "wide"),
            P("narrow", "wide"),
            P("narrow", "wide"),
            P("narrow", "wide"),
            P("narrow", "wide"),
            P("wide", "narrow"),
            P("wide", "narrow"),
            P("wide", "narrow"),
            P(),
            P(),
            P(),
            P(),
            P(),
            P(),
        ),
        out_specs=(
            P(("narrow", "wide"), None),
            P(("narrow", "wide"), None),
            P("narrow", "wide"),
            P("narrow", "wide"),
            P("narrow", "wide"),
            P("narrow", None),
            P("narrow", None),
            P("narrow", None),
            P("narrow", None),
            P("narrow", None),
            P("narrow", None),
            P("wide", "narrow"),
            P("wide", "narrow"),
            P("wide", "narrow"),
            P("narrow", "wide"),
            P("narrow", "wide"),
            P("narrow", "wide"),
            P("narrow", "wide"),
            P("narrow", "wide"),
            P("narrow", "wide"),
            P("wide", "narrow"),
            P("wide", "narrow"),
            P("wide", "narrow"),
            P(),
            P(),
            P(),
            P(),
            P(),
            P(),
        ),
        check_vma=False,
    )
```

```python
import functools
import math

import jax
import jax.numpy as jnp
from jax import lax
from jax.experimental import pallas as pl
from jax.experimental.pallas import tpu as pltpu
from jax.sharding import PartitionSpec as P

D = 2048
FF = 8192
SEQ_LEN = 4096
STEP = 10
O_FAN = 50


EPSILON = 1e-06
BETA_ONE = 0.9
BETA_TWO = 0.95
ADAM_EPSILON = 1e-08
WEIGHT_DECAY = 0.1
GAIN_RATE = 1.0
ROTARY_BASE = 10000.0
MASKED_SCORE = -1e30


def rms_scale(inputs, gain):
    return inputs * lax.rsqrt(jnp.mean(inputs * inputs, axis=-1, keepdims=True) + EPSILON) * gain


def rotate(inputs, cosine, sine_part):
    half_width = inputs.shape[-1] // 2
    first_half = inputs[..., :half_width]
    second_half = inputs[..., half_width:]
    return jnp.concatenate(
        [
            first_half * cosine - second_half * sine_part,
            second_half * cosine + first_half * sine_part,
        ],
        axis=-1,
    )


def adam_update(weight, first_moment, second_moment, gradient, rate, decay):
    first_new = BETA_ONE * first_moment + (1.0 - BETA_ONE) * gradient
    second_new = BETA_TWO * second_moment + (1.0 - BETA_TWO) * gradient * gradient
    ratio = (
        first_new
        / (1.0 - BETA_ONE**STEP)
        / (jnp.sqrt(second_new / (1.0 - BETA_TWO**STEP)) + ADAM_EPSILON)
    )
    return (weight - rate * (ratio + decay * weight), first_new, second_new)


def dot_last(left, right):
    return jnp.dot(left, right, preferred_element_type=jnp.float32)


def dot_first(left, right):
    return lax.dot_general(
        left, right, (((0,), (0,)), ((), ())), preferred_element_type=jnp.float32
    )


def dot_back(left, right):
    return lax.dot_general(
        left, right, (((1,), (1,)), ((), ())), preferred_element_type=jnp.float32
    )


LOG2E = math.log2(math.e)

def nt(a, b):
    return lax.dot_general(a, b, (((1,), (1,)), ((), ())), preferred_element_type=jnp.float32)
def tn(a, b):
    return lax.dot_general(a, b, (((0,), (0,)), ((), ())), preferred_element_type=jnp.float32)
def nn(a, b):
    return jnp.dot(a, b, preferred_element_type=jnp.float32)

def low_lanes(rows):
    return lax.broadcasted_iota(jnp.int32, (rows, 128), 1) < 64

def attend_kernel(block, heads, q_ref, o_ref, s_ref, low_ref, kk_ref, va_ref, vb_ref, acc_ref):
    total = q_ref.shape[0]
    low = low_lanes(block)

    @pl.loop(0, total // block)
    def _(j):
        rows = pl.ds(pl.multiple_of(j * block, block), block)
        kv = q_ref[rows, pl.ds(heads * 64, 128)]
        vk = jnp.concatenate([kv[:, 64:], kv[:, :64]], axis=1)
        one = jnp.ones_like(kv)
        kk_ref[rows, :] = jnp.where(low, kv, vk)
        va_ref[rows, :] = jnp.where(low, vk, one)
        vb_ref[rows, :] = jnp.where(low, one, kv)

    causal = lax.broadcasted_iota(jnp.int32, (block, block), 0) >= lax.broadcasted_iota(
        jnp.int32, (block, block), 1
    )

    @pl.loop(0, total // block)
    def _(i):
        rows = pl.ds(pl.multiple_of(i * block, block), block)
        for pair in range(heads // 2):
            lanes = pl.ds(pair * 128, 128)
            both = q_ref[rows, lanes]
            zero = jnp.zeros_like(both)
            sides = (jnp.where(low, both, zero), jnp.where(low, zero, both))

            def step(j, diagonal):
                keys = pl.ds(pl.multiple_of(j * block, block), block)
                kk = kk_ref[keys, :]
                for side in range(2):
                    weights = jnp.exp2(nt(sides[side], kk))
                    if diagonal:
                        weights = jnp.where(causal, weights, 0.0)
                    part = nn(weights.astype(jnp.bfloat16), (va_ref, vb_ref)[side][keys, :])
                    if diagonal:
                        acc_ref[side] = part
                    else:
                        acc_ref[side] += part

            step(i, True)

            @pl.loop(0, i)
            def _(j):
                step(j, False)

            first, second = acc_ref[0], acc_ref[1]
            summed = jnp.where(low, first, second)
            sums = jnp.where(low, second, first)
            sums = jnp.concatenate([sums[:, 64:], sums[:, :64]], axis=1)
            result = summed / sums
            o_ref[rows, lanes] = result
            s_ref[rows, lanes] = sums
            low_ref[rows, lanes] = result.astype(jnp.bfloat16)

def attend(packed, heads, block=512):
    total = packed.shape[0]
    shape = (total, heads * 64)
    cost = heads * total * total // 2
    return pl.pallas_call(
        functools.partial(attend_kernel, block, heads),
        out_shape=[
            jax.ShapeDtypeStruct(shape, jnp.float32),
            jax.ShapeDtypeStruct(shape, jnp.float32),
            jax.ShapeDtypeStruct(shape, jnp.bfloat16),
        ],
        in_specs=[pl.BlockSpec(memory_space=pltpu.VMEM)],
        out_specs=[pl.BlockSpec(memory_space=pltpu.VMEM)] * 3,
        scratch_shapes=[pltpu.VMEM((total, 128), jnp.bfloat16)] * 3 + [pltpu.VMEM((2, block, 128), jnp.float32)],
        compiler_params=pltpu.CompilerParams(vmem_limit_bytes=56 << 20),
        cost_estimate=pl.CostEstimate(flops=4 * cost * 256, bytes_accessed=12 * packed.size, transcendentals=cost),
        name="attend",
    )(packed)

def back_kernel(block, heads, q_ref, g_ref, d_ref, out_ref, dq_ref, dkv_ref, kk_ref, vv_ref, ka_ref, kb_ref):
    total = q_ref.shape[0]
    low = low_lanes(block)
    count = total // block

    @pl.loop(0, count)
    def _(j):
        rows = pl.ds(pl.multiple_of(j * block, block), block)
        kv = q_ref[rows, pl.ds(heads * 64, 128)]
        vk = jnp.concatenate([kv[:, 64:], kv[:, :64]], axis=1)
        zero = jnp.zeros_like(kv)
        kk_ref[rows, :] = jnp.where(low, kv, vk)
        vv_ref[rows, :] = jnp.where(low, vk, kv)
        ka_ref[rows, :] = jnp.where(low, kv, zero)
        kb_ref[rows, :] = jnp.where(low, zero, vk)
        dkv_ref[0, rows, :] = jnp.zeros((block, 128), jnp.float32)
        dkv_ref[1, rows, :] = jnp.zeros((block, 128), jnp.float32)

    causal = lax.broadcasted_iota(jnp.int32, (block, block), 0) <= lax.broadcasted_iota(
        jnp.int32, (block, block), 1
    )

    @pl.loop(0, count)
    def _(i):
        rows = pl.ds(pl.multiple_of(i * block, block), block)
        for pair in range(heads // 2):
            lanes = pl.ds(pair * 128, 128)
            qboth = q_ref[rows, lanes]
            gboth = g_ref[rows, lanes]
            zero = jnp.zeros_like(qboth)
            qs = (jnp.where(low, qboth, zero), jnp.where(low, zero, qboth))
            gs = (jnp.where(low, gboth, zero), jnp.where(low, zero, gboth))

            def step(j, diagonal):
                keys = pl.ds(pl.multiple_of(j * block, block), block)
                kk = kk_ref[keys, :]
                vv = vv_ref[keys, :]
                for side in range(2):
                    weights = jnp.exp2(nt(kk, qs[side]))
                    if diagonal:
                        weights = jnp.where(causal, weights, 0.0)
                    dots = d_ref[pl.ds(pair * 2 + side, 1), rows]
                    grads = (weights * (nt(vv, gs[side]) - dots)).astype(jnp.bfloat16)
                    dkv_ref[1, keys, :] += nn(weights.astype(jnp.bfloat16), gs[side])
                    dkv_ref[0, keys, :] += nn(grads, qs[side])
                    part = tn(grads, (ka_ref, kb_ref)[side][keys, :])
                    if diagonal and side == 0:
                        dq_ref[:, lanes] = part
                    else:
                        dq_ref[:, lanes] += part

            step(i, True)

            @pl.loop(0, i)
            def _(j):
                step(j, False)

            out_ref[rows, lanes] = (dq_ref[:, lanes] * 0.125).astype(jnp.bfloat16)

    @pl.loop(0, count)
    def _(j):
        rows = pl.ds(pl.multiple_of(j * block, block), block)
        keys = dkv_ref[0, rows, :] * (1.0 / LOG2E)
        values = dkv_ref[1, rows, :]
        keys = keys + jnp.concatenate([keys[:, 64:], keys[:, :64]], axis=1)
        values = values + jnp.concatenate([values[:, 64:], values[:, :64]], axis=1)
        out_ref[rows, pl.ds(heads * 64, 128)] = jnp.where(low, keys, values).astype(jnp.bfloat16)

def attend_back(packed, g, dots, heads, block=512):
    total = packed.shape[0]
    cost = heads * total * total // 2
    return pl.pallas_call(
        functools.partial(back_kernel, block, heads),
        out_shape=jax.ShapeDtypeStruct(packed.shape, jnp.bfloat16),
        in_specs=[pl.BlockSpec(memory_space=pltpu.VMEM)] * 3,
        out_specs=pl.BlockSpec(memory_space=pltpu.VMEM),
        scratch_shapes=[
            pltpu.VMEM((block, heads * 64), jnp.float32),
            pltpu.VMEM((2, total, 128), jnp.float32),
        ]
        + [pltpu.VMEM((total, 128), jnp.bfloat16)] * 4,
        compiler_params=pltpu.CompilerParams(vmem_limit_bytes=56 << 20),
        cost_estimate=pl.CostEstimate(
            flops=10 * cost * 256, bytes_accessed=12 * packed.size, transcendentals=cost
        ),
        name="attend_back",
    )(packed, g, dots)


def remote(source, target, send, arrive, device):
    return pltpu.make_async_remote_copy(
        src_ref=source,
        dst_ref=target,
        send_sem=send,
        recv_sem=arrive,
        device_id=device,
        device_id_type=pl.DeviceIdType.MESH,
    )


def place():
    narrow = lax.axis_index("narrow")
    wide = lax.axis_index("wide")
    return narrow, wide, wide // 2, wide % 2


def greet_neighbours():
    narrow, wide, chip, core = place()
    barrier = pltpu.get_barrier_semaphore()

    def tell(device):
        pl.semaphore_signal(
            barrier, inc=1, device_id=device, device_id_type=pl.DeviceIdType.MESH
        )

    tell((narrow + 1 - 2 * (narrow % 2), wide))
    tell(((narrow + 2) % 4, wide))
    tell((narrow, 2 * chip + 1 - core))

    @pl.when(chip > 0)
    def _():
        tell((narrow, wide - 2))

    @pl.when(chip < 3)
    def _():
        tell((narrow, wide + 2))

    pl.semaphore_wait(barrier, 3 + jnp.minimum(chip, 1) + jnp.minimum(3 - chip, 1))


def gather_kernel(
    gate_ref, up_ref, down_ref, att_ref, grad_ref,
    gate_all, up_all, down_all, att_all, grad_all,
    own_sem, ffn_send, ffn_got, line_send, line_got, side_send, side_got,
    core_send, core_got, grad_send, grad_got, pair_send, pair_got,
):
    narrow, wide, chip, core = place()
    beside = narrow + 1 - 2 * (narrow % 2)
    across = (narrow + 2) % 4
    corner = (beside + 2) % 4
    rows = att_ref.shape[0]
    half_rows = rows // 2
    columns = down_ref.shape[1]
    other = (narrow, 2 * chip + 1 - core)
    left = (narrow, wide - 2)
    right = (narrow, wide + 2)
    sides = ((beside, wide), (across, wide))
    near = (beside, across)
    greet_neighbours()

    def ffn_own(k, who):
        if k == 2:
            return down_all.at[:, pl.ds(pl.multiple_of(who * columns, columns), columns)]
        return (gate_all, up_all)[k].at[who]

    def ffn_half(k, who, half):
        if k == 2:
            size = down_ref.shape[0] // 2
            return down_all.at[
                pl.ds(half * size, size), pl.ds(pl.multiple_of(who * columns, columns), columns)
            ]
        return (gate_all, up_all)[k].at[who, pl.ds(half * half_rows, half_rows), :]

    def att(slot, who):
        return att_all.at[slot, pl.ds(pl.multiple_of(who * rows, rows), rows), :]

    def att_half(slot, who, half):
        return att_all.at[
            slot, pl.ds(pl.multiple_of(who * rows + half * half_rows, half_rows), half_rows), :
        ]

    own = []
    for k, source in enumerate((gate_ref, up_ref, down_ref)):
        own.append(pltpu.make_async_copy(source, ffn_own(k, narrow), own_sem.at[k]))
    own.append(pltpu.make_async_copy(att_ref, att(wide, narrow), own_sem.at[3]))
    own.append(pltpu.make_async_copy(grad_ref, grad_all.at[wide], own_sem.at[4]))
    for copy in own:
        copy.start()

    def att_line(at, step, source):
        slot = 2 * at + core
        return remote(
            source, att(slot, narrow), line_send.at[at, (step + 1) // 2], line_got.at[at],
            right if step > 0 else left,
        )

    def grad_line(at, step, source):
        slot = 2 * at + core
        return remote(
            source, grad_all.at[slot], grad_send.at[at, (step + 1) // 2], grad_got.at[at],
            right if step > 0 else left,
        )

    def grad_pair(at, source):
        slot = 2 * at + core
        return remote(source, grad_all.at[slot], pair_send.at[at], pair_got.at[at], other)

    def both_ways(line, at, source_of, act):
        @pl.when(jnp.logical_and(at <= chip, chip < 3))
        def _():
            act(line(at, 1, source_of(at)))

        @pl.when(jnp.logical_and(at >= chip, chip > 0))
        def _():
            act(line(at, -1, source_of(at)))

    def att_side(at, k, source):
        slot = 2 * at + core
        return remote(source, att(slot, narrow), side_send.at[at, k], side_got.at[at, k], sides[k])

    def att_got(at, k):
        slot = 2 * at + core
        target = att(slot, near[k])
        return remote(target, target, side_send.at[at, k], side_got.at[at, k], sides[k])

    def att_forward(at, k):
        slot = 2 * at + core
        piece = att_half(slot, near[k], k)
        return remote(piece, piece, side_send.at[at, 2 + k], side_got.at[at, 2 + k], sides[1 - k])

    def att_corner(at, k):
        slot = 2 * at + core
        piece = att_half(slot, corner, k)
        return remote(piece, piece, side_send.at[at, 2 + k], side_got.at[at, 2 + k], sides[1 - k])

    def att_core(at, who):
        slot = 2 * at + core
        piece = att(slot, who)
        return remote(piece, piece, core_send.at[at, who], core_got.at[at, who], other)

    def att_core_got(at, who):
        slot = 2 * at + 1 - core
        piece = att(slot, who)
        return remote(piece, piece, core_send.at[at, who], core_got.at[at, who], other)

    def ffn_side(k, j):
        source = (gate_ref, up_ref, down_ref)[k]
        return remote(source, ffn_own(k, narrow), ffn_send.at[k, j], ffn_got.at[k, j], sides[j])

    def ffn_got_copy(k, j):
        target = ffn_own(k, near[j])
        return remote(target, target, ffn_send.at[k, j], ffn_got.at[k, j], sides[j])

    def ffn_forward(k, j):
        piece = ffn_half(k, near[j], j)
        return remote(piece, piece, ffn_send.at[k, 2 + j], ffn_got.at[k, 2 + j], sides[1 - j])

    def ffn_corner(k, j):
        piece = ffn_half(k, corner, j)
        return remote(piece, piece, ffn_send.at[k, 2 + j], ffn_got.at[k, 2 + j], sides[1 - j])

    start = lambda copy: copy.start()
    sent = lambda copy: copy.wait_send()
    got = lambda copy: copy.wait_recv()

    both_ways(att_line, chip, lambda at: att_ref, start)
    both_ways(grad_line, chip, lambda at: grad_ref, start)
    grad_pair(chip, grad_ref).start()
    for k in range(2):
        att_side(chip, k, att_ref).start()
    for k in range(3):
        for j in range(2):
            ffn_side(k, j).start()
    own[3].wait()
    att_core(chip, narrow).start()

    def att_hop(hop):
        for at, valid in ((chip - hop, chip >= hop), (chip + hop, chip + hop <= 3)):

            @pl.when(valid)
            def _():
                slot = 2 * at + core
                att_line(at, 1, att(slot, narrow)).wait_recv()
                both_ways(att_line, at, lambda at: att(2 * at + core, narrow), start)
                for k in range(2):
                    att_side(at, k, att(slot, narrow)).start()
                att_core(at, narrow).start()

    def ffn_step(k):
        for j in range(2):
            ffn_got_copy(k, j).wait_recv()
            ffn_forward(k, j).start()

    def grad_step(hop):
        for at, valid in ((chip - hop, chip >= hop), (chip + hop, chip + hop <= 3)):

            @pl.when(valid)
            def _():
                slot = 2 * at + core
                grad_line(at, 1, grad_all.at[slot]).wait_recv()
                both_ways(grad_line, at, lambda at: grad_all.at[2 * at + core], start)
                grad_pair(at, grad_all.at[slot]).start()

    def att_step(at):
        for k in range(2):
            att_got(at, k).wait_recv()
            att_forward(at, k).start()
            att_core(at, near[k]).start()

    att_hop(1)
    att_hop(2)
    grad_step(1)
    for k in range(3):
        ffn_step(k)
    att_hop(3)
    att_step(chip)
    att_step((chip + 1) % 4)
    grad_step(2)
    att_step((chip + 3) % 4)
    att_step((chip + 2) % 4)
    for at in range(4):
        for k in range(2):
            att_corner(at, k).wait_recv()
        att_core(at, corner).start()
    grad_step(3)

    for k in range(3):
        for j in range(2):
            ffn_corner(k, j).wait_recv()
            ffn_side(k, j).wait_send()
            ffn_forward(k, j).wait_send()
    for at in range(4):
        slot = 2 * at + 1 - core
        remote(
            grad_all.at[slot], grad_all.at[slot], pair_send.at[at], pair_got.at[at], other
        ).wait_recv()
        grad_pair(at, grad_ref).wait_send()
        both_ways(att_line, at, lambda at: att_ref, sent)
        both_ways(grad_line, at, lambda at: grad_ref, sent)
        for who in range(4):
            att_core_got(at, who).wait_recv()
            att_core(at, who).wait_send()
        for k in range(2):
            att_side(at, k, att_ref).wait_send()
            att_forward(at, k).wait_send()
    for k in (0, 1, 2, 4):
        own[k].wait()


def gather_all(gate, up, down, att, grad):
    narrow_count = lax.axis_size("narrow")
    wide_count = lax.axis_size("wide")
    rows = att.shape[0]
    if narrow_count != 4 or wide_count != 8:
        att = lax.all_gather(lax.all_gather(att, "wide", axis=0), "narrow", axis=1, tiled=True)
        return (
            lax.all_gather(gate, "narrow", axis=0, tiled=True),
            lax.all_gather(up, "narrow", axis=0, tiled=True),
            lax.all_gather(down, "narrow", axis=1, tiled=True),
            att,
            lax.all_gather(grad, "wide", axis=0, tiled=True),
        )
    low = jnp.bfloat16
    dma = pltpu.SemaphoreType.DMA
    gate_all, up_all, down_all, att_all, grad_all = pl.pallas_call(
        gather_kernel,
        out_shape=[
            jax.ShapeDtypeStruct((narrow_count,) + gate.shape, low),
            jax.ShapeDtypeStruct((narrow_count,) + up.shape, low),
            jax.ShapeDtypeStruct((down.shape[0], narrow_count * down.shape[1]), low),
            jax.ShapeDtypeStruct((wide_count, narrow_count * rows, att.shape[1]), low),
            jax.ShapeDtypeStruct((wide_count,) + grad.shape, low),
        ],
        in_specs=[pl.BlockSpec(memory_space=pl.ANY)] * 5,
        out_specs=[pl.BlockSpec(memory_space=pl.ANY)] * 5,
        scratch_shapes=[
            dma((5,)), dma((3, 4)), dma((3, 4)), dma((4, 2)), dma((4,)), dma((4, 4)), dma((4, 4)),
            dma((4, 4)), dma((4, 4)), dma((4, 2)), dma((4,)), dma((4,)), dma((4,)),
        ],
        compiler_params=pltpu.CompilerParams(collective_id=1, has_side_effects=True),
        name="gather_all",
    )(gate, up, down, att, grad)
    return (
        gate_all.reshape(-1, gate.shape[1]),
        up_all.reshape(-1, up.shape[1]),
        down_all,
        att_all,
        grad_all.reshape(-1, grad.shape[1]),
    )


def gather_rows(shard):
    return lax.all_gather(shard, "wide", axis=0, tiled=True)


def swap(blocks):
    return lax.all_to_all(blocks, "wide", 0, 0)


def sum_back(pairs, row_count):
    summed = jnp.zeros((row_count * lax.axis_size("wide"), pairs[0][1].shape[0]), jnp.float32)
    for gradient, weight in pairs:
        summed = summed + dot_back(gradient, weight)
    return lax.psum_scatter(
        summed.astype(jnp.bfloat16), "wide", scatter_dimension=0, tiled=True
    ).astype(jnp.float32)


def shards(
    tokens_in,
    out_grad,
    positions,
    query_weight,
    query_first,
    query_second,
    key_weight,
    key_first,
    key_second,
    value_weight,
    value_first,
    value_second,
    output_weight,
    output_first,
    output_second,
    gate_weight,
    gate_first,
    gate_second,
    up_weight,
    up_first,
    up_second,
    down_weight,
    down_first,
    down_second,
    norm_gains,
    norm_first,
    norm_second,
    head_gains,
    head_first,
    head_second,
):
    wide_count = lax.axis_size("wide")
    wide_rank = lax.axis_index("wide")
    narrow_count = lax.axis_size("narrow")
    head_dim = head_gains.shape[1]
    key_heads = key_weight.shape[1] // head_dim
    local_heads = query_weight.shape[1] // head_dim
    shard_rows, model_width = tokens_in.shape
    copies = wide_count // key_heads
    key_slot = wide_rank // copies
    key_own = lax.dynamic_slice_in_dim(key_weight, key_slot * head_dim, head_dim, 1)
    value_own = lax.dynamic_slice_in_dim(value_weight, key_slot * head_dim, head_dim, 1)
    query_columns = query_weight.shape[1]
    att_own = jnp.concatenate([query_weight, key_own, value_own, output_weight.T], axis=1)
    gate_local, up_local, down_local, att_full, grad_rows = gather_all(
        gate_weight.astype(jnp.bfloat16),
        up_weight.astype(jnp.bfloat16),
        down_weight.astype(jnp.bfloat16),
        att_own.astype(jnp.bfloat16),
        out_grad,
    )
    group_columns = query_columns + 2 * head_dim
    input_full = att_full[:, :, :group_columns]
    output_full = att_full[:, :, group_columns:]
    inverse = jnp.power(ROTARY_BASE, -2.0 * jnp.arange(head_dim // 2, dtype=jnp.float32) / head_dim)
    own_positions = lax.dynamic_slice_in_dim(positions, wide_rank * shard_rows, shard_rows, 0)
    angles = own_positions.astype(jnp.float32)[:, None] * inverse[None, :]
    cosine = jnp.cos(angles)
    sine_part = jnp.sin(angles)
    residual = tokens_in.astype(jnp.float32)
    normed_in, norm_in_back = jax.vjp(rms_scale, residual, norm_gains[0])
    rows_in = normed_in.astype(jnp.bfloat16)
    input_raw = jnp.einsum("td,gdc->gtc", rows_in, input_full, preferred_element_type=jnp.float32)
    query_raw = input_raw[:, :, :query_columns].reshape(
        wide_count, shard_rows, local_heads, head_dim
    )
    key_raw = input_raw[:, :, query_columns : query_columns + head_dim]
    value_rows = input_raw[:, :, query_columns + head_dim :].astype(jnp.bfloat16)

    def query_turn(raw_heads, gain):
        return rotate(
            rms_scale(raw_heads, gain), cosine[None, :, None, :], sine_part[None, :, None, :]
        )

    def key_turn(raw_heads, gain):
        return rotate(rms_scale(raw_heads, gain), cosine[None], sine_part[None])

    query_rot, query_back = jax.vjp(query_turn, query_raw, head_gains[0])
    key_rot, key_back = jax.vjp(key_turn, key_raw, head_gains[1])
    score_scale = head_dim ** (-0.5)
    query_rot = (
        (query_rot * (score_scale * LOG2E))
        .reshape(wide_count, shard_rows, query_columns)
        .astype(jnp.bfloat16)
    )
    packed = swap(jnp.concatenate([query_rot, key_rot.astype(jnp.bfloat16), value_rows], axis=2))
    packed = packed.reshape(wide_count * shard_rows, group_columns)
    attended, weight_sums, attended_low = attend(packed, local_heads)
    attended_low = swap(attended_low.reshape(wide_count, shard_rows, query_columns))
    branch = jnp.einsum("gth,gdh->td", attended_low, output_full, preferred_element_type=jnp.float32)
    middle = residual + branch
    normed_mid, norm_mid_back = jax.vjp(rms_scale, middle, norm_gains[1])
    rows_mid = gather_rows(normed_mid.astype(jnp.bfloat16))
    gate_pre = dot_last(rows_mid, gate_local)
    up_pre = dot_last(rows_mid, up_local)
    hidden, hidden_back = jax.vjp(
        lambda gate_in, up_in: jax.nn.silu(gate_in) * up_in, gate_pre, up_pre
    )
    hidden_low = hidden.astype(jnp.bfloat16)
    block_out = (
        middle
        + lax.psum_scatter(
            dot_last(hidden_low, down_local).astype(jnp.bfloat16),
            "wide",
            scatter_dimension=0,
            tiled=True,
        ).astype(jnp.float32)
    ).astype(jnp.bfloat16)
    hidden_grad = dot_back(grad_rows, down_local).astype(jnp.bfloat16)
    down_grad = dot_first(hidden_low, grad_rows)
    gate_grad, up_grad = hidden_back(hidden_grad.astype(jnp.float32))
    gate_grad = gate_grad.astype(jnp.bfloat16)
    up_grad = up_grad.astype(jnp.bfloat16)
    gate_wgrad = dot_first(rows_mid, gate_grad)
    up_wgrad = dot_first(rows_mid, up_grad)
    mid_back = sum_back(((gate_grad, gate_local), (up_grad, up_local)), shard_rows)
    middle_part, mid_gain_grad = norm_mid_back(mid_back)
    middle_grad = out_grad.astype(jnp.float32) + middle_part
    branch_grad = middle_grad.astype(jnp.bfloat16)
    attended_grad = jnp.einsum(
        "td,gdh->gth", branch_grad, output_full, preferred_element_type=jnp.float32
    ).astype(jnp.bfloat16)
    output_wgrad = jnp.einsum(
        "td,gth->gdh", branch_grad, attended_low, preferred_element_type=jnp.float32
    )
    head_grad = swap(attended_grad).reshape(wide_count * shard_rows, query_columns)
    head_grad = head_grad.astype(jnp.float32) / weight_sums
    scaled_grad = head_grad.astype(jnp.bfloat16)
    grad_dot = jnp.sum((head_grad * attended).reshape(-1, local_heads, head_dim), axis=-1).T
    packed_grad = attend_back(packed, scaled_grad, grad_dot, local_heads)
    packed_grad = swap(packed_grad.reshape(wide_count, shard_rows, group_columns))
    query_rot_grad = packed_grad[:, :, :query_columns].astype(jnp.float32).reshape(
        wide_count, shard_rows, local_heads, head_dim
    )
    key_rot_grad = packed_grad[:, :, query_columns : query_columns + head_dim]
    query_raw_grad, query_gain_grad = query_back(query_rot_grad)
    key_raw_grad, key_gain_grad = key_back(key_rot_grad.astype(jnp.float32))
    input_low = jnp.concatenate(
        [
            query_raw_grad.reshape(wide_count, shard_rows, query_columns).astype(jnp.bfloat16),
            key_raw_grad.astype(jnp.bfloat16),
            packed_grad[:, :, query_columns + head_dim :],
        ],
        axis=2,
    )
    input_wgrad = jnp.einsum("td,gtc->gdc", rows_in, input_low, preferred_element_type=jnp.float32)
    input_back = jnp.einsum("gtc,gdc->td", input_low, input_full, preferred_element_type=jnp.float32)
    input_part, in_gain_grad = norm_in_back(input_back)
    input_grad = middle_grad + input_part
    gain_stack = jnp.stack([in_gain_grad, mid_gain_grad])
    head_stack = jnp.stack([query_gain_grad, key_gain_grad])
    gain_total, head_total = lax.psum((gain_stack, head_stack), ("narrow", "wide"))
    att_wgrad = jnp.concatenate([input_wgrad, output_wgrad], axis=2).astype(jnp.bfloat16)
    att_total = lax.psum_scatter(att_wgrad, "narrow", scatter_dimension=1, tiled=True)
    input_total = lax.psum_scatter(att_total, "wide", scatter_dimension=0)
    output_total = input_total[:, group_columns:].astype(jnp.float32).T
    query_total = input_total[:, :query_columns].astype(jnp.float32)
    spread = lax.all_gather(input_total[:, query_columns:group_columns], "wide", axis=0)
    spread = jnp.sum(
        spread.reshape(key_heads, copies, -1, 2, head_dim).astype(jnp.float32), axis=1
    ).transpose(2, 1, 0, 3)
    key_total = spread[0].reshape(key_weight.shape)
    value_total = spread[1].reshape(value_weight.shape)
    gate_total, up_total, down_total = (
        lax.psum_scatter(
            gate_wgrad.astype(jnp.bfloat16), "narrow", scatter_dimension=0, tiled=True
        ).astype(jnp.float32),
        lax.psum_scatter(
            up_wgrad.astype(jnp.bfloat16), "narrow", scatter_dimension=0, tiled=True
        ).astype(jnp.float32),
        lax.psum_scatter(
            down_grad.astype(jnp.bfloat16), "narrow", scatter_dimension=1, tiled=True
        ).astype(jnp.float32),
    )
    wide_rate = D ** (-0.5)
    query_new = adam_update(
        query_weight, query_first, query_second, query_total, wide_rate, WEIGHT_DECAY
    )
    key_new = adam_update(key_weight, key_first, key_second, key_total, wide_rate, WEIGHT_DECAY)
    value_new = adam_update(
        value_weight, value_first, value_second, value_total, wide_rate, WEIGHT_DECAY
    )
    output_new = adam_update(
        output_weight, output_first, output_second, output_total, O_FAN ** (-0.5), WEIGHT_DECAY
    )
    gate_new = adam_update(
        gate_weight, gate_first, gate_second, gate_total, wide_rate, WEIGHT_DECAY
    )
    up_new = adam_update(up_weight, up_first, up_second, up_total, wide_rate, WEIGHT_DECAY)
    down_new = adam_update(
        down_weight, down_first, down_second, down_total, FF ** (-0.5), WEIGHT_DECAY
    )
    norm_new = adam_update(norm_gains, norm_first, norm_second, gain_total, GAIN_RATE, 0.0)
    head_new = adam_update(head_gains, head_first, head_second, head_total, GAIN_RATE, 0.0)
    return (
        block_out,
        input_grad,
        query_new[0],
        query_new[1],
        query_new[2],
        key_new[0],
        key_new[1],
        key_new[2],
        value_new[0],
        value_new[1],
        value_new[2],
        output_new[0],
        output_new[1],
        output_new[2],
        gate_new[0],
        gate_new[1],
        gate_new[2],
        up_new[0],
        up_new[1],
        up_new[2],
        down_new[0],
        down_new[1],
        down_new[2],
        norm_new[0],
        norm_new[1],
        norm_new[2],
        head_new[0],
        head_new[1],
        head_new[2],
    )


def solution(mesh):
    return jax.shard_map(
        shards,
        mesh=mesh,
        in_specs=(
            P(("narrow", "wide"), None),
            P(("narrow", "wide"), None),
            P("narrow"),
            P("narrow", "wide"),
            P("narrow", "wide"),
            P("narrow", "wide"),
            P("narrow", None),
            P("narrow", None),
            P("narrow", None),
            P("narrow", None),
            P("narrow", None),
            P("narrow", None),
            P("wide", "narrow"),
            P("wide", "narrow"),
            P("wide", "narrow"),
            P("narrow", "wide"),
            P("narrow", "wide"),
            P("narrow", "wide"),
            P("narrow", "wide"),
            P("narrow", "wide"),
            P("narrow", "wide"),
            P("wide", "narrow"),
            P("wide", "narrow"),
            P("wide", "narrow"),
            P(),
            P(),
            P(),
            P(),
            P(),
            P(),
        ),
        out_specs=(
            P(("narrow", "wide"), None),
            P(("narrow", "wide"), None),
            P("narrow", "wide"),
            P("narrow", "wide"),
            P("narrow", "wide"),
            P("narrow", None),
            P("narrow", None),
            P("narrow", None),
            P("narrow", None),
            P("narrow", None),
            P("narrow", None),
            P("wide", "narrow"),
            P("wide", "narrow"),
            P("wide", "narrow"),
            P("narrow", "wide"),
            P("narrow", "wide"),
            P("narrow", "wide"),
            P("narrow", "wide"),
            P("narrow", "wide"),
            P("narrow", "wide"),
            P("wide", "narrow"),
            P("wide", "narrow"),
            P("wide", "narrow"),
            P(),
            P(),
            P(),
            P(),
            P(),
            P(),
        ),
        check_vma=False,
    )
```

```python
import functools
import math

import jax
import jax.numpy as jnp
from jax import lax
from jax.experimental import pallas as pl
from jax.experimental.pallas import tpu as pltpu
from jax.sharding import PartitionSpec as P

D = 2048
FF = 8192
SEQ_LEN = 4096
STEP = 10
O_FAN = 50


EPSILON = 1e-06
BETA_ONE = 0.9
BETA_TWO = 0.95
ADAM_EPSILON = 1e-08
WEIGHT_DECAY = 0.1
GAIN_RATE = 1.0
ROTARY_BASE = 10000.0
MASKED_SCORE = -1e30


def rms_scale(inputs, gain):
    return inputs * lax.rsqrt(jnp.mean(inputs * inputs, axis=-1, keepdims=True) + EPSILON) * gain


def rotate(inputs, cosine, sine_part):
    half_width = inputs.shape[-1] // 2
    first_half = inputs[..., :half_width]
    second_half = inputs[..., half_width:]
    return jnp.concatenate(
        [
            first_half * cosine - second_half * sine_part,
            second_half * cosine + first_half * sine_part,
        ],
        axis=-1,
    )


def adam_update(weight, first_moment, second_moment, gradient, rate, decay):
    first_new = BETA_ONE * first_moment + (1.0 - BETA_ONE) * gradient
    second_new = BETA_TWO * second_moment + (1.0 - BETA_TWO) * gradient * gradient
    ratio = (
        first_new
        / (1.0 - BETA_ONE**STEP)
        / (jnp.sqrt(second_new / (1.0 - BETA_TWO**STEP)) + ADAM_EPSILON)
    )
    return (weight - rate * (ratio + decay * weight), first_new, second_new)


def dot_last(left, right):
    return jnp.dot(left, right, preferred_element_type=jnp.float32)


def dot_first(left, right):
    return lax.dot_general(
        left, right, (((0,), (0,)), ((), ())), preferred_element_type=jnp.float32
    )


def dot_back(left, right):
    return lax.dot_general(
        left, right, (((1,), (1,)), ((), ())), preferred_element_type=jnp.float32
    )


LOG2E = math.log2(math.e)

def nt(a, b):
    return lax.dot_general(a, b, (((1,), (1,)), ((), ())), preferred_element_type=jnp.float32)
def tn(a, b):
    return lax.dot_general(a, b, (((0,), (0,)), ((), ())), preferred_element_type=jnp.float32)
def nn(a, b):
    return jnp.dot(a, b, preferred_element_type=jnp.float32)

def low_lanes(rows):
    return lax.broadcasted_iota(jnp.int32, (rows, 128), 1) < 64

def attend_kernel(block, heads, q_ref, o_ref, s_ref, low_ref, kk_ref, va_ref, vb_ref, acc_ref):
    total = q_ref.shape[0]
    low = low_lanes(block)

    @pl.loop(0, total // block)
    def _(j):
        rows = pl.ds(pl.multiple_of(j * block, block), block)
        kv = q_ref[rows, pl.ds(heads * 64, 128)]
        vk = jnp.concatenate([kv[:, 64:], kv[:, :64]], axis=1)
        one = jnp.ones_like(kv)
        kk_ref[rows, :] = jnp.where(low, kv, vk)
        va_ref[rows, :] = jnp.where(low, vk, one)
        vb_ref[rows, :] = jnp.where(low, one, kv)

    causal = lax.broadcasted_iota(jnp.int32, (block, block), 0) >= lax.broadcasted_iota(
        jnp.int32, (block, block), 1
    )

    @pl.loop(0, total // block)
    def _(i):
        rows = pl.ds(pl.multiple_of(i * block, block), block)
        for pair in range(heads // 2):
            lanes = pl.ds(pair * 128, 128)
            both = q_ref[rows, lanes]
            zero = jnp.zeros_like(both)
            sides = (jnp.where(low, both, zero), jnp.where(low, zero, both))

            def step(j, diagonal):
                keys = pl.ds(pl.multiple_of(j * block, block), block)
                kk = kk_ref[keys, :]
                for side in range(2):
                    weights = jnp.exp2(nt(sides[side], kk))
                    if diagonal:
                        weights = jnp.where(causal, weights, 0.0)
                    part = nn(weights.astype(jnp.bfloat16), (va_ref, vb_ref)[side][keys, :])
                    if diagonal:
                        acc_ref[side] = part
                    else:
                        acc_ref[side] += part

            step(i, True)

            @pl.loop(0, i)
            def _(j):
                step(j, False)

            first, second = acc_ref[0], acc_ref[1]
            summed = jnp.where(low, first, second)
            sums = jnp.where(low, second, first)
            sums = jnp.concatenate([sums[:, 64:], sums[:, :64]], axis=1)
            result = summed / sums
            o_ref[rows, lanes] = result
            s_ref[rows, lanes] = sums
            low_ref[rows, lanes] = result.astype(jnp.bfloat16)

def attend(packed, heads, block=512):
    total = packed.shape[0]
    shape = (total, heads * 64)
    cost = heads * total * total // 2
    return pl.pallas_call(
        functools.partial(attend_kernel, block, heads),
        out_shape=[
            jax.ShapeDtypeStruct(shape, jnp.float32),
            jax.ShapeDtypeStruct(shape, jnp.float32),
            jax.ShapeDtypeStruct(shape, jnp.bfloat16),
        ],
        in_specs=[pl.BlockSpec(memory_space=pltpu.VMEM)],
        out_specs=[pl.BlockSpec(memory_space=pltpu.VMEM)] * 3,
        scratch_shapes=[pltpu.VMEM((total, 128), jnp.bfloat16)] * 3 + [pltpu.VMEM((2, block, 128), jnp.float32)],
        compiler_params=pltpu.CompilerParams(vmem_limit_bytes=56 << 20),
        cost_estimate=pl.CostEstimate(flops=4 * cost * 256, bytes_accessed=12 * packed.size, transcendentals=cost),
        name="attend",
    )(packed)

def back_kernel(block, heads, q_ref, g_ref, d_ref, out_ref, dq_ref, dkv_ref, kk_ref, vv_ref, ka_ref, kb_ref):
    total = q_ref.shape[0]
    low = low_lanes(block)
    count = total // block

    @pl.loop(0, count)
    def _(j):
        rows = pl.ds(pl.multiple_of(j * block, block), block)
        kv = q_ref[rows, pl.ds(heads * 64, 128)]
        vk = jnp.concatenate([kv[:, 64:], kv[:, :64]], axis=1)
        zero = jnp.zeros_like(kv)
        kk_ref[rows, :] = jnp.where(low, kv, vk)
        vv_ref[rows, :] = jnp.where(low, vk, kv)
        ka_ref[rows, :] = jnp.where(low, kv, zero)
        kb_ref[rows, :] = jnp.where(low, zero, vk)
        dkv_ref[0, rows, :] = jnp.zeros((block, 128), jnp.float32)
        dkv_ref[1, rows, :] = jnp.zeros((block, 128), jnp.float32)

    causal = lax.broadcasted_iota(jnp.int32, (block, block), 0) <= lax.broadcasted_iota(
        jnp.int32, (block, block), 1
    )

    @pl.loop(0, count)
    def _(i):
        rows = pl.ds(pl.multiple_of(i * block, block), block)
        for pair in range(heads // 2):
            lanes = pl.ds(pair * 128, 128)
            qboth = q_ref[rows, lanes]
            gboth = g_ref[rows, lanes]
            zero = jnp.zeros_like(qboth)
            qs = (jnp.where(low, qboth, zero), jnp.where(low, zero, qboth))
            gs = (jnp.where(low, gboth, zero), jnp.where(low, zero, gboth))

            def step(j, diagonal):
                keys = pl.ds(pl.multiple_of(j * block, block), block)
                kk = kk_ref[keys, :]
                vv = vv_ref[keys, :]
                for side in range(2):
                    weights = jnp.exp2(nt(kk, qs[side]))
                    if diagonal:
                        weights = jnp.where(causal, weights, 0.0)
                    dots = d_ref[pl.ds(pair * 2 + side, 1), rows]
                    grads = (weights * (nt(vv, gs[side]) - dots)).astype(jnp.bfloat16)
                    dkv_ref[1, keys, :] += nn(weights.astype(jnp.bfloat16), gs[side])
                    dkv_ref[0, keys, :] += nn(grads, qs[side])
                    part = tn(grads, (ka_ref, kb_ref)[side][keys, :])
                    if diagonal and side == 0:
                        dq_ref[:, lanes] = part
                    else:
                        dq_ref[:, lanes] += part

            step(i, True)

            @pl.loop(0, i)
            def _(j):
                step(j, False)

            out_ref[rows, lanes] = (dq_ref[:, lanes] * 0.125).astype(jnp.bfloat16)

    @pl.loop(0, count)
    def _(j):
        rows = pl.ds(pl.multiple_of(j * block, block), block)
        keys = dkv_ref[0, rows, :] * (1.0 / LOG2E)
        values = dkv_ref[1, rows, :]
        keys = keys + jnp.concatenate([keys[:, 64:], keys[:, :64]], axis=1)
        values = values + jnp.concatenate([values[:, 64:], values[:, :64]], axis=1)
        out_ref[rows, pl.ds(heads * 64, 128)] = jnp.where(low, keys, values).astype(jnp.bfloat16)

def attend_back(packed, g, dots, heads, block=512):
    total = packed.shape[0]
    cost = heads * total * total // 2
    return pl.pallas_call(
        functools.partial(back_kernel, block, heads),
        out_shape=jax.ShapeDtypeStruct(packed.shape, jnp.bfloat16),
        in_specs=[pl.BlockSpec(memory_space=pltpu.VMEM)] * 3,
        out_specs=pl.BlockSpec(memory_space=pltpu.VMEM),
        scratch_shapes=[
            pltpu.VMEM((block, heads * 64), jnp.float32),
            pltpu.VMEM((2, total, 128), jnp.float32),
        ]
        + [pltpu.VMEM((total, 128), jnp.bfloat16)] * 4,
        compiler_params=pltpu.CompilerParams(vmem_limit_bytes=56 << 20),
        cost_estimate=pl.CostEstimate(
            flops=10 * cost * 256, bytes_accessed=12 * packed.size, transcendentals=cost
        ),
        name="attend_back",
    )(packed, g, dots)


def remote(source, target, send, arrive, device):
    return pltpu.make_async_remote_copy(
        src_ref=source,
        dst_ref=target,
        send_sem=send,
        recv_sem=arrive,
        device_id=device,
        device_id_type=pl.DeviceIdType.MESH,
    )


def place():
    narrow = lax.axis_index("narrow")
    wide = lax.axis_index("wide")
    return narrow, wide, wide // 2, wide % 2


def greet_neighbours():
    narrow, wide, chip, core = place()
    barrier = pltpu.get_barrier_semaphore()

    def tell(device):
        pl.semaphore_signal(
            barrier, inc=1, device_id=device, device_id_type=pl.DeviceIdType.MESH
        )

    tell((narrow + 1 - 2 * (narrow % 2), wide))
    tell(((narrow + 2) % 4, wide))
    tell((narrow, 2 * chip + 1 - core))

    @pl.when(chip > 0)
    def _():
        tell((narrow, wide - 2))

    @pl.when(chip < 3)
    def _():
        tell((narrow, wide + 2))

    pl.semaphore_wait(barrier, 3 + jnp.minimum(chip, 1) + jnp.minimum(3 - chip, 1))


def gather_kernel(
    att_ref, att_all, own_sem, line_send, line_got, side_send, side_got, core_send, core_got
):
    narrow, wide, chip, core = place()
    beside = narrow + 1 - 2 * (narrow % 2)
    across = (narrow + 2) % 4
    corner = (beside + 2) % 4
    rows = att_ref.shape[0]
    half_rows = rows // 2
    other = (narrow, 2 * chip + 1 - core)
    left = (narrow, wide - 2)
    right = (narrow, wide + 2)
    sides = ((beside, wide), (across, wide))
    near = (beside, across)

    def att(slot, who):
        return att_all.at[slot, pl.ds(pl.multiple_of(who * rows, rows), rows), :]

    def att_half(slot, who, half):
        return att_all.at[
            slot, pl.ds(pl.multiple_of(who * rows + half * half_rows, half_rows), half_rows), :
        ]

    def line(at, step, source):
        return remote(
            source, att(2 * at + core, narrow), line_send.at[at, (step + 1) // 2],
            line_got.at[at], right if step > 0 else left,
        )

    def both_ways(at, source, act):
        @pl.when(jnp.logical_and(at <= chip, chip < 3))
        def _():
            act(line(at, 1, source))

        @pl.when(jnp.logical_and(at >= chip, chip > 0))
        def _():
            act(line(at, -1, source))

    def side(at, k, source):
        return remote(
            source, att(2 * at + core, narrow), side_send.at[at, k], side_got.at[at, k], sides[k]
        )

    def side_arrival(at, k):
        target = att(2 * at + core, near[k])
        return remote(target, target, side_send.at[at, k], side_got.at[at, k], sides[k])

    def forward(at, k):
        piece = att_half(2 * at + core, near[k], k)
        return remote(piece, piece, side_send.at[at, 2 + k], side_got.at[at, 2 + k], sides[1 - k])

    def corner_arrival(at, k):
        piece = att_half(2 * at + core, corner, k)
        return remote(piece, piece, side_send.at[at, 2 + k], side_got.at[at, 2 + k], sides[1 - k])

    def pair(at, who, half_of):
        piece = att(2 * at + half_of, who)
        return remote(piece, piece, core_send.at[at, who], core_got.at[at, who], other)

    start = lambda copy: copy.start()
    greet_neighbours()
    both_ways(chip, att_ref, start)
    for k in range(2):
        side(chip, k, att_ref).start()
    own = pltpu.make_async_copy(att_ref, att(wide, narrow), own_sem)
    own.start()
    own.wait()
    pair(chip, narrow, core).start()

    def hop(distance):
        for at, valid in (
            (chip - distance, chip >= distance), (chip + distance, chip + distance <= 3)
        ):

            @pl.when(valid)
            def _():
                piece = att(2 * at + core, narrow)
                line(at, 1, piece).wait_recv()
                both_ways(at, piece, start)
                for k in range(2):
                    side(at, k, piece).start()
                pair(at, narrow, core).start()

    def around(at):
        for k in range(2):
            side_arrival(at, k).wait_recv()
            forward(at, k).start()
            pair(at, near[k], core).start()

    upper = chip // 2
    second = chip + 1 - 2 * upper
    last = 3 - 3 * upper
    order = (chip, second, 6 - chip - second - last, last)
    for step in range(4):
        if step < 3:
            hop(step + 1)
        around(order[step])
    for at in order:
        for k in range(2):
            corner_arrival(at, k).wait_recv()
        pair(at, corner, core).start()

    for at in range(4):
        both_ways(at, att_ref, lambda copy: copy.wait_send())
        for who in range(4):
            pair(at, who, 1 - core).wait_recv()
            pair(at, who, core).wait_send()
        for k in range(2):
            side(at, k, att_ref).wait_send()
            forward(at, k).wait_send()


def gather_weights(att):
    narrow_count = lax.axis_size("narrow")
    wide_count = lax.axis_size("wide")
    if narrow_count != 4 or wide_count != 8:
        return lax.all_gather(lax.all_gather(att, "wide", axis=0), "narrow", axis=1, tiled=True)
    dma = pltpu.SemaphoreType.DMA
    return pl.pallas_call(
        gather_kernel,
        out_shape=jax.ShapeDtypeStruct((8, 4 * att.shape[0], att.shape[1]), jnp.bfloat16),
        in_specs=[pl.BlockSpec(memory_space=pl.ANY)],
        out_specs=pl.BlockSpec(memory_space=pl.ANY),
        scratch_shapes=[
            dma, dma((4, 2)), dma((4,)), dma((4, 4)), dma((4, 4)), dma((4, 4)), dma((4, 4)),
        ],
        compiler_params=pltpu.CompilerParams(collective_id=1, has_side_effects=True),
        cost_estimate=pl.CostEstimate(flops=0, bytes_accessed=300 << 20, transcendentals=0),
        name="gather_weights",
    )(att)


def gather_rows(shard):
    return lax.all_gather(shard, "wide", axis=0, tiled=True)


def swap(blocks):
    return lax.all_to_all(blocks, "wide", 0, 0)


def sum_back(pairs, row_count):
    summed = jnp.zeros((row_count * lax.axis_size("wide"), pairs[0][1].shape[0]), jnp.float32)
    for gradient, weight in pairs:
        summed = summed + dot_back(gradient, weight)
    return lax.psum_scatter(
        summed.astype(jnp.bfloat16), "wide", scatter_dimension=0, tiled=True
    ).astype(jnp.float32)


def shards(
    tokens_in,
    out_grad,
    positions,
    query_weight,
    query_first,
    query_second,
    key_weight,
    key_first,
    key_second,
    value_weight,
    value_first,
    value_second,
    output_weight,
    output_first,
    output_second,
    gate_weight,
    gate_first,
    gate_second,
    up_weight,
    up_first,
    up_second,
    down_weight,
    down_first,
    down_second,
    norm_gains,
    norm_first,
    norm_second,
    head_gains,
    head_first,
    head_second,
):
    wide_count = lax.axis_size("wide")
    wide_rank = lax.axis_index("wide")
    narrow_count = lax.axis_size("narrow")
    head_dim = head_gains.shape[1]
    key_heads = key_weight.shape[1] // head_dim
    local_heads = query_weight.shape[1] // head_dim
    shard_rows, model_width = tokens_in.shape
    copies = wide_count // key_heads
    key_slot = wide_rank // copies
    key_own = lax.dynamic_slice_in_dim(key_weight, key_slot * head_dim, head_dim, 1)
    value_own = lax.dynamic_slice_in_dim(value_weight, key_slot * head_dim, head_dim, 1)
    query_columns = query_weight.shape[1]
    att_own = jnp.concatenate([query_weight, key_own, value_own, output_weight.T], axis=1)
    att_full = gather_weights(att_own.astype(jnp.bfloat16))
    gate_local = lax.all_gather(gate_weight.astype(jnp.bfloat16), "narrow", axis=0, tiled=True)
    up_local = lax.all_gather(up_weight.astype(jnp.bfloat16), "narrow", axis=0, tiled=True)
    down_local = lax.all_gather(down_weight.astype(jnp.bfloat16), "narrow", axis=1, tiled=True)
    grad_rows = lax.all_gather(out_grad, "wide", axis=0, tiled=True)
    group_columns = query_columns + 2 * head_dim
    input_full = att_full[:, :, :group_columns]
    output_full = att_full[:, :, group_columns:]
    inverse = jnp.power(ROTARY_BASE, -2.0 * jnp.arange(head_dim // 2, dtype=jnp.float32) / head_dim)
    own_positions = lax.dynamic_slice_in_dim(positions, wide_rank * shard_rows, shard_rows, 0)
    angles = own_positions.astype(jnp.float32)[:, None] * inverse[None, :]
    cosine = jnp.cos(angles)
    sine_part = jnp.sin(angles)
    residual = tokens_in.astype(jnp.float32)
    normed_in, norm_in_back = jax.vjp(rms_scale, residual, norm_gains[0])
    rows_in = normed_in.astype(jnp.bfloat16)
    input_raw = jnp.einsum("td,gdc->gtc", rows_in, input_full, preferred_element_type=jnp.float32)
    query_raw = input_raw[:, :, :query_columns].reshape(
        wide_count, shard_rows, local_heads, head_dim
    )
    key_raw = input_raw[:, :, query_columns : query_columns + head_dim]
    value_rows = input_raw[:, :, query_columns + head_dim :].astype(jnp.bfloat16)

    def query_turn(raw_heads, gain):
        return rotate(
            rms_scale(raw_heads, gain), cosine[None, :, None, :], sine_part[None, :, None, :]
        )

    def key_turn(raw_heads, gain):
        return rotate(rms_scale(raw_heads, gain), cosine[None], sine_part[None])

    query_rot, query_back = jax.vjp(query_turn, query_raw, head_gains[0])
    key_rot, key_back = jax.vjp(key_turn, key_raw, head_gains[1])
    score_scale = head_dim ** (-0.5)
    query_rot = (
        (query_rot * (score_scale * LOG2E))
        .reshape(wide_count, shard_rows, query_columns)
        .astype(jnp.bfloat16)
    )
    packed = swap(jnp.concatenate([query_rot, key_rot.astype(jnp.bfloat16), value_rows], axis=2))
    packed = packed.reshape(wide_count * shard_rows, group_columns)
    packed, down_local, gate_local = lax.optimization_barrier((packed, down_local, gate_local))
    attended, weight_sums, attended_low = attend(packed, local_heads)
    attended_low = swap(attended_low.reshape(wide_count, shard_rows, query_columns))
    attended_low, up_local, grad_rows = lax.optimization_barrier(
        (attended_low, up_local, grad_rows)
    )
    branch = jnp.einsum("gth,gdh->td", attended_low, output_full, preferred_element_type=jnp.float32)
    middle = residual + branch
    normed_mid, norm_mid_back = jax.vjp(rms_scale, middle, norm_gains[1])
    rows_mid = gather_rows(normed_mid.astype(jnp.bfloat16))
    gate_pre = dot_last(rows_mid, gate_local)
    up_pre = dot_last(rows_mid, up_local)
    hidden, hidden_back = jax.vjp(
        lambda gate_in, up_in: jax.nn.silu(gate_in) * up_in, gate_pre, up_pre
    )
    hidden_low = hidden.astype(jnp.bfloat16)
    block_part = dot_last(hidden_low, down_local).astype(jnp.bfloat16)
    hidden_grad = dot_back(grad_rows, down_local).astype(jnp.bfloat16)
    gate_grad, up_grad = hidden_back(hidden_grad.astype(jnp.float32))
    gate_grad = gate_grad.astype(jnp.bfloat16)
    up_grad = up_grad.astype(jnp.bfloat16)
    mid_back = sum_back(((gate_grad, gate_local), (up_grad, up_local)), shard_rows)
    middle_part, mid_gain_grad = norm_mid_back(mid_back)
    middle_grad = out_grad.astype(jnp.float32) + middle_part
    branch_grad = middle_grad.astype(jnp.bfloat16)
    attended_grad = jnp.einsum(
        "td,gdh->gth", branch_grad, output_full, preferred_element_type=jnp.float32
    ).astype(jnp.bfloat16)
    output_wgrad = jnp.einsum(
        "td,gth->gdh", branch_grad, attended_low, preferred_element_type=jnp.float32
    )
    head_grad = swap(attended_grad).reshape(wide_count * shard_rows, query_columns)
    head_grad, block_part, hidden_low, gate_grad, up_grad = lax.optimization_barrier(
        (head_grad, block_part, hidden_low, gate_grad, up_grad)
    )
    block_sum = lax.psum_scatter(block_part, "wide", scatter_dimension=0, tiled=True)
    down_total = lax.psum_scatter(
        dot_first(hidden_low, grad_rows).astype(jnp.bfloat16),
        "narrow", scatter_dimension=1, tiled=True,
    )
    gate_total = lax.psum_scatter(
        dot_first(rows_mid, gate_grad).astype(jnp.bfloat16),
        "narrow", scatter_dimension=0, tiled=True,
    )
    up_total = lax.psum_scatter(
        dot_first(rows_mid, up_grad).astype(jnp.bfloat16),
        "narrow", scatter_dimension=0, tiled=True,
    )
    head_grad = head_grad.astype(jnp.float32) / weight_sums
    scaled_grad = head_grad.astype(jnp.bfloat16)
    grad_dot = jnp.sum((head_grad * attended).reshape(-1, local_heads, head_dim), axis=-1).T
    packed_grad = attend_back(packed, scaled_grad, grad_dot, local_heads)
    packed_grad = swap(packed_grad.reshape(wide_count, shard_rows, group_columns))
    packed_grad, block_sum = lax.optimization_barrier((packed_grad, block_sum))
    block_out = (middle + block_sum.astype(jnp.float32)).astype(jnp.bfloat16)
    query_rot_grad = packed_grad[:, :, :query_columns].astype(jnp.float32).reshape(
        wide_count, shard_rows, local_heads, head_dim
    )
    key_rot_grad = packed_grad[:, :, query_columns : query_columns + head_dim]
    query_raw_grad, query_gain_grad = query_back(query_rot_grad)
    key_raw_grad, key_gain_grad = key_back(key_rot_grad.astype(jnp.float32))
    input_low = jnp.concatenate(
        [
            query_raw_grad.reshape(wide_count, shard_rows, query_columns).astype(jnp.bfloat16),
            key_raw_grad.astype(jnp.bfloat16),
            packed_grad[:, :, query_columns + head_dim :],
        ],
        axis=2,
    )
    input_wgrad = jnp.einsum("td,gtc->gdc", rows_in, input_low, preferred_element_type=jnp.float32)
    input_back = jnp.einsum("gtc,gdc->td", input_low, input_full, preferred_element_type=jnp.float32)
    input_part, in_gain_grad = norm_in_back(input_back)
    input_grad = middle_grad + input_part
    gain_stack = jnp.stack([in_gain_grad, mid_gain_grad])
    head_stack = jnp.stack([query_gain_grad, key_gain_grad])
    gains = jnp.concatenate([gain_stack, head_stack], axis=1)
    gains = jnp.sum(lax.all_gather(gains, ("narrow", "wide"), axis=0), axis=0)
    gain_total = gains[:, :model_width]
    head_total = gains[:, model_width:]
    att_wgrad = jnp.concatenate([input_wgrad, output_wgrad], axis=2).astype(jnp.bfloat16)
    att_total = lax.psum_scatter(att_wgrad, "narrow", scatter_dimension=1, tiled=True)
    input_total = lax.psum_scatter(att_total, "wide", scatter_dimension=0)
    output_total = input_total[:, group_columns:].astype(jnp.float32).T
    query_total = input_total[:, :query_columns].astype(jnp.float32)
    spread = lax.all_gather(input_total[:, query_columns:group_columns], "wide", axis=0)
    spread = jnp.sum(
        spread.reshape(key_heads, copies, -1, 2, head_dim).astype(jnp.float32), axis=1
    ).transpose(2, 1, 0, 3)
    key_total = spread[0].reshape(key_weight.shape)
    value_total = spread[1].reshape(value_weight.shape)
    gate_total, up_total, down_total = (
        gate_total.astype(jnp.float32),
        up_total.astype(jnp.float32),
        down_total.astype(jnp.float32),
    )
    wide_rate = D ** (-0.5)
    query_new = adam_update(
        query_weight, query_first, query_second, query_total, wide_rate, WEIGHT_DECAY
    )
    key_new = adam_update(key_weight, key_first, key_second, key_total, wide_rate, WEIGHT_DECAY)
    value_new = adam_update(
        value_weight, value_first, value_second, value_total, wide_rate, WEIGHT_DECAY
    )
    output_new = adam_update(
        output_weight, output_first, output_second, output_total, O_FAN ** (-0.5), WEIGHT_DECAY
    )
    gate_new = adam_update(
        gate_weight, gate_first, gate_second, gate_total, wide_rate, WEIGHT_DECAY
    )
    up_new = adam_update(up_weight, up_first, up_second, up_total, wide_rate, WEIGHT_DECAY)
    down_new = adam_update(
        down_weight, down_first, down_second, down_total, FF ** (-0.5), WEIGHT_DECAY
    )
    norm_new = adam_update(norm_gains, norm_first, norm_second, gain_total, GAIN_RATE, 0.0)
    head_new = adam_update(head_gains, head_first, head_second, head_total, GAIN_RATE, 0.0)
    return (
        block_out,
        input_grad,
        query_new[0],
        query_new[1],
        query_new[2],
        key_new[0],
        key_new[1],
        key_new[2],
        value_new[0],
        value_new[1],
        value_new[2],
        output_new[0],
        output_new[1],
        output_new[2],
        gate_new[0],
        gate_new[1],
        gate_new[2],
        up_new[0],
        up_new[1],
        up_new[2],
        down_new[0],
        down_new[1],
        down_new[2],
        norm_new[0],
        norm_new[1],
        norm_new[2],
        head_new[0],
        head_new[1],
        head_new[2],
    )


def solution(mesh):
    return jax.shard_map(
        shards,
        mesh=mesh,
        in_specs=(
            P(("narrow", "wide"), None),
            P(("narrow", "wide"), None),
            P("narrow"),
            P("narrow", "wide"),
            P("narrow", "wide"),
            P("narrow", "wide"),
            P("narrow", None),
            P("narrow", None),
            P("narrow", None),
            P("narrow", None),
            P("narrow", None),
            P("narrow", None),
            P("wide", "narrow"),
            P("wide", "narrow"),
            P("wide", "narrow"),
            P("narrow", "wide"),
            P("narrow", "wide"),
            P("narrow", "wide"),
            P("narrow", "wide"),
            P("narrow", "wide"),
            P("narrow", "wide"),
            P("wide", "narrow"),
            P("wide", "narrow"),
            P("wide", "narrow"),
            P(),
            P(),
            P(),
            P(),
            P(),
            P(),
        ),
        out_specs=(
            P(("narrow", "wide"), None),
            P(("narrow", "wide"), None),
            P("narrow", "wide"),
            P("narrow", "wide"),
            P("narrow", "wide"),
            P("narrow", None),
            P("narrow", None),
            P("narrow", None),
            P("narrow", None),
            P("narrow", None),
            P("narrow", None),
            P("wide", "narrow"),
            P("wide", "narrow"),
            P("wide", "narrow"),
            P("narrow", "wide"),
            P("narrow", "wide"),
            P("narrow", "wide"),
            P("narrow", "wide"),
            P("narrow", "wide"),
            P("narrow", "wide"),
            P("wide", "narrow"),
            P("wide", "narrow"),
            P("wide", "narrow"),
            P(),
            P(),
            P(),
            P(),
            P(),
            P(),
        ),
        check_vma=False,
    )
```

```python
import functools
import math

import jax
import jax.numpy as jnp
from jax import lax
from jax.experimental import pallas as pl
from jax.experimental.pallas import tpu as pltpu
from jax.sharding import PartitionSpec as P

D = 2048
FF = 8192
SEQ_LEN = 4096
STEP = 10
O_FAN = 50


EPSILON = 1e-06
BETA_ONE = 0.9
BETA_TWO = 0.95
ADAM_EPSILON = 1e-08
WEIGHT_DECAY = 0.1
GAIN_RATE = 1.0
ROTARY_BASE = 10000.0
MASKED_SCORE = -1e30


def rms_scale(inputs, gain):
    return inputs * lax.rsqrt(jnp.mean(inputs * inputs, axis=-1, keepdims=True) + EPSILON) * gain


def rotate(inputs, cosine, sine_part):
    half_width = inputs.shape[-1] // 2
    first_half = inputs[..., :half_width]
    second_half = inputs[..., half_width:]
    return jnp.concatenate(
        [
            first_half * cosine - second_half * sine_part,
            second_half * cosine + first_half * sine_part,
        ],
        axis=-1,
    )


def adam_update(weight, first_moment, second_moment, gradient, rate, decay):
    first_new = BETA_ONE * first_moment + (1.0 - BETA_ONE) * gradient
    second_new = BETA_TWO * second_moment + (1.0 - BETA_TWO) * gradient * gradient
    ratio = (
        first_new
        / (1.0 - BETA_ONE**STEP)
        / (jnp.sqrt(second_new / (1.0 - BETA_TWO**STEP)) + ADAM_EPSILON)
    )
    return (weight - rate * (ratio + decay * weight), first_new, second_new)


def dot_last(left, right):
    return jnp.dot(left, right, preferred_element_type=jnp.float32)


def dot_first(left, right):
    return lax.dot_general(
        left, right, (((0,), (0,)), ((), ())), preferred_element_type=jnp.float32
    )


def dot_back(left, right):
    return lax.dot_general(
        left, right, (((1,), (1,)), ((), ())), preferred_element_type=jnp.float32
    )


LOG2E = math.log2(math.e)

def nt(a, b):
    return lax.dot_general(a, b, (((1,), (1,)), ((), ())), preferred_element_type=jnp.float32)
def tn(a, b):
    return lax.dot_general(a, b, (((0,), (0,)), ((), ())), preferred_element_type=jnp.float32)
def nn(a, b):
    return jnp.dot(a, b, preferred_element_type=jnp.float32)

def low_lanes(rows):
    return lax.broadcasted_iota(jnp.int32, (rows, 128), 1) < 64

def attend_kernel(block, heads, q_ref, o_ref, s_ref, low_ref, kk_ref, va_ref, vb_ref, acc_ref):
    total = q_ref.shape[0]
    low = low_lanes(block)

    @pl.loop(0, total // block)
    def _(j):
        rows = pl.ds(pl.multiple_of(j * block, block), block)
        kv = q_ref[rows, pl.ds(heads * 64, 128)]
        vk = jnp.concatenate([kv[:, 64:], kv[:, :64]], axis=1)
        one = jnp.ones_like(kv)
        kk_ref[rows, :] = jnp.where(low, kv, vk)
        va_ref[rows, :] = jnp.where(low, vk, one)
        vb_ref[rows, :] = jnp.where(low, one, kv)

    causal = lax.broadcasted_iota(jnp.int32, (block, block), 0) >= lax.broadcasted_iota(
        jnp.int32, (block, block), 1
    )

    @pl.loop(0, total // block)
    def _(i):
        rows = pl.ds(pl.multiple_of(i * block, block), block)
        for pair in range(heads // 2):
            lanes = pl.ds(pair * 128, 128)
            both = q_ref[rows, lanes]
            zero = jnp.zeros_like(both)
            sides = (jnp.where(low, both, zero), jnp.where(low, zero, both))

            def step(j, diagonal):
                keys = pl.ds(pl.multiple_of(j * block, block), block)
                kk = kk_ref[keys, :]
                for side in range(2):
                    weights = jnp.exp2(nt(sides[side], kk))
                    if diagonal:
                        weights = jnp.where(causal, weights, 0.0)
                    part = nn(weights.astype(jnp.bfloat16), (va_ref, vb_ref)[side][keys, :])
                    if diagonal:
                        acc_ref[side] = part
                    else:
                        acc_ref[side] += part

            step(i, True)

            @pl.loop(0, i)
            def _(j):
                step(j, False)

            first, second = acc_ref[0], acc_ref[1]
            summed = jnp.where(low, first, second)
            sums = jnp.where(low, second, first)
            sums = jnp.concatenate([sums[:, 64:], sums[:, :64]], axis=1)
            result = summed / sums
            o_ref[rows, lanes] = result
            s_ref[rows, lanes] = sums
            low_ref[rows, lanes] = result.astype(jnp.bfloat16)

def attend(packed, heads, block=512):
    total = packed.shape[0]
    shape = (total, heads * 64)
    cost = heads * total * total // 2
    return pl.pallas_call(
        functools.partial(attend_kernel, block, heads),
        out_shape=[
            jax.ShapeDtypeStruct(shape, jnp.float32),
            jax.ShapeDtypeStruct(shape, jnp.float32),
            jax.ShapeDtypeStruct(shape, jnp.bfloat16),
        ],
        in_specs=[pl.BlockSpec(memory_space=pltpu.VMEM)],
        out_specs=[pl.BlockSpec(memory_space=pltpu.VMEM)] * 3,
        scratch_shapes=[pltpu.VMEM((total, 128), jnp.bfloat16)] * 3 + [pltpu.VMEM((2, block, 128), jnp.float32)],
        compiler_params=pltpu.CompilerParams(vmem_limit_bytes=56 << 20),
        cost_estimate=pl.CostEstimate(flops=4 * cost * 256, bytes_accessed=12 * packed.size, transcendentals=cost),
        name="attend",
    )(packed)

def back_kernel(block, heads, q_ref, g_ref, d_ref, out_ref, dq_ref, dkv_ref, kk_ref, vv_ref, ka_ref, kb_ref):
    total = q_ref.shape[0]
    low = low_lanes(block)
    count = total // block

    @pl.loop(0, count)
    def _(j):
        rows = pl.ds(pl.multiple_of(j * block, block), block)
        kv = q_ref[rows, pl.ds(heads * 64, 128)]
        vk = jnp.concatenate([kv[:, 64:], kv[:, :64]], axis=1)
        zero = jnp.zeros_like(kv)
        kk_ref[rows, :] = jnp.where(low, kv, vk)
        vv_ref[rows, :] = jnp.where(low, vk, kv)
        ka_ref[rows, :] = jnp.where(low, kv, zero)
        kb_ref[rows, :] = jnp.where(low, zero, vk)
        dkv_ref[0, rows, :] = jnp.zeros((block, 128), jnp.float32)
        dkv_ref[1, rows, :] = jnp.zeros((block, 128), jnp.float32)

    causal = lax.broadcasted_iota(jnp.int32, (block, block), 0) <= lax.broadcasted_iota(
        jnp.int32, (block, block), 1
    )

    @pl.loop(0, count)
    def _(i):
        rows = pl.ds(pl.multiple_of(i * block, block), block)
        for pair in range(heads // 2):
            lanes = pl.ds(pair * 128, 128)
            qboth = q_ref[rows, lanes]
            gboth = g_ref[rows, lanes]
            zero = jnp.zeros_like(qboth)
            qs = (jnp.where(low, qboth, zero), jnp.where(low, zero, qboth))
            gs = (jnp.where(low, gboth, zero), jnp.where(low, zero, gboth))

            def step(j, diagonal):
                keys = pl.ds(pl.multiple_of(j * block, block), block)
                kk = kk_ref[keys, :]
                vv = vv_ref[keys, :]
                for side in range(2):
                    weights = jnp.exp2(nt(kk, qs[side]))
                    if diagonal:
                        weights = jnp.where(causal, weights, 0.0)
                    dots = d_ref[pl.ds(pair * 2 + side, 1), rows]
                    grads = (weights * (nt(vv, gs[side]) - dots)).astype(jnp.bfloat16)
                    dkv_ref[1, keys, :] += nn(weights.astype(jnp.bfloat16), gs[side])
                    dkv_ref[0, keys, :] += nn(grads, qs[side])
                    part = tn(grads, (ka_ref, kb_ref)[side][keys, :])
                    if diagonal and side == 0:
                        dq_ref[:, lanes] = part
                    else:
                        dq_ref[:, lanes] += part

            step(i, True)

            @pl.loop(0, i)
            def _(j):
                step(j, False)

            out_ref[rows, lanes] = (dq_ref[:, lanes] * 0.125).astype(jnp.bfloat16)

    @pl.loop(0, count)
    def _(j):
        rows = pl.ds(pl.multiple_of(j * block, block), block)
        keys = dkv_ref[0, rows, :] * (1.0 / LOG2E)
        values = dkv_ref[1, rows, :]
        keys = keys + jnp.concatenate([keys[:, 64:], keys[:, :64]], axis=1)
        values = values + jnp.concatenate([values[:, 64:], values[:, :64]], axis=1)
        out_ref[rows, pl.ds(heads * 64, 128)] = jnp.where(low, keys, values).astype(jnp.bfloat16)

def attend_back(packed, g, dots, heads, block=512):
    total = packed.shape[0]
    cost = heads * total * total // 2
    return pl.pallas_call(
        functools.partial(back_kernel, block, heads),
        out_shape=jax.ShapeDtypeStruct(packed.shape, jnp.bfloat16),
        in_specs=[pl.BlockSpec(memory_space=pltpu.VMEM)] * 3,
        out_specs=pl.BlockSpec(memory_space=pltpu.VMEM),
        scratch_shapes=[
            pltpu.VMEM((block, heads * 64), jnp.float32),
            pltpu.VMEM((2, total, 128), jnp.float32),
        ]
        + [pltpu.VMEM((total, 128), jnp.bfloat16)] * 4,
        compiler_params=pltpu.CompilerParams(vmem_limit_bytes=56 << 20),
        cost_estimate=pl.CostEstimate(
            flops=10 * cost * 256, bytes_accessed=12 * packed.size, transcendentals=cost
        ),
        name="attend_back",
    )(packed, g, dots)


def remote(source, target, send, arrive, device):
    return pltpu.make_async_remote_copy(
        src_ref=source,
        dst_ref=target,
        send_sem=send,
        recv_sem=arrive,
        device_id=device,
        device_id_type=pl.DeviceIdType.MESH,
    )


def place():
    narrow = lax.axis_index("narrow")
    wide = lax.axis_index("wide")
    return narrow, wide, wide // 2, wide % 2


def greet_neighbours():
    narrow, wide, chip, core = place()
    barrier = pltpu.get_barrier_semaphore()

    def tell(device):
        pl.semaphore_signal(
            barrier, inc=1, device_id=device, device_id_type=pl.DeviceIdType.MESH
        )

    tell((narrow + 1 - 2 * (narrow % 2), wide))
    tell(((narrow + 2) % 4, wide))
    tell((narrow, 2 * chip + 1 - core))

    @pl.when(chip > 0)
    def _():
        tell((narrow, wide - 2))

    @pl.when(chip < 3)
    def _():
        tell((narrow, wide + 2))

    pl.semaphore_wait(barrier, 3 + jnp.minimum(chip, 1) + jnp.minimum(3 - chip, 1))


def gather_kernel(
    att_ref, att_all, own_sem, line_send, line_got, side_send, side_got, core_send, core_got
):
    narrow, wide, chip, core = place()
    beside = narrow + 1 - 2 * (narrow % 2)
    across = (narrow + 2) % 4
    corner = (beside + 2) % 4
    rows = att_ref.shape[0]
    half_rows = rows // 2
    other = (narrow, 2 * chip + 1 - core)
    left = (narrow, wide - 2)
    right = (narrow, wide + 2)
    sides = ((beside, wide), (across, wide))
    near = (beside, across)

    def att(slot, who):
        return att_all.at[slot, pl.ds(pl.multiple_of(who * rows, rows), rows), :]

    def att_half(slot, who, half):
        return att_all.at[
            slot, pl.ds(pl.multiple_of(who * rows + half * half_rows, half_rows), half_rows), :
        ]

    def line(at, step, source):
        return remote(
            source, att(2 * at + core, narrow), line_send.at[at, (step + 1) // 2],
            line_got.at[at], right if step > 0 else left,
        )

    def both_ways(at, source, act):
        @pl.when(jnp.logical_and(at <= chip, chip < 3))
        def _():
            act(line(at, 1, source))

        @pl.when(jnp.logical_and(at >= chip, chip > 0))
        def _():
            act(line(at, -1, source))

    def side(at, k, source):
        return remote(
            source, att(2 * at + core, narrow), side_send.at[at, k], side_got.at[at, k], sides[k]
        )

    def side_arrival(at, k):
        target = att(2 * at + core, near[k])
        return remote(target, target, side_send.at[at, k], side_got.at[at, k], sides[k])

    def forward(at, k):
        piece = att_half(2 * at + core, near[k], k)
        return remote(piece, piece, side_send.at[at, 2 + k], side_got.at[at, 2 + k], sides[1 - k])

    def corner_arrival(at, k):
        piece = att_half(2 * at + core, corner, k)
        return remote(piece, piece, side_send.at[at, 2 + k], side_got.at[at, 2 + k], sides[1 - k])

    def pair(at, who, half_of):
        piece = att(2 * at + half_of, who)
        return remote(piece, piece, core_send.at[at, who], core_got.at[at, who], other)

    start = lambda copy: copy.start()
    greet_neighbours()
    both_ways(chip, att_ref, start)
    for k in range(2):
        side(chip, k, att_ref).start()
    own = pltpu.make_async_copy(att_ref, att(wide, narrow), own_sem)
    own.start()
    own.wait()
    pair(chip, narrow, core).start()

    def hop(distance):
        for at, valid in (
            (chip - distance, chip >= distance), (chip + distance, chip + distance <= 3)
        ):

            @pl.when(valid)
            def _():
                piece = att(2 * at + core, narrow)
                line(at, 1, piece).wait_recv()
                both_ways(at, piece, start)
                for k in range(2):
                    side(at, k, piece).start()
                pair(at, narrow, core).start()

    def around(at):
        for k in range(2):
            side_arrival(at, k).wait_recv()
            forward(at, k).start()
            pair(at, near[k], core).start()

    upper = chip // 2
    second = chip + 1 - 2 * upper
    last = 3 - 3 * upper
    order = (chip, second, 6 - chip - second - last, last)
    for step in range(4):
        if step < 3:
            hop(step + 1)
        around(order[step])
    for at in order:
        for k in range(2):
            corner_arrival(at, k).wait_recv()
        pair(at, corner, core).start()

    for at in range(4):
        both_ways(at, att_ref, lambda copy: copy.wait_send())
        for who in range(4):
            pair(at, who, 1 - core).wait_recv()
            pair(at, who, core).wait_send()
        for k in range(2):
            side(at, k, att_ref).wait_send()
            forward(at, k).wait_send()


def gather_weights(att):
    narrow_count = lax.axis_size("narrow")
    wide_count = lax.axis_size("wide")
    if narrow_count != 4 or wide_count != 8:
        return lax.all_gather(lax.all_gather(att, "wide", axis=0), "narrow", axis=1, tiled=True)
    dma = pltpu.SemaphoreType.DMA
    return pl.pallas_call(
        gather_kernel,
        out_shape=jax.ShapeDtypeStruct((8, 4 * att.shape[0], att.shape[1]), jnp.bfloat16),
        in_specs=[pl.BlockSpec(memory_space=pl.ANY)],
        out_specs=pl.BlockSpec(memory_space=pl.ANY),
        scratch_shapes=[
            dma, dma((4, 2)), dma((4,)), dma((4, 4)), dma((4, 4)), dma((4, 4)), dma((4, 4)),
        ],
        compiler_params=pltpu.CompilerParams(collective_id=1, has_side_effects=True),
        cost_estimate=pl.CostEstimate(flops=0, bytes_accessed=300 << 20, transcendentals=0),
        name="gather_weights",
    )(att)


def gather_rows(shard):
    return lax.all_gather(shard, "wide", axis=0, tiled=True)


def swap(blocks):
    return lax.all_to_all(blocks, "wide", 0, 0)


def sum_back(pairs):
    summed = 0.0
    for gradient, weight in pairs:
        summed = summed + dot_back(gradient, weight)
    return lax.psum_scatter(
        summed.astype(jnp.bfloat16), "wide", scatter_dimension=0, tiled=True
    ).astype(jnp.float32)


def gain_kernel(own_ref, out_ref, first_ref, middle_ref, second_ref, send, got, send_two, got_two):
    narrow = lax.axis_index("narrow")
    wide = lax.axis_index("wide")
    narrow_count = second_ref.shape[0]
    wide_count = first_ref.shape[0]
    barrier = pltpu.get_barrier_semaphore()
    wides = [(narrow, (wide + step) % wide_count) for step in range(1, wide_count)]
    narrows = [((narrow + step) % narrow_count, wide) for step in range(1, narrow_count)]
    for device in wides + narrows:
        pl.semaphore_signal(
            barrier, inc=1, device_id=device, device_id_type=pl.DeviceIdType.MESH
        )
    pl.semaphore_wait(barrier, len(wides) + len(narrows))
    copies = [
        remote(own_ref, first_ref.at[step + 1], send.at[step], got.at[step], device)
        for step, device in enumerate(wides)
    ]
    for copy in copies:
        copy.start()
    for copy in copies:
        copy.wait()
    total = own_ref[...]
    for step in range(1, wide_count):
        total = total + first_ref[step]
    middle_ref[...] = total
    copies = [
        remote(middle_ref, second_ref.at[step + 1], send_two.at[step], got_two.at[step], device)
        for step, device in enumerate(narrows)
    ]
    for copy in copies:
        copy.start()
    for copy in copies:
        copy.wait()
    for step in range(1, narrow_count):
        total = total + second_ref[step]
    out_ref[...] = total


def sum_gains(gains):
    narrow_count = lax.axis_size("narrow")
    wide_count = lax.axis_size("wide")
    size = gains.size
    rows = -(-size // 1024) * 8
    flat = jnp.pad(gains.reshape(-1), (0, rows * 128 - size)).reshape(rows, 128)
    dma = pltpu.SemaphoreType.DMA
    total = pl.pallas_call(
        gain_kernel,
        out_shape=jax.ShapeDtypeStruct(flat.shape, jnp.float32),
        in_specs=[pl.BlockSpec(memory_space=pltpu.VMEM)],
        out_specs=pl.BlockSpec(memory_space=pltpu.VMEM),
        scratch_shapes=[
            pltpu.VMEM((wide_count, rows, 128), jnp.float32),
            pltpu.VMEM((rows, 128), jnp.float32),
            pltpu.VMEM((narrow_count, rows, 128), jnp.float32),
            dma((wide_count - 1,)),
            dma((wide_count - 1,)),
            dma((narrow_count - 1,)),
            dma((narrow_count - 1,)),
        ],
        compiler_params=pltpu.CompilerParams(collective_id=2, has_side_effects=True),
        name="sum_gains",
    )(flat)
    return total.reshape(-1)[:size].reshape(gains.shape)


def shards(
    tokens_in,
    out_grad,
    positions,
    query_weight,
    query_first,
    query_second,
    key_weight,
    key_first,
    key_second,
    value_weight,
    value_first,
    value_second,
    output_weight,
    output_first,
    output_second,
    gate_weight,
    gate_first,
    gate_second,
    up_weight,
    up_first,
    up_second,
    down_weight,
    down_first,
    down_second,
    norm_gains,
    norm_first,
    norm_second,
    head_gains,
    head_first,
    head_second,
):
    wide_count = lax.axis_size("wide")
    wide_rank = lax.axis_index("wide")
    narrow_count = lax.axis_size("narrow")
    head_dim = head_gains.shape[1]
    key_heads = key_weight.shape[1] // head_dim
    local_heads = query_weight.shape[1] // head_dim
    shard_rows, model_width = tokens_in.shape
    copies = wide_count // key_heads
    key_slot = wide_rank // copies
    key_own = lax.dynamic_slice_in_dim(key_weight, key_slot * head_dim, head_dim, 1)
    value_own = lax.dynamic_slice_in_dim(value_weight, key_slot * head_dim, head_dim, 1)
    query_columns = query_weight.shape[1]
    att_own = jnp.concatenate([query_weight, key_own, value_own, output_weight.T], axis=1)
    half_rows = shard_rows // 2
    grad_halves = [
        lax.all_gather(out_grad[:half_rows], "wide", axis=0, tiled=True),
        lax.all_gather(out_grad[half_rows:], "wide", axis=0, tiled=True),
    ]
    att_full, gate_own, up_own, down_own = lax.optimization_barrier(
        (
            gather_weights(att_own.astype(jnp.bfloat16)),
            gate_weight.astype(jnp.bfloat16),
            up_weight.astype(jnp.bfloat16),
            down_weight.astype(jnp.bfloat16),
        )
    )
    gate_local = lax.all_gather(gate_own, "narrow", axis=0, tiled=True)
    up_local = lax.all_gather(up_own, "narrow", axis=0, tiled=True)
    down_local = lax.all_gather(down_own, "narrow", axis=1, tiled=True)
    group_columns = query_columns + 2 * head_dim
    input_full = att_full[:, :, :group_columns]
    output_full = att_full[:, :, group_columns:]
    inverse = jnp.power(ROTARY_BASE, -2.0 * jnp.arange(head_dim // 2, dtype=jnp.float32) / head_dim)
    own_positions = lax.dynamic_slice_in_dim(positions, wide_rank * shard_rows, shard_rows, 0)
    angles = own_positions.astype(jnp.float32)[:, None] * inverse[None, :]
    cosine = jnp.cos(angles)
    sine_part = jnp.sin(angles)
    residual = tokens_in.astype(jnp.float32)
    normed_in, norm_in_back = jax.vjp(rms_scale, residual, norm_gains[0])
    rows_in = normed_in.astype(jnp.bfloat16)
    input_raw = jnp.einsum("td,gdc->gtc", rows_in, input_full, preferred_element_type=jnp.float32)
    query_raw = input_raw[:, :, :query_columns].reshape(
        wide_count, shard_rows, local_heads, head_dim
    )
    key_raw = input_raw[:, :, query_columns : query_columns + head_dim]
    value_rows = input_raw[:, :, query_columns + head_dim :].astype(jnp.bfloat16)

    def query_turn(raw_heads, gain):
        return rotate(
            rms_scale(raw_heads, gain), cosine[None, :, None, :], sine_part[None, :, None, :]
        )

    def key_turn(raw_heads, gain):
        return rotate(rms_scale(raw_heads, gain), cosine[None], sine_part[None])

    query_rot, query_back = jax.vjp(query_turn, query_raw, head_gains[0])
    key_rot, key_back = jax.vjp(key_turn, key_raw, head_gains[1])
    score_scale = head_dim ** (-0.5)
    query_rot = (
        (query_rot * (score_scale * LOG2E))
        .reshape(wide_count, shard_rows, query_columns)
        .astype(jnp.bfloat16)
    )
    packed = jnp.concatenate([query_rot, key_rot.astype(jnp.bfloat16), value_rows], axis=2)
    packed, grad_halves = lax.optimization_barrier((packed, grad_halves))
    packed = swap(packed)
    packed = packed.reshape(wide_count * shard_rows, group_columns)
    attended, weight_sums, attended_low = attend(packed, local_heads)
    attended_low = swap(attended_low.reshape(wide_count, shard_rows, query_columns))
    attended_low, gate_local, up_local, down_local = lax.optimization_barrier(
        (attended_low, gate_local, up_local, down_local)
    )
    branch = jnp.einsum("gth,gdh->td", attended_low, output_full, preferred_element_type=jnp.float32)
    middle = residual + branch
    normed_mid, norm_mid_back = jax.vjp(rms_scale, middle, norm_gains[1])
    mid_low = normed_mid.astype(jnp.bfloat16)
    down_wgrad = gate_wgrad = up_wgrad = 0.0
    block_parts = []
    mid_sums = []
    rows_halves = [gather_rows(mid_low[:half_rows]), gather_rows(mid_low[half_rows:])]
    for rows_mid, grad_rows in zip(rows_halves, grad_halves):
        hidden_grad = dot_back(grad_rows, down_local).astype(jnp.bfloat16)
        gate_pre = dot_last(rows_mid, gate_local)
        up_pre = dot_last(rows_mid, up_local)
        hidden, hidden_back = jax.vjp(
            lambda gate_in, up_in: jax.nn.silu(gate_in) * up_in, gate_pre, up_pre
        )
        hidden_low = hidden.astype(jnp.bfloat16)
        gate_grad, up_grad = hidden_back(hidden_grad.astype(jnp.float32))
        gate_grad = gate_grad.astype(jnp.bfloat16)
        up_grad = up_grad.astype(jnp.bfloat16)
        mid_sums.append(sum_back(((gate_grad, gate_local), (up_grad, up_local))))
        block_parts.append(dot_last(hidden_low, down_local).astype(jnp.bfloat16))
        down_wgrad = down_wgrad + dot_first(hidden_low, grad_rows)
        gate_wgrad = gate_wgrad + dot_first(rows_mid, gate_grad)
        up_wgrad = up_wgrad + dot_first(rows_mid, up_grad)
    down_wgrad = down_wgrad.astype(jnp.bfloat16)
    gate_wgrad = gate_wgrad.astype(jnp.bfloat16)
    up_wgrad = up_wgrad.astype(jnp.bfloat16)
    mid_back = jnp.concatenate(mid_sums, axis=0)
    middle_part, mid_gain_grad = norm_mid_back(mid_back)
    middle_grad = out_grad.astype(jnp.float32) + middle_part
    branch_grad = middle_grad.astype(jnp.bfloat16)
    attended_grad = jnp.einsum(
        "td,gdh->gth", branch_grad, output_full, preferred_element_type=jnp.float32
    ).astype(jnp.bfloat16)
    output_wgrad = jnp.einsum(
        "td,gth->gdh", branch_grad, attended_low, preferred_element_type=jnp.float32
    )
    attended_grad, down_wgrad = lax.optimization_barrier((attended_grad, down_wgrad))
    down_total = lax.psum_scatter(down_wgrad, "narrow", scatter_dimension=1, tiled=True)
    head_grad = swap(attended_grad).reshape(wide_count * shard_rows, query_columns)
    head_grad, block_parts, gate_wgrad, up_wgrad = lax.optimization_barrier(
        (head_grad, block_parts, gate_wgrad, up_wgrad)
    )
    block_sums = [
        lax.psum_scatter(part, "wide", scatter_dimension=0, tiled=True) for part in block_parts
    ]
    gate_total = lax.psum_scatter(gate_wgrad, "narrow", scatter_dimension=0, tiled=True)
    up_total = lax.psum_scatter(up_wgrad, "narrow", scatter_dimension=0, tiled=True)
    head_grad = head_grad.astype(jnp.float32) / weight_sums
    scaled_grad = head_grad.astype(jnp.bfloat16)
    grad_dot = jnp.sum((head_grad * attended).reshape(-1, local_heads, head_dim), axis=-1).T
    packed_grad = attend_back(packed, scaled_grad, grad_dot, local_heads)
    packed_grad = swap(packed_grad.reshape(wide_count, shard_rows, group_columns))
    packed_grad, block_sums, gate_total, up_total, down_total = lax.optimization_barrier(
        (packed_grad, block_sums, gate_total, up_total, down_total)
    )
    block_out = (middle + jnp.concatenate(block_sums, axis=0).astype(jnp.float32)).astype(
        jnp.bfloat16
    )
    query_rot_grad = packed_grad[:, :, :query_columns].astype(jnp.float32).reshape(
        wide_count, shard_rows, local_heads, head_dim
    )
    key_rot_grad = packed_grad[:, :, query_columns : query_columns + head_dim]
    query_raw_grad, query_gain_grad = query_back(query_rot_grad)
    key_raw_grad, key_gain_grad = key_back(key_rot_grad.astype(jnp.float32))
    input_low = jnp.concatenate(
        [
            query_raw_grad.reshape(wide_count, shard_rows, query_columns).astype(jnp.bfloat16),
            key_raw_grad.astype(jnp.bfloat16),
            packed_grad[:, :, query_columns + head_dim :],
        ],
        axis=2,
    )
    input_wgrad = jnp.einsum("td,gtc->gdc", rows_in, input_low, preferred_element_type=jnp.float32)
    input_back = jnp.einsum("gtc,gdc->td", input_low, input_full, preferred_element_type=jnp.float32)
    input_part, in_gain_grad = norm_in_back(input_back)
    input_grad = middle_grad + input_part
    gain_stack = jnp.stack([in_gain_grad, mid_gain_grad])
    head_stack = jnp.stack([query_gain_grad, key_gain_grad])
    gains = sum_gains(jnp.concatenate([gain_stack, head_stack], axis=1))
    gain_total = gains[:, :model_width]
    head_total = gains[:, model_width:]
    att_wgrad = jnp.concatenate([input_wgrad, output_wgrad], axis=2).astype(jnp.bfloat16)
    att_total = lax.psum_scatter(att_wgrad, "narrow", scatter_dimension=1, tiled=True)
    input_total = lax.psum_scatter(att_total, "wide", scatter_dimension=0)
    output_total = input_total[:, group_columns:].astype(jnp.float32).T
    query_total = input_total[:, :query_columns].astype(jnp.float32)
    spread = lax.all_gather(input_total[:, query_columns:group_columns], "wide", axis=0)
    spread = jnp.sum(
        spread.reshape(key_heads, copies, -1, 2, head_dim).astype(jnp.float32), axis=1
    ).transpose(2, 1, 0, 3)
    key_total = spread[0].reshape(key_weight.shape)
    value_total = spread[1].reshape(value_weight.shape)
    gate_total, up_total, down_total = (
        gate_total.astype(jnp.float32),
        up_total.astype(jnp.float32),
        down_total.astype(jnp.float32),
    )
    wide_rate = D ** (-0.5)
    query_new = adam_update(
        query_weight, query_first, query_second, query_total, wide_rate, WEIGHT_DECAY
    )
    key_new = adam_update(key_weight, key_first, key_second, key_total, wide_rate, WEIGHT_DECAY)
    value_new = adam_update(
        value_weight, value_first, value_second, value_total, wide_rate, WEIGHT_DECAY
    )
    output_new = adam_update(
        output_weight, output_first, output_second, output_total, O_FAN ** (-0.5), WEIGHT_DECAY
    )
    gate_new = adam_update(
        gate_weight, gate_first, gate_second, gate_total, wide_rate, WEIGHT_DECAY
    )
    up_new = adam_update(up_weight, up_first, up_second, up_total, wide_rate, WEIGHT_DECAY)
    down_new = adam_update(
        down_weight, down_first, down_second, down_total, FF ** (-0.5), WEIGHT_DECAY
    )
    norm_new = adam_update(norm_gains, norm_first, norm_second, gain_total, GAIN_RATE, 0.0)
    head_new = adam_update(head_gains, head_first, head_second, head_total, GAIN_RATE, 0.0)
    return (
        block_out,
        input_grad,
        query_new[0],
        query_new[1],
        query_new[2],
        key_new[0],
        key_new[1],
        key_new[2],
        value_new[0],
        value_new[1],
        value_new[2],
        output_new[0],
        output_new[1],
        output_new[2],
        gate_new[0],
        gate_new[1],
        gate_new[2],
        up_new[0],
        up_new[1],
        up_new[2],
        down_new[0],
        down_new[1],
        down_new[2],
        norm_new[0],
        norm_new[1],
        norm_new[2],
        head_new[0],
        head_new[1],
        head_new[2],
    )


def solution(mesh):
    return jax.shard_map(
        shards,
        mesh=mesh,
        in_specs=(
            P(("narrow", "wide"), None),
            P(("narrow", "wide"), None),
            P("narrow"),
            P("narrow", "wide"),
            P("narrow", "wide"),
            P("narrow", "wide"),
            P("narrow", None),
            P("narrow", None),
            P("narrow", None),
            P("narrow", None),
            P("narrow", None),
            P("narrow", None),
            P("wide", "narrow"),
            P("wide", "narrow"),
            P("wide", "narrow"),
            P("narrow", "wide"),
            P("narrow", "wide"),
            P("narrow", "wide"),
            P("narrow", "wide"),
            P("narrow", "wide"),
            P("narrow", "wide"),
            P("wide", "narrow"),
            P("wide", "narrow"),
            P("wide", "narrow"),
            P(),
            P(),
            P(),
            P(),
            P(),
            P(),
        ),
        out_specs=(
            P(("narrow", "wide"), None),
            P(("narrow", "wide"), None),
            P("narrow", "wide"),
            P("narrow", "wide"),
            P("narrow", "wide"),
            P("narrow", None),
            P("narrow", None),
            P("narrow", None),
            P("narrow", None),
            P("narrow", None),
            P("narrow", None),
            P("wide", "narrow"),
            P("wide", "narrow"),
            P("wide", "narrow"),
            P("narrow", "wide"),
            P("narrow", "wide"),
            P("narrow", "wide"),
            P("narrow", "wide"),
            P("narrow", "wide"),
            P("narrow", "wide"),
            P("wide", "narrow"),
            P("wide", "narrow"),
            P("wide", "narrow"),
            P(),
            P(),
            P(),
            P(),
            P(),
            P(),
        ),
        check_vma=False,
    )
```

```python
import functools
import math

import jax
import jax.numpy as jnp
from jax import lax
from jax.experimental import pallas as pl
from jax.experimental.pallas import tpu as pltpu
from jax.sharding import PartitionSpec as P

D = 2048
FF = 8192
SEQ_LEN = 4096
STEP = 10
O_FAN = 50


EPSILON = 1e-06
BETA_ONE = 0.9
BETA_TWO = 0.95
ADAM_EPSILON = 1e-08
WEIGHT_DECAY = 0.1
GAIN_RATE = 1.0
ROTARY_BASE = 10000.0
MASKED_SCORE = -1e30


def rms_scale(inputs, gain):
    return inputs * lax.rsqrt(jnp.mean(inputs * inputs, axis=-1, keepdims=True) + EPSILON) * gain


def rotate(inputs, cosine, sine_part):
    half_width = inputs.shape[-1] // 2
    first_half = inputs[..., :half_width]
    second_half = inputs[..., half_width:]
    return jnp.concatenate(
        [
            first_half * cosine - second_half * sine_part,
            second_half * cosine + first_half * sine_part,
        ],
        axis=-1,
    )


def adam_update(weight, first_moment, second_moment, gradient, rate, decay):
    first_new = BETA_ONE * first_moment + (1.0 - BETA_ONE) * gradient
    second_new = BETA_TWO * second_moment + (1.0 - BETA_TWO) * gradient * gradient
    ratio = (
        first_new
        / (1.0 - BETA_ONE**STEP)
        / (jnp.sqrt(second_new / (1.0 - BETA_TWO**STEP)) + ADAM_EPSILON)
    )
    return (weight - rate * (ratio + decay * weight), first_new, second_new)


def dot_last(left, right):
    return jnp.dot(left, right, preferred_element_type=jnp.float32)


def dot_first(left, right):
    return lax.dot_general(
        left, right, (((0,), (0,)), ((), ())), preferred_element_type=jnp.float32
    )


def dot_back(left, right):
    return lax.dot_general(
        left, right, (((1,), (1,)), ((), ())), preferred_element_type=jnp.float32
    )


LOG2E = math.log2(math.e)

def nt(a, b):
    return lax.dot_general(a, b, (((1,), (1,)), ((), ())), preferred_element_type=jnp.float32)
def tn(a, b):
    return lax.dot_general(a, b, (((0,), (0,)), ((), ())), preferred_element_type=jnp.float32)
def nn(a, b):
    return jnp.dot(a, b, preferred_element_type=jnp.float32)

def low_lanes(rows):
    return lax.broadcasted_iota(jnp.int32, (rows, 128), 1) < 64

def attend_kernel(block, heads, q_ref, o_ref, s_ref, low_ref, kk_ref, va_ref, vb_ref, acc_ref):
    total = q_ref.shape[0]
    low = low_lanes(block)

    @pl.loop(0, total // block)
    def _(j):
        rows = pl.ds(pl.multiple_of(j * block, block), block)
        kv = q_ref[rows, pl.ds(heads * 64, 128)]
        vk = jnp.concatenate([kv[:, 64:], kv[:, :64]], axis=1)
        one = jnp.ones_like(kv)
        kk_ref[rows, :] = jnp.where(low, kv, vk)
        va_ref[rows, :] = jnp.where(low, vk, one)
        vb_ref[rows, :] = jnp.where(low, one, kv)

    causal = lax.broadcasted_iota(jnp.int32, (block, block), 0) >= lax.broadcasted_iota(
        jnp.int32, (block, block), 1
    )

    @pl.loop(0, total // block)
    def _(i):
        rows = pl.ds(pl.multiple_of(i * block, block), block)
        for pair in range(heads // 2):
            lanes = pl.ds(pair * 128, 128)
            both = q_ref[rows, lanes]
            zero = jnp.zeros_like(both)
            sides = (jnp.where(low, both, zero), jnp.where(low, zero, both))

            def step(j, diagonal):
                keys = pl.ds(pl.multiple_of(j * block, block), block)
                kk = kk_ref[keys, :]
                for side in range(2):
                    weights = jnp.exp2(nt(sides[side], kk))
                    if diagonal:
                        weights = jnp.where(causal, weights, 0.0)
                    part = nn(weights.astype(jnp.bfloat16), (va_ref, vb_ref)[side][keys, :])
                    if diagonal:
                        acc_ref[side] = part
                    else:
                        acc_ref[side] += part

            step(i, True)

            @pl.loop(0, i)
            def _(j):
                step(j, False)

            first, second = acc_ref[0], acc_ref[1]
            summed = jnp.where(low, first, second)
            sums = jnp.where(low, second, first)
            sums = jnp.concatenate([sums[:, 64:], sums[:, :64]], axis=1)
            result = summed / sums
            o_ref[rows, lanes] = result
            s_ref[rows, lanes] = sums
            low_ref[rows, lanes] = result.astype(jnp.bfloat16)

def attend(packed, heads, block=512):
    total = packed.shape[0]
    shape = (total, heads * 64)
    cost = heads * total * total // 2
    return pl.pallas_call(
        functools.partial(attend_kernel, block, heads),
        out_shape=[
            jax.ShapeDtypeStruct(shape, jnp.float32),
            jax.ShapeDtypeStruct(shape, jnp.float32),
            jax.ShapeDtypeStruct(shape, jnp.bfloat16),
        ],
        in_specs=[pl.BlockSpec(memory_space=pltpu.VMEM)],
        out_specs=[pl.BlockSpec(memory_space=pltpu.VMEM)] * 3,
        scratch_shapes=[pltpu.VMEM((total, 128), jnp.bfloat16)] * 3 + [pltpu.VMEM((2, block, 128), jnp.float32)],
        compiler_params=pltpu.CompilerParams(vmem_limit_bytes=56 << 20),
        cost_estimate=pl.CostEstimate(flops=4 * cost * 256, bytes_accessed=12 * packed.size, transcendentals=cost),
        name="attend",
    )(packed)

def back_kernel(block, heads, q_ref, g_ref, d_ref, out_ref, dq_ref, dkv_ref, kk_ref, vv_ref, ka_ref, kb_ref):
    total = q_ref.shape[0]
    low = low_lanes(block)
    count = total // block

    @pl.loop(0, count)
    def _(j):
        rows = pl.ds(pl.multiple_of(j * block, block), block)
        kv = q_ref[rows, pl.ds(heads * 64, 128)]
        vk = jnp.concatenate([kv[:, 64:], kv[:, :64]], axis=1)
        zero = jnp.zeros_like(kv)
        kk_ref[rows, :] = jnp.where(low, kv, vk)
        vv_ref[rows, :] = jnp.where(low, vk, kv)
        ka_ref[rows, :] = jnp.where(low, kv, zero)
        kb_ref[rows, :] = jnp.where(low, zero, vk)
        dkv_ref[0, rows, :] = jnp.zeros((block, 128), jnp.float32)
        dkv_ref[1, rows, :] = jnp.zeros((block, 128), jnp.float32)

    causal = lax.broadcasted_iota(jnp.int32, (block, block), 0) <= lax.broadcasted_iota(
        jnp.int32, (block, block), 1
    )

    @pl.loop(0, count)
    def _(i):
        rows = pl.ds(pl.multiple_of(i * block, block), block)
        for pair in range(heads // 2):
            lanes = pl.ds(pair * 128, 128)
            qboth = q_ref[rows, lanes]
            gboth = g_ref[rows, lanes]
            zero = jnp.zeros_like(qboth)
            qs = (jnp.where(low, qboth, zero), jnp.where(low, zero, qboth))
            gs = (jnp.where(low, gboth, zero), jnp.where(low, zero, gboth))

            def step(j, diagonal):
                keys = pl.ds(pl.multiple_of(j * block, block), block)
                kk = kk_ref[keys, :]
                vv = vv_ref[keys, :]
                for side in range(2):
                    weights = jnp.exp2(nt(kk, qs[side]))
                    if diagonal:
                        weights = jnp.where(causal, weights, 0.0)
                    dots = d_ref[pl.ds(pair * 2 + side, 1), rows]
                    grads = (weights * (nt(vv, gs[side]) - dots)).astype(jnp.bfloat16)
                    dkv_ref[1, keys, :] += nn(weights.astype(jnp.bfloat16), gs[side])
                    dkv_ref[0, keys, :] += nn(grads, qs[side])
                    part = tn(grads, (ka_ref, kb_ref)[side][keys, :])
                    if diagonal and side == 0:
                        dq_ref[:, lanes] = part
                    else:
                        dq_ref[:, lanes] += part

            step(i, True)

            @pl.loop(0, i)
            def _(j):
                step(j, False)

            out_ref[rows, lanes] = (dq_ref[:, lanes] * 0.125).astype(jnp.bfloat16)

    @pl.loop(0, count)
    def _(j):
        rows = pl.ds(pl.multiple_of(j * block, block), block)
        keys = dkv_ref[0, rows, :] * (1.0 / LOG2E)
        values = dkv_ref[1, rows, :]
        keys = keys + jnp.concatenate([keys[:, 64:], keys[:, :64]], axis=1)
        values = values + jnp.concatenate([values[:, 64:], values[:, :64]], axis=1)
        out_ref[rows, pl.ds(heads * 64, 128)] = jnp.where(low, keys, values).astype(jnp.bfloat16)

def attend_back(packed, g, dots, heads, block=512):
    total = packed.shape[0]
    cost = heads * total * total // 2
    return pl.pallas_call(
        functools.partial(back_kernel, block, heads),
        out_shape=jax.ShapeDtypeStruct(packed.shape, jnp.bfloat16),
        in_specs=[pl.BlockSpec(memory_space=pltpu.VMEM)] * 3,
        out_specs=pl.BlockSpec(memory_space=pltpu.VMEM),
        scratch_shapes=[
            pltpu.VMEM((block, heads * 64), jnp.float32),
            pltpu.VMEM((2, total, 128), jnp.float32),
        ]
        + [pltpu.VMEM((total, 128), jnp.bfloat16)] * 4,
        compiler_params=pltpu.CompilerParams(vmem_limit_bytes=56 << 20),
        cost_estimate=pl.CostEstimate(
            flops=10 * cost * 256, bytes_accessed=12 * packed.size, transcendentals=cost
        ),
        name="attend_back",
    )(packed, g, dots)


def remote(source, target, send, arrive, device):
    return pltpu.make_async_remote_copy(
        src_ref=source,
        dst_ref=target,
        send_sem=send,
        recv_sem=arrive,
        device_id=device,
        device_id_type=pl.DeviceIdType.MESH,
    )


def place():
    narrow = lax.axis_index("narrow")
    wide = lax.axis_index("wide")
    return narrow, wide, wide // 2, wide % 2


def greet_neighbours():
    narrow, wide, chip, core = place()
    barrier = pltpu.get_barrier_semaphore()

    def tell(device):
        pl.semaphore_signal(
            barrier, inc=1, device_id=device, device_id_type=pl.DeviceIdType.MESH
        )

    tell((narrow + 1 - 2 * (narrow % 2), wide))
    tell(((narrow + 2) % 4, wide))
    tell((narrow, 2 * chip + 1 - core))

    @pl.when(chip > 0)
    def _():
        tell((narrow, wide - 2))

    @pl.when(chip < 3)
    def _():
        tell((narrow, wide + 2))

    pl.semaphore_wait(barrier, 3 + jnp.minimum(chip, 1) + jnp.minimum(3 - chip, 1))


def gather_kernel(
    att_ref, att_all, own_sem, line_send, line_got, side_send, side_got, core_send, core_got
):
    narrow, wide, chip, core = place()
    beside = narrow + 1 - 2 * (narrow % 2)
    across = (narrow + 2) % 4
    corner = (beside + 2) % 4
    rows = att_ref.shape[0]
    half_rows = rows // 2
    other = (narrow, 2 * chip + 1 - core)
    left = (narrow, wide - 2)
    right = (narrow, wide + 2)
    sides = ((beside, wide), (across, wide))
    near = (beside, across)

    def att(slot, who):
        return att_all.at[slot, pl.ds(pl.multiple_of(who * rows, rows), rows), :]

    def att_half(slot, who, half):
        return att_all.at[
            slot, pl.ds(pl.multiple_of(who * rows + half * half_rows, half_rows), half_rows), :
        ]

    def line(at, step, source):
        return remote(
            source, att(2 * at + core, narrow), line_send.at[at, (step + 1) // 2],
            line_got.at[at], right if step > 0 else left,
        )

    def both_ways(at, source, act):
        @pl.when(jnp.logical_and(at <= chip, chip < 3))
        def _():
            act(line(at, 1, source))

        @pl.when(jnp.logical_and(at >= chip, chip > 0))
        def _():
            act(line(at, -1, source))

    def side(at, k, source):
        return remote(
            source, att(2 * at + core, narrow), side_send.at[at, k], side_got.at[at, k], sides[k]
        )

    def side_arrival(at, k):
        target = att(2 * at + core, near[k])
        return remote(target, target, side_send.at[at, k], side_got.at[at, k], sides[k])

    def forward(at, k):
        piece = att_half(2 * at + core, near[k], k)
        return remote(piece, piece, side_send.at[at, 2 + k], side_got.at[at, 2 + k], sides[1 - k])

    def corner_arrival(at, k):
        piece = att_half(2 * at + core, corner, k)
        return remote(piece, piece, side_send.at[at, 2 + k], side_got.at[at, 2 + k], sides[1 - k])

    def pair(at, who, half_of):
        piece = att(2 * at + half_of, who)
        return remote(piece, piece, core_send.at[at, who], core_got.at[at, who], other)

    start = lambda copy: copy.start()
    greet_neighbours()
    both_ways(chip, att_ref, start)
    for k in range(2):
        side(chip, k, att_ref).start()
    own = pltpu.make_async_copy(att_ref, att(wide, narrow), own_sem)
    own.start()
    own.wait()
    pair(chip, narrow, core).start()

    def hop(distance):
        for at, valid in (
            (chip - distance, chip >= distance), (chip + distance, chip + distance <= 3)
        ):

            @pl.when(valid)
            def _():
                piece = att(2 * at + core, narrow)
                line(at, 1, piece).wait_recv()
                both_ways(at, piece, start)
                for k in range(2):
                    side(at, k, piece).start()
                pair(at, narrow, core).start()

    def around(at):
        for k in range(2):
            side_arrival(at, k).wait_recv()
            forward(at, k).start()
            pair(at, near[k], core).start()

    upper = chip // 2
    second = chip + 1 - 2 * upper
    last = 3 - 3 * upper
    order = (chip, second, 6 - chip - second - last, last)
    for step in range(4):
        if step < 3:
            hop(step + 1)
        around(order[step])
    for at in order:
        for k in range(2):
            corner_arrival(at, k).wait_recv()
        pair(at, corner, core).start()

    for at in range(4):
        both_ways(at, att_ref, lambda copy: copy.wait_send())
        for who in range(4):
            pair(at, who, 1 - core).wait_recv()
            pair(at, who, core).wait_send()
        for k in range(2):
            side(at, k, att_ref).wait_send()
            forward(at, k).wait_send()


def gather_weights(att):
    narrow_count = lax.axis_size("narrow")
    wide_count = lax.axis_size("wide")
    if narrow_count != 4 or wide_count != 8:
        return lax.all_gather(lax.all_gather(att, "wide", axis=0), "narrow", axis=1, tiled=True)
    dma = pltpu.SemaphoreType.DMA
    return pl.pallas_call(
        gather_kernel,
        out_shape=jax.ShapeDtypeStruct((8, 4 * att.shape[0], att.shape[1]), jnp.bfloat16),
        in_specs=[pl.BlockSpec(memory_space=pl.ANY)],
        out_specs=pl.BlockSpec(memory_space=pl.ANY),
        scratch_shapes=[
            dma, dma((4, 2)), dma((4,)), dma((4, 4)), dma((4, 4)), dma((4, 4)), dma((4, 4)),
        ],
        compiler_params=pltpu.CompilerParams(collective_id=1, has_side_effects=True),
        cost_estimate=pl.CostEstimate(flops=0, bytes_accessed=300 << 20, transcendentals=0),
        name="gather_weights",
    )(att)


def gather_rows(shard):
    return lax.all_gather(shard, "wide", axis=0, tiled=True)


def swap(blocks):
    return lax.all_to_all(blocks, "wide", 0, 0)


def sum_back(pairs):
    summed = 0.0
    for gradient, weight in pairs:
        summed = summed + dot_back(gradient, weight)
    return lax.psum_scatter(
        summed.astype(jnp.bfloat16), "wide", scatter_dimension=0, tiled=True
    ).astype(jnp.float32)


def scatter_kernel(
    in_ref, out_ref, gain_ref, sum_ref, spread_ref, gain_sum_ref,
    own, other, halves, wholes, from_left, from_right, low, wide_gains, mid_gain, narrow_gains,
    load_sem, core_send, core_got, half_send, half_got, whole_send, whole_got,
    line_send, left_got, right_got, spread_send, spread_got, pass_send, pass_got,
    wide_send, wide_got, narrow_send, narrow_got,
):
    narrow, wide, chip, core = place()
    beside = narrow + 1 - 2 * (narrow % 2)
    across = (narrow + 2) % 4
    corner = (beside + 2) % 4
    rows = sum_ref.shape[0]
    half_rows = rows // 2
    split = in_ref.shape[2]
    twin = (narrow, 2 * chip + 1 - core)
    sides = ((beside, wide), (across, wide))
    near = (beside, across)
    wides = [(narrow, (wide + step) % 8) for step in range(1, 8)]
    narrows = [((narrow + step) % 4, wide) for step in range(1, 4)]
    upper = chip // 2
    last = 3 - 3 * upper
    second = chip + 1 - 2 * upper
    order = (last, 6 - chip - second - last, second, chip)
    f32 = jnp.float32

    barrier = pltpu.get_barrier_semaphore()
    for device in wides + narrows:
        pl.semaphore_signal(
            barrier, inc=1, device_id=device, device_id_type=pl.DeviceIdType.MESH
        )
    pl.semaphore_wait(barrier, 10)

    parts = ((in_ref, pl.ds(0, split)), (out_ref, pl.ds(split, out_ref.shape[2])))

    def load(at, k):
        source, lanes = parts[k]
        return pltpu.make_async_copy(
            source.at[2 * at + core], own.at[at, :, lanes], load_sem.at[at, k]
        )

    def exchange(at, k):
        source, lanes = parts[k]
        return remote(
            source.at[2 * at + 1 - core], other.at[at, :, lanes], core_send.at[at, k],
            core_got.at[at, k], twin,
        )

    def block(at, who):
        return own.at[at, pl.ds(pl.multiple_of(who * rows, rows), rows), :]

    def half_block(at, who, half):
        return own.at[
            at, pl.ds(pl.multiple_of(who * rows + half * half_rows, half_rows), half_rows), :
        ]

    def half(at, k):
        return remote(
            half_block(at, corner, k), halves.at[at, k], half_send.at[at, k], half_got.at[at, k],
            sides[k],
        )

    def whole(at, k):
        return remote(
            block(at, near[k]), wholes.at[at, k], whole_send.at[at, k], whole_got.at[at, k],
            sides[k],
        )

    def to_right(at):
        return remote(
            block(at, narrow), from_left.at[at], line_send.at[at], left_got.at[at],
            (narrow, wide + 2),
        )

    def to_left(at):
        return remote(
            block(at, narrow), from_right.at[at], line_send.at[at], right_got.at[at],
            (narrow, wide - 2),
        )

    def add(target, source, count, step=64):
        @pl.loop(0, count // step)
        def _(i):
            piece = pl.ds(pl.multiple_of(i * step, step), step)
            target[piece, :] = (
                target[piece, :].astype(f32) + source[piece, :].astype(f32)
            ).astype(jnp.bfloat16)

    for at in order:
        for k in range(2):
            load(at, k).start()
            exchange(at, k).start()
    gains = [
        remote(gain_ref, wide_gains.at[step], wide_send.at[step], wide_got.at[step], device)
        for step, device in enumerate(wides)
    ]
    for copy in gains:
        copy.start()

    def pair_up(at):
        for k in range(2):
            load(at, k).wait()
            exchange(at, k).wait_recv()
        add(own.at[at], other.at[at], 4 * rows)
        for k in range(2):
            half(at, k).start()

    def turn(at):
        for k in range(2):
            half(at, k).wait_recv()
            add(half_block(at, near[1 - k], k), halves.at[at, k], half_rows)
        for k in range(2):
            whole(at, k).start()

    def settle(at):
        for k in range(2):
            whole(at, k).wait_recv()
        target = block(at, narrow)

        @pl.loop(0, rows // 64)
        def _(i):
            piece = pl.ds(pl.multiple_of(i * 64, 64), 64)
            target[piece, :] = (
                target[piece, :].astype(f32)
                + wholes[at, 0, piece, :].astype(f32)
                + wholes[at, 1, piece, :].astype(f32)
            ).astype(jnp.bfloat16)

        @pl.when(at > chip)
        def _():
            @pl.when(chip > 0)
            def _():
                to_right(at).wait_recv()
                add(target, from_left.at[at], rows)

            to_right(at).start()

        @pl.when(at < chip)
        def _():
            @pl.when(chip < 3)
            def _():
                to_left(at).wait_recv()
                add(target, from_right.at[at], rows)

            to_left(at).start()

    pair_up(order[0])
    pair_up(order[1])
    turn(order[0])
    pair_up(order[2])
    turn(order[1])
    settle(order[0])
    pair_up(order[3])
    turn(order[2])
    settle(order[1])
    for copy in gains:
        copy.wait()
    total = gain_ref[...]
    for step in range(7):
        total = total + wide_gains[step]
    mid_gain[...] = total
    gains = [
        remote(mid_gain, narrow_gains.at[step], narrow_send.at[step], narrow_got.at[step], device)
        for step, device in enumerate(narrows)
    ]
    for copy in gains:
        copy.start()
    turn(order[3])
    settle(order[2])
    settle(order[3])
    target = block(chip, narrow)

    @pl.when(chip > 0)
    def _():
        to_right(chip).wait_recv()
        add(target, from_left.at[chip], rows)

    @pl.when(chip < 3)
    def _():
        to_left(chip).wait_recv()
        add(target, from_right.at[chip], rows)

    lanes = pl.ds(split - 128, 128)

    @pl.loop(0, rows // 64)
    def _(i):
        piece = pl.ds(pl.multiple_of(i * 64, 64), 64)
        value = target[piece, :]
        sum_ref[piece, :] = value.astype(f32)
        low[piece, :] = target[piece, lanes]

    spread_ref[wide] = low[...]

    def spread(step):
        return remote(
            low, spread_ref.at[wide], spread_send.at[step - 1], spread_got.at[step - 1],
            (narrow, (wide + 2 * step) % 8),
        )

    def arrival(step):
        target = spread_ref.at[(wide + 8 - 2 * step) % 8]
        return remote(target, target, spread_send.at[step - 1], spread_got.at[step - 1], twin)

    def pass_on(step):
        piece = spread_ref.at[(wide + 8 - 2 * step) % 8]
        return remote(piece, piece, pass_send.at[step], pass_got.at[step], twin)

    def passed(step):
        piece = spread_ref.at[(2 * chip + 1 - core + 8 - 2 * step) % 8]
        return remote(piece, piece, pass_send.at[step], pass_got.at[step], twin)

    for step in (1, 2, 3):
        spread(step).start()
    pass_on(0).start()
    for copy in gains:
        copy.wait()
    for step in range(3):
        total = total + narrow_gains[step]
    gain_sum_ref[...] = total
    for step in (1, 2, 3):
        arrival(step).wait_recv()
        pass_on(step).start()
    for step in range(4):
        passed(step).wait_recv()
        pass_on(step).wait_send()
    for step in (1, 2, 3):
        spread(step).wait_send()
    for at in range(4):
        for k in range(2):
            exchange(at, k).wait_send()
            half(at, k).wait_send()
            whole(at, k).wait_send()

        @pl.when(at != chip)
        def _():
            to_right(at).wait_send()


def sum_weights(input_wgrad, output_wgrad, gains):
    narrow_count = lax.axis_size("narrow")
    wide_count = lax.axis_size("wide")
    split = input_wgrad.shape[2]
    if narrow_count != 4 or wide_count != 8:
        total = jnp.concatenate([input_wgrad, output_wgrad], axis=2)
        total = lax.psum_scatter(total, "narrow", scatter_dimension=1, tiled=True)
        total = lax.psum_scatter(total, "wide", scatter_dimension=0)
        spread = lax.all_gather(total[:, split - 128 : split], "wide", axis=0)
        gains = jnp.sum(lax.all_gather(gains, ("narrow", "wide"), axis=0), axis=0)
        return total.astype(jnp.float32), spread, gains
    low = jnp.bfloat16
    rows = input_wgrad.shape[1] // 4
    columns = split + output_wgrad.shape[2]
    size = gains.size
    gain_rows = -(-size // 1024) * 8
    flat = jnp.pad(gains.reshape(-1), (0, gain_rows * 128 - size)).reshape(gain_rows, 128)
    dma = pltpu.SemaphoreType.DMA
    vmem = pltpu.VMEM
    total, spread, flat = pl.pallas_call(
        scatter_kernel,
        out_shape=[
            jax.ShapeDtypeStruct((rows, columns), jnp.float32),
            jax.ShapeDtypeStruct((8, rows, 128), low),
            jax.ShapeDtypeStruct(flat.shape, jnp.float32),
        ],
        in_specs=[
            pl.BlockSpec(memory_space=pl.ANY),
            pl.BlockSpec(memory_space=pl.ANY),
            pl.BlockSpec(memory_space=vmem),
        ],
        out_specs=[pl.BlockSpec(memory_space=vmem)] * 3,
        scratch_shapes=[
            vmem((4, 4 * rows, columns), low),
            vmem((4, 4 * rows, columns), low),
            vmem((4, 2, rows // 2, columns), low),
            vmem((4, 2, rows, columns), low),
            vmem((4, rows, columns), low),
            vmem((4, rows, columns), low),
            vmem((rows, 128), low),
            vmem((7, gain_rows, 128), jnp.float32),
            vmem((gain_rows, 128), jnp.float32),
            vmem((3, gain_rows, 128), jnp.float32),
            dma((4, 2)), dma((4, 2)), dma((4, 2)), dma((4, 2)), dma((4, 2)), dma((4, 2)),
            dma((4, 2)), dma((4,)), dma((4,)), dma((4,)), dma((3,)), dma((3,)), dma((4,)),
            dma((4,)), dma((7,)), dma((7,)), dma((3,)), dma((3,)),
        ],
        compiler_params=pltpu.CompilerParams(
            collective_id=3, has_side_effects=True, vmem_limit_bytes=52 << 20
        ),
        cost_estimate=pl.CostEstimate(flops=0, bytes_accessed=300 << 20, transcendentals=0),
        name="sum_weights",
    )(input_wgrad, output_wgrad, flat)
    return total, spread, flat.reshape(-1)[:size].reshape(gains.shape)


def shards(
    tokens_in,
    out_grad,
    positions,
    query_weight,
    query_first,
    query_second,
    key_weight,
    key_first,
    key_second,
    value_weight,
    value_first,
    value_second,
    output_weight,
    output_first,
    output_second,
    gate_weight,
    gate_first,
    gate_second,
    up_weight,
    up_first,
    up_second,
    down_weight,
    down_first,
    down_second,
    norm_gains,
    norm_first,
    norm_second,
    head_gains,
    head_first,
    head_second,
):
    wide_count = lax.axis_size("wide")
    wide_rank = lax.axis_index("wide")
    narrow_count = lax.axis_size("narrow")
    head_dim = head_gains.shape[1]
    key_heads = key_weight.shape[1] // head_dim
    local_heads = query_weight.shape[1] // head_dim
    shard_rows, model_width = tokens_in.shape
    copies = wide_count // key_heads
    key_slot = wide_rank // copies
    key_own = lax.dynamic_slice_in_dim(key_weight, key_slot * head_dim, head_dim, 1)
    value_own = lax.dynamic_slice_in_dim(value_weight, key_slot * head_dim, head_dim, 1)
    query_columns = query_weight.shape[1]
    att_own = jnp.concatenate([query_weight, key_own, value_own, output_weight.T], axis=1)
    half_rows = shard_rows // 2
    grad_halves = [
        lax.all_gather(out_grad[:half_rows], "wide", axis=0, tiled=True),
        lax.all_gather(out_grad[half_rows:], "wide", axis=0, tiled=True),
    ]
    att_full, gate_own, up_own, down_own = lax.optimization_barrier(
        (
            gather_weights(att_own.astype(jnp.bfloat16)),
            gate_weight.astype(jnp.bfloat16),
            up_weight.astype(jnp.bfloat16),
            down_weight.astype(jnp.bfloat16),
        )
    )
    gate_local = lax.all_gather(gate_own, "narrow", axis=0, tiled=True)
    up_local = lax.all_gather(up_own, "narrow", axis=0, tiled=True)
    down_local = lax.all_gather(down_own, "narrow", axis=1, tiled=True)
    group_columns = query_columns + 2 * head_dim
    input_full = att_full[:, :, :group_columns]
    output_full = att_full[:, :, group_columns:]
    inverse = jnp.power(ROTARY_BASE, -2.0 * jnp.arange(head_dim // 2, dtype=jnp.float32) / head_dim)
    own_positions = lax.dynamic_slice_in_dim(positions, wide_rank * shard_rows, shard_rows, 0)
    angles = own_positions.astype(jnp.float32)[:, None] * inverse[None, :]
    cosine = jnp.cos(angles)
    sine_part = jnp.sin(angles)
    residual = tokens_in.astype(jnp.float32)
    normed_in, norm_in_back = jax.vjp(rms_scale, residual, norm_gains[0])
    rows_in = normed_in.astype(jnp.bfloat16)
    input_raw = jnp.einsum("td,gdc->gtc", rows_in, input_full, preferred_element_type=jnp.float32)
    query_raw = input_raw[:, :, :query_columns].reshape(
        wide_count, shard_rows, local_heads, head_dim
    )
    key_raw = input_raw[:, :, query_columns : query_columns + head_dim]
    value_rows = input_raw[:, :, query_columns + head_dim :].astype(jnp.bfloat16)

    def query_turn(raw_heads, gain):
        return rotate(
            rms_scale(raw_heads, gain), cosine[None, :, None, :], sine_part[None, :, None, :]
        )

    def key_turn(raw_heads, gain):
        return rotate(rms_scale(raw_heads, gain), cosine[None], sine_part[None])

    query_rot, query_back = jax.vjp(query_turn, query_raw, head_gains[0])
    key_rot, key_back = jax.vjp(key_turn, key_raw, head_gains[1])
    score_scale = head_dim ** (-0.5)
    query_rot = (
        (query_rot * (score_scale * LOG2E))
        .reshape(wide_count, shard_rows, query_columns)
        .astype(jnp.bfloat16)
    )
    packed = jnp.concatenate([query_rot, key_rot.astype(jnp.bfloat16), value_rows], axis=2)
    packed, grad_halves = lax.optimization_barrier((packed, grad_halves))
    packed = swap(packed)
    packed = packed.reshape(wide_count * shard_rows, group_columns)
    attended, weight_sums, attended_low = attend(packed, local_heads)
    attended_low = swap(attended_low.reshape(wide_count, shard_rows, query_columns))
    attended_low, gate_local, up_local, down_local = lax.optimization_barrier(
        (attended_low, gate_local, up_local, down_local)
    )
    branch = jnp.einsum("gth,gdh->td", attended_low, output_full, preferred_element_type=jnp.float32)
    middle = residual + branch
    normed_mid, norm_mid_back = jax.vjp(rms_scale, middle, norm_gains[1])
    mid_low = normed_mid.astype(jnp.bfloat16)
    down_wgrad = gate_wgrad = up_wgrad = 0.0
    block_parts = []
    mid_sums = []
    rows_halves = [gather_rows(mid_low[:half_rows]), gather_rows(mid_low[half_rows:])]
    for rows_mid, grad_rows in zip(rows_halves, grad_halves):
        hidden_grad = dot_back(grad_rows, down_local).astype(jnp.bfloat16)
        gate_pre = dot_last(rows_mid, gate_local)
        up_pre = dot_last(rows_mid, up_local)
        hidden, hidden_back = jax.vjp(
            lambda gate_in, up_in: jax.nn.silu(gate_in) * up_in, gate_pre, up_pre
        )
        hidden_low = hidden.astype(jnp.bfloat16)
        gate_grad, up_grad = hidden_back(hidden_grad.astype(jnp.float32))
        gate_grad = gate_grad.astype(jnp.bfloat16)
        up_grad = up_grad.astype(jnp.bfloat16)
        mid_sums.append(sum_back(((gate_grad, gate_local), (up_grad, up_local))))
        block_parts.append(dot_last(hidden_low, down_local).astype(jnp.bfloat16))
        down_wgrad = down_wgrad + dot_first(hidden_low, grad_rows)
        gate_wgrad = gate_wgrad + dot_first(rows_mid, gate_grad)
        up_wgrad = up_wgrad + dot_first(rows_mid, up_grad)
    down_wgrad = down_wgrad.astype(jnp.bfloat16)
    gate_wgrad = gate_wgrad.astype(jnp.bfloat16)
    up_wgrad = up_wgrad.astype(jnp.bfloat16)
    mid_sums, gate_wgrad, up_wgrad, down_wgrad, block_parts = lax.optimization_barrier(
        (mid_sums, gate_wgrad, up_wgrad, down_wgrad, block_parts)
    )
    mid_back = jnp.concatenate(mid_sums, axis=0)
    middle_part, mid_gain_grad = norm_mid_back(mid_back)
    middle_grad = out_grad.astype(jnp.float32) + middle_part
    branch_grad = middle_grad.astype(jnp.bfloat16)
    attended_grad = jnp.einsum(
        "td,gdh->gth", branch_grad, output_full, preferred_element_type=jnp.float32
    ).astype(jnp.bfloat16)
    output_wgrad = jnp.einsum(
        "td,gth->gdh", branch_grad, attended_low, preferred_element_type=jnp.float32
    )
    attended_grad, down_wgrad = lax.optimization_barrier((attended_grad, down_wgrad))
    down_total = lax.psum_scatter(down_wgrad, "narrow", scatter_dimension=1, tiled=True)
    head_grad = swap(attended_grad).reshape(wide_count * shard_rows, query_columns)
    head_grad, down_total, first_part, gate_wgrad = lax.optimization_barrier(
        (head_grad, down_total, block_parts[0], gate_wgrad)
    )
    first_sum = lax.psum_scatter(first_part, "wide", scatter_dimension=0, tiled=True)
    gate_total = lax.psum_scatter(gate_wgrad, "narrow", scatter_dimension=0, tiled=True)
    head_grad = head_grad.astype(jnp.float32) / weight_sums
    scaled_grad = head_grad.astype(jnp.bfloat16)
    grad_dot = jnp.sum((head_grad * attended).reshape(-1, local_heads, head_dim), axis=-1).T
    packed_grad = attend_back(packed, scaled_grad, grad_dot, local_heads)
    packed_grad, up_wgrad, first_sum = lax.optimization_barrier((packed_grad, up_wgrad, first_sum))
    up_total = lax.psum_scatter(up_wgrad, "narrow", scatter_dimension=0, tiled=True)
    packed_grad = swap(packed_grad.reshape(wide_count, shard_rows, group_columns))
    packed_grad, gate_total, second_part = lax.optimization_barrier(
        (packed_grad, gate_total, block_parts[1])
    )
    second_sum = lax.psum_scatter(second_part, "wide", scatter_dimension=0, tiled=True)
    query_rot_grad = packed_grad[:, :, :query_columns].astype(jnp.float32).reshape(
        wide_count, shard_rows, local_heads, head_dim
    )
    key_rot_grad = packed_grad[:, :, query_columns : query_columns + head_dim]
    query_raw_grad, query_gain_grad = query_back(query_rot_grad)
    key_raw_grad, key_gain_grad = key_back(key_rot_grad.astype(jnp.float32))
    input_low = jnp.concatenate(
        [
            query_raw_grad.reshape(wide_count, shard_rows, query_columns).astype(jnp.bfloat16),
            key_raw_grad.astype(jnp.bfloat16),
            packed_grad[:, :, query_columns + head_dim :],
        ],
        axis=2,
    )
    input_wgrad = jnp.einsum(
        "td,gtc->gdc", rows_in, input_low, preferred_element_type=jnp.float32
    ).astype(jnp.bfloat16)
    input_back = jnp.einsum("gtc,gdc->td", input_low, input_full, preferred_element_type=jnp.float32)
    input_part, in_gain_grad = norm_in_back(input_back)
    input_grad = middle_grad + input_part
    gain_stack = jnp.stack([in_gain_grad, mid_gain_grad])
    head_stack = jnp.stack([query_gain_grad, key_gain_grad])
    input_wgrad, up_total = lax.optimization_barrier((input_wgrad, up_total))
    input_total, spread, gains = sum_weights(
        input_wgrad,
        output_wgrad.astype(jnp.bfloat16),
        jnp.concatenate([gain_stack, head_stack], axis=1),
    )
    input_total, second_sum = lax.optimization_barrier((input_total, second_sum))
    block_sum = jnp.concatenate([first_sum, second_sum], axis=0).astype(jnp.float32)
    block_out = (middle + block_sum).astype(jnp.bfloat16)
    gain_total = gains[:, :model_width]
    head_total = gains[:, model_width:]
    output_total = input_total[:, group_columns:].T
    query_total = input_total[:, :query_columns]
    spread = jnp.sum(
        spread.reshape(key_heads, copies, -1, 2, head_dim).astype(jnp.float32), axis=1
    ).transpose(2, 1, 0, 3)
    key_total = spread[0].reshape(key_weight.shape)
    value_total = spread[1].reshape(value_weight.shape)
    gate_total, up_total, down_total = (
        gate_total.astype(jnp.float32),
        up_total.astype(jnp.float32),
        down_total.astype(jnp.float32),
    )
    wide_rate = D ** (-0.5)
    query_new = adam_update(
        query_weight, query_first, query_second, query_total, wide_rate, WEIGHT_DECAY
    )
    key_new = adam_update(key_weight, key_first, key_second, key_total, wide_rate, WEIGHT_DECAY)
    value_new = adam_update(
        value_weight, value_first, value_second, value_total, wide_rate, WEIGHT_DECAY
    )
    output_new = adam_update(
        output_weight, output_first, output_second, output_total, O_FAN ** (-0.5), WEIGHT_DECAY
    )
    gate_new = adam_update(
        gate_weight, gate_first, gate_second, gate_total, wide_rate, WEIGHT_DECAY
    )
    up_new = adam_update(up_weight, up_first, up_second, up_total, wide_rate, WEIGHT_DECAY)
    down_new = adam_update(
        down_weight, down_first, down_second, down_total, FF ** (-0.5), WEIGHT_DECAY
    )
    norm_new = adam_update(norm_gains, norm_first, norm_second, gain_total, GAIN_RATE, 0.0)
    head_new = adam_update(head_gains, head_first, head_second, head_total, GAIN_RATE, 0.0)
    return (
        block_out,
        input_grad,
        query_new[0],
        query_new[1],
        query_new[2],
        key_new[0],
        key_new[1],
        key_new[2],
        value_new[0],
        value_new[1],
        value_new[2],
        output_new[0],
        output_new[1],
        output_new[2],
        gate_new[0],
        gate_new[1],
        gate_new[2],
        up_new[0],
        up_new[1],
        up_new[2],
        down_new[0],
        down_new[1],
        down_new[2],
        norm_new[0],
        norm_new[1],
        norm_new[2],
        head_new[0],
        head_new[1],
        head_new[2],
    )


def solution(mesh):
    return jax.shard_map(
        shards,
        mesh=mesh,
        in_specs=(
            P(("narrow", "wide"), None),
            P(("narrow", "wide"), None),
            P("narrow"),
            P("narrow", "wide"),
            P("narrow", "wide"),
            P("narrow", "wide"),
            P("narrow", None),
            P("narrow", None),
            P("narrow", None),
            P("narrow", None),
            P("narrow", None),
            P("narrow", None),
            P("wide", "narrow"),
            P("wide", "narrow"),
            P("wide", "narrow"),
            P("narrow", "wide"),
            P("narrow", "wide"),
            P("narrow", "wide"),
            P("narrow", "wide"),
            P("narrow", "wide"),
            P("narrow", "wide"),
            P("wide", "narrow"),
            P("wide", "narrow"),
            P("wide", "narrow"),
            P(),
            P(),
            P(),
            P(),
            P(),
            P(),
        ),
        out_specs=(
            P(("narrow", "wide"), None),
            P(("narrow", "wide"), None),
            P("narrow", "wide"),
            P("narrow", "wide"),
            P("narrow", "wide"),
            P("narrow", None),
            P("narrow", None),
            P("narrow", None),
            P("narrow", None),
            P("narrow", None),
            P("narrow", None),
            P("wide", "narrow"),
            P("wide", "narrow"),
            P("wide", "narrow"),
            P("narrow", "wide"),
            P("narrow", "wide"),
            P("narrow", "wide"),
            P("narrow", "wide"),
            P("narrow", "wide"),
            P("narrow", "wide"),
            P("wide", "narrow"),
            P("wide", "narrow"),
            P("wide", "narrow"),
            P(),
            P(),
            P(),
            P(),
            P(),
            P(),
        ),
        check_vma=False,
    )
```

```python
import functools
import math

import jax
import jax.numpy as jnp
from jax import lax
from jax.experimental import pallas as pl
from jax.experimental.pallas import tpu as pltpu
from jax.sharding import PartitionSpec as P

D = 2048
FF = 8192
SEQ_LEN = 4096
STEP = 10
O_FAN = 50


EPSILON = 1e-06
BETA_ONE = 0.9
BETA_TWO = 0.95
ADAM_EPSILON = 1e-08
WEIGHT_DECAY = 0.1
GAIN_RATE = 1.0
ROTARY_BASE = 10000.0
MASKED_SCORE = -1e30


def rms_scale(inputs, gain):
    return inputs * lax.rsqrt(jnp.mean(inputs * inputs, axis=-1, keepdims=True) + EPSILON) * gain


def rotate(inputs, cosine, sine_part):
    half_width = inputs.shape[-1] // 2
    first_half = inputs[..., :half_width]
    second_half = inputs[..., half_width:]
    return jnp.concatenate(
        [
            first_half * cosine - second_half * sine_part,
            second_half * cosine + first_half * sine_part,
        ],
        axis=-1,
    )


def adam_update(weight, first_moment, second_moment, gradient, rate, decay):
    first_new = BETA_ONE * first_moment + (1.0 - BETA_ONE) * gradient
    second_new = BETA_TWO * second_moment + (1.0 - BETA_TWO) * gradient * gradient
    ratio = (
        first_new
        / (1.0 - BETA_ONE**STEP)
        / (jnp.sqrt(second_new / (1.0 - BETA_TWO**STEP)) + ADAM_EPSILON)
    )
    return (weight - rate * (ratio + decay * weight), first_new, second_new)


def dot_last(left, right):
    return jnp.dot(left, right, preferred_element_type=jnp.float32)


def dot_first(left, right):
    return lax.dot_general(
        left, right, (((0,), (0,)), ((), ())), preferred_element_type=jnp.float32
    )


def dot_back(left, right):
    return lax.dot_general(
        left, right, (((1,), (1,)), ((), ())), preferred_element_type=jnp.float32
    )


LOG2E = math.log2(math.e)

def nt(a, b):
    return lax.dot_general(a, b, (((1,), (1,)), ((), ())), preferred_element_type=jnp.float32)
def tn(a, b):
    return lax.dot_general(a, b, (((0,), (0,)), ((), ())), preferred_element_type=jnp.float32)
def nn(a, b):
    return jnp.dot(a, b, preferred_element_type=jnp.float32)

def low_lanes(rows):
    return lax.broadcasted_iota(jnp.int32, (rows, 128), 1) < 64

def attend_kernel(block, heads, q_ref, o_ref, s_ref, low_ref, kk_ref, va_ref, vb_ref, acc_ref):
    total = q_ref.shape[0]
    low = low_lanes(block)

    @pl.loop(0, total // block)
    def _(j):
        rows = pl.ds(pl.multiple_of(j * block, block), block)
        kv = q_ref[rows, pl.ds(heads * 64, 128)]
        vk = jnp.concatenate([kv[:, 64:], kv[:, :64]], axis=1)
        one = jnp.ones_like(kv)
        kk_ref[rows, :] = jnp.where(low, kv, vk)
        va_ref[rows, :] = jnp.where(low, vk, one)
        vb_ref[rows, :] = jnp.where(low, one, kv)

    causal = lax.broadcasted_iota(jnp.int32, (block, block), 0) >= lax.broadcasted_iota(
        jnp.int32, (block, block), 1
    )

    @pl.loop(0, total // block)
    def _(i):
        rows = pl.ds(pl.multiple_of(i * block, block), block)
        for pair in range(heads // 2):
            lanes = pl.ds(pair * 128, 128)
            both = q_ref[rows, lanes]
            zero = jnp.zeros_like(both)
            sides = (jnp.where(low, both, zero), jnp.where(low, zero, both))

            def step(j, diagonal):
                keys = pl.ds(pl.multiple_of(j * block, block), block)
                kk = kk_ref[keys, :]
                for side in range(2):
                    weights = jnp.exp2(nt(sides[side], kk))
                    if diagonal:
                        weights = jnp.where(causal, weights, 0.0)
                    part = nn(weights.astype(jnp.bfloat16), (va_ref, vb_ref)[side][keys, :])
                    if diagonal:
                        acc_ref[side] = part
                    else:
                        acc_ref[side] += part

            step(i, True)

            @pl.loop(0, i)
            def _(j):
                step(j, False)

            first, second = acc_ref[0], acc_ref[1]
            summed = jnp.where(low, first, second)
            sums = jnp.where(low, second, first)
            sums = jnp.concatenate([sums[:, 64:], sums[:, :64]], axis=1)
            result = summed / sums
            o_ref[rows, lanes] = result
            s_ref[rows, lanes] = sums
            low_ref[rows, lanes] = result.astype(jnp.bfloat16)

def attend(packed, heads, block=512):
    total = packed.shape[0]
    shape = (total, heads * 64)
    cost = heads * total * total // 2
    return pl.pallas_call(
        functools.partial(attend_kernel, block, heads),
        out_shape=[
            jax.ShapeDtypeStruct(shape, jnp.float32),
            jax.ShapeDtypeStruct(shape, jnp.float32),
            jax.ShapeDtypeStruct(shape, jnp.bfloat16),
        ],
        in_specs=[pl.BlockSpec(memory_space=pltpu.VMEM)],
        out_specs=[pl.BlockSpec(memory_space=pltpu.VMEM)] * 3,
        scratch_shapes=[pltpu.VMEM((total, 128), jnp.bfloat16)] * 3 + [pltpu.VMEM((2, block, 128), jnp.float32)],
        compiler_params=pltpu.CompilerParams(vmem_limit_bytes=56 << 20),
        cost_estimate=pl.CostEstimate(flops=4 * cost * 256, bytes_accessed=12 * packed.size, transcendentals=cost),
        name="attend",
    )(packed)

def back_kernel(block, heads, q_ref, g_ref, d_ref, out_ref, dq_ref, dkv_ref, kk_ref, vv_ref, ka_ref, kb_ref):
    total = q_ref.shape[0]
    low = low_lanes(block)
    count = total // block

    @pl.loop(0, count)
    def _(j):
        rows = pl.ds(pl.multiple_of(j * block, block), block)
        kv = q_ref[rows, pl.ds(heads * 64, 128)]
        vk = jnp.concatenate([kv[:, 64:], kv[:, :64]], axis=1)
        zero = jnp.zeros_like(kv)
        kk_ref[rows, :] = jnp.where(low, kv, vk)
        vv_ref[rows, :] = jnp.where(low, vk, kv)
        ka_ref[rows, :] = jnp.where(low, kv, zero)
        kb_ref[rows, :] = jnp.where(low, zero, vk)
        dkv_ref[0, rows, :] = jnp.zeros((block, 128), jnp.float32)
        dkv_ref[1, rows, :] = jnp.zeros((block, 128), jnp.float32)

    causal = lax.broadcasted_iota(jnp.int32, (block, block), 0) <= lax.broadcasted_iota(
        jnp.int32, (block, block), 1
    )

    @pl.loop(0, count)
    def _(i):
        rows = pl.ds(pl.multiple_of(i * block, block), block)
        for pair in range(heads // 2):
            lanes = pl.ds(pair * 128, 128)
            qboth = q_ref[rows, lanes]
            gboth = g_ref[rows, lanes]
            zero = jnp.zeros_like(qboth)
            qs = (jnp.where(low, qboth, zero), jnp.where(low, zero, qboth))
            gs = (jnp.where(low, gboth, zero), jnp.where(low, zero, gboth))

            def step(j, diagonal):
                keys = pl.ds(pl.multiple_of(j * block, block), block)
                kk = kk_ref[keys, :]
                vv = vv_ref[keys, :]
                for side in range(2):
                    weights = jnp.exp2(nt(kk, qs[side]))
                    if diagonal:
                        weights = jnp.where(causal, weights, 0.0)
                    dots = d_ref[pl.ds(pair * 2 + side, 1), rows]
                    grads = (weights * (nt(vv, gs[side]) - dots)).astype(jnp.bfloat16)
                    dkv_ref[1, keys, :] += nn(weights.astype(jnp.bfloat16), gs[side])
                    dkv_ref[0, keys, :] += nn(grads, qs[side])
                    part = tn(grads, (ka_ref, kb_ref)[side][keys, :])
                    if diagonal and side == 0:
                        dq_ref[:, lanes] = part
                    else:
                        dq_ref[:, lanes] += part

            step(i, True)

            @pl.loop(0, i)
            def _(j):
                step(j, False)

            out_ref[rows, lanes] = (dq_ref[:, lanes] * 0.125).astype(jnp.bfloat16)

    @pl.loop(0, count)
    def _(j):
        rows = pl.ds(pl.multiple_of(j * block, block), block)
        keys = dkv_ref[0, rows, :] * (1.0 / LOG2E)
        values = dkv_ref[1, rows, :]
        keys = keys + jnp.concatenate([keys[:, 64:], keys[:, :64]], axis=1)
        values = values + jnp.concatenate([values[:, 64:], values[:, :64]], axis=1)
        out_ref[rows, pl.ds(heads * 64, 128)] = jnp.where(low, keys, values).astype(jnp.bfloat16)

def attend_back(packed, g, dots, heads, block=512):
    total = packed.shape[0]
    cost = heads * total * total // 2
    return pl.pallas_call(
        functools.partial(back_kernel, block, heads),
        out_shape=jax.ShapeDtypeStruct(packed.shape, jnp.bfloat16),
        in_specs=[pl.BlockSpec(memory_space=pltpu.VMEM)] * 3,
        out_specs=pl.BlockSpec(memory_space=pltpu.VMEM),
        scratch_shapes=[
            pltpu.VMEM((block, heads * 64), jnp.float32),
            pltpu.VMEM((2, total, 128), jnp.float32),
        ]
        + [pltpu.VMEM((total, 128), jnp.bfloat16)] * 4,
        compiler_params=pltpu.CompilerParams(vmem_limit_bytes=56 << 20),
        cost_estimate=pl.CostEstimate(
            flops=10 * cost * 256, bytes_accessed=12 * packed.size, transcendentals=cost
        ),
        name="attend_back",
    )(packed, g, dots)


def remote(source, target, send, arrive, device):
    return pltpu.make_async_remote_copy(
        src_ref=source,
        dst_ref=target,
        send_sem=send,
        recv_sem=arrive,
        device_id=device,
        device_id_type=pl.DeviceIdType.MESH,
    )


def place():
    narrow = lax.axis_index("narrow")
    wide = lax.axis_index("wide")
    return narrow, wide, wide // 2, wide % 2


def greet_neighbours():
    narrow, wide, chip, core = place()
    barrier = pltpu.get_barrier_semaphore()

    def tell(device):
        pl.semaphore_signal(
            barrier, inc=1, device_id=device, device_id_type=pl.DeviceIdType.MESH
        )

    tell((narrow + 1 - 2 * (narrow % 2), wide))
    tell(((narrow + 2) % 4, wide))
    tell((narrow, 2 * chip + 1 - core))

    @pl.when(chip > 0)
    def _():
        tell((narrow, wide - 2))

    @pl.when(chip < 3)
    def _():
        tell((narrow, wide + 2))

    pl.semaphore_wait(barrier, 3 + jnp.minimum(chip, 1) + jnp.minimum(3 - chip, 1))


def gather_kernel(
    att_ref, att_all, own_sem, line_send, line_got, side_send, side_got, core_send, core_got
):
    narrow, wide, chip, core = place()
    beside = narrow + 1 - 2 * (narrow % 2)
    across = (narrow + 2) % 4
    corner = (beside + 2) % 4
    rows = att_ref.shape[0]
    half_rows = rows // 2
    other = (narrow, 2 * chip + 1 - core)
    left = (narrow, wide - 2)
    right = (narrow, wide + 2)
    sides = ((beside, wide), (across, wide))
    near = (beside, across)

    def att(slot, who):
        return att_all.at[slot, pl.ds(pl.multiple_of(who * rows, rows), rows), :]

    def att_half(slot, who, half):
        return att_all.at[
            slot, pl.ds(pl.multiple_of(who * rows + half * half_rows, half_rows), half_rows), :
        ]

    def line(at, step, source):
        return remote(
            source, att(2 * at + core, narrow), line_send.at[at, (step + 1) // 2],
            line_got.at[at], right if step > 0 else left,
        )

    def both_ways(at, source, act):
        @pl.when(jnp.logical_and(at <= chip, chip < 3))
        def _():
            act(line(at, 1, source))

        @pl.when(jnp.logical_and(at >= chip, chip > 0))
        def _():
            act(line(at, -1, source))

    def side(at, k, source):
        return remote(
            source, att(2 * at + core, narrow), side_send.at[at, k], side_got.at[at, k], sides[k]
        )

    def side_arrival(at, k):
        target = att(2 * at + core, near[k])
        return remote(target, target, side_send.at[at, k], side_got.at[at, k], sides[k])

    def forward(at, k):
        piece = att_half(2 * at + core, near[k], k)
        return remote(piece, piece, side_send.at[at, 2 + k], side_got.at[at, 2 + k], sides[1 - k])

    def corner_arrival(at, k):
        piece = att_half(2 * at + core, corner, k)
        return remote(piece, piece, side_send.at[at, 2 + k], side_got.at[at, 2 + k], sides[1 - k])

    def pair(at, who, half_of):
        piece = att(2 * at + half_of, who)
        return remote(piece, piece, core_send.at[at, who], core_got.at[at, who], other)

    start = lambda copy: copy.start()
    greet_neighbours()
    both_ways(chip, att_ref, start)
    for k in range(2):
        side(chip, k, att_ref).start()
    own = pltpu.make_async_copy(att_ref, att(wide, narrow), own_sem)
    own.start()
    own.wait()
    pair(chip, narrow, core).start()

    def hop(distance):
        for at, valid in (
            (chip - distance, chip >= distance), (chip + distance, chip + distance <= 3)
        ):

            @pl.when(valid)
            def _():
                piece = att(2 * at + core, narrow)
                line(at, 1, piece).wait_recv()
                both_ways(at, piece, start)
                for k in range(2):
                    side(at, k, piece).start()
                pair(at, narrow, core).start()

    def around(at):
        for k in range(2):
            side_arrival(at, k).wait_recv()
            forward(at, k).start()
            pair(at, near[k], core).start()

    upper = chip // 2
    second = chip + 1 - 2 * upper
    last = 3 - 3 * upper
    order = (chip, second, 6 - chip - second - last, last)
    for step in range(4):
        if step < 3:
            hop(step + 1)
        around(order[step])
    for at in order:
        for k in range(2):
            corner_arrival(at, k).wait_recv()
        pair(at, corner, core).start()

    for at in range(4):
        both_ways(at, att_ref, lambda copy: copy.wait_send())
        for who in range(4):
            pair(at, who, 1 - core).wait_recv()
            pair(at, who, core).wait_send()
        for k in range(2):
            side(at, k, att_ref).wait_send()
            forward(at, k).wait_send()


def gather_weights(att):
    narrow_count = lax.axis_size("narrow")
    wide_count = lax.axis_size("wide")
    if narrow_count != 4 or wide_count != 8:
        return lax.all_gather(lax.all_gather(att, "wide", axis=0), "narrow", axis=1, tiled=True)
    dma = pltpu.SemaphoreType.DMA
    return pl.pallas_call(
        gather_kernel,
        out_shape=jax.ShapeDtypeStruct((8, 4 * att.shape[0], att.shape[1]), jnp.bfloat16),
        in_specs=[pl.BlockSpec(memory_space=pl.ANY)],
        out_specs=pl.BlockSpec(memory_space=pl.ANY),
        scratch_shapes=[
            dma, dma((4, 2)), dma((4,)), dma((4, 4)), dma((4, 4)), dma((4, 4)), dma((4, 4)),
        ],
        compiler_params=pltpu.CompilerParams(collective_id=1, has_side_effects=True),
        cost_estimate=pl.CostEstimate(flops=0, bytes_accessed=300 << 20, transcendentals=0),
        name="gather_weights",
    )(att)


def gather_rows(shard):
    return lax.all_gather(shard, "wide", axis=0, tiled=True)


def swap(blocks):
    return lax.all_to_all(blocks, "wide", 0, 0)


def sum_back(pairs):
    summed = 0.0
    for gradient, weight in pairs:
        summed = summed + dot_back(gradient, weight)
    return lax.psum_scatter(
        summed.astype(jnp.bfloat16), "wide", scatter_dimension=0, tiled=True
    ).astype(jnp.float32)


def scatter_kernel(
    in_ref, out_ref, gain_ref, sum_ref, spread_ref, gain_sum_ref,
    own, other, halves, wholes, from_left, from_right, low, wide_gains, mid_gain, narrow_gains,
    load_sem, core_send, core_got, half_send, half_got, whole_send, whole_got,
    line_send, left_got, right_got, spread_send, spread_got, pass_send, pass_got,
    wide_send, wide_got, narrow_send, narrow_got,
):
    narrow, wide, chip, core = place()
    beside = narrow + 1 - 2 * (narrow % 2)
    across = (narrow + 2) % 4
    corner = (beside + 2) % 4
    rows = sum_ref.shape[0]
    half_rows = rows // 2
    split = in_ref.shape[2]
    twin = (narrow, 2 * chip + 1 - core)
    sides = ((beside, wide), (across, wide))
    near = (beside, across)
    wides = [(narrow, (wide + step) % 8) for step in range(1, 8)]
    narrows = [((narrow + step) % 4, wide) for step in range(1, 4)]
    upper = chip // 2
    last = 3 - 3 * upper
    second = chip + 1 - 2 * upper
    order = (last, 6 - chip - second - last, second, chip)
    f32 = jnp.float32

    barrier = pltpu.get_barrier_semaphore()
    for device in wides + narrows:
        pl.semaphore_signal(
            barrier, inc=1, device_id=device, device_id_type=pl.DeviceIdType.MESH
        )
    pl.semaphore_wait(barrier, 10)

    parts = ((in_ref, pl.ds(0, split)), (out_ref, pl.ds(split, out_ref.shape[2])))

    def load(at, k):
        source, lanes = parts[k]
        return pltpu.make_async_copy(
            source.at[2 * at + core], own.at[at, :, lanes], load_sem.at[at, k]
        )

    def exchange(at, k):
        source, lanes = parts[k]
        return remote(
            source.at[2 * at + 1 - core], other.at[at, :, lanes], core_send.at[at, k],
            core_got.at[at, k], twin,
        )

    def block(at, who):
        return own.at[at, pl.ds(pl.multiple_of(who * rows, rows), rows), :]

    def half_block(at, who, half):
        return own.at[
            at, pl.ds(pl.multiple_of(who * rows + half * half_rows, half_rows), half_rows), :
        ]

    def half(at, k):
        return remote(
            half_block(at, corner, k), halves.at[at, k], half_send.at[at, k], half_got.at[at, k],
            sides[k],
        )

    def whole(at, k):
        return remote(
            block(at, near[k]), wholes.at[at, k], whole_send.at[at, k], whole_got.at[at, k],
            sides[k],
        )

    def to_right(at):
        return remote(
            block(at, narrow), from_left.at[at], line_send.at[at], left_got.at[at],
            (narrow, wide + 2),
        )

    def to_left(at):
        return remote(
            block(at, narrow), from_right.at[at], line_send.at[at], right_got.at[at],
            (narrow, wide - 2),
        )

    def add(target, source, count, step=64):
        @pl.loop(0, count // step)
        def _(i):
            piece = pl.ds(pl.multiple_of(i * step, step), step)
            target[piece, :] = (
                target[piece, :].astype(f32) + source[piece, :].astype(f32)
            ).astype(jnp.bfloat16)

    for at in order:
        for k in range(2):
            load(at, k).start()
            exchange(at, k).start()
    gains = [
        remote(gain_ref, wide_gains.at[step], wide_send.at[step], wide_got.at[step], device)
        for step, device in enumerate(wides)
    ]
    for copy in gains:
        copy.start()

    def pair_up(at):
        for k in range(2):
            load(at, k).wait()
            exchange(at, k).wait_recv()
        add(own.at[at], other.at[at], 4 * rows)
        for k in range(2):
            half(at, k).start()

    def turn(at):
        for k in range(2):
            half(at, k).wait_recv()
            add(half_block(at, near[1 - k], k), halves.at[at, k], half_rows)
        for k in range(2):
            whole(at, k).start()

    def settle(at):
        for k in range(2):
            whole(at, k).wait_recv()
        target = block(at, narrow)

        @pl.loop(0, rows // 64)
        def _(i):
            piece = pl.ds(pl.multiple_of(i * 64, 64), 64)
            target[piece, :] = (
                target[piece, :].astype(f32)
                + wholes[at, 0, piece, :].astype(f32)
                + wholes[at, 1, piece, :].astype(f32)
            ).astype(jnp.bfloat16)

        @pl.when(at > chip)
        def _():
            @pl.when(chip > 0)
            def _():
                to_right(at).wait_recv()
                add(target, from_left.at[at], rows)

            to_right(at).start()

        @pl.when(at < chip)
        def _():
            @pl.when(chip < 3)
            def _():
                to_left(at).wait_recv()
                add(target, from_right.at[at], rows)

            to_left(at).start()

    pair_up(order[0])
    pair_up(order[1])
    turn(order[0])
    pair_up(order[2])
    turn(order[1])
    settle(order[0])
    pair_up(order[3])
    turn(order[2])
    settle(order[1])
    for copy in gains:
        copy.wait()
    total = gain_ref[...]
    for step in range(7):
        total = total + wide_gains[step]
    mid_gain[...] = total
    gains = [
        remote(mid_gain, narrow_gains.at[step], narrow_send.at[step], narrow_got.at[step], device)
        for step, device in enumerate(narrows)
    ]
    for copy in gains:
        copy.start()
    turn(order[3])
    settle(order[2])
    settle(order[3])
    target = block(chip, narrow)

    @pl.when(chip > 0)
    def _():
        to_right(chip).wait_recv()
        add(target, from_left.at[chip], rows)

    @pl.when(chip < 3)
    def _():
        to_left(chip).wait_recv()
        add(target, from_right.at[chip], rows)

    lanes = pl.ds(split - 128, 128)

    @pl.loop(0, rows // 64)
    def _(i):
        piece = pl.ds(pl.multiple_of(i * 64, 64), 64)
        value = target[piece, :]
        sum_ref[piece, :] = value.astype(f32)
        low[piece, :] = target[piece, lanes]

    spread_ref[wide] = low[...]

    def spread(step):
        return remote(
            low, spread_ref.at[wide], spread_send.at[step - 1], spread_got.at[step - 1],
            (narrow, (wide + 2 * step) % 8),
        )

    def arrival(step):
        target = spread_ref.at[(wide + 8 - 2 * step) % 8]
        return remote(target, target, spread_send.at[step - 1], spread_got.at[step - 1], twin)

    def pass_on(step):
        piece = spread_ref.at[(wide + 8 - 2 * step) % 8]
        return remote(piece, piece, pass_send.at[step], pass_got.at[step], twin)

    def passed(step):
        piece = spread_ref.at[(2 * chip + 1 - core + 8 - 2 * step) % 8]
        return remote(piece, piece, pass_send.at[step], pass_got.at[step], twin)

    for step in (1, 2, 3):
        spread(step).start()
    pass_on(0).start()
    for copy in gains:
        copy.wait()
    for step in range(3):
        total = total + narrow_gains[step]
    gain_sum_ref[...] = total
    for step in (1, 2, 3):
        arrival(step).wait_recv()
        pass_on(step).start()
    for step in range(4):
        passed(step).wait_recv()
        pass_on(step).wait_send()
    for step in (1, 2, 3):
        spread(step).wait_send()
    for at in range(4):
        for k in range(2):
            exchange(at, k).wait_send()
            half(at, k).wait_send()
            whole(at, k).wait_send()

        @pl.when(at != chip)
        def _():
            to_right(at).wait_send()


def sum_weights(input_wgrad, output_wgrad, gains):
    narrow_count = lax.axis_size("narrow")
    wide_count = lax.axis_size("wide")
    split = input_wgrad.shape[2]
    if narrow_count != 4 or wide_count != 8:
        total = jnp.concatenate([input_wgrad, output_wgrad], axis=2)
        total = lax.psum_scatter(total, "narrow", scatter_dimension=1, tiled=True)
        total = lax.psum_scatter(total, "wide", scatter_dimension=0)
        spread = lax.all_gather(total[:, split - 128 : split], "wide", axis=0)
        gains = jnp.sum(lax.all_gather(gains, ("narrow", "wide"), axis=0), axis=0)
        return total.astype(jnp.float32), spread, gains
    low = jnp.bfloat16
    rows = input_wgrad.shape[1] // 4
    columns = split + output_wgrad.shape[2]
    size = gains.size
    gain_rows = -(-size // 1024) * 8
    flat = jnp.pad(gains.reshape(-1), (0, gain_rows * 128 - size)).reshape(gain_rows, 128)
    dma = pltpu.SemaphoreType.DMA
    vmem = pltpu.VMEM
    total, spread, flat = pl.pallas_call(
        scatter_kernel,
        out_shape=[
            jax.ShapeDtypeStruct((rows, columns), jnp.float32),
            jax.ShapeDtypeStruct((8, rows, 128), low),
            jax.ShapeDtypeStruct(flat.shape, jnp.float32),
        ],
        in_specs=[
            pl.BlockSpec(memory_space=pl.ANY),
            pl.BlockSpec(memory_space=pl.ANY),
            pl.BlockSpec(memory_space=vmem),
        ],
        out_specs=[pl.BlockSpec(memory_space=vmem)] * 3,
        scratch_shapes=[
            vmem((4, 4 * rows, columns), low),
            vmem((4, 4 * rows, columns), low),
            vmem((4, 2, rows // 2, columns), low),
            vmem((4, 2, rows, columns), low),
            vmem((4, rows, columns), low),
            vmem((4, rows, columns), low),
            vmem((rows, 128), low),
            vmem((7, gain_rows, 128), jnp.float32),
            vmem((gain_rows, 128), jnp.float32),
            vmem((3, gain_rows, 128), jnp.float32),
            dma((4, 2)), dma((4, 2)), dma((4, 2)), dma((4, 2)), dma((4, 2)), dma((4, 2)),
            dma((4, 2)), dma((4,)), dma((4,)), dma((4,)), dma((3,)), dma((3,)), dma((4,)),
            dma((4,)), dma((7,)), dma((7,)), dma((3,)), dma((3,)),
        ],
        compiler_params=pltpu.CompilerParams(
            collective_id=3, has_side_effects=True, vmem_limit_bytes=52 << 20
        ),
        cost_estimate=pl.CostEstimate(flops=0, bytes_accessed=300 << 20, transcendentals=0),
        name="sum_weights",
    )(input_wgrad, output_wgrad, flat)
    return total, spread, flat.reshape(-1)[:size].reshape(gains.shape)


def tell_wide():
    narrow = lax.axis_index("narrow")
    wide = lax.axis_index("wide")
    barrier = pltpu.get_barrier_semaphore()
    for step in range(1, 8):
        pl.semaphore_signal(
            barrier, inc=1, device_id=(narrow, (wide + step) % 8),
            device_id_type=pl.DeviceIdType.MESH,
        )
    pl.semaphore_wait(barrier, 7)


def attend_swap_kernel(
    heads, src_ref, packed_ref, o_ref, s_ref, out_ref, kk_ref, va_ref, vb_ref, acc_ref, low_ref,
    own_sem, send_sem, got_sem, out_send, out_got,
):
    narrow, wide, chip, core = place()
    block = src_ref.shape[1]
    base = 4 * (chip // 2)
    away = 4 - base
    low = low_lanes(block)
    tell_wide()

    def send(to):
        return remote(
            src_ref.at[to], packed_ref.at[wide], send_sem.at[to], got_sem.at[wide], (narrow, to)
        )

    def arrival(at):
        target = packed_ref.at[at]
        return remote(target, target, send_sem.at[at], got_sem.at[at], (narrow, at))

    def send_out(to):
        return remote(
            low_ref.at[to], out_ref.at[wide], out_send.at[to], out_got.at[wide], (narrow, to)
        )

    own = pltpu.make_async_copy(src_ref.at[wide], packed_ref.at[wide], own_sem)
    own.start()
    for step in (1, 2, 3, 4, 5, 6, 7):
        send((wide + step) % 8).start()

    def prepare(j):
        rows = pl.ds(pl.multiple_of(j * block, block), block)
        kv = packed_ref[j, :, pl.ds(heads * 64, 128)]
        vk = jnp.concatenate([kv[:, 64:], kv[:, :64]], axis=1)
        one = jnp.ones_like(kv)
        kk_ref[rows, :] = jnp.where(low, kv, vk)
        va_ref[rows, :] = jnp.where(low, vk, one)
        vb_ref[rows, :] = jnp.where(low, one, kv)

    def await_blocks(start):
        @pl.loop(start, start + 4)
        def _(j):
            @pl.when(j != wide)
            def _():
                arrival(j).wait_recv()

            prepare(j)

    causal = lax.broadcasted_iota(jnp.int32, (block, block), 0) >= lax.broadcasted_iota(
        jnp.int32, (block, block), 1
    )

    def pairs(i, first, stop, diagonal):
        for pair in range(heads // 2):
            both = packed_ref[i, :, pl.ds(pair * 128, 128)]
            zero = jnp.zeros_like(both)
            sides = (jnp.where(low, both, zero), jnp.where(low, zero, both))

            def step(j, masked, fresh):
                keys = pl.ds(pl.multiple_of(j * block, block), block)
                kk = kk_ref[keys, :]
                for side in range(2):
                    weights = jnp.exp2(nt(sides[side], kk))
                    if masked:
                        weights = jnp.where(causal, weights, 0.0)
                    part = nn(weights.astype(jnp.bfloat16), (va_ref, vb_ref)[side][keys, :])
                    if fresh:
                        acc_ref[i, pair * 2 + side] = part
                    else:
                        acc_ref[i, pair * 2 + side] += part

            if diagonal:
                step(i, True, True)

            @pl.loop(first, stop)
            def _(j):
                step(j, False, False)

    def finish(i):
        rows = pl.ds(pl.multiple_of(i * block, block), block)
        for pair in range(heads // 2):
            lanes = pl.ds(pair * 128, 128)
            first, second = acc_ref[i, pair * 2], acc_ref[i, pair * 2 + 1]
            summed = jnp.where(low, first, second)
            sums = jnp.where(low, second, first)
            sums = jnp.concatenate([sums[:, 64:], sums[:, :64]], axis=1)
            result = summed / sums
            o_ref[rows, lanes] = result
            s_ref[rows, lanes] = sums
            low_ref[i, :, lanes] = result.astype(jnp.bfloat16)

        @pl.when(i != wide)
        def _():
            send_out(i).start()

        @pl.when(i == wide)
        def _():
            out_ref[i] = low_ref[i]

    own.wait()
    await_blocks(base)

    @pl.loop(base, base + 4)
    def _(i):
        pairs(i, base, i, True)

        @pl.when(base == 0)
        def _():
            finish(i)

    await_blocks(away)

    @pl.loop(away, away + 4)
    def _(i):
        pairs(i, 0, i, True)
        finish(i)

    @pl.when(base > 0)
    def _():
        @pl.loop(4, 8)
        def _(i):
            pairs(i, 0, 4, False)
            finish(i)

    for step in range(1, 8):
        to = (wide + step) % 8
        target = out_ref.at[to]
        remote(target, target, out_send.at[to], out_got.at[to], (narrow, to)).wait_recv()
        send_out(to).wait_send()
        send(to).wait_send()


def attend_swap(src, heads):
    if lax.axis_size("narrow") != 4 or lax.axis_size("wide") != 8:
        packed = swap(src)
        flat = packed.reshape(-1, src.shape[2])
        attended, weight_sums, attended_low = attend(flat, heads)
        return packed, attended, weight_sums, swap(attended_low.reshape(src.shape[0], -1, heads * 64))
    count, block, lanes = src.shape
    total = count * block
    dma = pltpu.SemaphoreType.DMA
    vmem = pltpu.VMEM
    cost = heads * total * total // 2
    return pl.pallas_call(
        functools.partial(attend_swap_kernel, heads),
        out_shape=[
            jax.ShapeDtypeStruct(src.shape, jnp.bfloat16),
            jax.ShapeDtypeStruct((total, heads * 64), jnp.float32),
            jax.ShapeDtypeStruct((total, heads * 64), jnp.float32),
            jax.ShapeDtypeStruct((count, block, heads * 64), jnp.bfloat16),
        ],
        in_specs=[pl.BlockSpec(memory_space=pl.ANY)],
        out_specs=[pl.BlockSpec(memory_space=vmem)] * 4,
        scratch_shapes=[vmem((total, 128), jnp.bfloat16)] * 3
        + [
            vmem((count, heads, block, 128), jnp.float32),
            vmem((count, block, heads * 64), jnp.bfloat16),
            dma, dma((8,)), dma((8,)), dma((8,)), dma((8,)),
        ],
        compiler_params=pltpu.CompilerParams(
            collective_id=4, has_side_effects=True, vmem_limit_bytes=52 << 20
        ),
        cost_estimate=pl.CostEstimate(
            flops=8 * cost * 256, bytes_accessed=12 * src.size, transcendentals=cost
        ),
        name="attend_swap",
    )(src)


def back_swap_kernel(
    heads, packed_ref, g_ref, o_ref, s_ref, dq_out, dkv_out,
    grad_ref, scaled_ref, dots_ref, dq_ref, dkv_ref, kk_ref, vv_ref, ka_ref, kb_ref,
    low_q, low_kv, own_sem, send_sem, got_sem, q_send, q_got, kv_send, kv_got,
):
    narrow, wide, chip, core = place()
    count, block, _ = packed_ref.shape
    base = 4 * (chip // 2)
    away = 4 - base
    low = low_lanes(block)
    tell_wide()

    def send(to):
        return remote(
            g_ref.at[to], grad_ref.at[wide], send_sem.at[to], got_sem.at[wide], (narrow, to)
        )

    def send_q(to):
        return remote(low_q.at[to], dq_out.at[wide], q_send.at[to], q_got.at[wide], (narrow, to))

    def send_kv(to):
        return remote(
            low_kv.at[to], dkv_out.at[wide], kv_send.at[to], kv_got.at[wide], (narrow, to)
        )

    own = pltpu.make_async_copy(g_ref.at[wide], grad_ref.at[wide], own_sem)
    own.start()
    for step in range(1, 8):
        send((wide + step) % 8).start()

    @pl.loop(0, count)
    def _(j):
        rows = pl.ds(pl.multiple_of(j * block, block), block)
        kv = packed_ref[j, :, pl.ds(heads * 64, 128)]
        vk = jnp.concatenate([kv[:, 64:], kv[:, :64]], axis=1)
        zero = jnp.zeros_like(kv)
        kk_ref[rows, :] = jnp.where(low, kv, vk)
        vv_ref[rows, :] = jnp.where(low, vk, kv)
        ka_ref[rows, :] = jnp.where(low, kv, zero)
        kb_ref[rows, :] = jnp.where(low, zero, vk)
        dkv_ref[0, rows, :] = jnp.zeros((block, 128), jnp.float32)
        dkv_ref[1, rows, :] = jnp.zeros((block, 128), jnp.float32)

    causal = lax.broadcasted_iota(jnp.int32, (block, block), 0) <= lax.broadcasted_iota(
        jnp.int32, (block, block), 1
    )
    first_lanes = lax.broadcasted_iota(jnp.int32, (8, 128), 1) < 64
    picks = (
        jnp.where(first_lanes, 1.0, 0.0).astype(jnp.bfloat16),
        jnp.where(first_lanes, 0.0, 1.0).astype(jnp.bfloat16),
    )

    def rows_back(i):
        rows = pl.ds(pl.multiple_of(i * block, block), block)
        for pair in range(heads // 2):
            lanes = pl.ds(pair * 128, 128)
            grad = grad_ref[i, :, lanes].astype(jnp.float32) / s_ref[rows, lanes]
            scaled_ref[...] = grad.astype(jnp.bfloat16)
            product = grad * o_ref[rows, lanes]
            high = product.astype(jnp.bfloat16)
            rest = (product - high.astype(jnp.float32)).astype(jnp.bfloat16)
            for side in range(2):
                dots_ref[side] = nt(picks[side], high) + nt(picks[side], rest)
            qboth = packed_ref[i, :, lanes]
            gboth = scaled_ref[...]
            zero = jnp.zeros_like(qboth)
            qs = (jnp.where(low, qboth, zero), jnp.where(low, zero, qboth))
            gs = (jnp.where(low, gboth, zero), jnp.where(low, zero, gboth))

            def step(j, diagonal):
                keys = pl.ds(pl.multiple_of(j * block, block), block)
                kk = kk_ref[keys, :]
                vv = vv_ref[keys, :]
                for side in range(2):
                    weights = jnp.exp2(nt(kk, qs[side]))
                    if diagonal:
                        weights = jnp.where(causal, weights, 0.0)
                    dots = dots_ref[side, pl.ds(0, 1), :]
                    grads = (weights * (nt(vv, gs[side]) - dots)).astype(jnp.bfloat16)
                    dkv_ref[1, keys, :] += nn(weights.astype(jnp.bfloat16), gs[side])
                    dkv_ref[0, keys, :] += nn(grads, qs[side])
                    part = tn(grads, (ka_ref, kb_ref)[side][keys, :])
                    if diagonal and side == 0:
                        dq_ref[...] = part
                    else:
                        dq_ref[...] += part

            step(i, True)

            @pl.loop(0, i)
            def _(j):
                step(j, False)

            low_q[i, :, lanes] = (dq_ref[...] * 0.125).astype(jnp.bfloat16)

        @pl.when(i != wide)
        def _():
            send_q(i).start()

        @pl.when(i == wide)
        def _():
            dq_out[i] = low_q[i]

    def keys_back(j):
        rows = pl.ds(pl.multiple_of(j * block, block), block)
        keys = dkv_ref[0, rows, :] * (1.0 / LOG2E)
        values = dkv_ref[1, rows, :]
        keys = keys + jnp.concatenate([keys[:, 64:], keys[:, :64]], axis=1)
        values = values + jnp.concatenate([values[:, 64:], values[:, :64]], axis=1)
        low_kv[j] = jnp.where(low, keys, values).astype(jnp.bfloat16)

        @pl.when(j != wide)
        def _():
            send_kv(j).start()

        @pl.when(j == wide)
        def _():
            dkv_out[j] = low_kv[j]

    own.wait()

    @pl.loop(0, 4)
    def _(k):
        i = base + 3 - k

        @pl.when(i != wide)
        def _():
            target = grad_ref.at[i]
            remote(target, target, send_sem.at[i], got_sem.at[i], (narrow, i)).wait_recv()

        rows_back(i)

        @pl.when(base > 0)
        def _():
            keys_back(i)

    @pl.loop(0, 4)
    def _(k):
        i = away + 3 - k
        target = grad_ref.at[i]
        remote(target, target, send_sem.at[i], got_sem.at[i], (narrow, i)).wait_recv()
        rows_back(i)
        keys_back(i)

    @pl.when(base == 0)
    def _():
        @pl.loop(0, 4)
        def _(k):
            keys_back(3 - k)

    for step in range(1, 8):
        to = (wide + step) % 8
        target = dq_out.at[to]
        remote(target, target, q_send.at[to], q_got.at[to], (narrow, to)).wait_recv()
        target = dkv_out.at[to]
        remote(target, target, kv_send.at[to], kv_got.at[to], (narrow, to)).wait_recv()
        send(to).wait_send()
        send_q(to).wait_send()
        send_kv(to).wait_send()


def back_swap(packed, grad, attended, weight_sums, heads):
    count, block, lanes = packed.shape
    split = heads * 64
    if lax.axis_size("narrow") != 4 or lax.axis_size("wide") != 8:
        head_grad = swap(grad).reshape(-1, split).astype(jnp.float32) / weight_sums
        dots = jnp.sum((head_grad * attended).reshape(-1, heads, 64), axis=-1).T
        result = attend_back(
            packed.reshape(-1, lanes), head_grad.astype(jnp.bfloat16), dots, heads
        )
        result = swap(result.reshape(packed.shape))
        return result[:, :, :split], result[:, :, split:]
    total = count * block
    dma = pltpu.SemaphoreType.DMA
    vmem = pltpu.VMEM
    low = jnp.bfloat16
    cost = heads * total * total // 2
    return pl.pallas_call(
        functools.partial(back_swap_kernel, heads),
        out_shape=[
            jax.ShapeDtypeStruct((count, block, split), low),
            jax.ShapeDtypeStruct((count, block, 128), low),
        ],
        in_specs=[
            pl.BlockSpec(memory_space=vmem),
            pl.BlockSpec(memory_space=pl.ANY),
            pl.BlockSpec(memory_space=vmem),
            pl.BlockSpec(memory_space=vmem),
        ],
        out_specs=[pl.BlockSpec(memory_space=vmem)] * 2,
        scratch_shapes=[
            vmem((count, block, split), low),
            vmem((block, 128), low),
            vmem((2, 8, block), jnp.float32),
            vmem((block, 128), jnp.float32),
            vmem((2, total, 128), jnp.float32),
        ]
        + [vmem((total, 128), low)] * 4
        + [
            vmem((count, block, split), low),
            vmem((count, block, 128), low),
            dma, dma((8,)), dma((8,)), dma((8,)), dma((8,)), dma((8,)), dma((8,)),
        ],
        compiler_params=pltpu.CompilerParams(
            collective_id=5, has_side_effects=True, vmem_limit_bytes=52 << 20
        ),
        cost_estimate=pl.CostEstimate(
            flops=12 * cost * 256, bytes_accessed=12 * packed.size, transcendentals=cost
        ),
        name="back_swap",
    )(packed, grad, attended, weight_sums)


def shards(
    tokens_in,
    out_grad,
    positions,
    query_weight,
    query_first,
    query_second,
    key_weight,
    key_first,
    key_second,
    value_weight,
    value_first,
    value_second,
    output_weight,
    output_first,
    output_second,
    gate_weight,
    gate_first,
    gate_second,
    up_weight,
    up_first,
    up_second,
    down_weight,
    down_first,
    down_second,
    norm_gains,
    norm_first,
    norm_second,
    head_gains,
    head_first,
    head_second,
):
    wide_count = lax.axis_size("wide")
    wide_rank = lax.axis_index("wide")
    narrow_count = lax.axis_size("narrow")
    head_dim = head_gains.shape[1]
    key_heads = key_weight.shape[1] // head_dim
    local_heads = query_weight.shape[1] // head_dim
    shard_rows, model_width = tokens_in.shape
    copies = wide_count // key_heads
    key_slot = wide_rank // copies
    key_own = lax.dynamic_slice_in_dim(key_weight, key_slot * head_dim, head_dim, 1)
    value_own = lax.dynamic_slice_in_dim(value_weight, key_slot * head_dim, head_dim, 1)
    query_columns = query_weight.shape[1]
    att_own = jnp.concatenate([query_weight, key_own, value_own, output_weight.T], axis=1)
    half_rows = shard_rows // 2
    grad_halves = [
        lax.all_gather(out_grad[:half_rows], "wide", axis=0, tiled=True),
        lax.all_gather(out_grad[half_rows:], "wide", axis=0, tiled=True),
    ]
    att_full, gate_own, up_own, down_own = lax.optimization_barrier(
        (
            gather_weights(att_own.astype(jnp.bfloat16)),
            gate_weight.astype(jnp.bfloat16),
            up_weight.astype(jnp.bfloat16),
            down_weight.astype(jnp.bfloat16),
        )
    )
    gate_local = lax.all_gather(gate_own, "narrow", axis=0, tiled=True)
    up_local = lax.all_gather(up_own, "narrow", axis=0, tiled=True)
    down_local = lax.all_gather(down_own, "narrow", axis=1, tiled=True)
    group_columns = query_columns + 2 * head_dim
    input_full = att_full[:, :, :group_columns]
    output_full = att_full[:, :, group_columns:]
    inverse = jnp.power(ROTARY_BASE, -2.0 * jnp.arange(head_dim // 2, dtype=jnp.float32) / head_dim)
    own_positions = lax.dynamic_slice_in_dim(positions, wide_rank * shard_rows, shard_rows, 0)
    angles = own_positions.astype(jnp.float32)[:, None] * inverse[None, :]
    cosine = jnp.cos(angles)
    sine_part = jnp.sin(angles)
    residual = tokens_in.astype(jnp.float32)
    normed_in, norm_in_back = jax.vjp(rms_scale, residual, norm_gains[0])
    rows_in = normed_in.astype(jnp.bfloat16)
    input_raw = jnp.einsum("td,gdc->gtc", rows_in, input_full, preferred_element_type=jnp.float32)
    query_raw = input_raw[:, :, :query_columns].reshape(
        wide_count, shard_rows, local_heads, head_dim
    )
    key_raw = input_raw[:, :, query_columns : query_columns + head_dim]
    value_rows = input_raw[:, :, query_columns + head_dim :].astype(jnp.bfloat16)

    def query_turn(raw_heads, gain):
        return rotate(
            rms_scale(raw_heads, gain), cosine[None, :, None, :], sine_part[None, :, None, :]
        )

    def key_turn(raw_heads, gain):
        return rotate(rms_scale(raw_heads, gain), cosine[None], sine_part[None])

    query_rot, query_back = jax.vjp(query_turn, query_raw, head_gains[0])
    key_rot, key_back = jax.vjp(key_turn, key_raw, head_gains[1])
    score_scale = head_dim ** (-0.5)
    query_rot = (
        (query_rot * (score_scale * LOG2E))
        .reshape(wide_count, shard_rows, query_columns)
        .astype(jnp.bfloat16)
    )
    packed = jnp.concatenate([query_rot, key_rot.astype(jnp.bfloat16), value_rows], axis=2)
    packed, grad_halves = lax.optimization_barrier((packed, grad_halves))
    packed, attended, weight_sums, attended_low = attend_swap(packed, local_heads)
    attended_low, gate_local, up_local, down_local = lax.optimization_barrier(
        (attended_low, gate_local, up_local, down_local)
    )
    branch = jnp.einsum("gth,gdh->td", attended_low, output_full, preferred_element_type=jnp.float32)
    middle = residual + branch
    normed_mid, norm_mid_back = jax.vjp(rms_scale, middle, norm_gains[1])
    mid_low = normed_mid.astype(jnp.bfloat16)
    down_wgrad = gate_wgrad = up_wgrad = 0.0
    block_parts = []
    mid_sums = []
    rows_halves = [gather_rows(mid_low[:half_rows]), gather_rows(mid_low[half_rows:])]
    hidden_grads = [dot_back(rows, down_local).astype(jnp.bfloat16) for rows in grad_halves]
    rows_halves[0], hidden_grads = lax.optimization_barrier((rows_halves[0], hidden_grads))
    for rows_mid, grad_rows, hidden_grad in zip(rows_halves, grad_halves, hidden_grads):
        gate_pre = dot_last(rows_mid, gate_local)
        up_pre = dot_last(rows_mid, up_local)
        hidden, hidden_back = jax.vjp(
            lambda gate_in, up_in: jax.nn.silu(gate_in) * up_in, gate_pre, up_pre
        )
        hidden_low = hidden.astype(jnp.bfloat16)
        gate_grad, up_grad = hidden_back(hidden_grad.astype(jnp.float32))
        gate_grad = gate_grad.astype(jnp.bfloat16)
        up_grad = up_grad.astype(jnp.bfloat16)
        mid_sums.append(sum_back(((gate_grad, gate_local), (up_grad, up_local))))
        block_parts.append(dot_last(hidden_low, down_local).astype(jnp.bfloat16))
        down_wgrad = down_wgrad + dot_first(hidden_low, grad_rows)
        gate_wgrad = gate_wgrad + dot_first(rows_mid, gate_grad)
        up_wgrad = up_wgrad + dot_first(rows_mid, up_grad)
    down_wgrad = down_wgrad.astype(jnp.bfloat16)
    gate_wgrad = gate_wgrad.astype(jnp.bfloat16)
    up_wgrad = up_wgrad.astype(jnp.bfloat16)
    mid_sums, gate_wgrad, up_wgrad, down_wgrad, block_parts = lax.optimization_barrier(
        (mid_sums, gate_wgrad, up_wgrad, down_wgrad, block_parts)
    )
    mid_back = jnp.concatenate(mid_sums, axis=0)
    middle_part, mid_gain_grad = norm_mid_back(mid_back)
    middle_grad = out_grad.astype(jnp.float32) + middle_part
    branch_grad = middle_grad.astype(jnp.bfloat16)
    attended_grad = jnp.einsum(
        "td,gdh->gth", branch_grad, output_full, preferred_element_type=jnp.float32
    ).astype(jnp.bfloat16)
    output_wgrad = jnp.einsum(
        "td,gth->gdh", branch_grad, attended_low, preferred_element_type=jnp.float32
    )
    attended_grad, down_wgrad = lax.optimization_barrier((attended_grad, down_wgrad))
    down_total = lax.psum_scatter(down_wgrad, "narrow", scatter_dimension=1, tiled=True)
    attended_grad, first_part, gate_wgrad = lax.optimization_barrier(
        (attended_grad, block_parts[0], gate_wgrad)
    )
    first_sum = lax.psum_scatter(first_part, "wide", scatter_dimension=0, tiled=True)
    gate_total = lax.psum_scatter(gate_wgrad, "narrow", scatter_dimension=0, tiled=True)
    query_rot_grad, key_value_grad = back_swap(
        packed, attended_grad, attended, weight_sums, local_heads
    )
    query_rot_grad, first_sum, gate_total, down_total, up_wgrad, second_part = (
        lax.optimization_barrier(
            (query_rot_grad, first_sum, gate_total, down_total, up_wgrad, block_parts[1])
        )
    )
    up_total = lax.psum_scatter(up_wgrad, "narrow", scatter_dimension=0, tiled=True)
    second_sum = lax.psum_scatter(second_part, "wide", scatter_dimension=0, tiled=True)
    query_rot_grad = query_rot_grad.astype(jnp.float32).reshape(
        wide_count, shard_rows, local_heads, head_dim
    )
    key_rot_grad = key_value_grad[:, :, :head_dim]
    query_raw_grad, query_gain_grad = query_back(query_rot_grad)
    key_raw_grad, key_gain_grad = key_back(key_rot_grad.astype(jnp.float32))
    input_low = jnp.concatenate(
        [
            query_raw_grad.reshape(wide_count, shard_rows, query_columns).astype(jnp.bfloat16),
            key_raw_grad.astype(jnp.bfloat16),
            key_value_grad[:, :, head_dim:],
        ],
        axis=2,
    )
    input_wgrad = jnp.einsum(
        "td,gtc->gdc", rows_in, input_low, preferred_element_type=jnp.float32
    ).astype(jnp.bfloat16)
    input_back = jnp.einsum("gtc,gdc->td", input_low, input_full, preferred_element_type=jnp.float32)
    input_part, in_gain_grad = norm_in_back(input_back)
    input_grad = middle_grad + input_part
    gain_stack = jnp.stack([in_gain_grad, mid_gain_grad])
    head_stack = jnp.stack([query_gain_grad, key_gain_grad])
    input_wgrad, up_total = lax.optimization_barrier((input_wgrad, up_total))
    input_total, spread, gains = sum_weights(
        input_wgrad,
        output_wgrad.astype(jnp.bfloat16),
        jnp.concatenate([gain_stack, head_stack], axis=1),
    )
    input_total, second_sum = lax.optimization_barrier((input_total, second_sum))
    block_sum = jnp.concatenate([first_sum, second_sum], axis=0).astype(jnp.float32)
    block_out = (middle + block_sum).astype(jnp.bfloat16)
    gain_total = gains[:, :model_width]
    head_total = gains[:, model_width:]
    output_total = input_total[:, group_columns:].T
    query_total = input_total[:, :query_columns]
    spread = jnp.sum(
        spread.reshape(key_heads, copies, -1, 2, head_dim).astype(jnp.float32), axis=1
    ).transpose(2, 1, 0, 3)
    key_total = spread[0].reshape(key_weight.shape)
    value_total = spread[1].reshape(value_weight.shape)
    gate_total, up_total, down_total = (
        gate_total.astype(jnp.float32),
        up_total.astype(jnp.float32),
        down_total.astype(jnp.float32),
    )
    wide_rate = D ** (-0.5)
    query_new = adam_update(
        query_weight, query_first, query_second, query_total, wide_rate, WEIGHT_DECAY
    )
    key_new = adam_update(key_weight, key_first, key_second, key_total, wide_rate, WEIGHT_DECAY)
    value_new = adam_update(
        value_weight, value_first, value_second, value_total, wide_rate, WEIGHT_DECAY
    )
    output_new = adam_update(
        output_weight, output_first, output_second, output_total, O_FAN ** (-0.5), WEIGHT_DECAY
    )
    gate_new = adam_update(
        gate_weight, gate_first, gate_second, gate_total, wide_rate, WEIGHT_DECAY
    )
    up_new = adam_update(up_weight, up_first, up_second, up_total, wide_rate, WEIGHT_DECAY)
    down_new = adam_update(
        down_weight, down_first, down_second, down_total, FF ** (-0.5), WEIGHT_DECAY
    )
    norm_new = adam_update(norm_gains, norm_first, norm_second, gain_total, GAIN_RATE, 0.0)
    head_new = adam_update(head_gains, head_first, head_second, head_total, GAIN_RATE, 0.0)
    return (
        block_out,
        input_grad,
        query_new[0],
        query_new[1],
        query_new[2],
        key_new[0],
        key_new[1],
        key_new[2],
        value_new[0],
        value_new[1],
        value_new[2],
        output_new[0],
        output_new[1],
        output_new[2],
        gate_new[0],
        gate_new[1],
        gate_new[2],
        up_new[0],
        up_new[1],
        up_new[2],
        down_new[0],
        down_new[1],
        down_new[2],
        norm_new[0],
        norm_new[1],
        norm_new[2],
        head_new[0],
        head_new[1],
        head_new[2],
    )


def solution(mesh):
    return jax.shard_map(
        shards,
        mesh=mesh,
        in_specs=(
            P(("narrow", "wide"), None),
            P(("narrow", "wide"), None),
            P("narrow"),
            P("narrow", "wide"),
            P("narrow", "wide"),
            P("narrow", "wide"),
            P("narrow", None),
            P("narrow", None),
            P("narrow", None),
            P("narrow", None),
            P("narrow", None),
            P("narrow", None),
            P("wide", "narrow"),
            P("wide", "narrow"),
            P("wide", "narrow"),
            P("narrow", "wide"),
            P("narrow", "wide"),
            P("narrow", "wide"),
            P("narrow", "wide"),
            P("narrow", "wide"),
            P("narrow", "wide"),
            P("wide", "narrow"),
            P("wide", "narrow"),
            P("wide", "narrow"),
            P(),
            P(),
            P(),
            P(),
            P(),
            P(),
        ),
        out_specs=(
            P(("narrow", "wide"), None),
            P(("narrow", "wide"), None),
            P("narrow", "wide"),
            P("narrow", "wide"),
            P("narrow", "wide"),
            P("narrow", None),
            P("narrow", None),
            P("narrow", None),
            P("narrow", None),
            P("narrow", None),
            P("narrow", None),
            P("wide", "narrow"),
            P("wide", "narrow"),
            P("wide", "narrow"),
            P("narrow", "wide"),
            P("narrow", "wide"),
            P("narrow", "wide"),
            P("narrow", "wide"),
            P("narrow", "wide"),
            P("narrow", "wide"),
            P("wide", "narrow"),
            P("wide", "narrow"),
            P("wide", "narrow"),
            P(),
            P(),
            P(),
            P(),
            P(),
            P(),
        ),
        check_vma=False,
    )
```

```python
import functools
import math

import jax
import jax.numpy as jnp
from jax import lax
from jax.experimental import pallas as pl
from jax.experimental.pallas import tpu as pltpu
from jax.sharding import PartitionSpec as P

D = 2048
FF = 8192
SEQ_LEN = 4096
STEP = 10
O_FAN = 50


EPSILON = 1e-06
BETA_ONE = 0.9
BETA_TWO = 0.95
ADAM_EPSILON = 1e-08
WEIGHT_DECAY = 0.1
GAIN_RATE = 1.0
ROTARY_BASE = 10000.0
MASKED_SCORE = -1e30


def rms_scale(inputs, gain):
    return inputs * lax.rsqrt(jnp.mean(inputs * inputs, axis=-1, keepdims=True) + EPSILON) * gain


def rotate(inputs, cosine, sine_part):
    half_width = inputs.shape[-1] // 2
    first_half = inputs[..., :half_width]
    second_half = inputs[..., half_width:]
    return jnp.concatenate(
        [
            first_half * cosine - second_half * sine_part,
            second_half * cosine + first_half * sine_part,
        ],
        axis=-1,
    )


def adam_update(weight, first_moment, second_moment, gradient, rate, decay):
    first_new = BETA_ONE * first_moment + (1.0 - BETA_ONE) * gradient
    second_new = BETA_TWO * second_moment + (1.0 - BETA_TWO) * gradient * gradient
    ratio = (
        first_new
        / (1.0 - BETA_ONE**STEP)
        / (jnp.sqrt(second_new / (1.0 - BETA_TWO**STEP)) + ADAM_EPSILON)
    )
    return (weight - rate * (ratio + decay * weight), first_new, second_new)


def dot_last(left, right):
    return jnp.dot(left, right, preferred_element_type=jnp.float32)


def dot_first(left, right):
    return lax.dot_general(
        left, right, (((0,), (0,)), ((), ())), preferred_element_type=jnp.float32
    )


def dot_back(left, right):
    return lax.dot_general(
        left, right, (((1,), (1,)), ((), ())), preferred_element_type=jnp.float32
    )


LOG2E = math.log2(math.e)

def nt(a, b):
    return lax.dot_general(a, b, (((1,), (1,)), ((), ())), preferred_element_type=jnp.float32)
def tn(a, b):
    return lax.dot_general(a, b, (((0,), (0,)), ((), ())), preferred_element_type=jnp.float32)
def nn(a, b):
    return jnp.dot(a, b, preferred_element_type=jnp.float32)

def low_lanes(rows):
    return lax.broadcasted_iota(jnp.int32, (rows, 128), 1) < 64

def attend_kernel(block, heads, q_ref, o_ref, s_ref, low_ref, kk_ref, va_ref, vb_ref, acc_ref):
    total = q_ref.shape[0]
    low = low_lanes(block)

    @pl.loop(0, total // block)
    def _(j):
        rows = pl.ds(pl.multiple_of(j * block, block), block)
        kv = q_ref[rows, pl.ds(heads * 64, 128)]
        vk = jnp.concatenate([kv[:, 64:], kv[:, :64]], axis=1)
        one = jnp.ones_like(kv)
        kk_ref[rows, :] = jnp.where(low, kv, vk)
        va_ref[rows, :] = jnp.where(low, vk, one)
        vb_ref[rows, :] = jnp.where(low, one, kv)

    causal = lax.broadcasted_iota(jnp.int32, (block, block), 0) >= lax.broadcasted_iota(
        jnp.int32, (block, block), 1
    )

    @pl.loop(0, total // block)
    def _(i):
        rows = pl.ds(pl.multiple_of(i * block, block), block)
        for pair in range(heads // 2):
            lanes = pl.ds(pair * 128, 128)
            both = q_ref[rows, lanes]
            zero = jnp.zeros_like(both)
            sides = (jnp.where(low, both, zero), jnp.where(low, zero, both))

            def step(j, diagonal):
                keys = pl.ds(pl.multiple_of(j * block, block), block)
                kk = kk_ref[keys, :]
                for side in range(2):
                    weights = jnp.exp2(nt(sides[side], kk))
                    if diagonal:
                        weights = jnp.where(causal, weights, 0.0)
                    part = nn(weights.astype(jnp.bfloat16), (va_ref, vb_ref)[side][keys, :])
                    if diagonal:
                        acc_ref[side] = part
                    else:
                        acc_ref[side] += part

            step(i, True)

            @pl.loop(0, i)
            def _(j):
                step(j, False)

            first, second = acc_ref[0], acc_ref[1]
            summed = jnp.where(low, first, second)
            sums = jnp.where(low, second, first)
            sums = jnp.concatenate([sums[:, 64:], sums[:, :64]], axis=1)
            result = summed / sums
            o_ref[rows, lanes] = result
            s_ref[rows, lanes] = sums
            low_ref[rows, lanes] = result.astype(jnp.bfloat16)

def attend(packed, heads, block=512):
    total = packed.shape[0]
    shape = (total, heads * 64)
    cost = heads * total * total // 2
    return pl.pallas_call(
        functools.partial(attend_kernel, block, heads),
        out_shape=[
            jax.ShapeDtypeStruct(shape, jnp.float32),
            jax.ShapeDtypeStruct(shape, jnp.float32),
            jax.ShapeDtypeStruct(shape, jnp.bfloat16),
        ],
        in_specs=[pl.BlockSpec(memory_space=pltpu.VMEM)],
        out_specs=[pl.BlockSpec(memory_space=pltpu.VMEM)] * 3,
        scratch_shapes=[pltpu.VMEM((total, 128), jnp.bfloat16)] * 3 + [pltpu.VMEM((2, block, 128), jnp.float32)],
        compiler_params=pltpu.CompilerParams(vmem_limit_bytes=56 << 20),
        cost_estimate=pl.CostEstimate(flops=4 * cost * 256, bytes_accessed=12 * packed.size, transcendentals=cost),
        name="attend",
    )(packed)

def back_kernel(block, heads, q_ref, g_ref, d_ref, out_ref, dq_ref, dkv_ref, kk_ref, vv_ref, ka_ref, kb_ref):
    total = q_ref.shape[0]
    low = low_lanes(block)
    count = total // block

    @pl.loop(0, count)
    def _(j):
        rows = pl.ds(pl.multiple_of(j * block, block), block)
        kv = q_ref[rows, pl.ds(heads * 64, 128)]
        vk = jnp.concatenate([kv[:, 64:], kv[:, :64]], axis=1)
        zero = jnp.zeros_like(kv)
        kk_ref[rows, :] = jnp.where(low, kv, vk)
        vv_ref[rows, :] = jnp.where(low, vk, kv)
        ka_ref[rows, :] = jnp.where(low, kv, zero)
        kb_ref[rows, :] = jnp.where(low, zero, vk)
        dkv_ref[0, rows, :] = jnp.zeros((block, 128), jnp.float32)
        dkv_ref[1, rows, :] = jnp.zeros((block, 128), jnp.float32)

    causal = lax.broadcasted_iota(jnp.int32, (block, block), 0) <= lax.broadcasted_iota(
        jnp.int32, (block, block), 1
    )

    @pl.loop(0, count)
    def _(i):
        rows = pl.ds(pl.multiple_of(i * block, block), block)
        for pair in range(heads // 2):
            lanes = pl.ds(pair * 128, 128)
            qboth = q_ref[rows, lanes]
            gboth = g_ref[rows, lanes]
            zero = jnp.zeros_like(qboth)
            qs = (jnp.where(low, qboth, zero), jnp.where(low, zero, qboth))
            gs = (jnp.where(low, gboth, zero), jnp.where(low, zero, gboth))

            def step(j, diagonal):
                keys = pl.ds(pl.multiple_of(j * block, block), block)
                kk = kk_ref[keys, :]
                vv = vv_ref[keys, :]
                for side in range(2):
                    weights = jnp.exp2(nt(kk, qs[side]))
                    if diagonal:
                        weights = jnp.where(causal, weights, 0.0)
                    dots = d_ref[pl.ds(pair * 2 + side, 1), rows]
                    grads = (weights * (nt(vv, gs[side]) - dots)).astype(jnp.bfloat16)
                    dkv_ref[1, keys, :] += nn(weights.astype(jnp.bfloat16), gs[side])
                    dkv_ref[0, keys, :] += nn(grads, qs[side])
                    part = tn(grads, (ka_ref, kb_ref)[side][keys, :])
                    if diagonal and side == 0:
                        dq_ref[:, lanes] = part
                    else:
                        dq_ref[:, lanes] += part

            step(i, True)

            @pl.loop(0, i)
            def _(j):
                step(j, False)

            out_ref[rows, lanes] = (dq_ref[:, lanes] * 0.125).astype(jnp.bfloat16)

    @pl.loop(0, count)
    def _(j):
        rows = pl.ds(pl.multiple_of(j * block, block), block)
        keys = dkv_ref[0, rows, :] * (1.0 / LOG2E)
        values = dkv_ref[1, rows, :]
        keys = keys + jnp.concatenate([keys[:, 64:], keys[:, :64]], axis=1)
        values = values + jnp.concatenate([values[:, 64:], values[:, :64]], axis=1)
        out_ref[rows, pl.ds(heads * 64, 128)] = jnp.where(low, keys, values).astype(jnp.bfloat16)

def attend_back(packed, g, dots, heads, block=512):
    total = packed.shape[0]
    cost = heads * total * total // 2
    return pl.pallas_call(
        functools.partial(back_kernel, block, heads),
        out_shape=jax.ShapeDtypeStruct(packed.shape, jnp.bfloat16),
        in_specs=[pl.BlockSpec(memory_space=pltpu.VMEM)] * 3,
        out_specs=pl.BlockSpec(memory_space=pltpu.VMEM),
        scratch_shapes=[
            pltpu.VMEM((block, heads * 64), jnp.float32),
            pltpu.VMEM((2, total, 128), jnp.float32),
        ]
        + [pltpu.VMEM((total, 128), jnp.bfloat16)] * 4,
        compiler_params=pltpu.CompilerParams(vmem_limit_bytes=56 << 20),
        cost_estimate=pl.CostEstimate(
            flops=10 * cost * 256, bytes_accessed=12 * packed.size, transcendentals=cost
        ),
        name="attend_back",
    )(packed, g, dots)


def remote(source, target, send, arrive, device):
    return pltpu.make_async_remote_copy(
        src_ref=source,
        dst_ref=target,
        send_sem=send,
        recv_sem=arrive,
        device_id=device,
        device_id_type=pl.DeviceIdType.MESH,
    )


def place():
    narrow = lax.axis_index("narrow")
    wide = lax.axis_index("wide")
    return narrow, wide, wide // 2, wide % 2


def greet_neighbours():
    narrow, wide, chip, core = place()
    barrier = pltpu.get_barrier_semaphore()

    def tell(device):
        pl.semaphore_signal(
            barrier, inc=1, device_id=device, device_id_type=pl.DeviceIdType.MESH
        )

    tell((narrow + 1 - 2 * (narrow % 2), wide))
    tell(((narrow + 2) % 4, wide))
    tell((narrow, 2 * chip + 1 - core))

    @pl.when(chip > 0)
    def _():
        tell((narrow, wide - 2))

    @pl.when(chip < 3)
    def _():
        tell((narrow, wide + 2))

    pl.semaphore_wait(barrier, 3 + jnp.minimum(chip, 1) + jnp.minimum(3 - chip, 1))


def gather_kernel(
    att_ref, att_all, own_sem, line_send, line_got, side_send, side_got, core_send, core_got
):
    narrow, wide, chip, core = place()
    beside = narrow + 1 - 2 * (narrow % 2)
    across = (narrow + 2) % 4
    corner = (beside + 2) % 4
    rows = att_ref.shape[0]
    half_rows = rows // 2
    other = (narrow, 2 * chip + 1 - core)
    left = (narrow, wide - 2)
    right = (narrow, wide + 2)
    sides = ((beside, wide), (across, wide))
    near = (beside, across)

    def att(slot, who):
        return att_all.at[slot, pl.ds(pl.multiple_of(who * rows, rows), rows), :]

    def att_half(slot, who, half):
        return att_all.at[
            slot, pl.ds(pl.multiple_of(who * rows + half * half_rows, half_rows), half_rows), :
        ]

    def line(at, step, source):
        return remote(
            source, att(2 * at + core, narrow), line_send.at[at, (step + 1) // 2],
            line_got.at[at], right if step > 0 else left,
        )

    def both_ways(at, source, act):
        @pl.when(jnp.logical_and(at <= chip, chip < 3))
        def _():
            act(line(at, 1, source))

        @pl.when(jnp.logical_and(at >= chip, chip > 0))
        def _():
            act(line(at, -1, source))

    def side(at, k, source):
        return remote(
            source, att(2 * at + core, narrow), side_send.at[at, k], side_got.at[at, k], sides[k]
        )

    def side_arrival(at, k):
        target = att(2 * at + core, near[k])
        return remote(target, target, side_send.at[at, k], side_got.at[at, k], sides[k])

    def forward(at, k):
        piece = att_half(2 * at + core, near[k], k)
        return remote(piece, piece, side_send.at[at, 2 + k], side_got.at[at, 2 + k], sides[1 - k])

    def corner_arrival(at, k):
        piece = att_half(2 * at + core, corner, k)
        return remote(piece, piece, side_send.at[at, 2 + k], side_got.at[at, 2 + k], sides[1 - k])

    def pair(at, who, half_of):
        piece = att(2 * at + half_of, who)
        return remote(piece, piece, core_send.at[at, who], core_got.at[at, who], other)

    start = lambda copy: copy.start()
    greet_neighbours()
    both_ways(chip, att_ref, start)
    for k in range(2):
        side(chip, k, att_ref).start()
    own = pltpu.make_async_copy(att_ref, att(wide, narrow), own_sem)
    own.start()
    own.wait()
    pair(chip, narrow, core).start()

    def hop(distance):
        for at, valid in (
            (chip - distance, chip >= distance), (chip + distance, chip + distance <= 3)
        ):

            @pl.when(valid)
            def _():
                piece = att(2 * at + core, narrow)
                line(at, 1, piece).wait_recv()
                both_ways(at, piece, start)
                for k in range(2):
                    side(at, k, piece).start()
                pair(at, narrow, core).start()

    def around(at):
        for k in range(2):
            side_arrival(at, k).wait_recv()
            forward(at, k).start()
            pair(at, near[k], core).start()

    upper = chip // 2
    second = chip + 1 - 2 * upper
    last = 3 - 3 * upper
    order = (chip, second, 6 - chip - second - last, last)
    for step in range(4):
        if step < 3:
            hop(step + 1)
        around(order[step])
    for at in order:
        for k in range(2):
            corner_arrival(at, k).wait_recv()
        pair(at, corner, core).start()

    for at in range(4):
        both_ways(at, att_ref, lambda copy: copy.wait_send())
        for who in range(4):
            pair(at, who, 1 - core).wait_recv()
            pair(at, who, core).wait_send()
        for k in range(2):
            side(at, k, att_ref).wait_send()
            forward(at, k).wait_send()


def gather_weights(att):
    narrow_count = lax.axis_size("narrow")
    wide_count = lax.axis_size("wide")
    if narrow_count != 4 or wide_count != 8:
        return lax.all_gather(lax.all_gather(att, "wide", axis=0), "narrow", axis=1, tiled=True)
    dma = pltpu.SemaphoreType.DMA
    return pl.pallas_call(
        gather_kernel,
        out_shape=jax.ShapeDtypeStruct((8, 4 * att.shape[0], att.shape[1]), jnp.bfloat16),
        in_specs=[pl.BlockSpec(memory_space=pl.ANY)],
        out_specs=pl.BlockSpec(memory_space=pl.ANY),
        scratch_shapes=[
            dma, dma((4, 2)), dma((4,)), dma((4, 4)), dma((4, 4)), dma((4, 4)), dma((4, 4)),
        ],
        compiler_params=pltpu.CompilerParams(collective_id=1, has_side_effects=True),
        cost_estimate=pl.CostEstimate(flops=0, bytes_accessed=300 << 20, transcendentals=0),
        name="gather_weights",
    )(att)


def gather_rows(shard):
    return lax.all_gather(shard, "wide", axis=0, tiled=True)


def swap(blocks):
    return lax.all_to_all(blocks, "wide", 0, 0)


def sum_back(pairs):
    summed = 0.0
    for gradient, weight in pairs:
        summed = summed + dot_back(gradient, weight)
    return lax.psum_scatter(
        summed.astype(jnp.bfloat16), "wide", scatter_dimension=0, tiled=True
    ).astype(jnp.float32)


def scatter_kernel(
    in_ref, out_ref, gain_ref, sum_ref, spread_ref, gain_sum_ref,
    own, other, halves, wholes, from_left, from_right, low, wide_gains, mid_gain, narrow_gains,
    load_sem, core_send, core_got, half_send, half_got, whole_send, whole_got,
    line_send, left_got, right_got, spread_send, spread_got, pass_send, pass_got,
    wide_send, wide_got, narrow_send, narrow_got,
):
    narrow, wide, chip, core = place()
    beside = narrow + 1 - 2 * (narrow % 2)
    across = (narrow + 2) % 4
    corner = (beside + 2) % 4
    rows = sum_ref.shape[0]
    half_rows = rows // 2
    split = in_ref.shape[2]
    twin = (narrow, 2 * chip + 1 - core)
    sides = ((beside, wide), (across, wide))
    near = (beside, across)
    wides = [(narrow, (wide + step) % 8) for step in range(1, 8)]
    narrows = [((narrow + step) % 4, wide) for step in range(1, 4)]
    upper = chip // 2
    last = 3 - 3 * upper
    second = chip + 1 - 2 * upper
    order = (last, 6 - chip - second - last, second, chip)
    f32 = jnp.float32

    barrier = pltpu.get_barrier_semaphore()
    for device in wides + narrows:
        pl.semaphore_signal(
            barrier, inc=1, device_id=device, device_id_type=pl.DeviceIdType.MESH
        )
    pl.semaphore_wait(barrier, 10)

    parts = ((in_ref, pl.ds(0, split)), (out_ref, pl.ds(split, out_ref.shape[2])))

    def load(at, k):
        source, lanes = parts[k]
        return pltpu.make_async_copy(
            source.at[2 * at + core], own.at[at, :, lanes], load_sem.at[at, k]
        )

    def exchange(at, k):
        source, lanes = parts[k]
        return remote(
            source.at[2 * at + 1 - core], other.at[at, :, lanes], core_send.at[at, k],
            core_got.at[at, k], twin,
        )

    def block(at, who):
        return own.at[at, pl.ds(pl.multiple_of(who * rows, rows), rows), :]

    def half_block(at, who, half):
        return own.at[
            at, pl.ds(pl.multiple_of(who * rows + half * half_rows, half_rows), half_rows), :
        ]

    def half(at, k):
        return remote(
            half_block(at, corner, k), halves.at[at, k], half_send.at[at, k], half_got.at[at, k],
            sides[k],
        )

    def whole(at, k):
        return remote(
            block(at, near[k]), wholes.at[at, k], whole_send.at[at, k], whole_got.at[at, k],
            sides[k],
        )

    def to_right(at):
        return remote(
            block(at, narrow), from_left.at[at], line_send.at[at], left_got.at[at],
            (narrow, wide + 2),
        )

    def to_left(at):
        return remote(
            block(at, narrow), from_right.at[at], line_send.at[at], right_got.at[at],
            (narrow, wide - 2),
        )

    def add(target, source, count, step=64):
        @pl.loop(0, count // step)
        def _(i):
            piece = pl.ds(pl.multiple_of(i * step, step), step)
            target[piece, :] = (
                target[piece, :].astype(f32) + source[piece, :].astype(f32)
            ).astype(jnp.bfloat16)

    for at in order:
        for k in range(2):
            load(at, k).start()
            exchange(at, k).start()
    gains = [
        remote(gain_ref, wide_gains.at[step], wide_send.at[step], wide_got.at[step], device)
        for step, device in enumerate(wides)
    ]
    for copy in gains:
        copy.start()

    def pair_up(at):
        for k in range(2):
            load(at, k).wait()
            exchange(at, k).wait_recv()
        add(own.at[at], other.at[at], 4 * rows)
        for k in range(2):
            half(at, k).start()

    def turn(at):
        for k in range(2):
            half(at, k).wait_recv()
            add(half_block(at, near[1 - k], k), halves.at[at, k], half_rows)
        for k in range(2):
            whole(at, k).start()

    def settle(at):
        for k in range(2):
            whole(at, k).wait_recv()
        target = block(at, narrow)

        @pl.loop(0, rows // 64)
        def _(i):
            piece = pl.ds(pl.multiple_of(i * 64, 64), 64)
            target[piece, :] = (
                target[piece, :].astype(f32)
                + wholes[at, 0, piece, :].astype(f32)
                + wholes[at, 1, piece, :].astype(f32)
            ).astype(jnp.bfloat16)

        @pl.when(at > chip)
        def _():
            @pl.when(chip > 0)
            def _():
                to_right(at).wait_recv()
                add(target, from_left.at[at], rows)

            to_right(at).start()

        @pl.when(at < chip)
        def _():
            @pl.when(chip < 3)
            def _():
                to_left(at).wait_recv()
                add(target, from_right.at[at], rows)

            to_left(at).start()

    pair_up(order[0])
    pair_up(order[1])
    turn(order[0])
    pair_up(order[2])
    turn(order[1])
    settle(order[0])
    pair_up(order[3])
    turn(order[2])
    settle(order[1])
    for copy in gains:
        copy.wait()
    total = gain_ref[...]
    for step in range(7):
        total = total + wide_gains[step]
    mid_gain[...] = total
    gains = [
        remote(mid_gain, narrow_gains.at[step], narrow_send.at[step], narrow_got.at[step], device)
        for step, device in enumerate(narrows)
    ]
    for copy in gains:
        copy.start()
    turn(order[3])
    settle(order[2])
    settle(order[3])
    target = block(chip, narrow)

    @pl.when(chip > 0)
    def _():
        to_right(chip).wait_recv()
        add(target, from_left.at[chip], rows)

    @pl.when(chip < 3)
    def _():
        to_left(chip).wait_recv()
        add(target, from_right.at[chip], rows)

    lanes = pl.ds(split - 128, 128)

    @pl.loop(0, rows // 64)
    def _(i):
        piece = pl.ds(pl.multiple_of(i * 64, 64), 64)
        value = target[piece, :]
        sum_ref[piece, :] = value.astype(f32)
        low[piece, :] = target[piece, lanes]

    spread_ref[wide] = low[...]

    def spread(step):
        return remote(
            low, spread_ref.at[wide], spread_send.at[step - 1], spread_got.at[step - 1],
            (narrow, (wide + 2 * step) % 8),
        )

    def arrival(step):
        target = spread_ref.at[(wide + 8 - 2 * step) % 8]
        return remote(target, target, spread_send.at[step - 1], spread_got.at[step - 1], twin)

    def pass_on(step):
        piece = spread_ref.at[(wide + 8 - 2 * step) % 8]
        return remote(piece, piece, pass_send.at[step], pass_got.at[step], twin)

    def passed(step):
        piece = spread_ref.at[(2 * chip + 1 - core + 8 - 2 * step) % 8]
        return remote(piece, piece, pass_send.at[step], pass_got.at[step], twin)

    for step in (1, 2, 3):
        spread(step).start()
    pass_on(0).start()
    for copy in gains:
        copy.wait()
    for step in range(3):
        total = total + narrow_gains[step]
    gain_sum_ref[...] = total
    for step in (1, 2, 3):
        arrival(step).wait_recv()
        pass_on(step).start()
    for step in range(4):
        passed(step).wait_recv()
        pass_on(step).wait_send()
    for step in (1, 2, 3):
        spread(step).wait_send()
    for at in range(4):
        for k in range(2):
            exchange(at, k).wait_send()
            half(at, k).wait_send()
            whole(at, k).wait_send()

        @pl.when(at != chip)
        def _():
            to_right(at).wait_send()


def sum_weights(input_wgrad, output_wgrad, gains):
    narrow_count = lax.axis_size("narrow")
    wide_count = lax.axis_size("wide")
    split = input_wgrad.shape[2]
    if narrow_count != 4 or wide_count != 8:
        total = jnp.concatenate([input_wgrad, output_wgrad], axis=2)
        total = lax.psum_scatter(total, "narrow", scatter_dimension=1, tiled=True)
        total = lax.psum_scatter(total, "wide", scatter_dimension=0)
        spread = lax.all_gather(total[:, split - 128 : split], "wide", axis=0)
        gains = jnp.sum(lax.all_gather(gains, ("narrow", "wide"), axis=0), axis=0)
        return total.astype(jnp.float32), spread, gains
    low = jnp.bfloat16
    rows = input_wgrad.shape[1] // 4
    columns = split + output_wgrad.shape[2]
    size = gains.size
    gain_rows = -(-size // 1024) * 8
    flat = jnp.pad(gains.reshape(-1), (0, gain_rows * 128 - size)).reshape(gain_rows, 128)
    dma = pltpu.SemaphoreType.DMA
    vmem = pltpu.VMEM
    total, spread, flat = pl.pallas_call(
        scatter_kernel,
        out_shape=[
            jax.ShapeDtypeStruct((rows, columns), jnp.float32),
            jax.ShapeDtypeStruct((8, rows, 128), low),
            jax.ShapeDtypeStruct(flat.shape, jnp.float32),
        ],
        in_specs=[
            pl.BlockSpec(memory_space=pl.ANY),
            pl.BlockSpec(memory_space=pl.ANY),
            pl.BlockSpec(memory_space=vmem),
        ],
        out_specs=[pl.BlockSpec(memory_space=vmem)] * 3,
        scratch_shapes=[
            vmem((4, 4 * rows, columns), low),
            vmem((4, 4 * rows, columns), low),
            vmem((4, 2, rows // 2, columns), low),
            vmem((4, 2, rows, columns), low),
            vmem((4, rows, columns), low),
            vmem((4, rows, columns), low),
            vmem((rows, 128), low),
            vmem((7, gain_rows, 128), jnp.float32),
            vmem((gain_rows, 128), jnp.float32),
            vmem((3, gain_rows, 128), jnp.float32),
            dma((4, 2)), dma((4, 2)), dma((4, 2)), dma((4, 2)), dma((4, 2)), dma((4, 2)),
            dma((4, 2)), dma((4,)), dma((4,)), dma((4,)), dma((3,)), dma((3,)), dma((4,)),
            dma((4,)), dma((7,)), dma((7,)), dma((3,)), dma((3,)),
        ],
        compiler_params=pltpu.CompilerParams(
            collective_id=3, has_side_effects=True, vmem_limit_bytes=52 << 20
        ),
        cost_estimate=pl.CostEstimate(flops=0, bytes_accessed=300 << 20, transcendentals=0),
        name="sum_weights",
    )(input_wgrad, output_wgrad, flat)
    return total, spread, flat.reshape(-1)[:size].reshape(gains.shape)


def tell_all():
    narrow = lax.axis_index("narrow")
    wide = lax.axis_index("wide")
    barrier = pltpu.get_barrier_semaphore()
    for step in range(1, 8):
        pl.semaphore_signal(
            barrier, inc=1, device_id=(narrow, (wide + step) % 8),
            device_id_type=pl.DeviceIdType.MESH,
        )
    for step in range(1, 4):
        pl.semaphore_signal(
            barrier, inc=1, device_id=((narrow + step) % 4, wide),
            device_id_type=pl.DeviceIdType.MESH,
        )
    pl.semaphore_wait(barrier, 10)


def tell_wide():
    narrow = lax.axis_index("narrow")
    wide = lax.axis_index("wide")
    barrier = pltpu.get_barrier_semaphore()
    for step in range(1, 8):
        pl.semaphore_signal(
            barrier, inc=1, device_id=(narrow, (wide + step) % 8),
            device_id_type=pl.DeviceIdType.MESH,
        )
    pl.semaphore_wait(barrier, 7)


def attend_swap_kernel(
    heads, src_ref, up_ref, down_ref, packed_ref, o_ref, s_ref, out_ref, up_all, down_all,
    kk_ref, va_ref, vb_ref, acc_ref, low_ref,
    own_sem, send_sem, got_sem, out_send, out_got, ffn_own, ffn_send, ffn_got,
):
    narrow, wide, chip, core = place()
    block = src_ref.shape[1]
    base = 4 * (chip // 2)
    away = 4 - base
    low = low_lanes(block)
    columns = down_ref.shape[1]
    tell_all()

    def ffn_slot(k, who):
        if k:
            return down_all.at[:, pl.ds(pl.multiple_of(who * columns, columns), columns)]
        return up_all.at[who]

    def ffn(k, step):
        return remote(
            (up_ref, down_ref)[k], ffn_slot(k, narrow), ffn_send.at[k, step],
            ffn_got.at[k, step], ((narrow + step) % 4, wide),
        )

    def ffn_arrival(k, step):
        target = ffn_slot(k, (narrow + 4 - step) % 4)
        return remote(
            target, target, ffn_send.at[k, step], ffn_got.at[k, step], ((narrow + step) % 4, wide)
        )

    def send(to):
        return remote(
            src_ref.at[to], packed_ref.at[wide], send_sem.at[to], got_sem.at[wide], (narrow, to)
        )

    def arrival(at):
        target = packed_ref.at[at]
        return remote(target, target, send_sem.at[at], got_sem.at[at], (narrow, at))

    def send_out(to):
        return remote(
            low_ref.at[to], out_ref.at[wide], out_send.at[to], out_got.at[wide], (narrow, to)
        )

    own = pltpu.make_async_copy(src_ref.at[wide], packed_ref.at[wide], own_sem)
    own.start()
    for step in range(1, 8):
        send((wide + step) % 8).start()
    keep = [
        pltpu.make_async_copy((up_ref, down_ref)[k], ffn_slot(k, narrow), ffn_own.at[k])
        for k in range(2)
    ]
    for k in (1, 0):
        keep[k].start()
        for step in range(1, 4):
            ffn(k, step).start()

    def prepare(j):
        rows = pl.ds(pl.multiple_of(j * block, block), block)
        kv = packed_ref[j, :, pl.ds(heads * 64, 128)]
        vk = jnp.concatenate([kv[:, 64:], kv[:, :64]], axis=1)
        one = jnp.ones_like(kv)
        kk_ref[rows, :] = jnp.where(low, kv, vk)
        va_ref[rows, :] = jnp.where(low, vk, one)
        vb_ref[rows, :] = jnp.where(low, one, kv)

    def await_blocks(start):
        @pl.loop(start, start + 4)
        def _(j):
            @pl.when(j != wide)
            def _():
                arrival(j).wait_recv()

            prepare(j)

    causal = lax.broadcasted_iota(jnp.int32, (block, block), 0) >= lax.broadcasted_iota(
        jnp.int32, (block, block), 1
    )

    def pairs(i, first, stop, diagonal):
        for pair in range(heads // 2):
            both = packed_ref[i, :, pl.ds(pair * 128, 128)]
            zero = jnp.zeros_like(both)
            sides = (jnp.where(low, both, zero), jnp.where(low, zero, both))

            def step(j, masked, fresh):
                keys = pl.ds(pl.multiple_of(j * block, block), block)
                kk = kk_ref[keys, :]
                for side in range(2):
                    weights = jnp.exp2(nt(sides[side], kk))
                    if masked:
                        weights = jnp.where(causal, weights, 0.0)
                    part = nn(weights.astype(jnp.bfloat16), (va_ref, vb_ref)[side][keys, :])
                    if fresh:
                        acc_ref[i, pair * 2 + side] = part
                    else:
                        acc_ref[i, pair * 2 + side] += part

            if diagonal:
                step(i, True, True)

            @pl.loop(first, stop)
            def _(j):
                step(j, False, False)

    def finish(i):
        rows = pl.ds(pl.multiple_of(i * block, block), block)
        for pair in range(heads // 2):
            lanes = pl.ds(pair * 128, 128)
            first, second = acc_ref[i, pair * 2], acc_ref[i, pair * 2 + 1]
            summed = jnp.where(low, first, second)
            sums = jnp.where(low, second, first)
            sums = jnp.concatenate([sums[:, 64:], sums[:, :64]], axis=1)
            result = summed / sums
            o_ref[rows, lanes] = result
            s_ref[rows, lanes] = sums
            low_ref[i, :, lanes] = result.astype(jnp.bfloat16)

        @pl.when(i != wide)
        def _():
            send_out(i).start()

        @pl.when(i == wide)
        def _():
            out_ref[i] = low_ref[i]

    own.wait()
    await_blocks(base)

    @pl.loop(base, base + 4)
    def _(i):
        pairs(i, base, i, True)

        @pl.when(base == 0)
        def _():
            finish(i)

    await_blocks(away)

    @pl.loop(away, away + 4)
    def _(i):
        pairs(i, 0, i, True)
        finish(i)

    @pl.when(base > 0)
    def _():
        @pl.loop(4, 8)
        def _(i):
            pairs(i, 0, 4, False)
            finish(i)

    for step in range(1, 8):
        to = (wide + step) % 8
        target = out_ref.at[to]
        remote(target, target, out_send.at[to], out_got.at[to], (narrow, to)).wait_recv()
        send_out(to).wait_send()
        send(to).wait_send()
    for k in range(2):
        keep[k].wait()
        for step in range(1, 4):
            ffn_arrival(k, step).wait_recv()
            ffn(k, step).wait_send()


def attend_swap(src, up, down, heads):
    if lax.axis_size("narrow") != 4 or lax.axis_size("wide") != 8:
        packed = swap(src)
        flat = packed.reshape(-1, src.shape[2])
        attended, weight_sums, attended_low = attend(flat, heads)
        attended_low = swap(attended_low.reshape(src.shape[0], -1, heads * 64))
        up_all = lax.all_gather(up, "narrow", axis=0, tiled=True)
        down_all = lax.all_gather(down, "narrow", axis=1, tiled=True)
        return packed, attended, weight_sums, attended_low, up_all, down_all
    count, block, lanes = src.shape
    total = count * block
    dma = pltpu.SemaphoreType.DMA
    vmem = pltpu.VMEM
    cost = heads * total * total // 2
    *results, up_all, down_all = pl.pallas_call(
        functools.partial(attend_swap_kernel, heads),
        out_shape=[
            jax.ShapeDtypeStruct(src.shape, jnp.bfloat16),
            jax.ShapeDtypeStruct((total, heads * 64), jnp.float32),
            jax.ShapeDtypeStruct((total, heads * 64), jnp.float32),
            jax.ShapeDtypeStruct((count, block, heads * 64), jnp.bfloat16),
            jax.ShapeDtypeStruct((4,) + up.shape, jnp.bfloat16),
            jax.ShapeDtypeStruct((down.shape[0], 4 * down.shape[1]), jnp.bfloat16),
        ],
        in_specs=[pl.BlockSpec(memory_space=pl.ANY)] * 3,
        out_specs=[pl.BlockSpec(memory_space=vmem)] * 4 + [pl.BlockSpec(memory_space=pl.ANY)] * 2,
        scratch_shapes=[vmem((total, 128), jnp.bfloat16)] * 3
        + [
            vmem((count, heads, block, 128), jnp.float32),
            vmem((count, block, heads * 64), jnp.bfloat16),
            dma, dma((8,)), dma((8,)), dma((8,)), dma((8,)), dma((2,)), dma((2, 4)), dma((2, 4)),
        ],
        compiler_params=pltpu.CompilerParams(
            collective_id=4, has_side_effects=True, vmem_limit_bytes=52 << 20
        ),
        cost_estimate=pl.CostEstimate(
            flops=8 * cost * 256, bytes_accessed=12 * src.size, transcendentals=cost
        ),
        name="attend_swap",
    )(src, up, down)
    return *results, up_all.reshape(-1, up.shape[1]), down_all


def back_swap_kernel(
    heads, packed_ref, g_ref, o_ref, s_ref, dq_out, dkv_out,
    grad_ref, scaled_ref, dots_ref, dq_ref, dkv_ref, kk_ref, vv_ref, ka_ref, kb_ref,
    low_q, low_kv, own_sem, send_sem, got_sem, q_send, q_got, kv_send, kv_got,
):
    narrow, wide, chip, core = place()
    count, block, _ = packed_ref.shape
    base = 4 * (chip // 2)
    away = 4 - base
    low = low_lanes(block)
    tell_wide()

    def send(to):
        return remote(
            g_ref.at[to], grad_ref.at[wide], send_sem.at[to], got_sem.at[wide], (narrow, to)
        )

    def send_q(to):
        return remote(low_q.at[to], dq_out.at[wide], q_send.at[to], q_got.at[wide], (narrow, to))

    def send_kv(to):
        return remote(
            low_kv.at[to], dkv_out.at[wide], kv_send.at[to], kv_got.at[wide], (narrow, to)
        )

    own = pltpu.make_async_copy(g_ref.at[wide], grad_ref.at[wide], own_sem)
    own.start()
    for step in range(1, 8):
        send((wide + step) % 8).start()

    @pl.loop(0, count)
    def _(j):
        rows = pl.ds(pl.multiple_of(j * block, block), block)
        kv = packed_ref[j, :, pl.ds(heads * 64, 128)]
        vk = jnp.concatenate([kv[:, 64:], kv[:, :64]], axis=1)
        zero = jnp.zeros_like(kv)
        kk_ref[rows, :] = jnp.where(low, kv, vk)
        vv_ref[rows, :] = jnp.where(low, vk, kv)
        ka_ref[rows, :] = jnp.where(low, kv, zero)
        kb_ref[rows, :] = jnp.where(low, zero, vk)
        dkv_ref[0, rows, :] = jnp.zeros((block, 128), jnp.float32)
        dkv_ref[1, rows, :] = jnp.zeros((block, 128), jnp.float32)

    causal = lax.broadcasted_iota(jnp.int32, (block, block), 0) <= lax.broadcasted_iota(
        jnp.int32, (block, block), 1
    )
    first_lanes = lax.broadcasted_iota(jnp.int32, (8, 128), 1) < 64
    picks = (
        jnp.where(first_lanes, 1.0, 0.0).astype(jnp.bfloat16),
        jnp.where(first_lanes, 0.0, 1.0).astype(jnp.bfloat16),
    )

    def rows_back(i):
        rows = pl.ds(pl.multiple_of(i * block, block), block)
        for pair in range(heads // 2):
            lanes = pl.ds(pair * 128, 128)
            grad = grad_ref[i, :, lanes].astype(jnp.float32) / s_ref[rows, lanes]
            scaled_ref[...] = grad.astype(jnp.bfloat16)
            product = grad * o_ref[rows, lanes]
            high = product.astype(jnp.bfloat16)
            rest = (product - high.astype(jnp.float32)).astype(jnp.bfloat16)
            for side in range(2):
                dots_ref[side] = nt(picks[side], high) + nt(picks[side], rest)
            qboth = packed_ref[i, :, lanes]
            gboth = scaled_ref[...]
            zero = jnp.zeros_like(qboth)
            qs = (jnp.where(low, qboth, zero), jnp.where(low, zero, qboth))
            gs = (jnp.where(low, gboth, zero), jnp.where(low, zero, gboth))

            def step(j, diagonal):
                keys = pl.ds(pl.multiple_of(j * block, block), block)
                kk = kk_ref[keys, :]
                vv = vv_ref[keys, :]
                for side in range(2):
                    weights = jnp.exp2(nt(kk, qs[side]))
                    if diagonal:
                        weights = jnp.where(causal, weights, 0.0)
                    dots = dots_ref[side, pl.ds(0, 1), :]
                    grads = (weights * (nt(vv, gs[side]) - dots)).astype(jnp.bfloat16)
                    dkv_ref[1, keys, :] += nn(weights.astype(jnp.bfloat16), gs[side])
                    dkv_ref[0, keys, :] += nn(grads, qs[side])
                    part = tn(grads, (ka_ref, kb_ref)[side][keys, :])
                    if diagonal and side == 0:
                        dq_ref[...] = part
                    else:
                        dq_ref[...] += part

            step(i, True)

            @pl.loop(0, i)
            def _(j):
                step(j, False)

            low_q[i, :, lanes] = (dq_ref[...] * 0.125).astype(jnp.bfloat16)

        @pl.when(i != wide)
        def _():
            send_q(i).start()

        @pl.when(i == wide)
        def _():
            dq_out[i] = low_q[i]

    def keys_back(j):
        rows = pl.ds(pl.multiple_of(j * block, block), block)
        keys = dkv_ref[0, rows, :] * (1.0 / LOG2E)
        values = dkv_ref[1, rows, :]
        keys = keys + jnp.concatenate([keys[:, 64:], keys[:, :64]], axis=1)
        values = values + jnp.concatenate([values[:, 64:], values[:, :64]], axis=1)
        low_kv[j] = jnp.where(low, keys, values).astype(jnp.bfloat16)

        @pl.when(j != wide)
        def _():
            send_kv(j).start()

        @pl.when(j == wide)
        def _():
            dkv_out[j] = low_kv[j]

    own.wait()

    @pl.loop(0, 4)
    def _(k):
        i = base + 3 - k

        @pl.when(i != wide)
        def _():
            target = grad_ref.at[i]
            remote(target, target, send_sem.at[i], got_sem.at[i], (narrow, i)).wait_recv()

        rows_back(i)

        @pl.when(base > 0)
        def _():
            keys_back(i)

    @pl.loop(0, 4)
    def _(k):
        i = away + 3 - k
        target = grad_ref.at[i]
        remote(target, target, send_sem.at[i], got_sem.at[i], (narrow, i)).wait_recv()
        rows_back(i)
        keys_back(i)

    @pl.when(base == 0)
    def _():
        @pl.loop(0, 4)
        def _(k):
            keys_back(3 - k)

    for step in range(1, 8):
        to = (wide + step) % 8
        target = dq_out.at[to]
        remote(target, target, q_send.at[to], q_got.at[to], (narrow, to)).wait_recv()
        target = dkv_out.at[to]
        remote(target, target, kv_send.at[to], kv_got.at[to], (narrow, to)).wait_recv()
        send(to).wait_send()
        send_q(to).wait_send()
        send_kv(to).wait_send()


def back_swap(packed, grad, attended, weight_sums, heads):
    count, block, lanes = packed.shape
    split = heads * 64
    if lax.axis_size("narrow") != 4 or lax.axis_size("wide") != 8:
        head_grad = swap(grad).reshape(-1, split).astype(jnp.float32) / weight_sums
        dots = jnp.sum((head_grad * attended).reshape(-1, heads, 64), axis=-1).T
        result = attend_back(
            packed.reshape(-1, lanes), head_grad.astype(jnp.bfloat16), dots, heads
        )
        result = swap(result.reshape(packed.shape))
        return result[:, :, :split], result[:, :, split:]
    total = count * block
    dma = pltpu.SemaphoreType.DMA
    vmem = pltpu.VMEM
    low = jnp.bfloat16
    cost = heads * total * total // 2
    return pl.pallas_call(
        functools.partial(back_swap_kernel, heads),
        out_shape=[
            jax.ShapeDtypeStruct((count, block, split), low),
            jax.ShapeDtypeStruct((count, block, 128), low),
        ],
        in_specs=[
            pl.BlockSpec(memory_space=vmem),
            pl.BlockSpec(memory_space=pl.ANY),
            pl.BlockSpec(memory_space=vmem),
            pl.BlockSpec(memory_space=vmem),
        ],
        out_specs=[pl.BlockSpec(memory_space=vmem)] * 2,
        scratch_shapes=[
            vmem((count, block, split), low),
            vmem((block, 128), low),
            vmem((2, 8, block), jnp.float32),
            vmem((block, 128), jnp.float32),
            vmem((2, total, 128), jnp.float32),
        ]
        + [vmem((total, 128), low)] * 4
        + [
            vmem((count, block, split), low),
            vmem((count, block, 128), low),
            dma, dma((8,)), dma((8,)), dma((8,)), dma((8,)), dma((8,)), dma((8,)),
        ],
        compiler_params=pltpu.CompilerParams(
            collective_id=5, has_side_effects=True, vmem_limit_bytes=52 << 20
        ),
        cost_estimate=pl.CostEstimate(
            flops=12 * cost * 256, bytes_accessed=12 * packed.size, transcendentals=cost
        ),
        name="back_swap",
    )(packed, grad, attended, weight_sums)


def shards(
    tokens_in,
    out_grad,
    positions,
    query_weight,
    query_first,
    query_second,
    key_weight,
    key_first,
    key_second,
    value_weight,
    value_first,
    value_second,
    output_weight,
    output_first,
    output_second,
    gate_weight,
    gate_first,
    gate_second,
    up_weight,
    up_first,
    up_second,
    down_weight,
    down_first,
    down_second,
    norm_gains,
    norm_first,
    norm_second,
    head_gains,
    head_first,
    head_second,
):
    wide_count = lax.axis_size("wide")
    wide_rank = lax.axis_index("wide")
    narrow_count = lax.axis_size("narrow")
    head_dim = head_gains.shape[1]
    key_heads = key_weight.shape[1] // head_dim
    local_heads = query_weight.shape[1] // head_dim
    shard_rows, model_width = tokens_in.shape
    copies = wide_count // key_heads
    key_slot = wide_rank // copies
    key_own = lax.dynamic_slice_in_dim(key_weight, key_slot * head_dim, head_dim, 1)
    value_own = lax.dynamic_slice_in_dim(value_weight, key_slot * head_dim, head_dim, 1)
    query_columns = query_weight.shape[1]
    att_own = jnp.concatenate([query_weight, key_own, value_own, output_weight.T], axis=1)
    half_rows = shard_rows // 2
    grad_halves = [
        lax.all_gather(out_grad[:half_rows], "wide", axis=0, tiled=True),
        lax.all_gather(out_grad[half_rows:], "wide", axis=0, tiled=True),
    ]
    att_full, gate_own = lax.optimization_barrier(
        (gather_weights(att_own.astype(jnp.bfloat16)), gate_weight.astype(jnp.bfloat16))
    )
    gate_local = lax.all_gather(gate_own, "narrow", axis=0, tiled=True)
    group_columns = query_columns + 2 * head_dim
    input_full = att_full[:, :, :group_columns]
    output_full = att_full[:, :, group_columns:]
    inverse = jnp.power(ROTARY_BASE, -2.0 * jnp.arange(head_dim // 2, dtype=jnp.float32) / head_dim)
    own_positions = lax.dynamic_slice_in_dim(positions, wide_rank * shard_rows, shard_rows, 0)
    angles = own_positions.astype(jnp.float32)[:, None] * inverse[None, :]
    cosine = jnp.cos(angles)
    sine_part = jnp.sin(angles)
    residual = tokens_in.astype(jnp.float32)
    normed_in, norm_in_back = jax.vjp(rms_scale, residual, norm_gains[0])
    rows_in = normed_in.astype(jnp.bfloat16)
    input_raw = jnp.einsum("td,gdc->gtc", rows_in, input_full, preferred_element_type=jnp.float32)
    query_raw = input_raw[:, :, :query_columns].reshape(
        wide_count, shard_rows, local_heads, head_dim
    )
    key_raw = input_raw[:, :, query_columns : query_columns + head_dim]
    value_rows = input_raw[:, :, query_columns + head_dim :].astype(jnp.bfloat16)

    def query_turn(raw_heads, gain):
        return rotate(
            rms_scale(raw_heads, gain), cosine[None, :, None, :], sine_part[None, :, None, :]
        )

    def key_turn(raw_heads, gain):
        return rotate(rms_scale(raw_heads, gain), cosine[None], sine_part[None])

    query_rot, query_back = jax.vjp(query_turn, query_raw, head_gains[0])
    key_rot, key_back = jax.vjp(key_turn, key_raw, head_gains[1])
    score_scale = head_dim ** (-0.5)
    query_rot = (
        (query_rot * (score_scale * LOG2E))
        .reshape(wide_count, shard_rows, query_columns)
        .astype(jnp.bfloat16)
    )
    packed = jnp.concatenate([query_rot, key_rot.astype(jnp.bfloat16), value_rows], axis=2)
    packed, grad_halves[0] = lax.optimization_barrier((packed, grad_halves[0]))
    packed, attended, weight_sums, attended_low, up_local, down_local = attend_swap(
        packed, up_weight.astype(jnp.bfloat16), down_weight.astype(jnp.bfloat16), local_heads
    )
    attended_low, gate_local, grad_halves[1] = lax.optimization_barrier(
        (attended_low, gate_local, grad_halves[1])
    )
    branch = jnp.einsum("gth,gdh->td", attended_low, output_full, preferred_element_type=jnp.float32)
    middle = residual + branch
    normed_mid, norm_mid_back = jax.vjp(rms_scale, middle, norm_gains[1])
    mid_low = normed_mid.astype(jnp.bfloat16)
    down_wgrad = gate_wgrad = up_wgrad = 0.0
    block_parts = []
    mid_sums = []
    rows_halves = [gather_rows(mid_low[:half_rows]), gather_rows(mid_low[half_rows:])]
    hidden_grads = [dot_back(rows, down_local).astype(jnp.bfloat16) for rows in grad_halves]
    rows_halves[0], hidden_grads = lax.optimization_barrier((rows_halves[0], hidden_grads))
    for rows_mid, grad_rows, hidden_grad in zip(rows_halves, grad_halves, hidden_grads):
        gate_pre = dot_last(rows_mid, gate_local)
        up_pre = dot_last(rows_mid, up_local)
        hidden, hidden_back = jax.vjp(
            lambda gate_in, up_in: jax.nn.silu(gate_in) * up_in, gate_pre, up_pre
        )
        hidden_low = hidden.astype(jnp.bfloat16)
        gate_grad, up_grad = hidden_back(hidden_grad.astype(jnp.float32))
        gate_grad = gate_grad.astype(jnp.bfloat16)
        up_grad = up_grad.astype(jnp.bfloat16)
        mid_sums.append(sum_back(((gate_grad, gate_local), (up_grad, up_local))))
        block_parts.append(dot_last(hidden_low, down_local).astype(jnp.bfloat16))
        down_wgrad = down_wgrad + dot_first(hidden_low, grad_rows)
        gate_wgrad = gate_wgrad + dot_first(rows_mid, gate_grad)
        up_wgrad = up_wgrad + dot_first(rows_mid, up_grad)
    down_wgrad = down_wgrad.astype(jnp.bfloat16)
    gate_wgrad = gate_wgrad.astype(jnp.bfloat16)
    up_wgrad = up_wgrad.astype(jnp.bfloat16)
    mid_sums, gate_wgrad, up_wgrad, down_wgrad, block_parts = lax.optimization_barrier(
        (mid_sums, gate_wgrad, up_wgrad, down_wgrad, block_parts)
    )
    mid_back = jnp.concatenate(mid_sums, axis=0)
    middle_part, mid_gain_grad = norm_mid_back(mid_back)
    middle_grad = out_grad.astype(jnp.float32) + middle_part
    branch_grad = middle_grad.astype(jnp.bfloat16)
    attended_grad = jnp.einsum(
        "td,gdh->gth", branch_grad, output_full, preferred_element_type=jnp.float32
    ).astype(jnp.bfloat16)
    output_wgrad = jnp.einsum(
        "td,gth->gdh", branch_grad, attended_low, preferred_element_type=jnp.float32
    )
    attended_grad, down_wgrad = lax.optimization_barrier((attended_grad, down_wgrad))
    down_total = lax.psum_scatter(down_wgrad, "narrow", scatter_dimension=1, tiled=True)
    attended_grad, up_wgrad, gate_wgrad = lax.optimization_barrier(
        (attended_grad, up_wgrad, gate_wgrad)
    )
    up_total = lax.psum_scatter(up_wgrad, "narrow", scatter_dimension=0, tiled=True)
    gate_total = lax.psum_scatter(gate_wgrad, "narrow", scatter_dimension=0, tiled=True)
    query_rot_grad, key_value_grad = back_swap(
        packed, attended_grad, attended, weight_sums, local_heads
    )
    query_rot_grad, gate_total, down_total, up_total, first_part, second_part = (
        lax.optimization_barrier(
            (query_rot_grad, gate_total, down_total, up_total, block_parts[0], block_parts[1])
        )
    )
    first_sum = lax.psum_scatter(first_part, "wide", scatter_dimension=0, tiled=True)
    second_sum = lax.psum_scatter(second_part, "wide", scatter_dimension=0, tiled=True)
    query_rot_grad = query_rot_grad.astype(jnp.float32).reshape(
        wide_count, shard_rows, local_heads, head_dim
    )
    key_rot_grad = key_value_grad[:, :, :head_dim]
    query_raw_grad, query_gain_grad = query_back(query_rot_grad)
    key_raw_grad, key_gain_grad = key_back(key_rot_grad.astype(jnp.float32))
    input_low = jnp.concatenate(
        [
            query_raw_grad.reshape(wide_count, shard_rows, query_columns).astype(jnp.bfloat16),
            key_raw_grad.astype(jnp.bfloat16),
            key_value_grad[:, :, head_dim:],
        ],
        axis=2,
    )
    input_wgrad = jnp.einsum(
        "td,gtc->gdc", rows_in, input_low, preferred_element_type=jnp.float32
    ).astype(jnp.bfloat16)
    input_back = jnp.einsum("gtc,gdc->td", input_low, input_full, preferred_element_type=jnp.float32)
    input_part, in_gain_grad = norm_in_back(input_back)
    input_grad = middle_grad + input_part
    gain_stack = jnp.stack([in_gain_grad, mid_gain_grad])
    head_stack = jnp.stack([query_gain_grad, key_gain_grad])
    input_wgrad, first_sum = lax.optimization_barrier((input_wgrad, first_sum))
    input_total, spread, gains = sum_weights(
        input_wgrad,
        output_wgrad.astype(jnp.bfloat16),
        jnp.concatenate([gain_stack, head_stack], axis=1),
    )
    input_total, second_sum = lax.optimization_barrier((input_total, second_sum))
    block_sum = jnp.concatenate([first_sum, second_sum], axis=0).astype(jnp.float32)
    block_out = (middle + block_sum).astype(jnp.bfloat16)
    gain_total = gains[:, :model_width]
    head_total = gains[:, model_width:]
    output_total = lax.optimization_barrier(input_total[:, group_columns:].T)
    query_total = input_total[:, :query_columns]
    spread = jnp.sum(
        spread.reshape(key_heads, copies, -1, 2, head_dim).astype(jnp.float32), axis=1
    ).transpose(2, 1, 0, 3)
    key_total = spread[0].reshape(key_weight.shape)
    value_total = spread[1].reshape(value_weight.shape)
    gate_total, up_total, down_total = (
        gate_total.astype(jnp.float32),
        up_total.astype(jnp.float32),
        down_total.astype(jnp.float32),
    )
    wide_rate = D ** (-0.5)
    query_new = adam_update(
        query_weight, query_first, query_second, query_total, wide_rate, WEIGHT_DECAY
    )
    key_new = adam_update(key_weight, key_first, key_second, key_total, wide_rate, WEIGHT_DECAY)
    value_new = adam_update(
        value_weight, value_first, value_second, value_total, wide_rate, WEIGHT_DECAY
    )
    output_new = adam_update(
        output_weight, output_first, output_second, output_total, O_FAN ** (-0.5), WEIGHT_DECAY
    )
    gate_new = adam_update(
        gate_weight, gate_first, gate_second, gate_total, wide_rate, WEIGHT_DECAY
    )
    up_new = adam_update(up_weight, up_first, up_second, up_total, wide_rate, WEIGHT_DECAY)
    down_new = adam_update(
        down_weight, down_first, down_second, down_total, FF ** (-0.5), WEIGHT_DECAY
    )
    norm_new = adam_update(norm_gains, norm_first, norm_second, gain_total, GAIN_RATE, 0.0)
    head_new = adam_update(head_gains, head_first, head_second, head_total, GAIN_RATE, 0.0)
    return (
        block_out,
        input_grad,
        query_new[0],
        query_new[1],
        query_new[2],
        key_new[0],
        key_new[1],
        key_new[2],
        value_new[0],
        value_new[1],
        value_new[2],
        output_new[0],
        output_new[1],
        output_new[2],
        gate_new[0],
        gate_new[1],
        gate_new[2],
        up_new[0],
        up_new[1],
        up_new[2],
        down_new[0],
        down_new[1],
        down_new[2],
        norm_new[0],
        norm_new[1],
        norm_new[2],
        head_new[0],
        head_new[1],
        head_new[2],
    )


def solution(mesh):
    return jax.shard_map(
        shards,
        mesh=mesh,
        in_specs=(
            P(("narrow", "wide"), None),
            P(("narrow", "wide"), None),
            P("narrow"),
            P("narrow", "wide"),
            P("narrow", "wide"),
            P("narrow", "wide"),
            P("narrow", None),
            P("narrow", None),
            P("narrow", None),
            P("narrow", None),
            P("narrow", None),
            P("narrow", None),
            P("wide", "narrow"),
            P("wide", "narrow"),
            P("wide", "narrow"),
            P("narrow", "wide"),
            P("narrow", "wide"),
            P("narrow", "wide"),
            P("narrow", "wide"),
            P("narrow", "wide"),
            P("narrow", "wide"),
            P("wide", "narrow"),
            P("wide", "narrow"),
            P("wide", "narrow"),
            P(),
            P(),
            P(),
            P(),
            P(),
            P(),
        ),
        out_specs=(
            P(("narrow", "wide"), None),
            P(("narrow", "wide"), None),
            P("narrow", "wide"),
            P("narrow", "wide"),
            P("narrow", "wide"),
            P("narrow", None),
            P("narrow", None),
            P("narrow", None),
            P("narrow", None),
            P("narrow", None),
            P("narrow", None),
            P("wide", "narrow"),
            P("wide", "narrow"),
            P("wide", "narrow"),
            P("narrow", "wide"),
            P("narrow", "wide"),
            P("narrow", "wide"),
            P("narrow", "wide"),
            P("narrow", "wide"),
            P("narrow", "wide"),
            P("wide", "narrow"),
            P("wide", "narrow"),
            P("wide", "narrow"),
            P(),
            P(),
            P(),
            P(),
            P(),
            P(),
        ),
        check_vma=False,
    )
```

```python
import functools
import math

import jax
import jax.numpy as jnp
from jax import lax
from jax.experimental import pallas as pl
from jax.experimental.pallas import tpu as pltpu
from jax.sharding import PartitionSpec as P

D = 2048
FF = 8192
SEQ_LEN = 4096
STEP = 10
O_FAN = 50


EPSILON = 1e-06
BETA_ONE = 0.9
BETA_TWO = 0.95
ADAM_EPSILON = 1e-08
WEIGHT_DECAY = 0.1
GAIN_RATE = 1.0
ROTARY_BASE = 10000.0
MASKED_SCORE = -1e30


def rms_scale(inputs, gain):
    return inputs * lax.rsqrt(jnp.mean(inputs * inputs, axis=-1, keepdims=True) + EPSILON) * gain


def rotate(inputs, cosine, sine_part):
    half_width = inputs.shape[-1] // 2
    first_half = inputs[..., :half_width]
    second_half = inputs[..., half_width:]
    return jnp.concatenate(
        [
            first_half * cosine - second_half * sine_part,
            second_half * cosine + first_half * sine_part,
        ],
        axis=-1,
    )


def adam_update(weight, first_moment, second_moment, gradient, rate, decay):
    first_new = BETA_ONE * first_moment + (1.0 - BETA_ONE) * gradient
    second_new = BETA_TWO * second_moment + (1.0 - BETA_TWO) * gradient * gradient
    ratio = (
        first_new
        / (1.0 - BETA_ONE**STEP)
        / (jnp.sqrt(second_new / (1.0 - BETA_TWO**STEP)) + ADAM_EPSILON)
    )
    return (weight - rate * (ratio + decay * weight), first_new, second_new)


def dot_last(left, right):
    return jnp.dot(left, right, preferred_element_type=jnp.float32)


def dot_first(left, right):
    return lax.dot_general(
        left, right, (((0,), (0,)), ((), ())), preferred_element_type=jnp.float32
    )


def dot_back(left, right):
    return lax.dot_general(
        left, right, (((1,), (1,)), ((), ())), preferred_element_type=jnp.float32
    )


LOG2E = math.log2(math.e)

def nt(a, b):
    return lax.dot_general(a, b, (((1,), (1,)), ((), ())), preferred_element_type=jnp.float32)
def tn(a, b):
    return lax.dot_general(a, b, (((0,), (0,)), ((), ())), preferred_element_type=jnp.float32)
def nn(a, b):
    return jnp.dot(a, b, preferred_element_type=jnp.float32)

def low_lanes(rows):
    return lax.broadcasted_iota(jnp.int32, (rows, 128), 1) < 64

def attend_kernel(block, heads, q_ref, o_ref, s_ref, low_ref, kk_ref, va_ref, vb_ref, acc_ref):
    total = q_ref.shape[0]
    low = low_lanes(block)

    @pl.loop(0, total // block)
    def _(j):
        rows = pl.ds(pl.multiple_of(j * block, block), block)
        kv = q_ref[rows, pl.ds(heads * 64, 128)]
        vk = jnp.concatenate([kv[:, 64:], kv[:, :64]], axis=1)
        one = jnp.ones_like(kv)
        kk_ref[rows, :] = jnp.where(low, kv, vk)
        va_ref[rows, :] = jnp.where(low, vk, one)
        vb_ref[rows, :] = jnp.where(low, one, kv)

    causal = lax.broadcasted_iota(jnp.int32, (block, block), 0) >= lax.broadcasted_iota(
        jnp.int32, (block, block), 1
    )

    @pl.loop(0, total // block)
    def _(i):
        rows = pl.ds(pl.multiple_of(i * block, block), block)
        for pair in range(heads // 2):
            lanes = pl.ds(pair * 128, 128)
            both = q_ref[rows, lanes]
            zero = jnp.zeros_like(both)
            sides = (jnp.where(low, both, zero), jnp.where(low, zero, both))

            def step(j, diagonal):
                keys = pl.ds(pl.multiple_of(j * block, block), block)
                kk = kk_ref[keys, :]
                for side in range(2):
                    weights = jnp.exp2(nt(sides[side], kk))
                    if diagonal:
                        weights = jnp.where(causal, weights, 0.0)
                    part = nn(weights.astype(jnp.bfloat16), (va_ref, vb_ref)[side][keys, :])
                    if diagonal:
                        acc_ref[side] = part
                    else:
                        acc_ref[side] += part

            step(i, True)

            @pl.loop(0, i)
            def _(j):
                step(j, False)

            first, second = acc_ref[0], acc_ref[1]
            summed = jnp.where(low, first, second)
            sums = jnp.where(low, second, first)
            sums = jnp.concatenate([sums[:, 64:], sums[:, :64]], axis=1)
            result = summed / sums
            o_ref[rows, lanes] = result
            s_ref[rows, lanes] = sums
            low_ref[rows, lanes] = result.astype(jnp.bfloat16)

def attend(packed, heads, block=512):
    total = packed.shape[0]
    shape = (total, heads * 64)
    cost = heads * total * total // 2
    return pl.pallas_call(
        functools.partial(attend_kernel, block, heads),
        out_shape=[
            jax.ShapeDtypeStruct(shape, jnp.float32),
            jax.ShapeDtypeStruct(shape, jnp.float32),
            jax.ShapeDtypeStruct(shape, jnp.bfloat16),
        ],
        in_specs=[pl.BlockSpec(memory_space=pltpu.VMEM)],
        out_specs=[pl.BlockSpec(memory_space=pltpu.VMEM)] * 3,
        scratch_shapes=[pltpu.VMEM((total, 128), jnp.bfloat16)] * 3 + [pltpu.VMEM((2, block, 128), jnp.float32)],
        compiler_params=pltpu.CompilerParams(vmem_limit_bytes=56 << 20),
        cost_estimate=pl.CostEstimate(flops=4 * cost * 256, bytes_accessed=12 * packed.size, transcendentals=cost),
        name="attend",
    )(packed)

def back_kernel(block, heads, q_ref, g_ref, d_ref, out_ref, dq_ref, dkv_ref, kk_ref, vv_ref, ka_ref, kb_ref):
    total = q_ref.shape[0]
    low = low_lanes(block)
    count = total // block

    @pl.loop(0, count)
    def _(j):
        rows = pl.ds(pl.multiple_of(j * block, block), block)
        kv = q_ref[rows, pl.ds(heads * 64, 128)]
        vk = jnp.concatenate([kv[:, 64:], kv[:, :64]], axis=1)
        zero = jnp.zeros_like(kv)
        kk_ref[rows, :] = jnp.where(low, kv, vk)
        vv_ref[rows, :] = jnp.where(low, vk, kv)
        ka_ref[rows, :] = jnp.where(low, kv, zero)
        kb_ref[rows, :] = jnp.where(low, zero, vk)
        dkv_ref[0, rows, :] = jnp.zeros((block, 128), jnp.float32)
        dkv_ref[1, rows, :] = jnp.zeros((block, 128), jnp.float32)

    causal = lax.broadcasted_iota(jnp.int32, (block, block), 0) <= lax.broadcasted_iota(
        jnp.int32, (block, block), 1
    )

    @pl.loop(0, count)
    def _(i):
        rows = pl.ds(pl.multiple_of(i * block, block), block)
        for pair in range(heads // 2):
            lanes = pl.ds(pair * 128, 128)
            qboth = q_ref[rows, lanes]
            gboth = g_ref[rows, lanes]
            zero = jnp.zeros_like(qboth)
            qs = (jnp.where(low, qboth, zero), jnp.where(low, zero, qboth))
            gs = (jnp.where(low, gboth, zero), jnp.where(low, zero, gboth))

            def step(j, diagonal):
                keys = pl.ds(pl.multiple_of(j * block, block), block)
                kk = kk_ref[keys, :]
                vv = vv_ref[keys, :]
                for side in range(2):
                    weights = jnp.exp2(nt(kk, qs[side]))
                    if diagonal:
                        weights = jnp.where(causal, weights, 0.0)
                    dots = d_ref[pl.ds(pair * 2 + side, 1), rows]
                    grads = (weights * (nt(vv, gs[side]) - dots)).astype(jnp.bfloat16)
                    dkv_ref[1, keys, :] += nn(weights.astype(jnp.bfloat16), gs[side])
                    dkv_ref[0, keys, :] += nn(grads, qs[side])
                    part = tn(grads, (ka_ref, kb_ref)[side][keys, :])
                    if diagonal and side == 0:
                        dq_ref[:, lanes] = part
                    else:
                        dq_ref[:, lanes] += part

            step(i, True)

            @pl.loop(0, i)
            def _(j):
                step(j, False)

            out_ref[rows, lanes] = (dq_ref[:, lanes] * 0.125).astype(jnp.bfloat16)

    @pl.loop(0, count)
    def _(j):
        rows = pl.ds(pl.multiple_of(j * block, block), block)
        keys = dkv_ref[0, rows, :] * (1.0 / LOG2E)
        values = dkv_ref[1, rows, :]
        keys = keys + jnp.concatenate([keys[:, 64:], keys[:, :64]], axis=1)
        values = values + jnp.concatenate([values[:, 64:], values[:, :64]], axis=1)
        out_ref[rows, pl.ds(heads * 64, 128)] = jnp.where(low, keys, values).astype(jnp.bfloat16)

def attend_back(packed, g, dots, heads, block=512):
    total = packed.shape[0]
    cost = heads * total * total // 2
    return pl.pallas_call(
        functools.partial(back_kernel, block, heads),
        out_shape=jax.ShapeDtypeStruct(packed.shape, jnp.bfloat16),
        in_specs=[pl.BlockSpec(memory_space=pltpu.VMEM)] * 3,
        out_specs=pl.BlockSpec(memory_space=pltpu.VMEM),
        scratch_shapes=[
            pltpu.VMEM((block, heads * 64), jnp.float32),
            pltpu.VMEM((2, total, 128), jnp.float32),
        ]
        + [pltpu.VMEM((total, 128), jnp.bfloat16)] * 4,
        compiler_params=pltpu.CompilerParams(vmem_limit_bytes=56 << 20),
        cost_estimate=pl.CostEstimate(
            flops=10 * cost * 256, bytes_accessed=12 * packed.size, transcendentals=cost
        ),
        name="attend_back",
    )(packed, g, dots)


def remote(source, target, send, arrive, device):
    return pltpu.make_async_remote_copy(
        src_ref=source,
        dst_ref=target,
        send_sem=send,
        recv_sem=arrive,
        device_id=device,
        device_id_type=pl.DeviceIdType.MESH,
    )


def place():
    narrow = lax.axis_index("narrow")
    wide = lax.axis_index("wide")
    return narrow, wide, wide // 2, wide % 2


def greet_neighbours():
    narrow, wide, chip, core = place()
    barrier = pltpu.get_barrier_semaphore()

    def tell(device):
        pl.semaphore_signal(
            barrier, inc=1, device_id=device, device_id_type=pl.DeviceIdType.MESH
        )

    tell((narrow + 1 - 2 * (narrow % 2), wide))
    tell(((narrow + 2) % 4, wide))
    tell((narrow, 2 * chip + 1 - core))

    @pl.when(chip > 0)
    def _():
        tell((narrow, wide - 2))

    @pl.when(chip < 3)
    def _():
        tell((narrow, wide + 2))

    pl.semaphore_wait(barrier, 3 + jnp.minimum(chip, 1) + jnp.minimum(3 - chip, 1))


def gather_kernel(
    att_ref, att_all, own_sem, line_send, line_got, side_send, side_got, core_send, core_got
):
    narrow, wide, chip, core = place()
    beside = narrow + 1 - 2 * (narrow % 2)
    across = (narrow + 2) % 4
    corner = (beside + 2) % 4
    rows = att_ref.shape[0]
    half_rows = rows // 2
    other = (narrow, 2 * chip + 1 - core)
    left = (narrow, wide - 2)
    right = (narrow, wide + 2)
    sides = ((beside, wide), (across, wide))
    near = (beside, across)

    def att(slot, who):
        return att_all.at[slot, pl.ds(pl.multiple_of(who * rows, rows), rows), :]

    def att_half(slot, who, half):
        return att_all.at[
            slot, pl.ds(pl.multiple_of(who * rows + half * half_rows, half_rows), half_rows), :
        ]

    def line(at, step, source):
        return remote(
            source, att(2 * at + core, narrow), line_send.at[at, (step + 1) // 2],
            line_got.at[at], right if step > 0 else left,
        )

    def both_ways(at, source, act):
        @pl.when(jnp.logical_and(at <= chip, chip < 3))
        def _():
            act(line(at, 1, source))

        @pl.when(jnp.logical_and(at >= chip, chip > 0))
        def _():
            act(line(at, -1, source))

    def side(at, k, source):
        return remote(
            source, att(2 * at + core, narrow), side_send.at[at, k], side_got.at[at, k], sides[k]
        )

    def side_arrival(at, k):
        target = att(2 * at + core, near[k])
        return remote(target, target, side_send.at[at, k], side_got.at[at, k], sides[k])

    def forward(at, k):
        piece = att_half(2 * at + core, near[k], k)
        return remote(piece, piece, side_send.at[at, 2 + k], side_got.at[at, 2 + k], sides[1 - k])

    def corner_arrival(at, k):
        piece = att_half(2 * at + core, corner, k)
        return remote(piece, piece, side_send.at[at, 2 + k], side_got.at[at, 2 + k], sides[1 - k])

    def pair(at, who, half_of):
        piece = att(2 * at + half_of, who)
        return remote(piece, piece, core_send.at[at, who], core_got.at[at, who], other)

    start = lambda copy: copy.start()
    greet_neighbours()
    both_ways(chip, att_ref, start)
    for k in range(2):
        side(chip, k, att_ref).start()
    own = pltpu.make_async_copy(att_ref, att(wide, narrow), own_sem)
    own.start()
    own.wait()
    pair(chip, narrow, core).start()

    def hop(distance):
        for at, valid in (
            (chip - distance, chip >= distance), (chip + distance, chip + distance <= 3)
        ):

            @pl.when(valid)
            def _():
                piece = att(2 * at + core, narrow)
                line(at, 1, piece).wait_recv()
                both_ways(at, piece, start)
                for k in range(2):
                    side(at, k, piece).start()
                pair(at, narrow, core).start()

    def around(at):
        for k in range(2):
            side_arrival(at, k).wait_recv()
            forward(at, k).start()
            pair(at, near[k], core).start()

    upper = chip // 2
    second = chip + 1 - 2 * upper
    last = 3 - 3 * upper
    order = (chip, second, 6 - chip - second - last, last)
    for step in range(4):
        if step < 3:
            hop(step + 1)
        around(order[step])
    for at in order:
        for k in range(2):
            corner_arrival(at, k).wait_recv()
        pair(at, corner, core).start()

    for at in range(4):
        both_ways(at, att_ref, lambda copy: copy.wait_send())
        for who in range(4):
            pair(at, who, 1 - core).wait_recv()
            pair(at, who, core).wait_send()
        for k in range(2):
            side(at, k, att_ref).wait_send()
            forward(at, k).wait_send()


def gather_weights(att):
    narrow_count = lax.axis_size("narrow")
    wide_count = lax.axis_size("wide")
    if narrow_count != 4 or wide_count != 8:
        return lax.all_gather(lax.all_gather(att, "wide", axis=0), "narrow", axis=1, tiled=True)
    dma = pltpu.SemaphoreType.DMA
    return pl.pallas_call(
        gather_kernel,
        out_shape=jax.ShapeDtypeStruct((8, 4 * att.shape[0], att.shape[1]), jnp.bfloat16),
        in_specs=[pl.BlockSpec(memory_space=pl.ANY)],
        out_specs=pl.BlockSpec(memory_space=pl.ANY),
        scratch_shapes=[
            dma, dma((4, 2)), dma((4,)), dma((4, 4)), dma((4, 4)), dma((4, 4)), dma((4, 4)),
        ],
        compiler_params=pltpu.CompilerParams(collective_id=1, has_side_effects=True),
        cost_estimate=pl.CostEstimate(flops=0, bytes_accessed=300 << 20, transcendentals=0),
        name="gather_weights",
    )(att)


def gather_rows(shard):
    return lax.all_gather(shard, "wide", axis=0, tiled=True)


def swap(blocks):
    return lax.all_to_all(blocks, "wide", 0, 0)


def sum_back(pairs):
    summed = 0.0
    for gradient, weight in pairs:
        summed = summed + dot_back(gradient, weight)
    return lax.psum_scatter(
        summed.astype(jnp.bfloat16), "wide", scatter_dimension=0, tiled=True
    ).astype(jnp.float32)


def scatter_kernel(
    in_ref, out_ref, gain_ref, sum_ref, spread_ref, gain_sum_ref,
    own, other, halves, wholes, from_left, from_right, low, wide_gains, mid_gain, narrow_gains,
    load_sem, core_send, core_got, half_send, half_got, whole_send, whole_got,
    line_send, left_got, right_got, spread_send, spread_got, pass_send, pass_got,
    wide_send, wide_got, narrow_send, narrow_got,
):
    narrow, wide, chip, core = place()
    beside = narrow + 1 - 2 * (narrow % 2)
    across = (narrow + 2) % 4
    corner = (beside + 2) % 4
    rows = sum_ref.shape[0]
    half_rows = rows // 2
    split = in_ref.shape[2]
    twin = (narrow, 2 * chip + 1 - core)
    sides = ((beside, wide), (across, wide))
    near = (beside, across)
    wides = [(narrow, (wide + step) % 8) for step in range(1, 8)]
    narrows = [((narrow + step) % 4, wide) for step in range(1, 4)]
    upper = chip // 2
    last = 3 - 3 * upper
    second = chip + 1 - 2 * upper
    order = (last, 6 - chip - second - last, second, chip)
    f32 = jnp.float32

    barrier = pltpu.get_barrier_semaphore()
    for device in wides + narrows:
        pl.semaphore_signal(
            barrier, inc=1, device_id=device, device_id_type=pl.DeviceIdType.MESH
        )
    pl.semaphore_wait(barrier, 10)

    parts = ((in_ref, pl.ds(0, split)), (out_ref, pl.ds(split, out_ref.shape[2])))

    def load(at, k):
        source, lanes = parts[k]
        return pltpu.make_async_copy(
            source.at[2 * at + core], own.at[at, :, lanes], load_sem.at[at, k]
        )

    def exchange(at, k):
        source, lanes = parts[k]
        return remote(
            source.at[2 * at + 1 - core], other.at[at, :, lanes], core_send.at[at, k],
            core_got.at[at, k], twin,
        )

    def block(at, who):
        return own.at[at, pl.ds(pl.multiple_of(who * rows, rows), rows), :]

    def half_block(at, who, half):
        return own.at[
            at, pl.ds(pl.multiple_of(who * rows + half * half_rows, half_rows), half_rows), :
        ]

    def half(at, k):
        return remote(
            half_block(at, corner, k), halves.at[at, k], half_send.at[at, k], half_got.at[at, k],
            sides[k],
        )

    def whole(at, k):
        return remote(
            block(at, near[k]), wholes.at[at, k], whole_send.at[at, k], whole_got.at[at, k],
            sides[k],
        )

    def to_right(at):
        return remote(
            block(at, narrow), from_left.at[at], line_send.at[at], left_got.at[at],
            (narrow, wide + 2),
        )

    def to_left(at):
        return remote(
            block(at, narrow), from_right.at[at], line_send.at[at], right_got.at[at],
            (narrow, wide - 2),
        )

    def add(target, source, count, step=64):
        @pl.loop(0, count // step)
        def _(i):
            piece = pl.ds(pl.multiple_of(i * step, step), step)
            target[piece, :] = (
                target[piece, :].astype(f32) + source[piece, :].astype(f32)
            ).astype(jnp.bfloat16)

    for at in order:
        for k in range(2):
            load(at, k).start()
            exchange(at, k).start()
    gains = [
        remote(gain_ref, wide_gains.at[step], wide_send.at[step], wide_got.at[step], device)
        for step, device in enumerate(wides)
    ]
    for copy in gains:
        copy.start()

    def pair_up(at):
        for k in range(2):
            load(at, k).wait()
            exchange(at, k).wait_recv()
        add(own.at[at], other.at[at], 4 * rows)
        for k in range(2):
            half(at, k).start()

    def turn(at):
        for k in range(2):
            half(at, k).wait_recv()
            add(half_block(at, near[1 - k], k), halves.at[at, k], half_rows)
        for k in range(2):
            whole(at, k).start()

    def settle(at):
        for k in range(2):
            whole(at, k).wait_recv()
        target = block(at, narrow)

        @pl.loop(0, rows // 64)
        def _(i):
            piece = pl.ds(pl.multiple_of(i * 64, 64), 64)
            target[piece, :] = (
                target[piece, :].astype(f32)
                + wholes[at, 0, piece, :].astype(f32)
                + wholes[at, 1, piece, :].astype(f32)
            ).astype(jnp.bfloat16)

        @pl.when(at > chip)
        def _():
            @pl.when(chip > 0)
            def _():
                to_right(at).wait_recv()
                add(target, from_left.at[at], rows)

            to_right(at).start()

        @pl.when(at < chip)
        def _():
            @pl.when(chip < 3)
            def _():
                to_left(at).wait_recv()
                add(target, from_right.at[at], rows)

            to_left(at).start()

    pair_up(order[0])
    pair_up(order[1])
    turn(order[0])
    pair_up(order[2])
    turn(order[1])
    settle(order[0])
    pair_up(order[3])
    turn(order[2])
    settle(order[1])
    for copy in gains:
        copy.wait()
    total = gain_ref[...]
    for step in range(7):
        total = total + wide_gains[step]
    mid_gain[...] = total
    gains = [
        remote(mid_gain, narrow_gains.at[step], narrow_send.at[step], narrow_got.at[step], device)
        for step, device in enumerate(narrows)
    ]
    for copy in gains:
        copy.start()
    turn(order[3])
    settle(order[2])
    settle(order[3])
    target = block(chip, narrow)

    @pl.when(chip > 0)
    def _():
        to_right(chip).wait_recv()
        add(target, from_left.at[chip], rows)

    @pl.when(chip < 3)
    def _():
        to_left(chip).wait_recv()
        add(target, from_right.at[chip], rows)

    lanes = pl.ds(split - 128, 128)

    @pl.loop(0, rows // 64)
    def _(i):
        piece = pl.ds(pl.multiple_of(i * 64, 64), 64)
        value = target[piece, :]
        sum_ref[piece, :] = value.astype(f32)
        low[piece, :] = target[piece, lanes]

    spread_ref[wide] = low[...]

    def spread(step):
        return remote(
            low, spread_ref.at[wide], spread_send.at[step - 1], spread_got.at[step - 1],
            (narrow, (wide + 2 * step) % 8),
        )

    def arrival(step):
        target = spread_ref.at[(wide + 8 - 2 * step) % 8]
        return remote(target, target, spread_send.at[step - 1], spread_got.at[step - 1], twin)

    def pass_on(step):
        piece = spread_ref.at[(wide + 8 - 2 * step) % 8]
        return remote(piece, piece, pass_send.at[step], pass_got.at[step], twin)

    def passed(step):
        piece = spread_ref.at[(2 * chip + 1 - core + 8 - 2 * step) % 8]
        return remote(piece, piece, pass_send.at[step], pass_got.at[step], twin)

    for step in (1, 2, 3):
        spread(step).start()
    pass_on(0).start()
    for copy in gains:
        copy.wait()
    for step in range(3):
        total = total + narrow_gains[step]
    gain_sum_ref[...] = total
    for step in (1, 2, 3):
        arrival(step).wait_recv()
        pass_on(step).start()
    for step in range(4):
        passed(step).wait_recv()
        pass_on(step).wait_send()
    for step in (1, 2, 3):
        spread(step).wait_send()
    for at in range(4):
        for k in range(2):
            exchange(at, k).wait_send()
            half(at, k).wait_send()
            whole(at, k).wait_send()

        @pl.when(at != chip)
        def _():
            to_right(at).wait_send()


def sum_weights(input_wgrad, output_wgrad, gains):
    narrow_count = lax.axis_size("narrow")
    wide_count = lax.axis_size("wide")
    split = input_wgrad.shape[2]
    if narrow_count != 4 or wide_count != 8:
        total = jnp.concatenate([input_wgrad, output_wgrad], axis=2)
        total = lax.psum_scatter(total, "narrow", scatter_dimension=1, tiled=True)
        total = lax.psum_scatter(total, "wide", scatter_dimension=0)
        spread = lax.all_gather(total[:, split - 128 : split], "wide", axis=0)
        gains = jnp.sum(lax.all_gather(gains, ("narrow", "wide"), axis=0), axis=0)
        return total.astype(jnp.float32), spread, gains
    low = jnp.bfloat16
    rows = input_wgrad.shape[1] // 4
    columns = split + output_wgrad.shape[2]
    size = gains.size
    gain_rows = -(-size // 1024) * 8
    flat = jnp.pad(gains.reshape(-1), (0, gain_rows * 128 - size)).reshape(gain_rows, 128)
    dma = pltpu.SemaphoreType.DMA
    vmem = pltpu.VMEM
    total, spread, flat = pl.pallas_call(
        scatter_kernel,
        out_shape=[
            jax.ShapeDtypeStruct((rows, columns), jnp.float32),
            jax.ShapeDtypeStruct((8, rows, 128), low),
            jax.ShapeDtypeStruct(flat.shape, jnp.float32),
        ],
        in_specs=[
            pl.BlockSpec(memory_space=pl.ANY),
            pl.BlockSpec(memory_space=pl.ANY),
            pl.BlockSpec(memory_space=vmem),
        ],
        out_specs=[pl.BlockSpec(memory_space=vmem)] * 3,
        scratch_shapes=[
            vmem((4, 4 * rows, columns), low),
            vmem((4, 4 * rows, columns), low),
            vmem((4, 2, rows // 2, columns), low),
            vmem((4, 2, rows, columns), low),
            vmem((4, rows, columns), low),
            vmem((4, rows, columns), low),
            vmem((rows, 128), low),
            vmem((7, gain_rows, 128), jnp.float32),
            vmem((gain_rows, 128), jnp.float32),
            vmem((3, gain_rows, 128), jnp.float32),
            dma((4, 2)), dma((4, 2)), dma((4, 2)), dma((4, 2)), dma((4, 2)), dma((4, 2)),
            dma((4, 2)), dma((4,)), dma((4,)), dma((4,)), dma((3,)), dma((3,)), dma((4,)),
            dma((4,)), dma((7,)), dma((7,)), dma((3,)), dma((3,)),
        ],
        compiler_params=pltpu.CompilerParams(
            collective_id=3, has_side_effects=True, vmem_limit_bytes=52 << 20
        ),
        cost_estimate=pl.CostEstimate(flops=0, bytes_accessed=300 << 20, transcendentals=0),
        name="sum_weights",
    )(input_wgrad, output_wgrad, flat)
    return total, spread, flat.reshape(-1)[:size].reshape(gains.shape)


def tell_all():
    narrow = lax.axis_index("narrow")
    wide = lax.axis_index("wide")
    barrier = pltpu.get_barrier_semaphore()
    for step in range(1, 8):
        pl.semaphore_signal(
            barrier, inc=1, device_id=(narrow, (wide + step) % 8),
            device_id_type=pl.DeviceIdType.MESH,
        )
    for step in range(1, 4):
        pl.semaphore_signal(
            barrier, inc=1, device_id=((narrow + step) % 4, wide),
            device_id_type=pl.DeviceIdType.MESH,
        )
    pl.semaphore_wait(barrier, 10)


def attend_swap_kernel(
    heads, src_ref, up_ref, down_ref, packed_ref, o_ref, s_ref, out_ref, up_all, down_all,
    kk_ref, va_ref, vb_ref, acc_ref, low_ref,
    own_sem, send_sem, got_sem, out_send, out_got, ffn_own, ffn_send, ffn_got,
):
    narrow, wide, chip, core = place()
    block = src_ref.shape[1]
    base = 4 * (chip // 2)
    away = 4 - base
    low = low_lanes(block)
    columns = down_ref.shape[1]
    tell_all()

    def ffn_slot(k, who):
        if k:
            return down_all.at[:, pl.ds(pl.multiple_of(who * columns, columns), columns)]
        return up_all.at[who]

    def ffn(k, step):
        return remote(
            (up_ref, down_ref)[k], ffn_slot(k, narrow), ffn_send.at[k, step],
            ffn_got.at[k, step], ((narrow + step) % 4, wide),
        )

    def ffn_arrival(k, step):
        target = ffn_slot(k, (narrow + 4 - step) % 4)
        return remote(
            target, target, ffn_send.at[k, step], ffn_got.at[k, step], ((narrow + step) % 4, wide)
        )

    def send(to):
        return remote(
            src_ref.at[to], packed_ref.at[wide], send_sem.at[to], got_sem.at[wide], (narrow, to)
        )

    def arrival(at):
        target = packed_ref.at[at]
        return remote(target, target, send_sem.at[at], got_sem.at[at], (narrow, at))

    def send_out(to):
        return remote(
            low_ref.at[to], out_ref.at[wide], out_send.at[to], out_got.at[wide], (narrow, to)
        )

    own = pltpu.make_async_copy(src_ref.at[wide], packed_ref.at[wide], own_sem)
    own.start()
    for step in range(1, 8):
        send((wide + step) % 8).start()
    keep = [
        pltpu.make_async_copy((up_ref, down_ref)[k], ffn_slot(k, narrow), ffn_own.at[k])
        for k in range(2)
    ]
    for k in (1, 0):
        keep[k].start()
        for step in range(1, 4):
            ffn(k, step).start()

    def prepare(j):
        rows = pl.ds(pl.multiple_of(j * block, block), block)
        kv = packed_ref[j, :, pl.ds(heads * 64, 128)]
        vk = jnp.concatenate([kv[:, 64:], kv[:, :64]], axis=1)
        one = jnp.ones_like(kv)
        kk_ref[rows, :] = jnp.where(low, kv, vk)
        va_ref[rows, :] = jnp.where(low, vk, one)
        vb_ref[rows, :] = jnp.where(low, one, kv)

    def await_blocks(start):
        @pl.loop(start, start + 4)
        def _(j):
            @pl.when(j != wide)
            def _():
                arrival(j).wait_recv()

            prepare(j)

    causal = lax.broadcasted_iota(jnp.int32, (block, block), 0) >= lax.broadcasted_iota(
        jnp.int32, (block, block), 1
    )

    def pairs(i, first, stop, diagonal):
        for pair in range(heads // 2):
            both = packed_ref[i, :, pl.ds(pair * 128, 128)]
            zero = jnp.zeros_like(both)
            sides = (jnp.where(low, both, zero), jnp.where(low, zero, both))

            def step(j, masked, fresh):
                keys = pl.ds(pl.multiple_of(j * block, block), block)
                kk = kk_ref[keys, :]
                for side in range(2):
                    weights = jnp.exp2(nt(sides[side], kk))
                    if masked:
                        weights = jnp.where(causal, weights, 0.0)
                    part = nn(weights.astype(jnp.bfloat16), (va_ref, vb_ref)[side][keys, :])
                    if fresh:
                        acc_ref[i, pair * 2 + side] = part
                    else:
                        acc_ref[i, pair * 2 + side] += part

            if diagonal:
                step(i, True, True)

            @pl.loop(first, stop)
            def _(j):
                step(j, False, False)

    def finish(i):
        rows = pl.ds(pl.multiple_of(i * block, block), block)
        for pair in range(heads // 2):
            lanes = pl.ds(pair * 128, 128)
            first, second = acc_ref[i, pair * 2], acc_ref[i, pair * 2 + 1]
            summed = jnp.where(low, first, second)
            sums = jnp.where(low, second, first)
            sums = jnp.concatenate([sums[:, 64:], sums[:, :64]], axis=1)
            result = summed / sums
            o_ref[rows, lanes] = result
            s_ref[rows, lanes] = sums
            low_ref[i, :, lanes] = result.astype(jnp.bfloat16)

        @pl.when(i != wide)
        def _():
            send_out(i).start()

        @pl.when(i == wide)
        def _():
            out_ref[i] = low_ref[i]

    own.wait()
    await_blocks(base)

    @pl.loop(base, base + 4)
    def _(i):
        pairs(i, base, i, True)

        @pl.when(base == 0)
        def _():
            finish(i)

    await_blocks(away)

    @pl.loop(away, away + 4)
    def _(i):
        pairs(i, 0, i, True)
        finish(i)

    @pl.when(base > 0)
    def _():
        @pl.loop(4, 8)
        def _(i):
            pairs(i, 0, 4, False)
            finish(i)

    for step in range(1, 8):
        to = (wide + step) % 8
        target = out_ref.at[to]
        remote(target, target, out_send.at[to], out_got.at[to], (narrow, to)).wait_recv()
        send_out(to).wait_send()
        send(to).wait_send()
    for k in range(2):
        keep[k].wait()
        for step in range(1, 4):
            ffn_arrival(k, step).wait_recv()
            ffn(k, step).wait_send()


def attend_swap(src, up, down, heads):
    if lax.axis_size("narrow") != 4 or lax.axis_size("wide") != 8:
        packed = swap(src)
        flat = packed.reshape(-1, src.shape[2])
        attended, weight_sums, attended_low = attend(flat, heads)
        attended_low = swap(attended_low.reshape(src.shape[0], -1, heads * 64))
        up_all = lax.all_gather(up, "narrow", axis=0, tiled=True)
        down_all = lax.all_gather(down, "narrow", axis=1, tiled=True)
        return packed, attended, weight_sums, attended_low, up_all, down_all
    count, block, lanes = src.shape
    total = count * block
    dma = pltpu.SemaphoreType.DMA
    vmem = pltpu.VMEM
    cost = heads * total * total // 2
    *results, up_all, down_all = pl.pallas_call(
        functools.partial(attend_swap_kernel, heads),
        out_shape=[
            jax.ShapeDtypeStruct(src.shape, jnp.bfloat16),
            jax.ShapeDtypeStruct((total, heads * 64), jnp.float32),
            jax.ShapeDtypeStruct((total, heads * 64), jnp.float32),
            jax.ShapeDtypeStruct((count, block, heads * 64), jnp.bfloat16),
            jax.ShapeDtypeStruct((4,) + up.shape, jnp.bfloat16),
            jax.ShapeDtypeStruct((down.shape[0], 4 * down.shape[1]), jnp.bfloat16),
        ],
        in_specs=[pl.BlockSpec(memory_space=pl.ANY)] * 3,
        out_specs=[pl.BlockSpec(memory_space=vmem)] * 4 + [pl.BlockSpec(memory_space=pl.ANY)] * 2,
        scratch_shapes=[vmem((total, 128), jnp.bfloat16)] * 3
        + [
            vmem((count, heads, block, 128), jnp.float32),
            vmem((count, block, heads * 64), jnp.bfloat16),
            dma, dma((8,)), dma((8,)), dma((8,)), dma((8,)), dma((2,)), dma((2, 4)), dma((2, 4)),
        ],
        compiler_params=pltpu.CompilerParams(
            collective_id=4, has_side_effects=True, vmem_limit_bytes=52 << 20
        ),
        cost_estimate=pl.CostEstimate(
            flops=8 * cost * 256, bytes_accessed=12 * src.size, transcendentals=cost
        ),
        name="attend_swap",
    )(src, up, down)
    return *results, up_all.reshape(-1, up.shape[1]), down_all


def back_swap_kernel(
    heads, packed_ref, g_ref, o_ref, s_ref, gate_ref, up_ref, down_ref,
    dq_out, dkv_out, gate_out, up_out, down_out,
    grad_ref, scaled_ref, dots_ref, dq_ref, dkv_ref, kk_ref, vv_ref, ka_ref, kb_ref,
    low_q, low_kv, own_sem, send_sem, got_sem, q_send, q_got, kv_send, kv_got,
    ffn_own, ffn_send, ffn_got,
):
    narrow, wide, chip, core = place()
    count, block, _ = packed_ref.shape
    base = 4 * (chip // 2)
    away = 4 - base
    low = low_lanes(block)
    rows_out = gate_out.shape[1]
    columns = down_out.shape[2]
    tell_all()

    def share(k, who):
        if k == 2:
            return down_ref.at[:, pl.ds(pl.multiple_of(who * columns, columns), columns)]
        return (gate_ref, up_ref)[k].at[pl.ds(pl.multiple_of(who * rows_out, rows_out), rows_out), :]

    def ffn(k, step):
        to = (narrow + step) % 4
        return remote(
            share(k, to), (gate_out, up_out, down_out)[k].at[step], ffn_send.at[k, step],
            ffn_got.at[k, step], (to, wide),
        )

    def send(to):
        return remote(
            g_ref.at[to], grad_ref.at[wide], send_sem.at[to], got_sem.at[wide], (narrow, to)
        )

    def send_q(to):
        return remote(low_q.at[to], dq_out.at[wide], q_send.at[to], q_got.at[wide], (narrow, to))

    def send_kv(to):
        return remote(
            low_kv.at[to], dkv_out.at[wide], kv_send.at[to], kv_got.at[wide], (narrow, to)
        )

    own = pltpu.make_async_copy(g_ref.at[wide], grad_ref.at[wide], own_sem)
    own.start()
    for step in range(1, 8):
        send((wide + step) % 8).start()
    keep = [
        pltpu.make_async_copy(
            share(k, narrow), (gate_out, up_out, down_out)[k].at[0], ffn_own.at[k]
        )
        for k in range(3)
    ]
    for k in range(3):
        keep[k].start()
        for step in range(1, 4):
            ffn(k, step).start()

    @pl.loop(0, count)
    def _(j):
        rows = pl.ds(pl.multiple_of(j * block, block), block)
        kv = packed_ref[j, :, pl.ds(heads * 64, 128)]
        vk = jnp.concatenate([kv[:, 64:], kv[:, :64]], axis=1)
        zero = jnp.zeros_like(kv)
        kk_ref[rows, :] = jnp.where(low, kv, vk)
        vv_ref[rows, :] = jnp.where(low, vk, kv)
        ka_ref[rows, :] = jnp.where(low, kv, zero)
        kb_ref[rows, :] = jnp.where(low, zero, vk)
        dkv_ref[0, rows, :] = jnp.zeros((block, 128), jnp.float32)
        dkv_ref[1, rows, :] = jnp.zeros((block, 128), jnp.float32)

    causal = lax.broadcasted_iota(jnp.int32, (block, block), 0) <= lax.broadcasted_iota(
        jnp.int32, (block, block), 1
    )
    first_lanes = lax.broadcasted_iota(jnp.int32, (8, 128), 1) < 64
    picks = (
        jnp.where(first_lanes, 1.0, 0.0).astype(jnp.bfloat16),
        jnp.where(first_lanes, 0.0, 1.0).astype(jnp.bfloat16),
    )

    def rows_back(i):
        rows = pl.ds(pl.multiple_of(i * block, block), block)
        for pair in range(heads // 2):
            lanes = pl.ds(pair * 128, 128)
            grad = grad_ref[i, :, lanes].astype(jnp.float32) / s_ref[rows, lanes]
            scaled_ref[...] = grad.astype(jnp.bfloat16)
            product = grad * o_ref[rows, lanes]
            high = product.astype(jnp.bfloat16)
            rest = (product - high.astype(jnp.float32)).astype(jnp.bfloat16)
            for side in range(2):
                dots_ref[side] = nt(picks[side], high) + nt(picks[side], rest)
            qboth = packed_ref[i, :, lanes]
            gboth = scaled_ref[...]
            zero = jnp.zeros_like(qboth)
            qs = (jnp.where(low, qboth, zero), jnp.where(low, zero, qboth))
            gs = (jnp.where(low, gboth, zero), jnp.where(low, zero, gboth))

            def step(j, diagonal):
                keys = pl.ds(pl.multiple_of(j * block, block), block)
                kk = kk_ref[keys, :]
                vv = vv_ref[keys, :]
                for side in range(2):
                    weights = jnp.exp2(nt(kk, qs[side]))
                    if diagonal:
                        weights = jnp.where(causal, weights, 0.0)
                    dots = dots_ref[side, pl.ds(0, 1), :]
                    grads = (weights * (nt(vv, gs[side]) - dots)).astype(jnp.bfloat16)
                    dkv_ref[1, keys, :] += nn(weights.astype(jnp.bfloat16), gs[side])
                    dkv_ref[0, keys, :] += nn(grads, qs[side])
                    part = tn(grads, (ka_ref, kb_ref)[side][keys, :])
                    if diagonal and side == 0:
                        dq_ref[...] = part
                    else:
                        dq_ref[...] += part

            step(i, True)

            @pl.loop(0, i)
            def _(j):
                step(j, False)

            low_q[i, :, lanes] = (dq_ref[...] * 0.125).astype(jnp.bfloat16)

        @pl.when(i != wide)
        def _():
            send_q(i).start()

        @pl.when(i == wide)
        def _():
            dq_out[i] = low_q[i]

    def keys_back(j):
        rows = pl.ds(pl.multiple_of(j * block, block), block)
        keys = dkv_ref[0, rows, :] * (1.0 / LOG2E)
        values = dkv_ref[1, rows, :]
        keys = keys + jnp.concatenate([keys[:, 64:], keys[:, :64]], axis=1)
        values = values + jnp.concatenate([values[:, 64:], values[:, :64]], axis=1)
        low_kv[j] = jnp.where(low, keys, values).astype(jnp.bfloat16)

        @pl.when(j != wide)
        def _():
            send_kv(j).start()

        @pl.when(j == wide)
        def _():
            dkv_out[j] = low_kv[j]

    own.wait()

    @pl.loop(0, 4)
    def _(k):
        i = base + 3 - k

        @pl.when(i != wide)
        def _():
            target = grad_ref.at[i]
            remote(target, target, send_sem.at[i], got_sem.at[i], (narrow, i)).wait_recv()

        rows_back(i)

        @pl.when(base > 0)
        def _():
            keys_back(i)

    @pl.loop(0, 4)
    def _(k):
        i = away + 3 - k
        target = grad_ref.at[i]
        remote(target, target, send_sem.at[i], got_sem.at[i], (narrow, i)).wait_recv()
        rows_back(i)
        keys_back(i)

    @pl.when(base == 0)
    def _():
        @pl.loop(0, 4)
        def _(k):
            keys_back(3 - k)

    for step in range(1, 8):
        to = (wide + step) % 8
        target = dq_out.at[to]
        remote(target, target, q_send.at[to], q_got.at[to], (narrow, to)).wait_recv()
        target = dkv_out.at[to]
        remote(target, target, kv_send.at[to], kv_got.at[to], (narrow, to)).wait_recv()
        send(to).wait_send()
        send_q(to).wait_send()
        send_kv(to).wait_send()
    for k in range(3):
        keep[k].wait()
        for step in range(1, 4):
            ffn(k, step).wait()


def back_swap(packed, grad, attended, weight_sums, gate, up, down, heads):
    count, block, lanes = packed.shape
    split = heads * 64
    if lax.axis_size("narrow") != 4 or lax.axis_size("wide") != 8:
        head_grad = swap(grad).reshape(-1, split).astype(jnp.float32) / weight_sums
        dots = jnp.sum((head_grad * attended).reshape(-1, heads, 64), axis=-1).T
        result = attend_back(
            packed.reshape(-1, lanes), head_grad.astype(jnp.bfloat16), dots, heads
        )
        result = swap(result.reshape(packed.shape))
        return (
            result[:, :, :split],
            result[:, :, split:],
            lax.psum_scatter(gate, "narrow", scatter_dimension=0, tiled=True)[None],
            lax.psum_scatter(up, "narrow", scatter_dimension=0, tiled=True)[None],
            lax.psum_scatter(down, "narrow", scatter_dimension=1, tiled=True)[None],
        )
    total = count * block
    dma = pltpu.SemaphoreType.DMA
    vmem = pltpu.VMEM
    low = jnp.bfloat16
    cost = heads * total * total // 2
    return pl.pallas_call(
        functools.partial(back_swap_kernel, heads),
        out_shape=[
            jax.ShapeDtypeStruct((count, block, split), low),
            jax.ShapeDtypeStruct((count, block, 128), low),
            jax.ShapeDtypeStruct((4, gate.shape[0] // 4, gate.shape[1]), low),
            jax.ShapeDtypeStruct((4, up.shape[0] // 4, up.shape[1]), low),
            jax.ShapeDtypeStruct((4, down.shape[0], down.shape[1] // 4), low),
        ],
        in_specs=[
            pl.BlockSpec(memory_space=vmem),
            pl.BlockSpec(memory_space=pl.ANY),
            pl.BlockSpec(memory_space=vmem),
            pl.BlockSpec(memory_space=vmem),
        ]
        + [pl.BlockSpec(memory_space=pl.ANY)] * 3,
        out_specs=[pl.BlockSpec(memory_space=vmem)] * 2 + [pl.BlockSpec(memory_space=pl.ANY)] * 3,
        scratch_shapes=[
            vmem((count, block, split), low),
            vmem((block, 128), low),
            vmem((2, 8, block), jnp.float32),
            vmem((block, 128), jnp.float32),
            vmem((2, total, 128), jnp.float32),
        ]
        + [vmem((total, 128), low)] * 4
        + [
            vmem((count, block, split), low),
            vmem((count, block, 128), low),
            dma, dma((8,)), dma((8,)), dma((8,)), dma((8,)), dma((8,)), dma((8,)),
            dma((3,)), dma((3, 4)), dma((3, 4)),
        ],
        compiler_params=pltpu.CompilerParams(
            collective_id=5, has_side_effects=True, vmem_limit_bytes=52 << 20
        ),
        cost_estimate=pl.CostEstimate(
            flops=12 * cost * 256, bytes_accessed=12 * packed.size, transcendentals=cost
        ),
        name="back_swap",
    )(packed, grad, attended, weight_sums, gate, up, down)


def shards(
    tokens_in,
    out_grad,
    positions,
    query_weight,
    query_first,
    query_second,
    key_weight,
    key_first,
    key_second,
    value_weight,
    value_first,
    value_second,
    output_weight,
    output_first,
    output_second,
    gate_weight,
    gate_first,
    gate_second,
    up_weight,
    up_first,
    up_second,
    down_weight,
    down_first,
    down_second,
    norm_gains,
    norm_first,
    norm_second,
    head_gains,
    head_first,
    head_second,
):
    wide_count = lax.axis_size("wide")
    wide_rank = lax.axis_index("wide")
    narrow_count = lax.axis_size("narrow")
    head_dim = head_gains.shape[1]
    key_heads = key_weight.shape[1] // head_dim
    local_heads = query_weight.shape[1] // head_dim
    shard_rows, model_width = tokens_in.shape
    copies = wide_count // key_heads
    key_slot = wide_rank // copies
    key_own = lax.dynamic_slice_in_dim(key_weight, key_slot * head_dim, head_dim, 1)
    value_own = lax.dynamic_slice_in_dim(value_weight, key_slot * head_dim, head_dim, 1)
    query_columns = query_weight.shape[1]
    att_own = jnp.concatenate([query_weight, key_own, value_own, output_weight.T], axis=1)
    half_rows = shard_rows // 2
    grad_halves = [
        lax.all_gather(out_grad[:half_rows], "wide", axis=0, tiled=True),
        lax.all_gather(out_grad[half_rows:], "wide", axis=0, tiled=True),
    ]
    att_full, gate_own = lax.optimization_barrier(
        (gather_weights(att_own.astype(jnp.bfloat16)), gate_weight.astype(jnp.bfloat16))
    )
    gate_local = lax.all_gather(gate_own, "narrow", axis=0, tiled=True)
    group_columns = query_columns + 2 * head_dim
    input_full = att_full[:, :, :group_columns]
    output_full = att_full[:, :, group_columns:]
    inverse = jnp.power(ROTARY_BASE, -2.0 * jnp.arange(head_dim // 2, dtype=jnp.float32) / head_dim)
    own_positions = lax.dynamic_slice_in_dim(positions, wide_rank * shard_rows, shard_rows, 0)
    angles = own_positions.astype(jnp.float32)[:, None] * inverse[None, :]
    cosine = jnp.cos(angles)
    sine_part = jnp.sin(angles)
    residual = tokens_in.astype(jnp.float32)
    normed_in, norm_in_back = jax.vjp(rms_scale, residual, norm_gains[0])
    rows_in = normed_in.astype(jnp.bfloat16)
    input_raw = jnp.einsum("td,gdc->gtc", rows_in, input_full, preferred_element_type=jnp.float32)
    query_raw = input_raw[:, :, :query_columns].reshape(
        wide_count, shard_rows, local_heads, head_dim
    )
    key_raw = input_raw[:, :, query_columns : query_columns + head_dim]
    value_rows = input_raw[:, :, query_columns + head_dim :].astype(jnp.bfloat16)

    def query_turn(raw_heads, gain):
        return rotate(
            rms_scale(raw_heads, gain), cosine[None, :, None, :], sine_part[None, :, None, :]
        )

    def key_turn(raw_heads, gain):
        return rotate(rms_scale(raw_heads, gain), cosine[None], sine_part[None])

    query_rot, query_back = jax.vjp(query_turn, query_raw, head_gains[0])
    key_rot, key_back = jax.vjp(key_turn, key_raw, head_gains[1])
    score_scale = head_dim ** (-0.5)
    query_rot = (
        (query_rot * (score_scale * LOG2E))
        .reshape(wide_count, shard_rows, query_columns)
        .astype(jnp.bfloat16)
    )
    packed = jnp.concatenate([query_rot, key_rot.astype(jnp.bfloat16), value_rows], axis=2)
    packed, grad_halves = lax.optimization_barrier((packed, grad_halves))
    packed, attended, weight_sums, attended_low, up_local, down_local = attend_swap(
        packed, up_weight.astype(jnp.bfloat16), down_weight.astype(jnp.bfloat16), local_heads
    )
    attended_low, gate_local = lax.optimization_barrier((attended_low, gate_local))
    branch = jnp.einsum("gth,gdh->td", attended_low, output_full, preferred_element_type=jnp.float32)
    middle = residual + branch
    normed_mid, norm_mid_back = jax.vjp(rms_scale, middle, norm_gains[1])
    mid_low = normed_mid.astype(jnp.bfloat16)
    down_wgrad = gate_wgrad = up_wgrad = 0.0
    block_parts = []
    mid_sums = []
    rows_halves = [gather_rows(mid_low[:half_rows]), gather_rows(mid_low[half_rows:])]
    hidden_grads = [dot_back(rows, down_local).astype(jnp.bfloat16) for rows in grad_halves]
    rows_halves[0], hidden_grads = lax.optimization_barrier((rows_halves[0], hidden_grads))
    for rows_mid, grad_rows, hidden_grad in zip(rows_halves, grad_halves, hidden_grads):
        gate_pre = dot_last(rows_mid, gate_local)
        up_pre = dot_last(rows_mid, up_local)
        hidden, hidden_back = jax.vjp(
            lambda gate_in, up_in: jax.nn.silu(gate_in) * up_in, gate_pre, up_pre
        )
        hidden_low = hidden.astype(jnp.bfloat16)
        gate_grad, up_grad = hidden_back(hidden_grad.astype(jnp.float32))
        gate_grad = gate_grad.astype(jnp.bfloat16)
        up_grad = up_grad.astype(jnp.bfloat16)
        mid_sums.append(sum_back(((gate_grad, gate_local), (up_grad, up_local))))
        block_parts.append(dot_last(hidden_low, down_local).astype(jnp.bfloat16))
        down_wgrad = down_wgrad + dot_first(hidden_low, grad_rows)
        gate_wgrad = gate_wgrad + dot_first(rows_mid, gate_grad)
        up_wgrad = up_wgrad + dot_first(rows_mid, up_grad)
    down_wgrad = down_wgrad.astype(jnp.bfloat16)
    gate_wgrad = gate_wgrad.astype(jnp.bfloat16)
    up_wgrad = up_wgrad.astype(jnp.bfloat16)
    mid_sums, gate_wgrad, up_wgrad, down_wgrad, block_parts = lax.optimization_barrier(
        (mid_sums, gate_wgrad, up_wgrad, down_wgrad, block_parts)
    )
    mid_back = jnp.concatenate(mid_sums, axis=0)
    middle_part, mid_gain_grad = norm_mid_back(mid_back)
    middle_grad = out_grad.astype(jnp.float32) + middle_part
    branch_grad = middle_grad.astype(jnp.bfloat16)
    attended_grad = jnp.einsum(
        "td,gdh->gth", branch_grad, output_full, preferred_element_type=jnp.float32
    ).astype(jnp.bfloat16)
    output_wgrad = jnp.einsum(
        "td,gth->gdh", branch_grad, attended_low, preferred_element_type=jnp.float32
    )
    attended_grad, first_part = lax.optimization_barrier((attended_grad, block_parts[0]))
    first_sum = lax.psum_scatter(first_part, "wide", scatter_dimension=0, tiled=True)
    query_rot_grad, key_value_grad, gate_shares, up_shares, down_shares = back_swap(
        packed, attended_grad, attended, weight_sums, gate_wgrad, up_wgrad, down_wgrad, local_heads
    )
    query_rot_grad, first_sum, second_part = lax.optimization_barrier(
        (query_rot_grad, first_sum, block_parts[1])
    )
    second_sum = lax.psum_scatter(second_part, "wide", scatter_dimension=0, tiled=True)
    query_rot_grad = query_rot_grad.astype(jnp.float32).reshape(
        wide_count, shard_rows, local_heads, head_dim
    )
    key_rot_grad = key_value_grad[:, :, :head_dim]
    query_raw_grad, query_gain_grad = query_back(query_rot_grad)
    key_raw_grad, key_gain_grad = key_back(key_rot_grad.astype(jnp.float32))
    input_low = jnp.concatenate(
        [
            query_raw_grad.reshape(wide_count, shard_rows, query_columns).astype(jnp.bfloat16),
            key_raw_grad.astype(jnp.bfloat16),
            key_value_grad[:, :, head_dim:],
        ],
        axis=2,
    )
    input_wgrad = jnp.einsum(
        "td,gtc->gdc", rows_in, input_low, preferred_element_type=jnp.float32
    ).astype(jnp.bfloat16)
    input_back = jnp.einsum("gtc,gdc->td", input_low, input_full, preferred_element_type=jnp.float32)
    input_part, in_gain_grad = norm_in_back(input_back)
    input_grad = middle_grad + input_part
    gain_stack = jnp.stack([in_gain_grad, mid_gain_grad])
    head_stack = jnp.stack([query_gain_grad, key_gain_grad])
    input_wgrad, second_sum = lax.optimization_barrier((input_wgrad, second_sum))
    input_total, spread, gains = sum_weights(
        input_wgrad,
        output_wgrad.astype(jnp.bfloat16),
        jnp.concatenate([gain_stack, head_stack], axis=1),
    )
    block_sum = jnp.concatenate([first_sum, second_sum], axis=0).astype(jnp.float32)
    block_out = (middle + block_sum).astype(jnp.bfloat16)
    gain_total = gains[:, :model_width]
    head_total = gains[:, model_width:]
    output_total = lax.optimization_barrier(input_total[:, group_columns:].T)
    query_total = input_total[:, :query_columns]
    spread = jnp.sum(
        spread.reshape(key_heads, copies, -1, 2, head_dim).astype(jnp.float32), axis=1
    ).transpose(2, 1, 0, 3)
    key_total = spread[0].reshape(key_weight.shape)
    value_total = spread[1].reshape(value_weight.shape)
    gate_total, up_total, down_total = (
        jnp.sum(gate_shares.astype(jnp.float32), axis=0),
        jnp.sum(up_shares.astype(jnp.float32), axis=0),
        jnp.sum(down_shares.astype(jnp.float32), axis=0),
    )
    wide_rate = D ** (-0.5)
    query_new = adam_update(
        query_weight, query_first, query_second, query_total, wide_rate, WEIGHT_DECAY
    )
    key_new = adam_update(key_weight, key_first, key_second, key_total, wide_rate, WEIGHT_DECAY)
    value_new = adam_update(
        value_weight, value_first, value_second, value_total, wide_rate, WEIGHT_DECAY
    )
    output_new = adam_update(
        output_weight, output_first, output_second, output_total, O_FAN ** (-0.5), WEIGHT_DECAY
    )
    gate_new = adam_update(
        gate_weight, gate_first, gate_second, gate_total, wide_rate, WEIGHT_DECAY
    )
    up_new = adam_update(up_weight, up_first, up_second, up_total, wide_rate, WEIGHT_DECAY)
    down_new = adam_update(
        down_weight, down_first, down_second, down_total, FF ** (-0.5), WEIGHT_DECAY
    )
    norm_new = adam_update(norm_gains, norm_first, norm_second, gain_total, GAIN_RATE, 0.0)
    head_new = adam_update(head_gains, head_first, head_second, head_total, GAIN_RATE, 0.0)
    return (
        block_out,
        input_grad,
        query_new[0],
        query_new[1],
        query_new[2],
        key_new[0],
        key_new[1],
        key_new[2],
        value_new[0],
        value_new[1],
        value_new[2],
        output_new[0],
        output_new[1],
        output_new[2],
        gate_new[0],
        gate_new[1],
        gate_new[2],
        up_new[0],
        up_new[1],
        up_new[2],
        down_new[0],
        down_new[1],
        down_new[2],
        norm_new[0],
        norm_new[1],
        norm_new[2],
        head_new[0],
        head_new[1],
        head_new[2],
    )


def solution(mesh):
    return jax.shard_map(
        shards,
        mesh=mesh,
        in_specs=(
            P(("narrow", "wide"), None),
            P(("narrow", "wide"), None),
            P("narrow"),
            P("narrow", "wide"),
            P("narrow", "wide"),
            P("narrow", "wide"),
            P("narrow", None),
            P("narrow", None),
            P("narrow", None),
            P("narrow", None),
            P("narrow", None),
            P("narrow", None),
            P("wide", "narrow"),
            P("wide", "narrow"),
            P("wide", "narrow"),
            P("narrow", "wide"),
            P("narrow", "wide"),
            P("narrow", "wide"),
            P("narrow", "wide"),
            P("narrow", "wide"),
            P("narrow", "wide"),
            P("wide", "narrow"),
            P("wide", "narrow"),
            P("wide", "narrow"),
            P(),
            P(),
            P(),
            P(),
            P(),
            P(),
        ),
        out_specs=(
            P(("narrow", "wide"), None),
            P(("narrow", "wide"), None),
            P("narrow", "wide"),
            P("narrow", "wide"),
            P("narrow", "wide"),
            P("narrow", None),
            P("narrow", None),
            P("narrow", None),
            P("narrow", None),
            P("narrow", None),
            P("narrow", None),
            P("wide", "narrow"),
            P("wide", "narrow"),
            P("wide", "narrow"),
            P("narrow", "wide"),
            P("narrow", "wide"),
            P("narrow", "wide"),
            P("narrow", "wide"),
            P("narrow", "wide"),
            P("narrow", "wide"),
            P("wide", "narrow"),
            P("wide", "narrow"),
            P("wide", "narrow"),
            P(),
            P(),
            P(),
            P(),
            P(),
            P(),
        ),
        check_vma=False,
    )
```

```python
import functools
import math

import jax
import jax.numpy as jnp
from jax import lax
from jax.experimental import pallas as pl
from jax.experimental.pallas import tpu as pltpu
from jax.sharding import PartitionSpec as P

D = 2048
FF = 8192
SEQ_LEN = 4096
STEP = 10
O_FAN = 50


EPSILON = 1e-06
BETA_ONE = 0.9
BETA_TWO = 0.95
ADAM_EPSILON = 1e-08
WEIGHT_DECAY = 0.1
GAIN_RATE = 1.0
ROTARY_BASE = 10000.0
MASKED_SCORE = -1e30


def rms_scale(inputs, gain):
    return inputs * lax.rsqrt(jnp.mean(inputs * inputs, axis=-1, keepdims=True) + EPSILON) * gain


def rotate(inputs, cosine, sine_part):
    half_width = inputs.shape[-1] // 2
    first_half = inputs[..., :half_width]
    second_half = inputs[..., half_width:]
    return jnp.concatenate(
        [
            first_half * cosine - second_half * sine_part,
            second_half * cosine + first_half * sine_part,
        ],
        axis=-1,
    )


def adam_update(weight, first_moment, second_moment, gradient, rate, decay):
    first_new = BETA_ONE * first_moment + (1.0 - BETA_ONE) * gradient
    second_new = BETA_TWO * second_moment + (1.0 - BETA_TWO) * gradient * gradient
    ratio = (
        first_new
        / (1.0 - BETA_ONE**STEP)
        / (jnp.sqrt(second_new / (1.0 - BETA_TWO**STEP)) + ADAM_EPSILON)
    )
    return (weight - rate * (ratio + decay * weight), first_new, second_new)


def dot_last(left, right):
    return jnp.dot(left, right, preferred_element_type=jnp.float32)


def dot_first(left, right):
    return lax.dot_general(
        left, right, (((0,), (0,)), ((), ())), preferred_element_type=jnp.float32
    )


def dot_back(left, right):
    return lax.dot_general(
        left, right, (((1,), (1,)), ((), ())), preferred_element_type=jnp.float32
    )


LOG2E = math.log2(math.e)

def nt(a, b):
    return lax.dot_general(a, b, (((1,), (1,)), ((), ())), preferred_element_type=jnp.float32)
def tn(a, b):
    return lax.dot_general(a, b, (((0,), (0,)), ((), ())), preferred_element_type=jnp.float32)
def nn(a, b):
    return jnp.dot(a, b, preferred_element_type=jnp.float32)

def low_lanes(rows):
    return lax.broadcasted_iota(jnp.int32, (rows, 128), 1) < 64

def attend_kernel(block, heads, q_ref, o_ref, s_ref, low_ref, kk_ref, va_ref, vb_ref, acc_ref):
    total = q_ref.shape[0]
    low = low_lanes(block)

    @pl.loop(0, total // block)
    def _(j):
        rows = pl.ds(pl.multiple_of(j * block, block), block)
        kv = q_ref[rows, pl.ds(heads * 64, 128)]
        vk = jnp.concatenate([kv[:, 64:], kv[:, :64]], axis=1)
        one = jnp.ones_like(kv)
        kk_ref[rows, :] = jnp.where(low, kv, vk)
        va_ref[rows, :] = jnp.where(low, vk, one)
        vb_ref[rows, :] = jnp.where(low, one, kv)

    causal = lax.broadcasted_iota(jnp.int32, (block, block), 0) >= lax.broadcasted_iota(
        jnp.int32, (block, block), 1
    )

    @pl.loop(0, total // block)
    def _(i):
        rows = pl.ds(pl.multiple_of(i * block, block), block)
        for pair in range(heads // 2):
            lanes = pl.ds(pair * 128, 128)
            both = q_ref[rows, lanes]
            zero = jnp.zeros_like(both)
            sides = (jnp.where(low, both, zero), jnp.where(low, zero, both))

            def step(j, diagonal):
                keys = pl.ds(pl.multiple_of(j * block, block), block)
                kk = kk_ref[keys, :]
                for side in range(2):
                    weights = jnp.exp2(nt(sides[side], kk))
                    if diagonal:
                        weights = jnp.where(causal, weights, 0.0)
                    part = nn(weights.astype(jnp.bfloat16), (va_ref, vb_ref)[side][keys, :])
                    if diagonal:
                        acc_ref[side] = part
                    else:
                        acc_ref[side] += part

            step(i, True)

            @pl.loop(0, i)
            def _(j):
                step(j, False)

            first, second = acc_ref[0], acc_ref[1]
            summed = jnp.where(low, first, second)
            sums = jnp.where(low, second, first)
            sums = jnp.concatenate([sums[:, 64:], sums[:, :64]], axis=1)
            result = summed / sums
            o_ref[rows, lanes] = result
            s_ref[rows, lanes] = sums
            low_ref[rows, lanes] = result.astype(jnp.bfloat16)

def attend(packed, heads, block=512):
    total = packed.shape[0]
    shape = (total, heads * 64)
    cost = heads * total * total // 2
    return pl.pallas_call(
        functools.partial(attend_kernel, block, heads),
        out_shape=[
            jax.ShapeDtypeStruct(shape, jnp.float32),
            jax.ShapeDtypeStruct(shape, jnp.float32),
            jax.ShapeDtypeStruct(shape, jnp.bfloat16),
        ],
        in_specs=[pl.BlockSpec(memory_space=pltpu.VMEM)],
        out_specs=[pl.BlockSpec(memory_space=pltpu.VMEM)] * 3,
        scratch_shapes=[pltpu.VMEM((total, 128), jnp.bfloat16)] * 3 + [pltpu.VMEM((2, block, 128), jnp.float32)],
        compiler_params=pltpu.CompilerParams(vmem_limit_bytes=56 << 20),
        cost_estimate=pl.CostEstimate(flops=4 * cost * 256, bytes_accessed=12 * packed.size, transcendentals=cost),
        name="attend",
    )(packed)

def back_kernel(block, heads, q_ref, g_ref, d_ref, out_ref, dq_ref, dkv_ref, kk_ref, vv_ref, ka_ref, kb_ref):
    total = q_ref.shape[0]
    low = low_lanes(block)
    count = total // block

    @pl.loop(0, count)
    def _(j):
        rows = pl.ds(pl.multiple_of(j * block, block), block)
        kv = q_ref[rows, pl.ds(heads * 64, 128)]
        vk = jnp.concatenate([kv[:, 64:], kv[:, :64]], axis=1)
        zero = jnp.zeros_like(kv)
        kk_ref[rows, :] = jnp.where(low, kv, vk)
        vv_ref[rows, :] = jnp.where(low, vk, kv)
        ka_ref[rows, :] = jnp.where(low, kv, zero)
        kb_ref[rows, :] = jnp.where(low, zero, vk)
        dkv_ref[0, rows, :] = jnp.zeros((block, 128), jnp.float32)
        dkv_ref[1, rows, :] = jnp.zeros((block, 128), jnp.float32)

    causal = lax.broadcasted_iota(jnp.int32, (block, block), 0) <= lax.broadcasted_iota(
        jnp.int32, (block, block), 1
    )

    @pl.loop(0, count)
    def _(i):
        rows = pl.ds(pl.multiple_of(i * block, block), block)
        for pair in range(heads // 2):
            lanes = pl.ds(pair * 128, 128)
            qboth = q_ref[rows, lanes]
            gboth = g_ref[rows, lanes]
            zero = jnp.zeros_like(qboth)
            qs = (jnp.where(low, qboth, zero), jnp.where(low, zero, qboth))
            gs = (jnp.where(low, gboth, zero), jnp.where(low, zero, gboth))

            def step(j, diagonal):
                keys = pl.ds(pl.multiple_of(j * block, block), block)
                kk = kk_ref[keys, :]
                vv = vv_ref[keys, :]
                for side in range(2):
                    weights = jnp.exp2(nt(kk, qs[side]))
                    if diagonal:
                        weights = jnp.where(causal, weights, 0.0)
                    dots = d_ref[pl.ds(pair * 2 + side, 1), rows]
                    grads = (weights * (nt(vv, gs[side]) - dots)).astype(jnp.bfloat16)
                    dkv_ref[1, keys, :] += nn(weights.astype(jnp.bfloat16), gs[side])
                    dkv_ref[0, keys, :] += nn(grads, qs[side])
                    part = tn(grads, (ka_ref, kb_ref)[side][keys, :])
                    if diagonal and side == 0:
                        dq_ref[:, lanes] = part
                    else:
                        dq_ref[:, lanes] += part

            step(i, True)

            @pl.loop(0, i)
            def _(j):
                step(j, False)

            out_ref[rows, lanes] = (dq_ref[:, lanes] * 0.125).astype(jnp.bfloat16)

    @pl.loop(0, count)
    def _(j):
        rows = pl.ds(pl.multiple_of(j * block, block), block)
        keys = dkv_ref[0, rows, :] * (1.0 / LOG2E)
        values = dkv_ref[1, rows, :]
        keys = keys + jnp.concatenate([keys[:, 64:], keys[:, :64]], axis=1)
        values = values + jnp.concatenate([values[:, 64:], values[:, :64]], axis=1)
        out_ref[rows, pl.ds(heads * 64, 128)] = jnp.where(low, keys, values).astype(jnp.bfloat16)

def attend_back(packed, g, dots, heads, block=512):
    total = packed.shape[0]
    cost = heads * total * total // 2
    return pl.pallas_call(
        functools.partial(back_kernel, block, heads),
        out_shape=jax.ShapeDtypeStruct(packed.shape, jnp.bfloat16),
        in_specs=[pl.BlockSpec(memory_space=pltpu.VMEM)] * 3,
        out_specs=pl.BlockSpec(memory_space=pltpu.VMEM),
        scratch_shapes=[
            pltpu.VMEM((block, heads * 64), jnp.float32),
            pltpu.VMEM((2, total, 128), jnp.float32),
        ]
        + [pltpu.VMEM((total, 128), jnp.bfloat16)] * 4,
        compiler_params=pltpu.CompilerParams(vmem_limit_bytes=56 << 20),
        cost_estimate=pl.CostEstimate(
            flops=10 * cost * 256, bytes_accessed=12 * packed.size, transcendentals=cost
        ),
        name="attend_back",
    )(packed, g, dots)


def remote(source, target, send, arrive, device):
    return pltpu.make_async_remote_copy(
        src_ref=source,
        dst_ref=target,
        send_sem=send,
        recv_sem=arrive,
        device_id=device,
        device_id_type=pl.DeviceIdType.MESH,
    )


def place():
    narrow = lax.axis_index("narrow")
    wide = lax.axis_index("wide")
    return narrow, wide, wide // 2, wide % 2


def greet_neighbours():
    narrow, wide, chip, core = place()
    barrier = pltpu.get_barrier_semaphore()

    def tell(device):
        pl.semaphore_signal(
            barrier, inc=1, device_id=device, device_id_type=pl.DeviceIdType.MESH
        )

    tell((narrow + 1 - 2 * (narrow % 2), wide))
    tell(((narrow + 2) % 4, wide))
    tell((narrow, 2 * chip + 1 - core))

    @pl.when(chip > 0)
    def _():
        tell((narrow, wide - 2))

    @pl.when(chip < 3)
    def _():
        tell((narrow, wide + 2))

    pl.semaphore_wait(barrier, 3 + jnp.minimum(chip, 1) + jnp.minimum(3 - chip, 1))


def gather_kernel(
    att_ref, att_all, own_sem, line_send, line_got, side_send, side_got, core_send, core_got
):
    narrow, wide, chip, core = place()
    beside = narrow + 1 - 2 * (narrow % 2)
    across = (narrow + 2) % 4
    corner = (beside + 2) % 4
    rows = att_ref.shape[0]
    half_rows = rows // 2
    other = (narrow, 2 * chip + 1 - core)
    left = (narrow, wide - 2)
    right = (narrow, wide + 2)
    sides = ((beside, wide), (across, wide))
    near = (beside, across)

    def att(slot, who):
        return att_all.at[slot, pl.ds(pl.multiple_of(who * rows, rows), rows), :]

    def att_half(slot, who, half):
        return att_all.at[
            slot, pl.ds(pl.multiple_of(who * rows + half * half_rows, half_rows), half_rows), :
        ]

    def line(at, step, source):
        return remote(
            source, att(2 * at + core, narrow), line_send.at[at, (step + 1) // 2],
            line_got.at[at], right if step > 0 else left,
        )

    def both_ways(at, source, act):
        @pl.when(jnp.logical_and(at <= chip, chip < 3))
        def _():
            act(line(at, 1, source))

        @pl.when(jnp.logical_and(at >= chip, chip > 0))
        def _():
            act(line(at, -1, source))

    def side(at, k, source):
        return remote(
            source, att(2 * at + core, narrow), side_send.at[at, k], side_got.at[at, k], sides[k]
        )

    def side_arrival(at, k):
        target = att(2 * at + core, near[k])
        return remote(target, target, side_send.at[at, k], side_got.at[at, k], sides[k])

    def forward(at, k):
        piece = att_half(2 * at + core, near[k], k)
        return remote(piece, piece, side_send.at[at, 2 + k], side_got.at[at, 2 + k], sides[1 - k])

    def corner_arrival(at, k):
        piece = att_half(2 * at + core, corner, k)
        return remote(piece, piece, side_send.at[at, 2 + k], side_got.at[at, 2 + k], sides[1 - k])

    def pair(at, who, half_of):
        piece = att(2 * at + half_of, who)
        return remote(piece, piece, core_send.at[at, who], core_got.at[at, who], other)

    start = lambda copy: copy.start()
    greet_neighbours()
    both_ways(chip, att_ref, start)
    for k in range(2):
        side(chip, k, att_ref).start()
    own = pltpu.make_async_copy(att_ref, att(wide, narrow), own_sem)
    own.start()
    own.wait()
    pair(chip, narrow, core).start()

    def hop(distance):
        for at, valid in (
            (chip - distance, chip >= distance), (chip + distance, chip + distance <= 3)
        ):

            @pl.when(valid)
            def _():
                piece = att(2 * at + core, narrow)
                line(at, 1, piece).wait_recv()
                both_ways(at, piece, start)
                for k in range(2):
                    side(at, k, piece).start()
                pair(at, narrow, core).start()

    def around(at):
        for k in range(2):
            side_arrival(at, k).wait_recv()
            forward(at, k).start()
            pair(at, near[k], core).start()

    upper = chip // 2
    second = chip + 1 - 2 * upper
    last = 3 - 3 * upper
    order = (chip, second, 6 - chip - second - last, last)
    for step in range(4):
        if step < 3:
            hop(step + 1)
        around(order[step])
    for at in order:
        for k in range(2):
            corner_arrival(at, k).wait_recv()
        pair(at, corner, core).start()

    for at in range(4):
        both_ways(at, att_ref, lambda copy: copy.wait_send())
        for who in range(4):
            pair(at, who, 1 - core).wait_recv()
            pair(at, who, core).wait_send()
        for k in range(2):
            side(at, k, att_ref).wait_send()
            forward(at, k).wait_send()


def gather_weights(att):
    narrow_count = lax.axis_size("narrow")
    wide_count = lax.axis_size("wide")
    if narrow_count != 4 or wide_count != 8:
        return lax.all_gather(lax.all_gather(att, "wide", axis=0), "narrow", axis=1, tiled=True)
    dma = pltpu.SemaphoreType.DMA
    return pl.pallas_call(
        gather_kernel,
        out_shape=jax.ShapeDtypeStruct((8, 4 * att.shape[0], att.shape[1]), jnp.bfloat16),
        in_specs=[pl.BlockSpec(memory_space=pl.ANY)],
        out_specs=pl.BlockSpec(memory_space=pl.ANY),
        scratch_shapes=[
            dma, dma((4, 2)), dma((4,)), dma((4, 4)), dma((4, 4)), dma((4, 4)), dma((4, 4)),
        ],
        compiler_params=pltpu.CompilerParams(collective_id=1, has_side_effects=True),
        cost_estimate=pl.CostEstimate(flops=0, bytes_accessed=300 << 20, transcendentals=0),
        name="gather_weights",
    )(att)


def gather_rows(shard):
    return lax.all_gather(shard, "wide", axis=0, tiled=True)


def swap(blocks):
    return lax.all_to_all(blocks, "wide", 0, 0)


def sum_back(pairs):
    summed = 0.0
    for gradient, weight in pairs:
        summed = summed + dot_back(gradient, weight)
    return lax.psum_scatter(
        summed.astype(jnp.bfloat16), "wide", scatter_dimension=0, tiled=True
    ).astype(jnp.float32)


def scatter_kernel(
    in_ref, out_ref, gain_ref, query_sum, output_sum, key_sum, value_sum, gain_sum_ref,
    own, other, halves, wholes, from_left, from_right, spread_ref, low, wide_gains, mid_gain,
    narrow_gains,
    load_sem, core_send, core_got, half_send, half_got, whole_send, whole_got,
    line_send, left_got, right_got, spread_send, spread_got, pass_send, pass_got,
    wide_send, wide_got, narrow_send, narrow_got,
):
    narrow, wide, chip, core = place()
    beside = narrow + 1 - 2 * (narrow % 2)
    across = (narrow + 2) % 4
    corner = (beside + 2) % 4
    rows = query_sum.shape[0]
    half_rows = rows // 2
    split = in_ref.shape[2]
    twin = (narrow, 2 * chip + 1 - core)
    sides = ((beside, wide), (across, wide))
    near = (beside, across)
    wides = [(narrow, (wide + step) % 8) for step in range(1, 8)]
    narrows = [((narrow + step) % 4, wide) for step in range(1, 4)]
    upper = chip // 2
    last = 3 - 3 * upper
    second = chip + 1 - 2 * upper
    order = (last, 6 - chip - second - last, second, chip)
    f32 = jnp.float32

    barrier = pltpu.get_barrier_semaphore()
    for device in wides + narrows:
        pl.semaphore_signal(
            barrier, inc=1, device_id=device, device_id_type=pl.DeviceIdType.MESH
        )
    pl.semaphore_wait(barrier, 10)

    parts = ((in_ref, pl.ds(0, split)), (out_ref, pl.ds(split, out_ref.shape[2])))

    def load(at, k):
        source, lanes = parts[k]
        return pltpu.make_async_copy(
            source.at[2 * at + core], own.at[at, :, lanes], load_sem.at[at, k]
        )

    def exchange(at, k):
        source, lanes = parts[k]
        return remote(
            source.at[2 * at + 1 - core], other.at[at, :, lanes], core_send.at[at, k],
            core_got.at[at, k], twin,
        )

    def block(at, who):
        return own.at[at, pl.ds(pl.multiple_of(who * rows, rows), rows), :]

    def half_block(at, who, half):
        return own.at[
            at, pl.ds(pl.multiple_of(who * rows + half * half_rows, half_rows), half_rows), :
        ]

    def half(at, k):
        return remote(
            half_block(at, corner, k), halves.at[at, k], half_send.at[at, k], half_got.at[at, k],
            sides[k],
        )

    def whole(at, k):
        return remote(
            block(at, near[k]), wholes.at[at, k], whole_send.at[at, k], whole_got.at[at, k],
            sides[k],
        )

    def to_right(at):
        return remote(
            block(at, narrow), from_left.at[at], line_send.at[at], left_got.at[at],
            (narrow, wide + 2),
        )

    def to_left(at):
        return remote(
            block(at, narrow), from_right.at[at], line_send.at[at], right_got.at[at],
            (narrow, wide - 2),
        )

    def add(target, source, count, step=64):
        @pl.loop(0, count // step)
        def _(i):
            piece = pl.ds(pl.multiple_of(i * step, step), step)
            target[piece, :] = (
                target[piece, :].astype(f32) + source[piece, :].astype(f32)
            ).astype(jnp.bfloat16)

    for at in order:
        for k in range(2):
            load(at, k).start()
            exchange(at, k).start()
    gains = [
        remote(gain_ref, wide_gains.at[step], wide_send.at[step], wide_got.at[step], device)
        for step, device in enumerate(wides)
    ]
    for copy in gains:
        copy.start()

    def pair_up(at):
        for k in range(2):
            load(at, k).wait()
            exchange(at, k).wait_recv()
        add(own.at[at], other.at[at], 4 * rows)
        for k in range(2):
            half(at, k).start()

    def turn(at):
        for k in range(2):
            half(at, k).wait_recv()
            add(half_block(at, near[1 - k], k), halves.at[at, k], half_rows)
        for k in range(2):
            whole(at, k).start()

    def settle(at):
        for k in range(2):
            whole(at, k).wait_recv()
        target = block(at, narrow)

        @pl.loop(0, rows // 64)
        def _(i):
            piece = pl.ds(pl.multiple_of(i * 64, 64), 64)
            target[piece, :] = (
                target[piece, :].astype(f32)
                + wholes[at, 0, piece, :].astype(f32)
                + wholes[at, 1, piece, :].astype(f32)
            ).astype(jnp.bfloat16)

        @pl.when(at > chip)
        def _():
            @pl.when(chip > 0)
            def _():
                to_right(at).wait_recv()
                add(target, from_left.at[at], rows)

            to_right(at).start()

        @pl.when(at < chip)
        def _():
            @pl.when(chip < 3)
            def _():
                to_left(at).wait_recv()
                add(target, from_right.at[at], rows)

            to_left(at).start()

    pair_up(order[0])
    pair_up(order[1])
    turn(order[0])
    pair_up(order[2])
    turn(order[1])
    settle(order[0])
    pair_up(order[3])
    turn(order[2])
    settle(order[1])
    for copy in gains:
        copy.wait()
    total = gain_ref[...]
    for step in range(7):
        total = total + wide_gains[step]
    mid_gain[...] = total
    gains = [
        remote(mid_gain, narrow_gains.at[step], narrow_send.at[step], narrow_got.at[step], device)
        for step, device in enumerate(narrows)
    ]
    for copy in gains:
        copy.start()
    turn(order[3])
    settle(order[2])
    settle(order[3])
    target = block(chip, narrow)

    @pl.when(chip > 0)
    def _():
        to_right(chip).wait_recv()
        add(target, from_left.at[chip], rows)

    @pl.when(chip < 3)
    def _():
        to_left(chip).wait_recv()
        add(target, from_right.at[chip], rows)

    lanes = pl.ds(split - 128, 128)
    for i in range(rows // 128):
        piece = pl.ds(pl.multiple_of(narrow * rows + i * 128, 128), 128)
        here = pl.ds(i * 128, 128)
        query_sum[here, :] = own[chip, piece, pl.ds(0, split - 128)].astype(f32)
        output_sum[:, here] = own[chip, piece, pl.ds(split, out_ref.shape[2])].astype(f32).T
        low[here, :] = own[chip, piece, lanes]

    spread_ref[wide] = low[...]

    def spread(step):
        return remote(
            low, spread_ref.at[wide], spread_send.at[step - 1], spread_got.at[step - 1],
            (narrow, (wide + 2 * step) % 8),
        )

    def arrival(step):
        target = spread_ref.at[(wide + 8 - 2 * step) % 8]
        return remote(target, target, spread_send.at[step - 1], spread_got.at[step - 1], twin)

    def pass_on(step):
        piece = spread_ref.at[(wide + 8 - 2 * step) % 8]
        return remote(piece, piece, pass_send.at[step], pass_got.at[step], twin)

    def passed(step):
        piece = spread_ref.at[(2 * chip + 1 - core + 8 - 2 * step) % 8]
        return remote(piece, piece, pass_send.at[step], pass_got.at[step], twin)

    for step in (1, 2, 3):
        spread(step).start()
    pass_on(0).start()
    for copy in gains:
        copy.wait()
    for step in range(3):
        total = total + narrow_gains[step]
    gain_sum_ref[...] = total
    for step in (1, 2, 3):
        arrival(step).wait_recv()
        pass_on(step).start()
    for step in range(4):
        passed(step).wait_recv()
        pass_on(step).wait_send()
    for step in (1, 2, 3):
        spread(step).wait_send()
    first = low_lanes(rows)
    for at in range(4):
        even = spread_ref[2 * at].astype(f32)
        odd = spread_ref[2 * at + 1].astype(f32)
        here = pl.ds(at * 128, 128)
        key_sum[:, here] = jnp.where(first, even, pltpu.roll(odd, 64, 1))
        value_sum[:, here] = jnp.where(first, pltpu.roll(even, 64, 1), odd)
    for at in range(4):
        for k in range(2):
            exchange(at, k).wait_send()
            half(at, k).wait_send()
            whole(at, k).wait_send()

        @pl.when(at != chip)
        def _():
            to_right(at).wait_send()


def sum_weights(input_wgrad, output_wgrad, gains, key_heads):
    narrow_count = lax.axis_size("narrow")
    wide_count = lax.axis_size("wide")
    split = input_wgrad.shape[2]
    if narrow_count != 4 or wide_count != 8 or key_heads != 8:
        total = jnp.concatenate([input_wgrad, output_wgrad], axis=2)
        total = lax.psum_scatter(total, "narrow", scatter_dimension=1, tiled=True)
        total = lax.psum_scatter(total, "wide", scatter_dimension=0)
        spread = lax.all_gather(total[:, split - 128 : split], "wide", axis=0)
        spread = spread.reshape(key_heads, wide_count // key_heads, -1, 2, 64)
        spread = jnp.sum(spread.astype(jnp.float32), axis=1).transpose(2, 1, 0, 3)
        spread = spread.reshape(2, -1, key_heads * 64)
        gains = jnp.sum(lax.all_gather(gains, ("narrow", "wide"), axis=0), axis=0)
        total = total.astype(jnp.float32)
        return total[:, : split - 128], total[:, split:].T, spread[0], spread[1], gains
    low = jnp.bfloat16
    rows = input_wgrad.shape[1] // 4
    columns = split + output_wgrad.shape[2]
    size = gains.size
    gain_rows = -(-size // 1024) * 8
    flat = jnp.pad(gains.reshape(-1), (0, gain_rows * 128 - size)).reshape(gain_rows, 128)
    dma = pltpu.SemaphoreType.DMA
    vmem = pltpu.VMEM
    *sums, flat = pl.pallas_call(
        scatter_kernel,
        out_shape=[
            jax.ShapeDtypeStruct((rows, split - 128), jnp.float32),
            jax.ShapeDtypeStruct((columns - split, rows), jnp.float32),
            jax.ShapeDtypeStruct((rows, 512), jnp.float32),
            jax.ShapeDtypeStruct((rows, 512), jnp.float32),
            jax.ShapeDtypeStruct(flat.shape, jnp.float32),
        ],
        in_specs=[
            pl.BlockSpec(memory_space=pl.ANY),
            pl.BlockSpec(memory_space=pl.ANY),
            pl.BlockSpec(memory_space=vmem),
        ],
        out_specs=[pl.BlockSpec(memory_space=vmem)] * 5,
        scratch_shapes=[
            vmem((4, 4 * rows, columns), low),
            vmem((4, 4 * rows, columns), low),
            vmem((4, 2, rows // 2, columns), low),
            vmem((4, 2, rows, columns), low),
            vmem((4, rows, columns), low),
            vmem((4, rows, columns), low),
            vmem((8, rows, 128), low),
            vmem((rows, 128), low),
            vmem((7, gain_rows, 128), jnp.float32),
            vmem((gain_rows, 128), jnp.float32),
            vmem((3, gain_rows, 128), jnp.float32),
            dma((4, 2)), dma((4, 2)), dma((4, 2)), dma((4, 2)), dma((4, 2)), dma((4, 2)),
            dma((4, 2)), dma((4,)), dma((4,)), dma((4,)), dma((3,)), dma((3,)), dma((4,)),
            dma((4,)), dma((7,)), dma((7,)), dma((3,)), dma((3,)),
        ],
        compiler_params=pltpu.CompilerParams(
            collective_id=3, has_side_effects=True, vmem_limit_bytes=52 << 20
        ),
        cost_estimate=pl.CostEstimate(flops=0, bytes_accessed=1 << 20, transcendentals=0),
        name="sum_weights",
    )(input_wgrad, output_wgrad, flat)
    return *sums, flat.reshape(-1)[:size].reshape(gains.shape)


def tell_all():
    narrow = lax.axis_index("narrow")
    wide = lax.axis_index("wide")
    barrier = pltpu.get_barrier_semaphore()
    for step in range(1, 8):
        pl.semaphore_signal(
            barrier, inc=1, device_id=(narrow, (wide + step) % 8),
            device_id_type=pl.DeviceIdType.MESH,
        )
    for step in range(1, 4):
        pl.semaphore_signal(
            barrier, inc=1, device_id=((narrow + step) % 4, wide),
            device_id_type=pl.DeviceIdType.MESH,
        )
    pl.semaphore_wait(barrier, 10)


def attend_swap_kernel(
    heads, src_ref, up_ref, down_ref, packed_ref, o_ref, s_ref, out_ref, up_all, down_all,
    kk_ref, va_ref, vb_ref, acc_ref, low_ref,
    own_sem, send_sem, got_sem, out_send, out_got, ffn_own, ffn_send, ffn_got,
):
    narrow, wide, chip, core = place()
    block = src_ref.shape[1]
    base = 4 * (chip // 2)
    away = 4 - base
    low = low_lanes(block)
    columns = down_ref.shape[1]
    tell_all()

    def ffn_slot(k, who):
        if k:
            return down_all.at[:, pl.ds(pl.multiple_of(who * columns, columns), columns)]
        return up_all.at[who]

    def ffn(k, step):
        return remote(
            (up_ref, down_ref)[k], ffn_slot(k, narrow), ffn_send.at[k, step],
            ffn_got.at[k, step], ((narrow + step) % 4, wide),
        )

    def ffn_arrival(k, step):
        target = ffn_slot(k, (narrow + 4 - step) % 4)
        return remote(
            target, target, ffn_send.at[k, step], ffn_got.at[k, step], ((narrow + step) % 4, wide)
        )

    def send(to):
        return remote(
            src_ref.at[to], packed_ref.at[wide], send_sem.at[to], got_sem.at[wide], (narrow, to)
        )

    def arrival(at):
        target = packed_ref.at[at]
        return remote(target, target, send_sem.at[at], got_sem.at[at], (narrow, at))

    def send_out(to):
        return remote(
            low_ref.at[to], out_ref.at[wide], out_send.at[to], out_got.at[wide], (narrow, to)
        )

    own = pltpu.make_async_copy(src_ref.at[wide], packed_ref.at[wide], own_sem)
    own.start()
    for step in range(1, 8):
        send((wide + step) % 8).start()
    keep = [
        pltpu.make_async_copy((up_ref, down_ref)[k], ffn_slot(k, narrow), ffn_own.at[k])
        for k in range(2)
    ]
    for k in (1, 0):
        keep[k].start()
        for step in range(1, 4):
            ffn(k, step).start()

    def prepare(j):
        rows = pl.ds(pl.multiple_of(j * block, block), block)
        kv = packed_ref[j, :, pl.ds(heads * 64, 128)]
        vk = jnp.concatenate([kv[:, 64:], kv[:, :64]], axis=1)
        one = jnp.ones_like(kv)
        kk_ref[rows, :] = jnp.where(low, kv, vk)
        va_ref[rows, :] = jnp.where(low, vk, one)
        vb_ref[rows, :] = jnp.where(low, one, kv)

    def await_blocks(start):
        @pl.loop(start, start + 4)
        def _(j):
            @pl.when(j != wide)
            def _():
                arrival(j).wait_recv()

            prepare(j)

    causal = lax.broadcasted_iota(jnp.int32, (block, block), 0) >= lax.broadcasted_iota(
        jnp.int32, (block, block), 1
    )

    def pairs(i, first, stop, diagonal):
        for pair in range(heads // 2):
            both = packed_ref[i, :, pl.ds(pair * 128, 128)]
            zero = jnp.zeros_like(both)
            sides = (jnp.where(low, both, zero), jnp.where(low, zero, both))

            def step(j, masked, fresh):
                keys = pl.ds(pl.multiple_of(j * block, block), block)
                kk = kk_ref[keys, :]
                for side in range(2):
                    weights = jnp.exp2(nt(sides[side], kk))
                    if masked:
                        weights = jnp.where(causal, weights, 0.0)
                    part = nn(weights.astype(jnp.bfloat16), (va_ref, vb_ref)[side][keys, :])
                    if fresh:
                        acc_ref[i, pair * 2 + side] = part
                    else:
                        acc_ref[i, pair * 2 + side] += part

            if diagonal:
                step(i, True, True)

            @pl.loop(first, stop)
            def _(j):
                step(j, False, False)

    def finish(i):
        rows = pl.ds(pl.multiple_of(i * block, block), block)
        for pair in range(heads // 2):
            lanes = pl.ds(pair * 128, 128)
            first, second = acc_ref[i, pair * 2], acc_ref[i, pair * 2 + 1]
            summed = jnp.where(low, first, second)
            sums = jnp.where(low, second, first)
            sums = jnp.concatenate([sums[:, 64:], sums[:, :64]], axis=1)
            result = summed / sums
            o_ref[rows, lanes] = result
            s_ref[rows, lanes] = sums
            low_ref[i, :, lanes] = result.astype(jnp.bfloat16)

        @pl.when(i != wide)
        def _():
            send_out(i).start()

        @pl.when(i == wide)
        def _():
            out_ref[i] = low_ref[i]

    own.wait()
    await_blocks(base)

    @pl.loop(base, base + 4)
    def _(i):
        pairs(i, base, i, True)

        @pl.when(base == 0)
        def _():
            finish(i)

    await_blocks(away)

    @pl.loop(away, away + 4)
    def _(i):
        pairs(i, 0, i, True)
        finish(i)

    @pl.when(base > 0)
    def _():
        @pl.loop(4, 8)
        def _(i):
            pairs(i, 0, 4, False)
            finish(i)

    for step in range(1, 8):
        to = (wide + step) % 8
        target = out_ref.at[to]
        remote(target, target, out_send.at[to], out_got.at[to], (narrow, to)).wait_recv()
        send_out(to).wait_send()
        send(to).wait_send()
    for k in range(2):
        keep[k].wait()
        for step in range(1, 4):
            ffn_arrival(k, step).wait_recv()
            ffn(k, step).wait_send()


def attend_swap(src, up, down, heads):
    if lax.axis_size("narrow") != 4 or lax.axis_size("wide") != 8:
        packed = swap(src)
        flat = packed.reshape(-1, src.shape[2])
        attended, weight_sums, attended_low = attend(flat, heads)
        attended_low = swap(attended_low.reshape(src.shape[0], -1, heads * 64))
        up_all = lax.all_gather(up, "narrow", axis=0, tiled=True)
        down_all = lax.all_gather(down, "narrow", axis=1, tiled=True)
        return packed, attended, weight_sums, attended_low, up_all, down_all
    count, block, lanes = src.shape
    total = count * block
    dma = pltpu.SemaphoreType.DMA
    vmem = pltpu.VMEM
    cost = heads * total * total // 2
    *results, up_all, down_all = pl.pallas_call(
        functools.partial(attend_swap_kernel, heads),
        out_shape=[
            jax.ShapeDtypeStruct(src.shape, jnp.bfloat16),
            jax.ShapeDtypeStruct((total, heads * 64), jnp.float32),
            jax.ShapeDtypeStruct((total, heads * 64), jnp.float32),
            jax.ShapeDtypeStruct((count, block, heads * 64), jnp.bfloat16),
            jax.ShapeDtypeStruct((4,) + up.shape, jnp.bfloat16),
            jax.ShapeDtypeStruct((down.shape[0], 4 * down.shape[1]), jnp.bfloat16),
        ],
        in_specs=[pl.BlockSpec(memory_space=pl.ANY)] * 3,
        out_specs=[pl.BlockSpec(memory_space=vmem)] * 4 + [pl.BlockSpec(memory_space=pl.ANY)] * 2,
        scratch_shapes=[vmem((total, 128), jnp.bfloat16)] * 3
        + [
            vmem((count, heads, block, 128), jnp.float32),
            vmem((count, block, heads * 64), jnp.bfloat16),
            dma, dma((8,)), dma((8,)), dma((8,)), dma((8,)), dma((2,)), dma((2, 4)), dma((2, 4)),
        ],
        compiler_params=pltpu.CompilerParams(
            collective_id=4, has_side_effects=True, vmem_limit_bytes=52 << 20
        ),
        cost_estimate=pl.CostEstimate(
            flops=8 * cost * 256, bytes_accessed=12 * src.size, transcendentals=cost
        ),
        name="attend_swap",
    )(src, up, down)
    return *results, up_all.reshape(-1, up.shape[1]), down_all


def back_swap_kernel(
    heads, packed_ref, g_ref, o_ref, s_ref, gate_ref, up_ref, down_ref,
    dq_out, dkv_out, gate_out, up_out, down_out,
    grad_ref, scaled_ref, dots_ref, dq_ref, dkv_ref, kk_ref, vv_ref, ka_ref, kb_ref,
    low_q, low_kv, own_sem, send_sem, got_sem, q_send, q_got, kv_send, kv_got,
    ffn_own, ffn_send, ffn_got,
):
    narrow, wide, chip, core = place()
    count, block, _ = packed_ref.shape
    base = 4 * (chip // 2)
    away = 4 - base
    low = low_lanes(block)
    rows_out = gate_out.shape[1]
    columns = down_out.shape[2]
    tell_all()

    def share(k, who):
        if k == 2:
            return down_ref.at[:, pl.ds(pl.multiple_of(who * columns, columns), columns)]
        return (gate_ref, up_ref)[k].at[pl.ds(pl.multiple_of(who * rows_out, rows_out), rows_out), :]

    def ffn(k, step):
        to = (narrow + step) % 4
        return remote(
            share(k, to), (gate_out, up_out, down_out)[k].at[step], ffn_send.at[k, step],
            ffn_got.at[k, step], (to, wide),
        )

    def send(to):
        return remote(
            g_ref.at[to], grad_ref.at[wide], send_sem.at[to], got_sem.at[wide], (narrow, to)
        )

    def send_q(to):
        return remote(low_q.at[to], dq_out.at[wide], q_send.at[to], q_got.at[wide], (narrow, to))

    def send_kv(to):
        return remote(
            low_kv.at[to], dkv_out.at[wide], kv_send.at[to], kv_got.at[wide], (narrow, to)
        )

    own = pltpu.make_async_copy(g_ref.at[wide], grad_ref.at[wide], own_sem)
    own.start()
    for step in range(1, 8):
        send((wide + step) % 8).start()
    keep = [
        pltpu.make_async_copy(
            share(k, narrow), (gate_out, up_out, down_out)[k].at[0], ffn_own.at[k]
        )
        for k in range(3)
    ]
    for k in range(3):
        keep[k].start()
        for step in range(1, 4):
            ffn(k, step).start()

    @pl.loop(0, count)
    def _(j):
        rows = pl.ds(pl.multiple_of(j * block, block), block)
        kv = packed_ref[j, :, pl.ds(heads * 64, 128)]
        vk = jnp.concatenate([kv[:, 64:], kv[:, :64]], axis=1)
        zero = jnp.zeros_like(kv)
        kk_ref[rows, :] = jnp.where(low, kv, vk)
        vv_ref[rows, :] = jnp.where(low, vk, kv)
        ka_ref[rows, :] = jnp.where(low, kv, zero)
        kb_ref[rows, :] = jnp.where(low, zero, vk)
        dkv_ref[0, rows, :] = jnp.zeros((block, 128), jnp.float32)
        dkv_ref[1, rows, :] = jnp.zeros((block, 128), jnp.float32)

    causal = lax.broadcasted_iota(jnp.int32, (block, block), 0) <= lax.broadcasted_iota(
        jnp.int32, (block, block), 1
    )
    first_lanes = lax.broadcasted_iota(jnp.int32, (8, 128), 1) < 64
    picks = (
        jnp.where(first_lanes, 1.0, 0.0).astype(jnp.bfloat16),
        jnp.where(first_lanes, 0.0, 1.0).astype(jnp.bfloat16),
    )

    def rows_back(i):
        rows = pl.ds(pl.multiple_of(i * block, block), block)
        for pair in range(heads // 2):
            lanes = pl.ds(pair * 128, 128)
            grad = grad_ref[i, :, lanes].astype(jnp.float32) / s_ref[rows, lanes]
            scaled_ref[...] = grad.astype(jnp.bfloat16)
            product = grad * o_ref[rows, lanes]
            high = product.astype(jnp.bfloat16)
            rest = (product - high.astype(jnp.float32)).astype(jnp.bfloat16)
            for side in range(2):
                dots_ref[side] = nt(picks[side], high) + nt(picks[side], rest)
            qboth = packed_ref[i, :, lanes]
            gboth = scaled_ref[...]
            zero = jnp.zeros_like(qboth)
            qs = (jnp.where(low, qboth, zero), jnp.where(low, zero, qboth))
            gs = (jnp.where(low, gboth, zero), jnp.where(low, zero, gboth))

            def step(j, diagonal):
                keys = pl.ds(pl.multiple_of(j * block, block), block)
                kk = kk_ref[keys, :]
                vv = vv_ref[keys, :]
                for side in range(2):
                    weights = jnp.exp2(nt(kk, qs[side]))
                    if diagonal:
                        weights = jnp.where(causal, weights, 0.0)
                    dots = dots_ref[side, pl.ds(0, 1), :]
                    grads = (weights * (nt(vv, gs[side]) - dots)).astype(jnp.bfloat16)
                    dkv_ref[1, keys, :] += nn(weights.astype(jnp.bfloat16), gs[side])
                    dkv_ref[0, keys, :] += nn(grads, qs[side])
                    part = tn(grads, (ka_ref, kb_ref)[side][keys, :])
                    if diagonal and side == 0:
                        dq_ref[...] = part
                    else:
                        dq_ref[...] += part

            step(i, True)

            @pl.loop(0, i)
            def _(j):
                step(j, False)

            low_q[i, :, lanes] = (dq_ref[...] * 0.125).astype(jnp.bfloat16)

        @pl.when(i != wide)
        def _():
            send_q(i).start()

        @pl.when(i == wide)
        def _():
            dq_out[i] = low_q[i]

    def keys_back(j):
        rows = pl.ds(pl.multiple_of(j * block, block), block)
        keys = dkv_ref[0, rows, :] * (1.0 / LOG2E)
        values = dkv_ref[1, rows, :]
        keys = keys + jnp.concatenate([keys[:, 64:], keys[:, :64]], axis=1)
        values = values + jnp.concatenate([values[:, 64:], values[:, :64]], axis=1)
        low_kv[j] = jnp.where(low, keys, values).astype(jnp.bfloat16)

        @pl.when(j != wide)
        def _():
            send_kv(j).start()

        @pl.when(j == wide)
        def _():
            dkv_out[j] = low_kv[j]

    own.wait()

    @pl.loop(0, 4)
    def _(k):
        i = base + 3 - k

        @pl.when(i != wide)
        def _():
            target = grad_ref.at[i]
            remote(target, target, send_sem.at[i], got_sem.at[i], (narrow, i)).wait_recv()

        rows_back(i)

        @pl.when(base > 0)
        def _():
            keys_back(i)

    @pl.loop(0, 4)
    def _(k):
        i = away + 3 - k
        target = grad_ref.at[i]
        remote(target, target, send_sem.at[i], got_sem.at[i], (narrow, i)).wait_recv()
        rows_back(i)
        keys_back(i)

    @pl.when(base == 0)
    def _():
        @pl.loop(0, 4)
        def _(k):
            keys_back(3 - k)

    for step in range(1, 8):
        to = (wide + step) % 8
        target = dq_out.at[to]
        remote(target, target, q_send.at[to], q_got.at[to], (narrow, to)).wait_recv()
        target = dkv_out.at[to]
        remote(target, target, kv_send.at[to], kv_got.at[to], (narrow, to)).wait_recv()
        send(to).wait_send()
        send_q(to).wait_send()
        send_kv(to).wait_send()
    for k in range(3):
        keep[k].wait()
        for step in range(1, 4):
            ffn(k, step).wait()


def back_swap(packed, grad, attended, weight_sums, gate, up, down, heads):
    count, block, lanes = packed.shape
    split = heads * 64
    if lax.axis_size("narrow") != 4 or lax.axis_size("wide") != 8:
        head_grad = swap(grad).reshape(-1, split).astype(jnp.float32) / weight_sums
        dots = jnp.sum((head_grad * attended).reshape(-1, heads, 64), axis=-1).T
        result = attend_back(
            packed.reshape(-1, lanes), head_grad.astype(jnp.bfloat16), dots, heads
        )
        result = swap(result.reshape(packed.shape))
        return (
            result[:, :, :split],
            result[:, :, split:],
            lax.psum_scatter(gate, "narrow", scatter_dimension=0, tiled=True)[None],
            lax.psum_scatter(up, "narrow", scatter_dimension=0, tiled=True)[None],
            lax.psum_scatter(down, "narrow", scatter_dimension=1, tiled=True)[None],
        )
    total = count * block
    dma = pltpu.SemaphoreType.DMA
    vmem = pltpu.VMEM
    low = jnp.bfloat16
    cost = heads * total * total // 2
    return pl.pallas_call(
        functools.partial(back_swap_kernel, heads),
        out_shape=[
            jax.ShapeDtypeStruct((count, block, split), low),
            jax.ShapeDtypeStruct((count, block, 128), low),
            jax.ShapeDtypeStruct((4, gate.shape[0] // 4, gate.shape[1]), low),
            jax.ShapeDtypeStruct((4, up.shape[0] // 4, up.shape[1]), low),
            jax.ShapeDtypeStruct((4, down.shape[0], down.shape[1] // 4), low),
        ],
        in_specs=[
            pl.BlockSpec(memory_space=vmem),
            pl.BlockSpec(memory_space=pl.ANY),
            pl.BlockSpec(memory_space=vmem),
            pl.BlockSpec(memory_space=vmem),
        ]
        + [pl.BlockSpec(memory_space=pl.ANY)] * 3,
        out_specs=[pl.BlockSpec(memory_space=vmem)] * 2 + [pl.BlockSpec(memory_space=pl.ANY)] * 3,
        scratch_shapes=[
            vmem((count, block, split), low),
            vmem((block, 128), low),
            vmem((2, 8, block), jnp.float32),
            vmem((block, 128), jnp.float32),
            vmem((2, total, 128), jnp.float32),
        ]
        + [vmem((total, 128), low)] * 4
        + [
            vmem((count, block, split), low),
            vmem((count, block, 128), low),
            dma, dma((8,)), dma((8,)), dma((8,)), dma((8,)), dma((8,)), dma((8,)),
            dma((3,)), dma((3, 4)), dma((3, 4)),
        ],
        compiler_params=pltpu.CompilerParams(
            collective_id=5, has_side_effects=True, vmem_limit_bytes=52 << 20
        ),
        cost_estimate=pl.CostEstimate(
            flops=12 * cost * 256, bytes_accessed=12 * packed.size, transcendentals=cost
        ),
        name="back_swap",
    )(packed, grad, attended, weight_sums, gate, up, down)


def swap_halves(values):
    lane = lax.broadcasted_iota(jnp.int32, values.shape, 1)
    return jnp.where(lane % 64 < 32, pltpu.roll(values, 96, 1), pltpu.roll(values, 32, 1))


def head_mean(values):
    row = lax.broadcasted_iota(jnp.int32, (128, 128), 0) < 64
    lane = lax.broadcasted_iota(jnp.int32, (128, 128), 1) < 64
    same = jnp.logical_or(
        jnp.logical_and(row, lane),
        jnp.logical_and(jnp.logical_not(row), jnp.logical_not(lane)),
    )
    spread = jnp.where(same, 1.0 / 64.0, 0.0).astype(jnp.bfloat16)
    high = values.astype(jnp.bfloat16)
    rest = (values - high.astype(jnp.float32)).astype(jnp.bfloat16)
    return nn(high, spread) + nn(rest, spread)


def project_kernel(pairs, rows_ref, weight_ref, cos_ref, sin_ref, gain_ref, src_ref, raw_ref):
    low = low_lanes(rows_ref.shape[0])
    raw_ref[0] = nn(rows_ref[...], weight_ref[0])
    for pair in range(pairs + 1):
        lanes = pl.ds(pair * 128, 128)
        raw = raw_ref[0, :, lanes]
        which = 0 if pair < pairs else 1
        scaled = raw * lax.rsqrt(head_mean(raw * raw) + EPSILON) * gain_ref[which : which + 1, :]
        turned = scaled * cos_ref[...] + swap_halves(scaled) * sin_ref[...]
        if pair < pairs:
            result = turned * (0.125 * LOG2E)
        else:
            result = jnp.where(low, turned, raw)
        src_ref[0, :, lanes] = result.astype(jnp.bfloat16)


def project(rows, weights, cosine, sine_part, gains, heads):
    count, width, _ = weights.shape
    length = rows.shape[0]
    lanes = heads * 64 + 128
    whole = lambda g: (0, 0)
    group = lambda g: (g, 0, 0)
    return pl.pallas_call(
        functools.partial(project_kernel, heads // 2),
        grid=(count,),
        out_shape=[
            jax.ShapeDtypeStruct((count, length, lanes), jnp.bfloat16),
            jax.ShapeDtypeStruct((count, length, lanes), jnp.float32),
        ],
        in_specs=[
            pl.BlockSpec((length, width), whole),
            pl.BlockSpec((1, width, lanes), group),
            pl.BlockSpec((length, 128), whole),
            pl.BlockSpec((length, 128), whole),
            pl.BlockSpec((2, 128), whole),
        ],
        out_specs=[pl.BlockSpec((1, length, lanes), group)] * 2,
        compiler_params=pltpu.CompilerParams(vmem_limit_bytes=48 << 20),
        cost_estimate=pl.CostEstimate(
            flops=2 * count * length * width * lanes,
            bytes_accessed=2 * count * width * lanes + 8 * count * length * lanes,
            transcendentals=0,
        ),
        name="project",
    )(rows, weights, cosine, sine_part, gains)


def project_back_kernel(
    pairs, dq_ref, dkv_ref, raw_ref, cos_ref, sin_ref, gain_ref, rows_ref, weight_ref,
    branch_ref, att_ref, in_ref, out_ref, back_ref, gain_out, low_ref, rows_turned, branch_turned,
):
    length, width = rows_ref.shape
    low = low_lanes(length)
    step = 512

    @pl.when(pl.program_id(0) == 0)
    def _():
        back_ref[...] = jnp.zeros_like(back_ref)
        gain_out[...] = jnp.zeros_like(gain_out)

        @pl.loop(0, width // step)
        def _(i):
            piece = pl.ds(pl.multiple_of(i * step, step), step)
            rows_turned[piece, :] = rows_ref[:, piece].T
            branch_turned[piece, :] = branch_ref[:, piece].T

    for pair in range(pairs + 1):
        lanes = pl.ds(pair * 128, 128)
        last = pair == pairs
        which = 1 if last else 0
        turned = (dkv_ref[0] if last else dq_ref[0, :, lanes]).astype(jnp.float32)
        raw = raw_ref[0, :, lanes]
        inverse = lax.rsqrt(head_mean(raw * raw) + EPSILON)
        unit = raw * inverse
        scaled = turned * cos_ref[...] + swap_halves(turned * sin_ref[...])
        part = jnp.sum(scaled * unit, axis=0, keepdims=True)
        scaled = scaled * gain_ref[which : which + 1, :]
        result = inverse * (scaled - unit * inverse * head_mean(scaled * raw))
        if last:
            result = jnp.where(low, result, turned)
        gain_out[which : which + 1, :] += part
        low_ref[:, lanes] = result.astype(jnp.bfloat16)

    @pl.loop(0, width // step)
    def _(i):
        piece = pl.ds(pl.multiple_of(i * step, step), step)
        in_ref[0, piece, :] = nn(rows_turned[piece, :], low_ref[...]).astype(jnp.bfloat16)
        out_ref[0, piece, :] = nn(branch_turned[piece, :], att_ref[0]).astype(jnp.bfloat16)
        back_ref[:, piece] += nt(low_ref[...], weight_ref[0, piece, :])


def project_back(dq, dkv, raw, cosine, sine_part, gains, rows, weights, branch, attended, heads):
    count, length, lanes = raw.shape
    width = rows.shape[1]
    split = heads * 64
    low = jnp.bfloat16
    whole = lambda g: (0, 0)
    group = lambda g: (g, 0, 0)
    return pl.pallas_call(
        functools.partial(project_back_kernel, heads // 2),
        grid=(count,),
        out_shape=[
            jax.ShapeDtypeStruct((count, width, lanes), low),
            jax.ShapeDtypeStruct((count, width, split), low),
            jax.ShapeDtypeStruct((length, width), jnp.float32),
            jax.ShapeDtypeStruct((8, 128), jnp.float32),
        ],
        in_specs=[
            pl.BlockSpec((1, length, split), group),
            pl.BlockSpec((1, length, 128), group),
            pl.BlockSpec((1, length, lanes), group),
            pl.BlockSpec((length, 128), whole),
            pl.BlockSpec((length, 128), whole),
            pl.BlockSpec((2, 128), whole),
            pl.BlockSpec((length, width), whole),
            pl.BlockSpec((1, width, lanes), group),
            pl.BlockSpec((length, width), whole),
            pl.BlockSpec((1, length, split), group),
        ],
        out_specs=[
            pl.BlockSpec((1, width, lanes), group),
            pl.BlockSpec((1, width, split), group),
            pl.BlockSpec((length, width), whole),
            pl.BlockSpec((8, 128), whole),
        ],
        scratch_shapes=[
            pltpu.VMEM((length, lanes), low),
            pltpu.VMEM((width, length), low),
            pltpu.VMEM((width, length), low),
        ],
        compiler_params=pltpu.CompilerParams(vmem_limit_bytes=48 << 20),
        cost_estimate=pl.CostEstimate(
            flops=2 * count * length * width * (2 * lanes + split),
            bytes_accessed=count * width * (4 * lanes + 2 * split) + 8 * count * length * lanes,
            transcendentals=0,
        ),
        name="project_back",
    )(dq, dkv, raw, cosine, sine_part, gains, rows, weights, branch, attended)


def shards(
    tokens_in,
    out_grad,
    positions,
    query_weight,
    query_first,
    query_second,
    key_weight,
    key_first,
    key_second,
    value_weight,
    value_first,
    value_second,
    output_weight,
    output_first,
    output_second,
    gate_weight,
    gate_first,
    gate_second,
    up_weight,
    up_first,
    up_second,
    down_weight,
    down_first,
    down_second,
    norm_gains,
    norm_first,
    norm_second,
    head_gains,
    head_first,
    head_second,
):
    wide_count = lax.axis_size("wide")
    wide_rank = lax.axis_index("wide")
    narrow_count = lax.axis_size("narrow")
    head_dim = head_gains.shape[1]
    key_heads = key_weight.shape[1] // head_dim
    local_heads = query_weight.shape[1] // head_dim
    shard_rows, model_width = tokens_in.shape
    copies = wide_count // key_heads
    key_slot = wide_rank // copies
    key_own = lax.dynamic_slice_in_dim(key_weight, key_slot * head_dim, head_dim, 1)
    value_own = lax.dynamic_slice_in_dim(value_weight, key_slot * head_dim, head_dim, 1)
    query_columns = query_weight.shape[1]
    att_own = jnp.concatenate([query_weight, key_own, value_own, output_weight.T], axis=1)
    half_rows = shard_rows // 2
    grad_halves = [
        lax.all_gather(out_grad[:half_rows], "wide", axis=0, tiled=True),
        lax.all_gather(out_grad[half_rows:], "wide", axis=0, tiled=True),
    ]
    att_full, gate_own = lax.optimization_barrier(
        (gather_weights(att_own.astype(jnp.bfloat16)), gate_weight.astype(jnp.bfloat16))
    )
    gate_local = lax.all_gather(gate_own, "narrow", axis=0, tiled=True)
    group_columns = query_columns + 2 * head_dim
    output_full = att_full[:, :, group_columns:]
    inverse = jnp.power(ROTARY_BASE, -2.0 * jnp.arange(head_dim // 2, dtype=jnp.float32) / head_dim)
    own_positions = lax.dynamic_slice_in_dim(positions, wide_rank * shard_rows, shard_rows, 0)
    angles = own_positions.astype(jnp.float32)[:, None] * inverse[None, :]
    cosine = jnp.cos(angles)
    sine_part = jnp.sin(angles)
    cosine = jnp.concatenate([cosine] * 4, axis=1)
    sine_part = jnp.concatenate([-sine_part, sine_part] * 2, axis=1)
    lane_gains = jnp.concatenate([head_gains, head_gains], axis=1)
    residual = tokens_in.astype(jnp.float32)
    normed_in, norm_in_back = jax.vjp(rms_scale, residual, norm_gains[0])
    rows_in = normed_in.astype(jnp.bfloat16)
    packed, input_raw = project(rows_in, att_full, cosine, sine_part, lane_gains, local_heads)
    packed, grad_halves = lax.optimization_barrier((packed, grad_halves))
    packed, attended, weight_sums, attended_low, up_local, down_local = attend_swap(
        packed, up_weight.astype(jnp.bfloat16), down_weight.astype(jnp.bfloat16), local_heads
    )
    attended_low, gate_local = lax.optimization_barrier((attended_low, gate_local))
    branch = jnp.einsum("gth,gdh->td", attended_low, output_full, preferred_element_type=jnp.float32)
    middle = residual + branch
    normed_mid, norm_mid_back = jax.vjp(rms_scale, middle, norm_gains[1])
    mid_low = normed_mid.astype(jnp.bfloat16)
    down_wgrad = gate_wgrad = up_wgrad = 0.0
    block_parts = []
    mid_sums = []
    rows_halves = [gather_rows(mid_low[:half_rows]), gather_rows(mid_low[half_rows:])]
    hidden_grads = [dot_back(rows, down_local).astype(jnp.bfloat16) for rows in grad_halves]
    rows_halves[0], hidden_grads = lax.optimization_barrier((rows_halves[0], hidden_grads))
    for rows_mid, grad_rows, hidden_grad in zip(rows_halves, grad_halves, hidden_grads):
        gate_pre = dot_last(rows_mid, gate_local)
        up_pre = dot_last(rows_mid, up_local)
        hidden, hidden_back = jax.vjp(
            lambda gate_in, up_in: jax.nn.silu(gate_in) * up_in, gate_pre, up_pre
        )
        hidden_low = hidden.astype(jnp.bfloat16)
        gate_grad, up_grad = hidden_back(hidden_grad.astype(jnp.float32))
        gate_grad = gate_grad.astype(jnp.bfloat16)
        up_grad = up_grad.astype(jnp.bfloat16)
        mid_sums.append(sum_back(((gate_grad, gate_local), (up_grad, up_local))))
        block_parts.append(dot_last(hidden_low, down_local).astype(jnp.bfloat16))
        down_wgrad = down_wgrad + dot_first(hidden_low, grad_rows)
        gate_wgrad = gate_wgrad + dot_first(rows_mid, gate_grad)
        up_wgrad = up_wgrad + dot_first(rows_mid, up_grad)
    down_wgrad = down_wgrad.astype(jnp.bfloat16)
    gate_wgrad = gate_wgrad.astype(jnp.bfloat16)
    up_wgrad = up_wgrad.astype(jnp.bfloat16)
    mid_sums, gate_wgrad, up_wgrad, down_wgrad, block_parts = lax.optimization_barrier(
        (mid_sums, gate_wgrad, up_wgrad, down_wgrad, block_parts)
    )
    mid_back = jnp.concatenate(mid_sums, axis=0)
    middle_part, mid_gain_grad = norm_mid_back(mid_back)
    middle_grad = out_grad.astype(jnp.float32) + middle_part
    branch_grad = middle_grad.astype(jnp.bfloat16)
    attended_grad = jnp.einsum(
        "td,gdh->gth", branch_grad, output_full, preferred_element_type=jnp.float32
    ).astype(jnp.bfloat16)
    attended_grad, first_part = lax.optimization_barrier((attended_grad, block_parts[0]))
    first_sum = lax.psum_scatter(first_part, "wide", scatter_dimension=0, tiled=True)
    query_rot_grad, key_value_grad, gate_shares, up_shares, down_shares = back_swap(
        packed, attended_grad, attended, weight_sums, gate_wgrad, up_wgrad, down_wgrad, local_heads
    )
    query_rot_grad, first_sum, second_part = lax.optimization_barrier(
        (query_rot_grad, first_sum, block_parts[1])
    )
    second_sum = lax.psum_scatter(second_part, "wide", scatter_dimension=0, tiled=True)
    input_wgrad, output_wgrad, input_back, head_sums = project_back(
        query_rot_grad, key_value_grad, input_raw, cosine, sine_part, lane_gains, rows_in,
        att_full, branch_grad, attended_low, local_heads,
    )
    input_part, in_gain_grad = norm_in_back(input_back)
    input_grad = middle_grad + input_part
    gain_stack = jnp.stack([in_gain_grad, mid_gain_grad])
    head_stack = jnp.stack(
        [head_sums[0, :head_dim] + head_sums[0, head_dim:], head_sums[1, :head_dim]]
    )
    query_total, output_total, key_total, value_total, gains = sum_weights(
        input_wgrad,
        output_wgrad,
        jnp.concatenate([gain_stack, head_stack], axis=1),
        key_heads,
    )
    query_total, second_sum = lax.optimization_barrier((query_total, second_sum))
    block_sum = jnp.concatenate([first_sum, second_sum], axis=0).astype(jnp.float32)
    block_out = (middle + block_sum).astype(jnp.bfloat16)
    gain_total = gains[:, :model_width]
    head_total = gains[:, model_width:]
    gate_total, up_total, down_total = (
        jnp.sum(gate_shares.astype(jnp.float32), axis=0),
        jnp.sum(up_shares.astype(jnp.float32), axis=0),
        jnp.sum(down_shares.astype(jnp.float32), axis=0),
    )
    wide_rate = D ** (-0.5)
    query_new = adam_update(
        query_weight, query_first, query_second, query_total, wide_rate, WEIGHT_DECAY
    )
    key_new = adam_update(key_weight, key_first, key_second, key_total, wide_rate, WEIGHT_DECAY)
    value_new = adam_update(
        value_weight, value_first, value_second, value_total, wide_rate, WEIGHT_DECAY
    )
    output_new = adam_update(
        output_weight, output_first, output_second, output_total, O_FAN ** (-0.5), WEIGHT_DECAY
    )
    gate_new = adam_update(
        gate_weight, gate_first, gate_second, gate_total, wide_rate, WEIGHT_DECAY
    )
    up_new = adam_update(up_weight, up_first, up_second, up_total, wide_rate, WEIGHT_DECAY)
    down_new = adam_update(
        down_weight, down_first, down_second, down_total, FF ** (-0.5), WEIGHT_DECAY
    )
    norm_new = adam_update(norm_gains, norm_first, norm_second, gain_total, GAIN_RATE, 0.0)
    head_new = adam_update(head_gains, head_first, head_second, head_total, GAIN_RATE, 0.0)
    return (
        block_out,
        input_grad,
        query_new[0],
        query_new[1],
        query_new[2],
        key_new[0],
        key_new[1],
        key_new[2],
        value_new[0],
        value_new[1],
        value_new[2],
        output_new[0],
        output_new[1],
        output_new[2],
        gate_new[0],
        gate_new[1],
        gate_new[2],
        up_new[0],
        up_new[1],
        up_new[2],
        down_new[0],
        down_new[1],
        down_new[2],
        norm_new[0],
        norm_new[1],
        norm_new[2],
        head_new[0],
        head_new[1],
        head_new[2],
    )


def solution(mesh):
    return jax.shard_map(
        shards,
        mesh=mesh,
        in_specs=(
            P(("narrow", "wide"), None),
            P(("narrow", "wide"), None),
            P("narrow"),
            P("narrow", "wide"),
            P("narrow", "wide"),
            P("narrow", "wide"),
            P("narrow", None),
            P("narrow", None),
            P("narrow", None),
            P("narrow", None),
            P("narrow", None),
            P("narrow", None),
            P("wide", "narrow"),
            P("wide", "narrow"),
            P("wide", "narrow"),
            P("narrow", "wide"),
            P("narrow", "wide"),
            P("narrow", "wide"),
            P("narrow", "wide"),
            P("narrow", "wide"),
            P("narrow", "wide"),
            P("wide", "narrow"),
            P("wide", "narrow"),
            P("wide", "narrow"),
            P(),
            P(),
            P(),
            P(),
            P(),
            P(),
        ),
        out_specs=(
            P(("narrow", "wide"), None),
            P(("narrow", "wide"), None),
            P("narrow", "wide"),
            P("narrow", "wide"),
            P("narrow", "wide"),
            P("narrow", None),
            P("narrow", None),
            P("narrow", None),
            P("narrow", None),
            P("narrow", None),
            P("narrow", None),
            P("wide", "narrow"),
            P("wide", "narrow"),
            P("wide", "narrow"),
            P("narrow", "wide"),
            P("narrow", "wide"),
            P("narrow", "wide"),
            P("narrow", "wide"),
            P("narrow", "wide"),
            P("narrow", "wide"),
            P("wide", "narrow"),
            P("wide", "narrow"),
            P("wide", "narrow"),
            P(),
            P(),
            P(),
            P(),
            P(),
            P(),
        ),
        check_vma=False,
    )
```

```python
import functools
import math

import jax
import jax.numpy as jnp
from jax import lax
from jax.experimental import pallas as pl
from jax.experimental.pallas import tpu as pltpu
from jax.sharding import PartitionSpec as P

D = 2048
FF = 8192
SEQ_LEN = 4096
STEP = 10
O_FAN = 50


EPSILON = 1e-06
BETA_ONE = 0.9
BETA_TWO = 0.95
ADAM_EPSILON = 1e-08
WEIGHT_DECAY = 0.1
GAIN_RATE = 1.0
ROTARY_BASE = 10000.0
MASKED_SCORE = -1e30


def rms_scale(inputs, gain):
    return inputs * lax.rsqrt(jnp.mean(inputs * inputs, axis=-1, keepdims=True) + EPSILON) * gain


def rotate(inputs, cosine, sine_part):
    half_width = inputs.shape[-1] // 2
    first_half = inputs[..., :half_width]
    second_half = inputs[..., half_width:]
    return jnp.concatenate(
        [
            first_half * cosine - second_half * sine_part,
            second_half * cosine + first_half * sine_part,
        ],
        axis=-1,
    )


def adam_update(weight, first_moment, second_moment, gradient, rate, decay):
    first_new = BETA_ONE * first_moment + (1.0 - BETA_ONE) * gradient
    second_new = BETA_TWO * second_moment + (1.0 - BETA_TWO) * gradient * gradient
    ratio = (
        first_new
        / (1.0 - BETA_ONE**STEP)
        / (jnp.sqrt(second_new / (1.0 - BETA_TWO**STEP)) + ADAM_EPSILON)
    )
    return (weight - rate * (ratio + decay * weight), first_new, second_new)


def dot_last(left, right):
    return jnp.dot(left, right, preferred_element_type=jnp.float32)


def dot_first(left, right):
    return lax.dot_general(
        left, right, (((0,), (0,)), ((), ())), preferred_element_type=jnp.float32
    )


def dot_back(left, right):
    return lax.dot_general(
        left, right, (((1,), (1,)), ((), ())), preferred_element_type=jnp.float32
    )


LOG2E = math.log2(math.e)

def nt(a, b):
    return lax.dot_general(a, b, (((1,), (1,)), ((), ())), preferred_element_type=jnp.float32)
def tn(a, b):
    return lax.dot_general(a, b, (((0,), (0,)), ((), ())), preferred_element_type=jnp.float32)
def nn(a, b):
    return jnp.dot(a, b, preferred_element_type=jnp.float32)

def low_lanes(rows):
    return lax.broadcasted_iota(jnp.int32, (rows, 128), 1) < 64

def attend_kernel(block, heads, q_ref, o_ref, s_ref, low_ref, kk_ref, va_ref, vb_ref, acc_ref):
    total = q_ref.shape[0]
    low = low_lanes(block)

    @pl.loop(0, total // block)
    def _(j):
        rows = pl.ds(pl.multiple_of(j * block, block), block)
        kv = q_ref[rows, pl.ds(heads * 64, 128)]
        vk = jnp.concatenate([kv[:, 64:], kv[:, :64]], axis=1)
        one = jnp.ones_like(kv)
        kk_ref[rows, :] = jnp.where(low, kv, vk)
        va_ref[rows, :] = jnp.where(low, vk, one)
        vb_ref[rows, :] = jnp.where(low, one, kv)

    causal = lax.broadcasted_iota(jnp.int32, (block, block), 0) >= lax.broadcasted_iota(
        jnp.int32, (block, block), 1
    )

    @pl.loop(0, total // block)
    def _(i):
        rows = pl.ds(pl.multiple_of(i * block, block), block)
        for pair in range(heads // 2):
            lanes = pl.ds(pair * 128, 128)
            both = q_ref[rows, lanes]
            zero = jnp.zeros_like(both)
            sides = (jnp.where(low, both, zero), jnp.where(low, zero, both))

            def step(j, diagonal):
                keys = pl.ds(pl.multiple_of(j * block, block), block)
                kk = kk_ref[keys, :]
                for side in range(2):
                    weights = jnp.exp2(nt(sides[side], kk))
                    if diagonal:
                        weights = jnp.where(causal, weights, 0.0)
                    part = nn(weights.astype(jnp.bfloat16), (va_ref, vb_ref)[side][keys, :])
                    if diagonal:
                        acc_ref[side] = part
                    else:
                        acc_ref[side] += part

            step(i, True)

            @pl.loop(0, i)
            def _(j):
                step(j, False)

            first, second = acc_ref[0], acc_ref[1]
            summed = jnp.where(low, first, second)
            sums = jnp.where(low, second, first)
            sums = jnp.concatenate([sums[:, 64:], sums[:, :64]], axis=1)
            result = summed / sums
            o_ref[rows, lanes] = result
            s_ref[rows, lanes] = sums
            low_ref[rows, lanes] = result.astype(jnp.bfloat16)

def attend(packed, heads, block=512):
    total = packed.shape[0]
    shape = (total, heads * 64)
    cost = heads * total * total // 2
    return pl.pallas_call(
        functools.partial(attend_kernel, block, heads),
        out_shape=[
            jax.ShapeDtypeStruct(shape, jnp.float32),
            jax.ShapeDtypeStruct(shape, jnp.float32),
            jax.ShapeDtypeStruct(shape, jnp.bfloat16),
        ],
        in_specs=[pl.BlockSpec(memory_space=pltpu.VMEM)],
        out_specs=[pl.BlockSpec(memory_space=pltpu.VMEM)] * 3,
        scratch_shapes=[pltpu.VMEM((total, 128), jnp.bfloat16)] * 3 + [pltpu.VMEM((2, block, 128), jnp.float32)],
        compiler_params=pltpu.CompilerParams(vmem_limit_bytes=56 << 20),
        cost_estimate=pl.CostEstimate(flops=4 * cost * 256, bytes_accessed=12 * packed.size, transcendentals=cost),
        name="attend",
    )(packed)

def back_kernel(block, heads, q_ref, g_ref, d_ref, out_ref, dq_ref, dkv_ref, kk_ref, vv_ref, ka_ref, kb_ref):
    total = q_ref.shape[0]
    low = low_lanes(block)
    count = total // block

    @pl.loop(0, count)
    def _(j):
        rows = pl.ds(pl.multiple_of(j * block, block), block)
        kv = q_ref[rows, pl.ds(heads * 64, 128)]
        vk = jnp.concatenate([kv[:, 64:], kv[:, :64]], axis=1)
        zero = jnp.zeros_like(kv)
        kk_ref[rows, :] = jnp.where(low, kv, vk)
        vv_ref[rows, :] = jnp.where(low, vk, kv)
        ka_ref[rows, :] = jnp.where(low, kv, zero)
        kb_ref[rows, :] = jnp.where(low, zero, vk)
        dkv_ref[0, rows, :] = jnp.zeros((block, 128), jnp.float32)
        dkv_ref[1, rows, :] = jnp.zeros((block, 128), jnp.float32)

    causal = lax.broadcasted_iota(jnp.int32, (block, block), 0) <= lax.broadcasted_iota(
        jnp.int32, (block, block), 1
    )

    @pl.loop(0, count)
    def _(i):
        rows = pl.ds(pl.multiple_of(i * block, block), block)
        for pair in range(heads // 2):
            lanes = pl.ds(pair * 128, 128)
            qboth = q_ref[rows, lanes]
            gboth = g_ref[rows, lanes]
            zero = jnp.zeros_like(qboth)
            qs = (jnp.where(low, qboth, zero), jnp.where(low, zero, qboth))
            gs = (jnp.where(low, gboth, zero), jnp.where(low, zero, gboth))

            def step(j, diagonal):
                keys = pl.ds(pl.multiple_of(j * block, block), block)
                kk = kk_ref[keys, :]
                vv = vv_ref[keys, :]
                for side in range(2):
                    weights = jnp.exp2(nt(kk, qs[side]))
                    if diagonal:
                        weights = jnp.where(causal, weights, 0.0)
                    dots = d_ref[pl.ds(pair * 2 + side, 1), rows]
                    grads = (weights * (nt(vv, gs[side]) - dots)).astype(jnp.bfloat16)
                    dkv_ref[1, keys, :] += nn(weights.astype(jnp.bfloat16), gs[side])
                    dkv_ref[0, keys, :] += nn(grads, qs[side])
                    part = tn(grads, (ka_ref, kb_ref)[side][keys, :])
                    if diagonal and side == 0:
                        dq_ref[:, lanes] = part
                    else:
                        dq_ref[:, lanes] += part

            step(i, True)

            @pl.loop(0, i)
            def _(j):
                step(j, False)

            out_ref[rows, lanes] = (dq_ref[:, lanes] * 0.125).astype(jnp.bfloat16)

    @pl.loop(0, count)
    def _(j):
        rows = pl.ds(pl.multiple_of(j * block, block), block)
        keys = dkv_ref[0, rows, :] * (1.0 / LOG2E)
        values = dkv_ref[1, rows, :]
        keys = keys + jnp.concatenate([keys[:, 64:], keys[:, :64]], axis=1)
        values = values + jnp.concatenate([values[:, 64:], values[:, :64]], axis=1)
        out_ref[rows, pl.ds(heads * 64, 128)] = jnp.where(low, keys, values).astype(jnp.bfloat16)

def attend_back(packed, g, dots, heads, block=512):
    total = packed.shape[0]
    cost = heads * total * total // 2
    return pl.pallas_call(
        functools.partial(back_kernel, block, heads),
        out_shape=jax.ShapeDtypeStruct(packed.shape, jnp.bfloat16),
        in_specs=[pl.BlockSpec(memory_space=pltpu.VMEM)] * 3,
        out_specs=pl.BlockSpec(memory_space=pltpu.VMEM),
        scratch_shapes=[
            pltpu.VMEM((block, heads * 64), jnp.float32),
            pltpu.VMEM((2, total, 128), jnp.float32),
        ]
        + [pltpu.VMEM((total, 128), jnp.bfloat16)] * 4,
        compiler_params=pltpu.CompilerParams(vmem_limit_bytes=56 << 20),
        cost_estimate=pl.CostEstimate(
            flops=10 * cost * 256, bytes_accessed=12 * packed.size, transcendentals=cost
        ),
        name="attend_back",
    )(packed, g, dots)


def remote(source, target, send, arrive, device):
    return pltpu.make_async_remote_copy(
        src_ref=source,
        dst_ref=target,
        send_sem=send,
        recv_sem=arrive,
        device_id=device,
        device_id_type=pl.DeviceIdType.MESH,
    )


def place():
    narrow = lax.axis_index("narrow")
    wide = lax.axis_index("wide")
    return narrow, wide, wide // 2, wide % 2


def greet_neighbours():
    narrow, wide, chip, core = place()
    barrier = pltpu.get_barrier_semaphore()

    def tell(device):
        pl.semaphore_signal(
            barrier, inc=1, device_id=device, device_id_type=pl.DeviceIdType.MESH
        )

    tell((narrow + 1 - 2 * (narrow % 2), wide))
    tell(((narrow + 2) % 4, wide))
    tell((narrow, 2 * chip + 1 - core))

    @pl.when(chip > 0)
    def _():
        tell((narrow, wide - 2))

    @pl.when(chip < 3)
    def _():
        tell((narrow, wide + 2))

    pl.semaphore_wait(barrier, 3 + jnp.minimum(chip, 1) + jnp.minimum(3 - chip, 1))


def gather_kernel(
    att_ref, att_all, own_sem, line_send, line_got, side_send, side_got, core_send, core_got
):
    narrow, wide, chip, core = place()
    beside = narrow + 1 - 2 * (narrow % 2)
    across = (narrow + 2) % 4
    corner = (beside + 2) % 4
    rows = att_ref.shape[0]
    half_rows = rows // 2
    other = (narrow, 2 * chip + 1 - core)
    left = (narrow, wide - 2)
    right = (narrow, wide + 2)
    sides = ((beside, wide), (across, wide))
    near = (beside, across)

    def att(slot, who):
        return att_all.at[slot, pl.ds(pl.multiple_of(who * rows, rows), rows), :]

    def att_half(slot, who, half):
        return att_all.at[
            slot, pl.ds(pl.multiple_of(who * rows + half * half_rows, half_rows), half_rows), :
        ]

    def line(at, step, source):
        return remote(
            source, att(2 * at + core, narrow), line_send.at[at, (step + 1) // 2],
            line_got.at[at], right if step > 0 else left,
        )

    def both_ways(at, source, act):
        @pl.when(jnp.logical_and(at <= chip, chip < 3))
        def _():
            act(line(at, 1, source))

        @pl.when(jnp.logical_and(at >= chip, chip > 0))
        def _():
            act(line(at, -1, source))

    def side(at, k, source):
        return remote(
            source, att(2 * at + core, narrow), side_send.at[at, k], side_got.at[at, k], sides[k]
        )

    def side_arrival(at, k):
        target = att(2 * at + core, near[k])
        return remote(target, target, side_send.at[at, k], side_got.at[at, k], sides[k])

    def forward(at, k):
        piece = att_half(2 * at + core, near[k], k)
        return remote(piece, piece, side_send.at[at, 2 + k], side_got.at[at, 2 + k], sides[1 - k])

    def corner_arrival(at, k):
        piece = att_half(2 * at + core, corner, k)
        return remote(piece, piece, side_send.at[at, 2 + k], side_got.at[at, 2 + k], sides[1 - k])

    def pair(at, who, half_of):
        piece = att(2 * at + half_of, who)
        return remote(piece, piece, core_send.at[at, who], core_got.at[at, who], other)

    start = lambda copy: copy.start()
    greet_neighbours()
    both_ways(chip, att_ref, start)
    for k in range(2):
        side(chip, k, att_ref).start()
    own = pltpu.make_async_copy(att_ref, att(wide, narrow), own_sem)
    own.start()
    own.wait()
    pair(chip, narrow, core).start()

    def hop(distance):
        for at, valid in (
            (chip - distance, chip >= distance), (chip + distance, chip + distance <= 3)
        ):

            @pl.when(valid)
            def _():
                piece = att(2 * at + core, narrow)
                line(at, 1, piece).wait_recv()
                both_ways(at, piece, start)
                for k in range(2):
                    side(at, k, piece).start()
                pair(at, narrow, core).start()

    def around(at):
        for k in range(2):
            side_arrival(at, k).wait_recv()
            forward(at, k).start()
            pair(at, near[k], core).start()

    upper = chip // 2
    second = chip + 1 - 2 * upper
    last = 3 - 3 * upper
    order = (chip, second, 6 - chip - second - last, last)
    for step in range(4):
        if step < 3:
            hop(step + 1)
        around(order[step])
    for at in order:
        for k in range(2):
            corner_arrival(at, k).wait_recv()
        pair(at, corner, core).start()

    for at in range(4):
        both_ways(at, att_ref, lambda copy: copy.wait_send())
        for who in range(4):
            pair(at, who, 1 - core).wait_recv()
            pair(at, who, core).wait_send()
        for k in range(2):
            side(at, k, att_ref).wait_send()
            forward(at, k).wait_send()


def gather_weights(att):
    narrow_count = lax.axis_size("narrow")
    wide_count = lax.axis_size("wide")
    if narrow_count != 4 or wide_count != 8:
        return lax.all_gather(lax.all_gather(att, "wide", axis=0), "narrow", axis=1, tiled=True)
    dma = pltpu.SemaphoreType.DMA
    return pl.pallas_call(
        gather_kernel,
        out_shape=jax.ShapeDtypeStruct((8, 4 * att.shape[0], att.shape[1]), jnp.bfloat16),
        in_specs=[pl.BlockSpec(memory_space=pl.ANY)],
        out_specs=pl.BlockSpec(memory_space=pl.ANY),
        scratch_shapes=[
            dma, dma((4, 2)), dma((4,)), dma((4, 4)), dma((4, 4)), dma((4, 4)), dma((4, 4)),
        ],
        compiler_params=pltpu.CompilerParams(collective_id=1, has_side_effects=True),
        cost_estimate=pl.CostEstimate(flops=0, bytes_accessed=300 << 20, transcendentals=0),
        name="gather_weights",
    )(att)


def gather_rows(shard):
    return lax.all_gather(shard, "wide", axis=0, tiled=True)


def swap(blocks):
    return lax.all_to_all(blocks, "wide", 0, 0)


def sum_back(pairs):
    summed = 0.0
    for gradient, weight in pairs:
        summed = summed + dot_back(gradient, weight)
    return lax.psum_scatter(
        summed.astype(jnp.bfloat16), "wide", scatter_dimension=0, tiled=True
    ).astype(jnp.float32)


def scatter_kernel(
    in_ref, out_ref, gain_ref, query_sum, output_sum, key_sum, value_sum, gain_sum_ref,
    own, other, halves, wholes, from_left, from_right, spread_ref, low, wide_gains, mid_gain,
    narrow_gains,
    load_sem, core_send, core_got, half_send, half_got, whole_send, whole_got,
    line_send, left_got, right_got, spread_send, spread_got, pass_send, pass_got,
    wide_send, wide_got, narrow_send, narrow_got,
):
    narrow, wide, chip, core = place()
    beside = narrow + 1 - 2 * (narrow % 2)
    across = (narrow + 2) % 4
    corner = (beside + 2) % 4
    rows = query_sum.shape[0]
    half_rows = rows // 2
    split = in_ref.shape[2]
    twin = (narrow, 2 * chip + 1 - core)
    sides = ((beside, wide), (across, wide))
    near = (beside, across)
    wides = [(narrow, (wide + step) % 8) for step in range(1, 8)]
    narrows = [((narrow + step) % 4, wide) for step in range(1, 4)]
    upper = chip // 2
    last = 3 - 3 * upper
    second = chip + 1 - 2 * upper
    order = (last, 6 - chip - second - last, second, chip)
    f32 = jnp.float32

    barrier = pltpu.get_barrier_semaphore()
    for device in wides + narrows:
        pl.semaphore_signal(
            barrier, inc=1, device_id=device, device_id_type=pl.DeviceIdType.MESH
        )
    pl.semaphore_wait(barrier, 10)

    parts = ((in_ref, pl.ds(0, split)), (out_ref, pl.ds(split, out_ref.shape[2])))

    def load(at, k):
        source, lanes = parts[k]
        return pltpu.make_async_copy(
            source.at[2 * at + core], own.at[at, :, lanes], load_sem.at[at, k]
        )

    def exchange(at, k):
        source, lanes = parts[k]
        return remote(
            source.at[2 * at + 1 - core], other.at[at, :, lanes], core_send.at[at, k],
            core_got.at[at, k], twin,
        )

    def block(at, who):
        return own.at[at, pl.ds(pl.multiple_of(who * rows, rows), rows), :]

    def half_block(at, who, half):
        return own.at[
            at, pl.ds(pl.multiple_of(who * rows + half * half_rows, half_rows), half_rows), :
        ]

    def half(at, k):
        return remote(
            half_block(at, corner, k), halves.at[at, k], half_send.at[at, k], half_got.at[at, k],
            sides[k],
        )

    def whole(at, k):
        return remote(
            block(at, near[k]), wholes.at[at, k], whole_send.at[at, k], whole_got.at[at, k],
            sides[k],
        )

    def to_right(at):
        return remote(
            block(at, narrow), from_left.at[at], line_send.at[at], left_got.at[at],
            (narrow, wide + 2),
        )

    def to_left(at):
        return remote(
            block(at, narrow), from_right.at[at], line_send.at[at], right_got.at[at],
            (narrow, wide - 2),
        )

    def add(target, source, count, step=64):
        @pl.loop(0, count // step)
        def _(i):
            piece = pl.ds(pl.multiple_of(i * step, step), step)
            target[piece, :] = (
                target[piece, :].astype(f32) + source[piece, :].astype(f32)
            ).astype(jnp.bfloat16)

    for at in order:
        for k in range(2):
            load(at, k).start()
            exchange(at, k).start()
    gains = [
        remote(gain_ref, wide_gains.at[step], wide_send.at[step], wide_got.at[step], device)
        for step, device in enumerate(wides)
    ]
    for copy in gains:
        copy.start()

    def pair_up(at):
        for k in range(2):
            load(at, k).wait()
            exchange(at, k).wait_recv()
        add(own.at[at], other.at[at], 4 * rows)
        for k in range(2):
            half(at, k).start()

    def turn(at):
        for k in range(2):
            half(at, k).wait_recv()
            add(half_block(at, near[1 - k], k), halves.at[at, k], half_rows)
        for k in range(2):
            whole(at, k).start()

    def settle(at):
        for k in range(2):
            whole(at, k).wait_recv()
        target = block(at, narrow)

        @pl.loop(0, rows // 64)
        def _(i):
            piece = pl.ds(pl.multiple_of(i * 64, 64), 64)
            target[piece, :] = (
                target[piece, :].astype(f32)
                + wholes[at, 0, piece, :].astype(f32)
                + wholes[at, 1, piece, :].astype(f32)
            ).astype(jnp.bfloat16)

        @pl.when(at > chip)
        def _():
            @pl.when(chip > 0)
            def _():
                to_right(at).wait_recv()
                add(target, from_left.at[at], rows)

            to_right(at).start()

        @pl.when(at < chip)
        def _():
            @pl.when(chip < 3)
            def _():
                to_left(at).wait_recv()
                add(target, from_right.at[at], rows)

            to_left(at).start()

    pair_up(order[0])
    pair_up(order[1])
    turn(order[0])
    pair_up(order[2])
    turn(order[1])
    settle(order[0])
    pair_up(order[3])
    turn(order[2])
    settle(order[1])
    for copy in gains:
        copy.wait()
    total = gain_ref[...]
    for step in range(7):
        total = total + wide_gains[step]
    mid_gain[...] = total
    gains = [
        remote(mid_gain, narrow_gains.at[step], narrow_send.at[step], narrow_got.at[step], device)
        for step, device in enumerate(narrows)
    ]
    for copy in gains:
        copy.start()
    turn(order[3])
    settle(order[2])
    settle(order[3])
    target = block(chip, narrow)

    @pl.when(chip > 0)
    def _():
        to_right(chip).wait_recv()
        add(target, from_left.at[chip], rows)

    @pl.when(chip < 3)
    def _():
        to_left(chip).wait_recv()
        add(target, from_right.at[chip], rows)

    lanes = pl.ds(split - 128, 128)
    for i in range(rows // 128):
        piece = pl.ds(pl.multiple_of(narrow * rows + i * 128, 128), 128)
        here = pl.ds(i * 128, 128)
        query_sum[here, :] = own[chip, piece, pl.ds(0, split - 128)].astype(f32)
        output_sum[:, here] = own[chip, piece, pl.ds(split, out_ref.shape[2])].astype(f32).T
        low[here, :] = own[chip, piece, lanes]

    spread_ref[wide] = low[...]

    def spread(step):
        return remote(
            low, spread_ref.at[wide], spread_send.at[step - 1], spread_got.at[step - 1],
            (narrow, (wide + 2 * step) % 8),
        )

    def arrival(step):
        target = spread_ref.at[(wide + 8 - 2 * step) % 8]
        return remote(target, target, spread_send.at[step - 1], spread_got.at[step - 1], twin)

    def pass_on(step):
        piece = spread_ref.at[(wide + 8 - 2 * step) % 8]
        return remote(piece, piece, pass_send.at[step], pass_got.at[step], twin)

    def passed(step):
        piece = spread_ref.at[(2 * chip + 1 - core + 8 - 2 * step) % 8]
        return remote(piece, piece, pass_send.at[step], pass_got.at[step], twin)

    for step in (1, 2, 3):
        spread(step).start()
    pass_on(0).start()
    for copy in gains:
        copy.wait()
    for step in range(3):
        total = total + narrow_gains[step]
    gain_sum_ref[...] = total
    for step in (1, 2, 3):
        arrival(step).wait_recv()
        pass_on(step).start()
    for step in range(4):
        passed(step).wait_recv()
        pass_on(step).wait_send()
    for step in (1, 2, 3):
        spread(step).wait_send()
    first = low_lanes(rows)
    for at in range(4):
        even = spread_ref[2 * at].astype(f32)
        odd = spread_ref[2 * at + 1].astype(f32)
        here = pl.ds(at * 128, 128)
        key_sum[:, here] = jnp.where(first, even, pltpu.roll(odd, 64, 1))
        value_sum[:, here] = jnp.where(first, pltpu.roll(even, 64, 1), odd)
    for at in range(4):
        for k in range(2):
            exchange(at, k).wait_send()
            half(at, k).wait_send()
            whole(at, k).wait_send()

        @pl.when(at != chip)
        def _():
            to_right(at).wait_send()


def sum_weights(input_wgrad, output_wgrad, gains, key_heads):
    narrow_count = lax.axis_size("narrow")
    wide_count = lax.axis_size("wide")
    split = input_wgrad.shape[2]
    if narrow_count != 4 or wide_count != 8 or key_heads != 8:
        total = jnp.concatenate([input_wgrad, output_wgrad], axis=2)
        total = lax.psum_scatter(total, "narrow", scatter_dimension=1, tiled=True)
        total = lax.psum_scatter(total, "wide", scatter_dimension=0)
        spread = lax.all_gather(total[:, split - 128 : split], "wide", axis=0)
        spread = spread.reshape(key_heads, wide_count // key_heads, -1, 2, 64)
        spread = jnp.sum(spread.astype(jnp.float32), axis=1).transpose(2, 1, 0, 3)
        spread = spread.reshape(2, -1, key_heads * 64)
        gains = jnp.sum(lax.all_gather(gains, ("narrow", "wide"), axis=0), axis=0)
        total = total.astype(jnp.float32)
        return total[:, : split - 128], total[:, split:].T, spread[0], spread[1], gains
    low = jnp.bfloat16
    rows = input_wgrad.shape[1] // 4
    columns = split + output_wgrad.shape[2]
    size = gains.size
    gain_rows = -(-size // 1024) * 8
    flat = jnp.pad(gains.reshape(-1), (0, gain_rows * 128 - size)).reshape(gain_rows, 128)
    dma = pltpu.SemaphoreType.DMA
    vmem = pltpu.VMEM
    *sums, flat = pl.pallas_call(
        scatter_kernel,
        out_shape=[
            jax.ShapeDtypeStruct((rows, split - 128), jnp.float32),
            jax.ShapeDtypeStruct((columns - split, rows), jnp.float32),
            jax.ShapeDtypeStruct((rows, 512), jnp.float32),
            jax.ShapeDtypeStruct((rows, 512), jnp.float32),
            jax.ShapeDtypeStruct(flat.shape, jnp.float32),
        ],
        in_specs=[
            pl.BlockSpec(memory_space=pl.ANY),
            pl.BlockSpec(memory_space=pl.ANY),
            pl.BlockSpec(memory_space=vmem),
        ],
        out_specs=[pl.BlockSpec(memory_space=vmem)] * 5,
        scratch_shapes=[
            vmem((4, 4 * rows, columns), low),
            vmem((4, 4 * rows, columns), low),
            vmem((4, 2, rows // 2, columns), low),
            vmem((4, 2, rows, columns), low),
            vmem((4, rows, columns), low),
            vmem((4, rows, columns), low),
            vmem((8, rows, 128), low),
            vmem((rows, 128), low),
            vmem((7, gain_rows, 128), jnp.float32),
            vmem((gain_rows, 128), jnp.float32),
            vmem((3, gain_rows, 128), jnp.float32),
            dma((4, 2)), dma((4, 2)), dma((4, 2)), dma((4, 2)), dma((4, 2)), dma((4, 2)),
            dma((4, 2)), dma((4,)), dma((4,)), dma((4,)), dma((3,)), dma((3,)), dma((4,)),
            dma((4,)), dma((7,)), dma((7,)), dma((3,)), dma((3,)),
        ],
        compiler_params=pltpu.CompilerParams(
            collective_id=3, has_side_effects=True, vmem_limit_bytes=52 << 20
        ),
        cost_estimate=pl.CostEstimate(flops=0, bytes_accessed=1 << 20, transcendentals=0),
        name="sum_weights",
    )(input_wgrad, output_wgrad, flat)
    return *sums, flat.reshape(-1)[:size].reshape(gains.shape)


def tell_all():
    narrow = lax.axis_index("narrow")
    wide = lax.axis_index("wide")
    barrier = pltpu.get_barrier_semaphore()
    for step in range(1, 8):
        pl.semaphore_signal(
            barrier, inc=1, device_id=(narrow, (wide + step) % 8),
            device_id_type=pl.DeviceIdType.MESH,
        )
    for step in range(1, 4):
        pl.semaphore_signal(
            barrier, inc=1, device_id=((narrow + step) % 4, wide),
            device_id_type=pl.DeviceIdType.MESH,
        )
    pl.semaphore_wait(barrier, 10)


def attend_swap_kernel(
    heads, src_ref, up_ref, down_ref, packed_ref, o_ref, s_ref, out_ref, up_all, down_all,
    kk_ref, va_ref, vb_ref, acc_ref, low_ref,
    own_sem, send_sem, got_sem, out_send, out_got, ffn_own, ffn_send, ffn_got,
):
    narrow, wide, chip, core = place()
    block = src_ref.shape[1]
    base = 4 * (chip // 2)
    away = 4 - base
    low = low_lanes(block)
    columns = down_ref.shape[1]
    tell_all()

    def ffn_slot(k, who):
        if k:
            return down_all.at[:, pl.ds(pl.multiple_of(who * columns, columns), columns)]
        return up_all.at[who]

    beside = narrow + 1 - 2 * (narrow % 2)
    across = (narrow + 2) % 4
    corner = (beside + 2) % 4
    near = (beside, across)
    sides = ((beside, wide), (across, wide))

    def ffn_half(k, who, half):
        size = (up_ref, down_ref)[k].shape[0] // 2
        if k:
            return down_all.at[
                pl.ds(half * size, size), pl.ds(pl.multiple_of(who * columns, columns), columns)
            ]
        return up_all.at[who, pl.ds(half * size, size), :]

    def ffn(k, j):
        return remote(
            (up_ref, down_ref)[k], ffn_slot(k, narrow), ffn_send.at[k, j], ffn_got.at[k, j],
            sides[j],
        )

    def ffn_arrival(k, j):
        target = ffn_slot(k, near[j])
        return remote(target, target, ffn_send.at[k, j], ffn_got.at[k, j], sides[j])

    def ffn_forward(k, j):
        piece = ffn_half(k, near[j], j)
        return remote(piece, piece, ffn_send.at[k, 2 + j], ffn_got.at[k, 2 + j], sides[1 - j])

    def ffn_corner(k, j):
        piece = ffn_half(k, corner, j)
        return remote(piece, piece, ffn_send.at[k, 2 + j], ffn_got.at[k, 2 + j], sides[1 - j])

    def send(to):
        return remote(
            src_ref.at[to], packed_ref.at[wide], send_sem.at[to], got_sem.at[wide], (narrow, to)
        )

    def arrival(at):
        target = packed_ref.at[at]
        return remote(target, target, send_sem.at[at], got_sem.at[at], (narrow, at))

    def send_out(to):
        return remote(
            low_ref.at[to], out_ref.at[wide], out_send.at[to], out_got.at[wide], (narrow, to)
        )

    own = pltpu.make_async_copy(src_ref.at[wide], packed_ref.at[wide], own_sem)
    own.start()
    for step in range(1, 8):
        send((wide + step) % 8).start()
    keep = [
        pltpu.make_async_copy((up_ref, down_ref)[k], ffn_slot(k, narrow), ffn_own.at[k])
        for k in range(2)
    ]
    for k in (1, 0):
        keep[k].start()
        for j in range(2):
            ffn(k, j).start()

    def prepare(j):
        rows = pl.ds(pl.multiple_of(j * block, block), block)
        kv = packed_ref[j, :, pl.ds(heads * 64, 128)]
        vk = jnp.concatenate([kv[:, 64:], kv[:, :64]], axis=1)
        one = jnp.ones_like(kv)
        kk_ref[rows, :] = jnp.where(low, kv, vk)
        va_ref[rows, :] = jnp.where(low, vk, one)
        vb_ref[rows, :] = jnp.where(low, one, kv)

    def await_blocks(start):
        @pl.loop(start, start + 4)
        def _(j):
            @pl.when(j != wide)
            def _():
                arrival(j).wait_recv()

            prepare(j)

    causal = lax.broadcasted_iota(jnp.int32, (block, block), 0) >= lax.broadcasted_iota(
        jnp.int32, (block, block), 1
    )

    def pairs(i, first, stop, diagonal):
        for pair in range(heads // 2):
            both = packed_ref[i, :, pl.ds(pair * 128, 128)]
            zero = jnp.zeros_like(both)
            sides = (jnp.where(low, both, zero), jnp.where(low, zero, both))

            def step(j, masked, fresh):
                keys = pl.ds(pl.multiple_of(j * block, block), block)
                kk = kk_ref[keys, :]
                for side in range(2):
                    weights = jnp.exp2(nt(sides[side], kk))
                    if masked:
                        weights = jnp.where(causal, weights, 0.0)
                    part = nn(weights.astype(jnp.bfloat16), (va_ref, vb_ref)[side][keys, :])
                    if fresh:
                        acc_ref[i, pair * 2 + side] = part
                    else:
                        acc_ref[i, pair * 2 + side] += part

            if diagonal:
                step(i, True, True)

            @pl.loop(first, stop)
            def _(j):
                step(j, False, False)

    def finish(i):
        rows = pl.ds(pl.multiple_of(i * block, block), block)
        for pair in range(heads // 2):
            lanes = pl.ds(pair * 128, 128)
            first, second = acc_ref[i, pair * 2], acc_ref[i, pair * 2 + 1]
            summed = jnp.where(low, first, second)
            sums = jnp.where(low, second, first)
            sums = jnp.concatenate([sums[:, 64:], sums[:, :64]], axis=1)
            result = summed / sums
            o_ref[rows, lanes] = result
            s_ref[rows, lanes] = sums
            low_ref[i, :, lanes] = result.astype(jnp.bfloat16)

        @pl.when(i != wide)
        def _():
            send_out(i).start()

        @pl.when(i == wide)
        def _():
            out_ref[i] = low_ref[i]

    own.wait()
    await_blocks(base)

    @pl.loop(base, base + 4)
    def _(i):
        pairs(i, base, i, True)

        @pl.when(base == 0)
        def _():
            finish(i)

    await_blocks(away)
    for k in (1, 0):
        for j in range(2):
            ffn_arrival(k, j).wait_recv()
            ffn_forward(k, j).start()

    @pl.loop(away, away + 4)
    def _(i):
        pairs(i, 0, i, True)
        finish(i)

    @pl.when(base > 0)
    def _():
        @pl.loop(4, 8)
        def _(i):
            pairs(i, 0, 4, False)
            finish(i)

    for step in range(1, 8):
        to = (wide + step) % 8
        target = out_ref.at[to]
        remote(target, target, out_send.at[to], out_got.at[to], (narrow, to)).wait_recv()
        send_out(to).wait_send()
        send(to).wait_send()
    for k in range(2):
        keep[k].wait()
        for j in range(2):
            ffn_corner(k, j).wait_recv()
            ffn_forward(k, j).wait_send()
            ffn(k, j).wait_send()


def attend_swap(src, up, down, heads):
    if lax.axis_size("narrow") != 4 or lax.axis_size("wide") != 8:
        packed = swap(src)
        flat = packed.reshape(-1, src.shape[2])
        attended, weight_sums, attended_low = attend(flat, heads)
        attended_low = swap(attended_low.reshape(src.shape[0], -1, heads * 64))
        up_all = lax.all_gather(up, "narrow", axis=0, tiled=True)
        down_all = lax.all_gather(down, "narrow", axis=1, tiled=True)
        return packed, attended, weight_sums, attended_low, up_all, down_all
    count, block, lanes = src.shape
    total = count * block
    dma = pltpu.SemaphoreType.DMA
    vmem = pltpu.VMEM
    cost = heads * total * total // 2
    *results, up_all, down_all = pl.pallas_call(
        functools.partial(attend_swap_kernel, heads),
        out_shape=[
            jax.ShapeDtypeStruct(src.shape, jnp.bfloat16),
            jax.ShapeDtypeStruct((total, heads * 64), jnp.float32),
            jax.ShapeDtypeStruct((total, heads * 64), jnp.float32),
            jax.ShapeDtypeStruct((count, block, heads * 64), jnp.bfloat16),
            jax.ShapeDtypeStruct((4,) + up.shape, jnp.bfloat16),
            jax.ShapeDtypeStruct((down.shape[0], 4 * down.shape[1]), jnp.bfloat16),
        ],
        in_specs=[pl.BlockSpec(memory_space=pl.ANY)] * 3,
        out_specs=[pl.BlockSpec(memory_space=vmem)] * 4 + [pl.BlockSpec(memory_space=pl.ANY)] * 2,
        scratch_shapes=[vmem((total, 128), jnp.bfloat16)] * 3
        + [
            vmem((count, heads, block, 128), jnp.float32),
            vmem((count, block, heads * 64), jnp.bfloat16),
            dma, dma((8,)), dma((8,)), dma((8,)), dma((8,)), dma((2,)), dma((2, 4)), dma((2, 4)),
        ],
        compiler_params=pltpu.CompilerParams(
            collective_id=4, has_side_effects=True, vmem_limit_bytes=52 << 20
        ),
        cost_estimate=pl.CostEstimate(
            flops=8 * cost * 256, bytes_accessed=12 * src.size, transcendentals=cost
        ),
        name="attend_swap",
    )(src, up, down)
    return *results, up_all.reshape(-1, up.shape[1]), down_all


def back_swap_kernel(
    heads, packed_ref, g_ref, o_ref, s_ref, gate_ref, up_ref, down_ref,
    dq_out, dkv_out, gate_out, up_out, down_out,
    grad_ref, scaled_ref, dots_ref, dq_ref, dkv_ref, kk_ref, vv_ref, ka_ref, kb_ref,
    low_q, low_kv, own_sem, send_sem, got_sem, q_send, q_got, kv_send, kv_got,
    ffn_own, ffn_send, ffn_got,
):
    narrow, wide, chip, core = place()
    count, block, _ = packed_ref.shape
    base = 4 * (chip // 2)
    away = 4 - base
    low = low_lanes(block)
    rows_out = gate_out.shape[1]
    columns = down_out.shape[2]
    tell_all()

    def share(k, who):
        if k == 2:
            return down_ref.at[:, pl.ds(pl.multiple_of(who * columns, columns), columns)]
        return (gate_ref, up_ref)[k].at[pl.ds(pl.multiple_of(who * rows_out, rows_out), rows_out), :]

    def ffn(k, step):
        to = (narrow + step) % 4
        return remote(
            share(k, to), (gate_out, up_out, down_out)[k].at[step], ffn_send.at[k, step],
            ffn_got.at[k, step], (to, wide),
        )

    def send(to):
        return remote(
            g_ref.at[to], grad_ref.at[wide], send_sem.at[to], got_sem.at[wide], (narrow, to)
        )

    def send_q(to):
        return remote(low_q.at[to], dq_out.at[wide], q_send.at[to], q_got.at[wide], (narrow, to))

    def send_kv(to):
        return remote(
            low_kv.at[to], dkv_out.at[wide], kv_send.at[to], kv_got.at[wide], (narrow, to)
        )

    own = pltpu.make_async_copy(g_ref.at[wide], grad_ref.at[wide], own_sem)
    own.start()
    for step in range(1, 8):
        send((wide + step) % 8).start()
    keep = [
        pltpu.make_async_copy(
            share(k, narrow), (gate_out, up_out, down_out)[k].at[0], ffn_own.at[k]
        )
        for k in range(3)
    ]
    for k in range(3):
        keep[k].start()
        for step in range(1, 4):
            ffn(k, step).start()

    @pl.loop(0, count)
    def _(j):
        rows = pl.ds(pl.multiple_of(j * block, block), block)
        kv = packed_ref[j, :, pl.ds(heads * 64, 128)]
        vk = jnp.concatenate([kv[:, 64:], kv[:, :64]], axis=1)
        zero = jnp.zeros_like(kv)
        kk_ref[rows, :] = jnp.where(low, kv, vk)
        vv_ref[rows, :] = jnp.where(low, vk, kv)
        ka_ref[rows, :] = jnp.where(low, kv, zero)
        kb_ref[rows, :] = jnp.where(low, zero, vk)
        dkv_ref[0, rows, :] = jnp.zeros((block, 128), jnp.float32)
        dkv_ref[1, rows, :] = jnp.zeros((block, 128), jnp.float32)

    causal = lax.broadcasted_iota(jnp.int32, (block, block), 0) <= lax.broadcasted_iota(
        jnp.int32, (block, block), 1
    )
    first_lanes = lax.broadcasted_iota(jnp.int32, (8, 128), 1) < 64
    picks = (
        jnp.where(first_lanes, 1.0, 0.0).astype(jnp.bfloat16),
        jnp.where(first_lanes, 0.0, 1.0).astype(jnp.bfloat16),
    )

    def rows_back(i):
        rows = pl.ds(pl.multiple_of(i * block, block), block)
        for pair in range(heads // 2):
            lanes = pl.ds(pair * 128, 128)
            grad = grad_ref[i, :, lanes].astype(jnp.float32) / s_ref[rows, lanes]
            scaled_ref[...] = grad.astype(jnp.bfloat16)
            product = grad * o_ref[rows, lanes]
            high = product.astype(jnp.bfloat16)
            rest = (product - high.astype(jnp.float32)).astype(jnp.bfloat16)
            for side in range(2):
                dots_ref[side] = nt(picks[side], high) + nt(picks[side], rest)
            qboth = packed_ref[i, :, lanes]
            gboth = scaled_ref[...]
            zero = jnp.zeros_like(qboth)
            qs = (jnp.where(low, qboth, zero), jnp.where(low, zero, qboth))
            gs = (jnp.where(low, gboth, zero), jnp.where(low, zero, gboth))

            def step(j, diagonal):
                keys = pl.ds(pl.multiple_of(j * block, block), block)
                kk = kk_ref[keys, :]
                vv = vv_ref[keys, :]
                for side in range(2):
                    weights = jnp.exp2(nt(kk, qs[side]))
                    if diagonal:
                        weights = jnp.where(causal, weights, 0.0)
                    dots = dots_ref[side, pl.ds(0, 1), :]
                    grads = (weights * (nt(vv, gs[side]) - dots)).astype(jnp.bfloat16)
                    dkv_ref[1, keys, :] += nn(weights.astype(jnp.bfloat16), gs[side])
                    dkv_ref[0, keys, :] += nn(grads, qs[side])
                    part = tn(grads, (ka_ref, kb_ref)[side][keys, :])
                    if diagonal and side == 0:
                        dq_ref[...] = part
                    else:
                        dq_ref[...] += part

            step(i, True)

            @pl.loop(0, i)
            def _(j):
                step(j, False)

            low_q[i, :, lanes] = (dq_ref[...] * 0.125).astype(jnp.bfloat16)

        @pl.when(i != wide)
        def _():
            send_q(i).start()

        @pl.when(i == wide)
        def _():
            dq_out[i] = low_q[i]

    def keys_back(j):
        rows = pl.ds(pl.multiple_of(j * block, block), block)
        keys = dkv_ref[0, rows, :] * (1.0 / LOG2E)
        values = dkv_ref[1, rows, :]
        keys = keys + jnp.concatenate([keys[:, 64:], keys[:, :64]], axis=1)
        values = values + jnp.concatenate([values[:, 64:], values[:, :64]], axis=1)
        low_kv[j] = jnp.where(low, keys, values).astype(jnp.bfloat16)

        @pl.when(j != wide)
        def _():
            send_kv(j).start()

        @pl.when(j == wide)
        def _():
            dkv_out[j] = low_kv[j]

    own.wait()

    @pl.loop(0, 4)
    def _(k):
        i = base + 3 - k

        @pl.when(i != wide)
        def _():
            target = grad_ref.at[i]
            remote(target, target, send_sem.at[i], got_sem.at[i], (narrow, i)).wait_recv()

        rows_back(i)

        @pl.when(base > 0)
        def _():
            keys_back(i)

    @pl.loop(0, 4)
    def _(k):
        i = away + 3 - k
        target = grad_ref.at[i]
        remote(target, target, send_sem.at[i], got_sem.at[i], (narrow, i)).wait_recv()
        rows_back(i)
        keys_back(i)

    @pl.when(base == 0)
    def _():
        @pl.loop(0, 4)
        def _(k):
            keys_back(3 - k)

    for step in range(1, 8):
        to = (wide + step) % 8
        target = dq_out.at[to]
        remote(target, target, q_send.at[to], q_got.at[to], (narrow, to)).wait_recv()
        target = dkv_out.at[to]
        remote(target, target, kv_send.at[to], kv_got.at[to], (narrow, to)).wait_recv()
        send(to).wait_send()
        send_q(to).wait_send()
        send_kv(to).wait_send()
    for k in range(3):
        keep[k].wait()
        for step in range(1, 4):
            ffn(k, step).wait()


def back_swap(packed, grad, attended, weight_sums, gate, up, down, heads):
    count, block, lanes = packed.shape
    split = heads * 64
    if lax.axis_size("narrow") != 4 or lax.axis_size("wide") != 8:
        head_grad = swap(grad).reshape(-1, split).astype(jnp.float32) / weight_sums
        dots = jnp.sum((head_grad * attended).reshape(-1, heads, 64), axis=-1).T
        result = attend_back(
            packed.reshape(-1, lanes), head_grad.astype(jnp.bfloat16), dots, heads
        )
        result = swap(result.reshape(packed.shape))
        return (
            result[:, :, :split],
            result[:, :, split:],
            lax.psum_scatter(gate, "narrow", scatter_dimension=0, tiled=True)[None],
            lax.psum_scatter(up, "narrow", scatter_dimension=0, tiled=True)[None],
            lax.psum_scatter(down, "narrow", scatter_dimension=1, tiled=True)[None],
        )
    total = count * block
    dma = pltpu.SemaphoreType.DMA
    vmem = pltpu.VMEM
    low = jnp.bfloat16
    cost = heads * total * total // 2
    return pl.pallas_call(
        functools.partial(back_swap_kernel, heads),
        out_shape=[
            jax.ShapeDtypeStruct((count, block, split), low),
            jax.ShapeDtypeStruct((count, block, 128), low),
            jax.ShapeDtypeStruct((4, gate.shape[0] // 4, gate.shape[1]), low),
            jax.ShapeDtypeStruct((4, up.shape[0] // 4, up.shape[1]), low),
            jax.ShapeDtypeStruct((4, down.shape[0], down.shape[1] // 4), low),
        ],
        in_specs=[
            pl.BlockSpec(memory_space=vmem),
            pl.BlockSpec(memory_space=pl.ANY),
            pl.BlockSpec(memory_space=vmem),
            pl.BlockSpec(memory_space=vmem),
        ]
        + [pl.BlockSpec(memory_space=pl.ANY)] * 3,
        out_specs=[pl.BlockSpec(memory_space=vmem)] * 2 + [pl.BlockSpec(memory_space=pl.ANY)] * 3,
        scratch_shapes=[
            vmem((count, block, split), low),
            vmem((block, 128), low),
            vmem((2, 8, block), jnp.float32),
            vmem((block, 128), jnp.float32),
            vmem((2, total, 128), jnp.float32),
        ]
        + [vmem((total, 128), low)] * 4
        + [
            vmem((count, block, split), low),
            vmem((count, block, 128), low),
            dma, dma((8,)), dma((8,)), dma((8,)), dma((8,)), dma((8,)), dma((8,)),
            dma((3,)), dma((3, 4)), dma((3, 4)),
        ],
        compiler_params=pltpu.CompilerParams(
            collective_id=5, has_side_effects=True, vmem_limit_bytes=52 << 20
        ),
        cost_estimate=pl.CostEstimate(
            flops=12 * cost * 256, bytes_accessed=12 * packed.size, transcendentals=cost
        ),
        name="back_swap",
    )(packed, grad, attended, weight_sums, gate, up, down)


def swap_halves(values):
    lane = lax.broadcasted_iota(jnp.int32, values.shape, 1)
    return jnp.where(lane % 64 < 32, pltpu.roll(values, 96, 1), pltpu.roll(values, 32, 1))


def head_mean(values):
    row = lax.broadcasted_iota(jnp.int32, (128, 128), 0) < 64
    lane = lax.broadcasted_iota(jnp.int32, (128, 128), 1) < 64
    same = jnp.logical_or(
        jnp.logical_and(row, lane),
        jnp.logical_and(jnp.logical_not(row), jnp.logical_not(lane)),
    )
    spread = jnp.where(same, 1.0 / 64.0, 0.0).astype(jnp.bfloat16)
    high = values.astype(jnp.bfloat16)
    rest = (values - high.astype(jnp.float32)).astype(jnp.bfloat16)
    return nn(high, spread) + nn(rest, spread)


def project_kernel(pairs, rows_ref, weight_ref, cos_ref, sin_ref, gain_ref, src_ref, raw_ref):
    low = low_lanes(rows_ref.shape[0])
    raw_ref[0] = nn(rows_ref[...], weight_ref[0])
    for pair in range(pairs + 1):
        lanes = pl.ds(pair * 128, 128)
        raw = raw_ref[0, :, lanes]
        which = 0 if pair < pairs else 1
        scaled = raw * lax.rsqrt(head_mean(raw * raw) + EPSILON) * gain_ref[which : which + 1, :]
        turned = scaled * cos_ref[...] + swap_halves(scaled) * sin_ref[...]
        if pair < pairs:
            result = turned * (0.125 * LOG2E)
        else:
            result = jnp.where(low, turned, raw)
        src_ref[0, :, lanes] = result.astype(jnp.bfloat16)


def project(rows, weights, cosine, sine_part, gains, heads):
    count, width, _ = weights.shape
    length = rows.shape[0]
    lanes = heads * 64 + 128
    whole = lambda g: (0, 0)
    group = lambda g: (g, 0, 0)
    return pl.pallas_call(
        functools.partial(project_kernel, heads // 2),
        grid=(count,),
        out_shape=[
            jax.ShapeDtypeStruct((count, length, lanes), jnp.bfloat16),
            jax.ShapeDtypeStruct((count, length, lanes), jnp.float32),
        ],
        in_specs=[
            pl.BlockSpec((length, width), whole),
            pl.BlockSpec((1, width, lanes), group),
            pl.BlockSpec((length, 128), whole),
            pl.BlockSpec((length, 128), whole),
            pl.BlockSpec((2, 128), whole),
        ],
        out_specs=[pl.BlockSpec((1, length, lanes), group)] * 2,
        compiler_params=pltpu.CompilerParams(vmem_limit_bytes=48 << 20),
        cost_estimate=pl.CostEstimate(
            flops=2 * count * length * width * lanes,
            bytes_accessed=2 * count * width * lanes + 8 * count * length * lanes,
            transcendentals=0,
        ),
        name="project",
    )(rows, weights, cosine, sine_part, gains)


def project_back_kernel(
    pairs, dq_ref, dkv_ref, raw_ref, cos_ref, sin_ref, gain_ref, rows_ref, weight_ref,
    branch_ref, att_ref, in_ref, out_ref, back_ref, gain_out, low_ref, rows_turned, branch_turned,
):
    length, width = rows_ref.shape
    low = low_lanes(length)
    step = 512

    @pl.when(pl.program_id(0) == 0)
    def _():
        back_ref[...] = jnp.zeros_like(back_ref)
        gain_out[...] = jnp.zeros_like(gain_out)

        @pl.loop(0, width // step)
        def _(i):
            piece = pl.ds(pl.multiple_of(i * step, step), step)
            rows_turned[piece, :] = rows_ref[:, piece].T
            branch_turned[piece, :] = branch_ref[:, piece].T

    for pair in range(pairs + 1):
        lanes = pl.ds(pair * 128, 128)
        last = pair == pairs
        which = 1 if last else 0
        turned = (dkv_ref[0] if last else dq_ref[0, :, lanes]).astype(jnp.float32)
        raw = raw_ref[0, :, lanes]
        inverse = lax.rsqrt(head_mean(raw * raw) + EPSILON)
        unit = raw * inverse
        scaled = turned * cos_ref[...] + swap_halves(turned * sin_ref[...])
        part = jnp.sum(scaled * unit, axis=0, keepdims=True)
        scaled = scaled * gain_ref[which : which + 1, :]
        result = inverse * (scaled - unit * inverse * head_mean(scaled * raw))
        if last:
            result = jnp.where(low, result, turned)
        gain_out[which : which + 1, :] += part
        low_ref[:, lanes] = result.astype(jnp.bfloat16)

    @pl.loop(0, width // step)
    def _(i):
        piece = pl.ds(pl.multiple_of(i * step, step), step)
        in_ref[0, piece, :] = nn(rows_turned[piece, :], low_ref[...]).astype(jnp.bfloat16)
        out_ref[0, piece, :] = nn(branch_turned[piece, :], att_ref[0]).astype(jnp.bfloat16)
        back_ref[:, piece] += nt(low_ref[...], weight_ref[0, piece, :])


def project_back(dq, dkv, raw, cosine, sine_part, gains, rows, weights, branch, attended, heads):
    count, length, lanes = raw.shape
    width = rows.shape[1]
    split = heads * 64
    low = jnp.bfloat16
    whole = lambda g: (0, 0)
    group = lambda g: (g, 0, 0)
    return pl.pallas_call(
        functools.partial(project_back_kernel, heads // 2),
        grid=(count,),
        out_shape=[
            jax.ShapeDtypeStruct((count, width, lanes), low),
            jax.ShapeDtypeStruct((count, width, split), low),
            jax.ShapeDtypeStruct((length, width), jnp.float32),
            jax.ShapeDtypeStruct((8, 128), jnp.float32),
        ],
        in_specs=[
            pl.BlockSpec((1, length, split), group),
            pl.BlockSpec((1, length, 128), group),
            pl.BlockSpec((1, length, lanes), group),
            pl.BlockSpec((length, 128), whole),
            pl.BlockSpec((length, 128), whole),
            pl.BlockSpec((2, 128), whole),
            pl.BlockSpec((length, width), whole),
            pl.BlockSpec((1, width, lanes), group),
            pl.BlockSpec((length, width), whole),
            pl.BlockSpec((1, length, split), group),
        ],
        out_specs=[
            pl.BlockSpec((1, width, lanes), group),
            pl.BlockSpec((1, width, split), group),
            pl.BlockSpec((length, width), whole),
            pl.BlockSpec((8, 128), whole),
        ],
        scratch_shapes=[
            pltpu.VMEM((length, lanes), low),
            pltpu.VMEM((width, length), low),
            pltpu.VMEM((width, length), low),
        ],
        compiler_params=pltpu.CompilerParams(vmem_limit_bytes=48 << 20),
        cost_estimate=pl.CostEstimate(
            flops=2 * count * length * width * (2 * lanes + split),
            bytes_accessed=count * width * (4 * lanes + 2 * split) + 8 * count * length * lanes,
            transcendentals=0,
        ),
        name="project_back",
    )(dq, dkv, raw, cosine, sine_part, gains, rows, weights, branch, attended)


def shards(
    tokens_in,
    out_grad,
    positions,
    query_weight,
    query_first,
    query_second,
    key_weight,
    key_first,
    key_second,
    value_weight,
    value_first,
    value_second,
    output_weight,
    output_first,
    output_second,
    gate_weight,
    gate_first,
    gate_second,
    up_weight,
    up_first,
    up_second,
    down_weight,
    down_first,
    down_second,
    norm_gains,
    norm_first,
    norm_second,
    head_gains,
    head_first,
    head_second,
):
    wide_count = lax.axis_size("wide")
    wide_rank = lax.axis_index("wide")
    narrow_count = lax.axis_size("narrow")
    head_dim = head_gains.shape[1]
    key_heads = key_weight.shape[1] // head_dim
    local_heads = query_weight.shape[1] // head_dim
    shard_rows, model_width = tokens_in.shape
    copies = wide_count // key_heads
    key_slot = wide_rank // copies
    key_own = lax.dynamic_slice_in_dim(key_weight, key_slot * head_dim, head_dim, 1)
    value_own = lax.dynamic_slice_in_dim(value_weight, key_slot * head_dim, head_dim, 1)
    query_columns = query_weight.shape[1]
    att_own = jnp.concatenate([query_weight, key_own, value_own, output_weight.T], axis=1)
    half_rows = shard_rows // 2
    grad_halves = [
        lax.all_gather(out_grad[:half_rows], "wide", axis=0, tiled=True),
        lax.all_gather(out_grad[half_rows:], "wide", axis=0, tiled=True),
    ]
    att_full, gate_own = lax.optimization_barrier(
        (gather_weights(att_own.astype(jnp.bfloat16)), gate_weight.astype(jnp.bfloat16))
    )
    gate_local = lax.all_gather(gate_own, "narrow", axis=0, tiled=True)
    group_columns = query_columns + 2 * head_dim
    output_full = att_full[:, :, group_columns:]
    inverse = jnp.power(ROTARY_BASE, -2.0 * jnp.arange(head_dim // 2, dtype=jnp.float32) / head_dim)
    own_positions = lax.dynamic_slice_in_dim(positions, wide_rank * shard_rows, shard_rows, 0)
    angles = own_positions.astype(jnp.float32)[:, None] * inverse[None, :]
    cosine = jnp.cos(angles)
    sine_part = jnp.sin(angles)
    cosine = jnp.concatenate([cosine] * 4, axis=1)
    sine_part = jnp.concatenate([-sine_part, sine_part] * 2, axis=1)
    lane_gains = jnp.concatenate([head_gains, head_gains], axis=1)
    residual = tokens_in.astype(jnp.float32)
    normed_in, norm_in_back = jax.vjp(rms_scale, residual, norm_gains[0])
    rows_in = normed_in.astype(jnp.bfloat16)
    packed, input_raw = project(rows_in, att_full, cosine, sine_part, lane_gains, local_heads)
    packed, grad_halves = lax.optimization_barrier((packed, grad_halves))
    packed, attended, weight_sums, attended_low, up_local, down_local = attend_swap(
        packed, up_weight.astype(jnp.bfloat16), down_weight.astype(jnp.bfloat16), local_heads
    )
    attended_low, gate_local = lax.optimization_barrier((attended_low, gate_local))
    branch = jnp.einsum("gth,gdh->td", attended_low, output_full, preferred_element_type=jnp.float32)
    middle = residual + branch
    normed_mid, norm_mid_back = jax.vjp(rms_scale, middle, norm_gains[1])
    mid_low = normed_mid.astype(jnp.bfloat16)
    down_wgrad = gate_wgrad = up_wgrad = 0.0
    block_parts = []
    mid_sums = []
    rows_halves = [gather_rows(mid_low[:half_rows]), gather_rows(mid_low[half_rows:])]
    hidden_grads = [dot_back(rows, down_local).astype(jnp.bfloat16) for rows in grad_halves]
    rows_halves[0], hidden_grads = lax.optimization_barrier((rows_halves[0], hidden_grads))
    for rows_mid, grad_rows, hidden_grad in zip(rows_halves, grad_halves, hidden_grads):
        gate_pre = dot_last(rows_mid, gate_local)
        up_pre = dot_last(rows_mid, up_local)
        hidden, hidden_back = jax.vjp(
            lambda gate_in, up_in: jax.nn.silu(gate_in) * up_in, gate_pre, up_pre
        )
        hidden_low = hidden.astype(jnp.bfloat16)
        gate_grad, up_grad = hidden_back(hidden_grad.astype(jnp.float32))
        gate_grad = gate_grad.astype(jnp.bfloat16)
        up_grad = up_grad.astype(jnp.bfloat16)
        mid_sums.append(sum_back(((gate_grad, gate_local), (up_grad, up_local))))
        block_parts.append(dot_last(hidden_low, down_local).astype(jnp.bfloat16))
        down_wgrad = down_wgrad + dot_first(hidden_low, grad_rows)
        gate_wgrad = gate_wgrad + dot_first(rows_mid, gate_grad)
        up_wgrad = up_wgrad + dot_first(rows_mid, up_grad)
    down_wgrad = down_wgrad.astype(jnp.bfloat16)
    gate_wgrad = gate_wgrad.astype(jnp.bfloat16)
    up_wgrad = up_wgrad.astype(jnp.bfloat16)
    mid_sums, gate_wgrad, up_wgrad, down_wgrad, block_parts = lax.optimization_barrier(
        (mid_sums, gate_wgrad, up_wgrad, down_wgrad, block_parts)
    )
    mid_back = jnp.concatenate(mid_sums, axis=0)
    middle_part, mid_gain_grad = norm_mid_back(mid_back)
    middle_grad = out_grad.astype(jnp.float32) + middle_part
    branch_grad = middle_grad.astype(jnp.bfloat16)
    attended_grad = jnp.einsum(
        "td,gdh->gth", branch_grad, output_full, preferred_element_type=jnp.float32
    ).astype(jnp.bfloat16)
    query_rot_grad, key_value_grad, gate_shares, up_shares, down_shares = back_swap(
        packed, attended_grad, attended, weight_sums, gate_wgrad, up_wgrad, down_wgrad, local_heads
    )
    query_rot_grad, first_part, second_part = lax.optimization_barrier(
        (query_rot_grad, block_parts[0], block_parts[1])
    )
    first_sum = lax.psum_scatter(first_part, "wide", scatter_dimension=0, tiled=True)
    second_sum = lax.psum_scatter(second_part, "wide", scatter_dimension=0, tiled=True)
    input_wgrad, output_wgrad, input_back, head_sums = project_back(
        query_rot_grad, key_value_grad, input_raw, cosine, sine_part, lane_gains, rows_in,
        att_full, branch_grad, attended_low, local_heads,
    )
    input_part, in_gain_grad = norm_in_back(input_back)
    input_grad = middle_grad + input_part
    gain_stack = jnp.stack([in_gain_grad, mid_gain_grad])
    head_stack = jnp.stack(
        [head_sums[0, :head_dim] + head_sums[0, head_dim:], head_sums[1, :head_dim]]
    )
    query_total, output_total, key_total, value_total, gains = sum_weights(
        input_wgrad,
        output_wgrad,
        jnp.concatenate([gain_stack, head_stack], axis=1),
        key_heads,
    )
    query_total, first_sum, second_sum = lax.optimization_barrier(
        (query_total, first_sum, second_sum)
    )
    block_sum = jnp.concatenate([first_sum, second_sum], axis=0).astype(jnp.float32)
    block_out = (middle + block_sum).astype(jnp.bfloat16)
    gain_total = gains[:, :model_width]
    head_total = gains[:, model_width:]
    gate_total, up_total, down_total = (
        jnp.sum(gate_shares.astype(jnp.float32), axis=0),
        jnp.sum(up_shares.astype(jnp.float32), axis=0),
        jnp.sum(down_shares.astype(jnp.float32), axis=0),
    )
    wide_rate = D ** (-0.5)
    query_new = adam_update(
        query_weight, query_first, query_second, query_total, wide_rate, WEIGHT_DECAY
    )
    key_new = adam_update(key_weight, key_first, key_second, key_total, wide_rate, WEIGHT_DECAY)
    value_new = adam_update(
        value_weight, value_first, value_second, value_total, wide_rate, WEIGHT_DECAY
    )
    output_new = adam_update(
        output_weight, output_first, output_second, output_total, O_FAN ** (-0.5), WEIGHT_DECAY
    )
    gate_new = adam_update(
        gate_weight, gate_first, gate_second, gate_total, wide_rate, WEIGHT_DECAY
    )
    up_new = adam_update(up_weight, up_first, up_second, up_total, wide_rate, WEIGHT_DECAY)
    down_new = adam_update(
        down_weight, down_first, down_second, down_total, FF ** (-0.5), WEIGHT_DECAY
    )
    norm_new = adam_update(norm_gains, norm_first, norm_second, gain_total, GAIN_RATE, 0.0)
    head_new = adam_update(head_gains, head_first, head_second, head_total, GAIN_RATE, 0.0)
    return (
        block_out,
        input_grad,
        query_new[0],
        query_new[1],
        query_new[2],
        key_new[0],
        key_new[1],
        key_new[2],
        value_new[0],
        value_new[1],
        value_new[2],
        output_new[0],
        output_new[1],
        output_new[2],
        gate_new[0],
        gate_new[1],
        gate_new[2],
        up_new[0],
        up_new[1],
        up_new[2],
        down_new[0],
        down_new[1],
        down_new[2],
        norm_new[0],
        norm_new[1],
        norm_new[2],
        head_new[0],
        head_new[1],
        head_new[2],
    )


def solution(mesh):
    return jax.shard_map(
        shards,
        mesh=mesh,
        in_specs=(
            P(("narrow", "wide"), None),
            P(("narrow", "wide"), None),
            P("narrow"),
            P("narrow", "wide"),
            P("narrow", "wide"),
            P("narrow", "wide"),
            P("narrow", None),
            P("narrow", None),
            P("narrow", None),
            P("narrow", None),
            P("narrow", None),
            P("narrow", None),
            P("wide", "narrow"),
            P("wide", "narrow"),
            P("wide", "narrow"),
            P("narrow", "wide"),
            P("narrow", "wide"),
            P("narrow", "wide"),
            P("narrow", "wide"),
            P("narrow", "wide"),
            P("narrow", "wide"),
            P("wide", "narrow"),
            P("wide", "narrow"),
            P("wide", "narrow"),
            P(),
            P(),
            P(),
            P(),
            P(),
            P(),
        ),
        out_specs=(
            P(("narrow", "wide"), None),
            P(("narrow", "wide"), None),
            P("narrow", "wide"),
            P("narrow", "wide"),
            P("narrow", "wide"),
            P("narrow", None),
            P("narrow", None),
            P("narrow", None),
            P("narrow", None),
            P("narrow", None),
            P("narrow", None),
            P("wide", "narrow"),
            P("wide", "narrow"),
            P("wide", "narrow"),
            P("narrow", "wide"),
            P("narrow", "wide"),
            P("narrow", "wide"),
            P("narrow", "wide"),
            P("narrow", "wide"),
            P("narrow", "wide"),
            P("wide", "narrow"),
            P("wide", "narrow"),
            P("wide", "narrow"),
            P(),
            P(),
            P(),
            P(),
            P(),
            P(),
        ),
        check_vma=False,
    )
```

```python
import functools
import math

import jax
import jax.numpy as jnp
from jax import lax
from jax.experimental import pallas as pl
from jax.experimental.pallas import tpu as pltpu
from jax.sharding import PartitionSpec as P

D = 2048
FF = 8192
SEQ_LEN = 4096
STEP = 10
O_FAN = 50


EPSILON = 1e-06
BETA_ONE = 0.9
BETA_TWO = 0.95
ADAM_EPSILON = 1e-08
WEIGHT_DECAY = 0.1
GAIN_RATE = 1.0
ROTARY_BASE = 10000.0
MASKED_SCORE = -1e30


def rms_scale(inputs, gain):
    return inputs * lax.rsqrt(jnp.mean(inputs * inputs, axis=-1, keepdims=True) + EPSILON) * gain


def rotate(inputs, cosine, sine_part):
    half_width = inputs.shape[-1] // 2
    first_half = inputs[..., :half_width]
    second_half = inputs[..., half_width:]
    return jnp.concatenate(
        [
            first_half * cosine - second_half * sine_part,
            second_half * cosine + first_half * sine_part,
        ],
        axis=-1,
    )


def adam_update(weight, first_moment, second_moment, gradient, rate, decay):
    first_new = BETA_ONE * first_moment + (1.0 - BETA_ONE) * gradient
    second_new = BETA_TWO * second_moment + (1.0 - BETA_TWO) * gradient * gradient
    ratio = (
        first_new
        / (1.0 - BETA_ONE**STEP)
        / (jnp.sqrt(second_new / (1.0 - BETA_TWO**STEP)) + ADAM_EPSILON)
    )
    return (weight - rate * (ratio + decay * weight), first_new, second_new)


def dot_last(left, right):
    return jnp.dot(left, right, preferred_element_type=jnp.float32)


def dot_first(left, right):
    return lax.dot_general(
        left, right, (((0,), (0,)), ((), ())), preferred_element_type=jnp.float32
    )


def dot_back(left, right):
    return lax.dot_general(
        left, right, (((1,), (1,)), ((), ())), preferred_element_type=jnp.float32
    )


LOG2E = math.log2(math.e)

def nt(a, b):
    return lax.dot_general(a, b, (((1,), (1,)), ((), ())), preferred_element_type=jnp.float32)
def tn(a, b):
    return lax.dot_general(a, b, (((0,), (0,)), ((), ())), preferred_element_type=jnp.float32)
def nn(a, b):
    return jnp.dot(a, b, preferred_element_type=jnp.float32)

def low_lanes(rows):
    return lax.broadcasted_iota(jnp.int32, (rows, 128), 1) < 64

def attend_kernel(block, heads, q_ref, o_ref, s_ref, low_ref, kk_ref, va_ref, vb_ref, acc_ref):
    total = q_ref.shape[0]
    low = low_lanes(block)

    @pl.loop(0, total // block)
    def _(j):
        rows = pl.ds(pl.multiple_of(j * block, block), block)
        kv = q_ref[rows, pl.ds(heads * 64, 128)]
        vk = jnp.concatenate([kv[:, 64:], kv[:, :64]], axis=1)
        one = jnp.ones_like(kv)
        kk_ref[rows, :] = jnp.where(low, kv, vk)
        va_ref[rows, :] = jnp.where(low, vk, one)
        vb_ref[rows, :] = jnp.where(low, one, kv)

    causal = lax.broadcasted_iota(jnp.int32, (block, block), 0) >= lax.broadcasted_iota(
        jnp.int32, (block, block), 1
    )

    @pl.loop(0, total // block)
    def _(i):
        rows = pl.ds(pl.multiple_of(i * block, block), block)
        for pair in range(heads // 2):
            lanes = pl.ds(pair * 128, 128)
            both = q_ref[rows, lanes]
            zero = jnp.zeros_like(both)
            sides = (jnp.where(low, both, zero), jnp.where(low, zero, both))

            def step(j, diagonal):
                keys = pl.ds(pl.multiple_of(j * block, block), block)
                kk = kk_ref[keys, :]
                for side in range(2):
                    weights = jnp.exp2(nt(sides[side], kk))
                    if diagonal:
                        weights = jnp.where(causal, weights, 0.0)
                    part = nn(weights.astype(jnp.bfloat16), (va_ref, vb_ref)[side][keys, :])
                    if diagonal:
                        acc_ref[side] = part
                    else:
                        acc_ref[side] += part

            step(i, True)

            @pl.loop(0, i)
            def _(j):
                step(j, False)

            first, second = acc_ref[0], acc_ref[1]
            summed = jnp.where(low, first, second)
            sums = jnp.where(low, second, first)
            sums = jnp.concatenate([sums[:, 64:], sums[:, :64]], axis=1)
            result = summed / sums
            o_ref[rows, lanes] = result
            s_ref[rows, lanes] = sums
            low_ref[rows, lanes] = result.astype(jnp.bfloat16)

def attend(packed, heads, block=512):
    total = packed.shape[0]
    shape = (total, heads * 64)
    cost = heads * total * total // 2
    return pl.pallas_call(
        functools.partial(attend_kernel, block, heads),
        out_shape=[
            jax.ShapeDtypeStruct(shape, jnp.float32),
            jax.ShapeDtypeStruct(shape, jnp.float32),
            jax.ShapeDtypeStruct(shape, jnp.bfloat16),
        ],
        in_specs=[pl.BlockSpec(memory_space=pltpu.VMEM)],
        out_specs=[pl.BlockSpec(memory_space=pltpu.VMEM)] * 3,
        scratch_shapes=[pltpu.VMEM((total, 128), jnp.bfloat16)] * 3 + [pltpu.VMEM((2, block, 128), jnp.float32)],
        compiler_params=pltpu.CompilerParams(vmem_limit_bytes=56 << 20),
        cost_estimate=pl.CostEstimate(flops=4 * cost * 256, bytes_accessed=12 * packed.size, transcendentals=cost),
        name="attend",
    )(packed)

def back_kernel(block, heads, q_ref, g_ref, d_ref, out_ref, dq_ref, dkv_ref, kk_ref, vv_ref, ka_ref, kb_ref):
    total = q_ref.shape[0]
    low = low_lanes(block)
    count = total // block

    @pl.loop(0, count)
    def _(j):
        rows = pl.ds(pl.multiple_of(j * block, block), block)
        kv = q_ref[rows, pl.ds(heads * 64, 128)]
        vk = jnp.concatenate([kv[:, 64:], kv[:, :64]], axis=1)
        zero = jnp.zeros_like(kv)
        kk_ref[rows, :] = jnp.where(low, kv, vk)
        vv_ref[rows, :] = jnp.where(low, vk, kv)
        ka_ref[rows, :] = jnp.where(low, kv, zero)
        kb_ref[rows, :] = jnp.where(low, zero, vk)
        dkv_ref[0, rows, :] = jnp.zeros((block, 128), jnp.float32)
        dkv_ref[1, rows, :] = jnp.zeros((block, 128), jnp.float32)

    causal = lax.broadcasted_iota(jnp.int32, (block, block), 0) <= lax.broadcasted_iota(
        jnp.int32, (block, block), 1
    )

    @pl.loop(0, count)
    def _(i):
        rows = pl.ds(pl.multiple_of(i * block, block), block)
        for pair in range(heads // 2):
            lanes = pl.ds(pair * 128, 128)
            qboth = q_ref[rows, lanes]
            gboth = g_ref[rows, lanes]
            zero = jnp.zeros_like(qboth)
            qs = (jnp.where(low, qboth, zero), jnp.where(low, zero, qboth))
            gs = (jnp.where(low, gboth, zero), jnp.where(low, zero, gboth))

            def step(j, diagonal):
                keys = pl.ds(pl.multiple_of(j * block, block), block)
                kk = kk_ref[keys, :]
                vv = vv_ref[keys, :]
                for side in range(2):
                    weights = jnp.exp2(nt(kk, qs[side]))
                    if diagonal:
                        weights = jnp.where(causal, weights, 0.0)
                    dots = d_ref[pl.ds(pair * 2 + side, 1), rows]
                    grads = (weights * (nt(vv, gs[side]) - dots)).astype(jnp.bfloat16)
                    dkv_ref[1, keys, :] += nn(weights.astype(jnp.bfloat16), gs[side])
                    dkv_ref[0, keys, :] += nn(grads, qs[side])
                    part = tn(grads, (ka_ref, kb_ref)[side][keys, :])
                    if diagonal and side == 0:
                        dq_ref[:, lanes] = part
                    else:
                        dq_ref[:, lanes] += part

            step(i, True)

            @pl.loop(0, i)
            def _(j):
                step(j, False)

            out_ref[rows, lanes] = (dq_ref[:, lanes] * 0.125).astype(jnp.bfloat16)

    @pl.loop(0, count)
    def _(j):
        rows = pl.ds(pl.multiple_of(j * block, block), block)
        keys = dkv_ref[0, rows, :] * (1.0 / LOG2E)
        values = dkv_ref[1, rows, :]
        keys = keys + jnp.concatenate([keys[:, 64:], keys[:, :64]], axis=1)
        values = values + jnp.concatenate([values[:, 64:], values[:, :64]], axis=1)
        out_ref[rows, pl.ds(heads * 64, 128)] = jnp.where(low, keys, values).astype(jnp.bfloat16)

def attend_back(packed, g, dots, heads, block=512):
    total = packed.shape[0]
    cost = heads * total * total // 2
    return pl.pallas_call(
        functools.partial(back_kernel, block, heads),
        out_shape=jax.ShapeDtypeStruct(packed.shape, jnp.bfloat16),
        in_specs=[pl.BlockSpec(memory_space=pltpu.VMEM)] * 3,
        out_specs=pl.BlockSpec(memory_space=pltpu.VMEM),
        scratch_shapes=[
            pltpu.VMEM((block, heads * 64), jnp.float32),
            pltpu.VMEM((2, total, 128), jnp.float32),
        ]
        + [pltpu.VMEM((total, 128), jnp.bfloat16)] * 4,
        compiler_params=pltpu.CompilerParams(vmem_limit_bytes=56 << 20),
        cost_estimate=pl.CostEstimate(
            flops=10 * cost * 256, bytes_accessed=12 * packed.size, transcendentals=cost
        ),
        name="attend_back",
    )(packed, g, dots)


def remote(source, target, send, arrive, device):
    return pltpu.make_async_remote_copy(
        src_ref=source,
        dst_ref=target,
        send_sem=send,
        recv_sem=arrive,
        device_id=device,
        device_id_type=pl.DeviceIdType.MESH,
    )


def place():
    narrow = lax.axis_index("narrow")
    wide = lax.axis_index("wide")
    return narrow, wide, wide // 2, wide % 2


def greet_neighbours():
    narrow, wide, chip, core = place()
    barrier = pltpu.get_barrier_semaphore()

    def tell(device):
        pl.semaphore_signal(
            barrier, inc=1, device_id=device, device_id_type=pl.DeviceIdType.MESH
        )

    tell((narrow + 1 - 2 * (narrow % 2), wide))
    tell(((narrow + 2) % 4, wide))
    tell((narrow, 2 * chip + 1 - core))

    @pl.when(chip > 0)
    def _():
        tell((narrow, wide - 2))

    @pl.when(chip < 3)
    def _():
        tell((narrow, wide + 2))

    pl.semaphore_wait(barrier, 3 + jnp.minimum(chip, 1) + jnp.minimum(3 - chip, 1))


def gather_kernel(
    att_ref, att_all, own_sem, line_send, line_got, side_send, side_got, core_send, core_got
):
    narrow, wide, chip, core = place()
    beside = narrow + 1 - 2 * (narrow % 2)
    across = (narrow + 2) % 4
    corner = (beside + 2) % 4
    rows = att_ref.shape[0]
    half_rows = rows // 2
    other = (narrow, 2 * chip + 1 - core)
    left = (narrow, wide - 2)
    right = (narrow, wide + 2)
    sides = ((beside, wide), (across, wide))
    near = (beside, across)

    def att(slot, who):
        return att_all.at[slot, pl.ds(pl.multiple_of(who * rows, rows), rows), :]

    def att_half(slot, who, half):
        return att_all.at[
            slot, pl.ds(pl.multiple_of(who * rows + half * half_rows, half_rows), half_rows), :
        ]

    def line(at, step, source):
        return remote(
            source, att(2 * at + core, narrow), line_send.at[at, (step + 1) // 2],
            line_got.at[at], right if step > 0 else left,
        )

    def both_ways(at, source, act):
        @pl.when(jnp.logical_and(at <= chip, chip < 3))
        def _():
            act(line(at, 1, source))

        @pl.when(jnp.logical_and(at >= chip, chip > 0))
        def _():
            act(line(at, -1, source))

    def side(at, k, source):
        return remote(
            source, att(2 * at + core, narrow), side_send.at[at, k], side_got.at[at, k], sides[k]
        )

    def side_arrival(at, k):
        target = att(2 * at + core, near[k])
        return remote(target, target, side_send.at[at, k], side_got.at[at, k], sides[k])

    def forward(at, k):
        piece = att_half(2 * at + core, near[k], k)
        return remote(piece, piece, side_send.at[at, 2 + k], side_got.at[at, 2 + k], sides[1 - k])

    def corner_arrival(at, k):
        piece = att_half(2 * at + core, corner, k)
        return remote(piece, piece, side_send.at[at, 2 + k], side_got.at[at, 2 + k], sides[1 - k])

    def pair(at, who, half_of):
        piece = att(2 * at + half_of, who)
        return remote(piece, piece, core_send.at[at, who], core_got.at[at, who], other)

    start = lambda copy: copy.start()
    greet_neighbours()
    both_ways(chip, att_ref, start)
    for k in range(2):
        side(chip, k, att_ref).start()
    own = pltpu.make_async_copy(att_ref, att(wide, narrow), own_sem)
    own.start()
    own.wait()
    pair(chip, narrow, core).start()

    def hop(distance):
        for at, valid in (
            (chip - distance, chip >= distance), (chip + distance, chip + distance <= 3)
        ):

            @pl.when(valid)
            def _():
                piece = att(2 * at + core, narrow)
                line(at, 1, piece).wait_recv()
                both_ways(at, piece, start)
                for k in range(2):
                    side(at, k, piece).start()
                pair(at, narrow, core).start()

    def around(at):
        for k in range(2):
            side_arrival(at, k).wait_recv()
            forward(at, k).start()
            pair(at, near[k], core).start()

    upper = chip // 2
    second = chip + 1 - 2 * upper
    last = 3 - 3 * upper
    order = (chip, second, 6 - chip - second - last, last)
    for step in range(4):
        if step < 3:
            hop(step + 1)
        around(order[step])
    for at in order:
        for k in range(2):
            corner_arrival(at, k).wait_recv()
        pair(at, corner, core).start()

    for at in range(4):
        both_ways(at, att_ref, lambda copy: copy.wait_send())
        for who in range(4):
            pair(at, who, 1 - core).wait_recv()
            pair(at, who, core).wait_send()
        for k in range(2):
            side(at, k, att_ref).wait_send()
            forward(at, k).wait_send()


def gather_weights(att):
    narrow_count = lax.axis_size("narrow")
    wide_count = lax.axis_size("wide")
    if narrow_count != 4 or wide_count != 8:
        return lax.all_gather(lax.all_gather(att, "wide", axis=0), "narrow", axis=1, tiled=True)
    dma = pltpu.SemaphoreType.DMA
    return pl.pallas_call(
        gather_kernel,
        out_shape=jax.ShapeDtypeStruct((8, 4 * att.shape[0], att.shape[1]), jnp.bfloat16),
        in_specs=[pl.BlockSpec(memory_space=pl.ANY)],
        out_specs=pl.BlockSpec(memory_space=pl.ANY),
        scratch_shapes=[
            dma, dma((4, 2)), dma((4,)), dma((4, 4)), dma((4, 4)), dma((4, 4)), dma((4, 4)),
        ],
        compiler_params=pltpu.CompilerParams(collective_id=1, has_side_effects=True),
        cost_estimate=pl.CostEstimate(flops=0, bytes_accessed=300 << 20, transcendentals=0),
        name="gather_weights",
    )(att)


def gather_rows(shard):
    return lax.all_gather(shard, "wide", axis=0, tiled=True)


def swap(blocks):
    return lax.all_to_all(blocks, "wide", 0, 0)


def sum_back(pairs):
    summed = 0.0
    for gradient, weight in pairs:
        summed = summed + dot_back(gradient, weight)
    return lax.psum_scatter(
        summed.astype(jnp.bfloat16), "wide", scatter_dimension=0, tiled=True
    ).astype(jnp.float32)


def scatter_kernel(
    in_ref, out_ref, gain_ref, query_sum, output_sum, key_sum, value_sum, gain_sum_ref,
    own, other, halves, wholes, from_left, from_right, spread_ref, low, wide_gains, mid_gain,
    narrow_gains,
    load_sem, core_send, core_got, half_send, half_got, whole_send, whole_got,
    line_send, left_got, right_got, spread_send, spread_got, pass_send, pass_got,
    wide_send, wide_got, narrow_send, narrow_got,
):
    narrow, wide, chip, core = place()
    beside = narrow + 1 - 2 * (narrow % 2)
    across = (narrow + 2) % 4
    corner = (beside + 2) % 4
    rows = query_sum.shape[0]
    half_rows = rows // 2
    split = in_ref.shape[2]
    twin = (narrow, 2 * chip + 1 - core)
    sides = ((beside, wide), (across, wide))
    near = (beside, across)
    wides = [(narrow, (wide + step) % 8) for step in range(1, 8)]
    narrows = [((narrow + step) % 4, wide) for step in range(1, 4)]
    upper = chip // 2
    last = 3 - 3 * upper
    second = chip + 1 - 2 * upper
    order = (last, 6 - chip - second - last, second, chip)
    f32 = jnp.float32

    barrier = pltpu.get_barrier_semaphore()
    for device in wides + narrows:
        pl.semaphore_signal(
            barrier, inc=1, device_id=device, device_id_type=pl.DeviceIdType.MESH
        )
    pl.semaphore_wait(barrier, 10)

    parts = ((in_ref, pl.ds(0, split)), (out_ref, pl.ds(split, out_ref.shape[2])))

    def load(at, k):
        source, lanes = parts[k]
        return pltpu.make_async_copy(
            source.at[2 * at + core], own.at[at, :, lanes], load_sem.at[at, k]
        )

    def exchange(at, k):
        source, lanes = parts[k]
        return remote(
            source.at[2 * at + 1 - core], other.at[at, :, lanes], core_send.at[at, k],
            core_got.at[at, k], twin,
        )

    def block(at, who):
        return own.at[at, pl.ds(pl.multiple_of(who * rows, rows), rows), :]

    def half_block(at, who, half):
        return own.at[
            at, pl.ds(pl.multiple_of(who * rows + half * half_rows, half_rows), half_rows), :
        ]

    def half(at, k):
        return remote(
            half_block(at, corner, k), halves.at[at, k], half_send.at[at, k], half_got.at[at, k],
            sides[k],
        )

    def whole(at, k):
        return remote(
            block(at, near[k]), wholes.at[at, k], whole_send.at[at, k], whole_got.at[at, k],
            sides[k],
        )

    def to_right(at):
        return remote(
            block(at, narrow), from_left.at[at], line_send.at[at], left_got.at[at],
            (narrow, wide + 2),
        )

    def to_left(at):
        return remote(
            block(at, narrow), from_right.at[at], line_send.at[at], right_got.at[at],
            (narrow, wide - 2),
        )

    def add(target, source, count, step=64):
        @pl.loop(0, count // step)
        def _(i):
            piece = pl.ds(pl.multiple_of(i * step, step), step)
            target[piece, :] = (
                target[piece, :].astype(f32) + source[piece, :].astype(f32)
            ).astype(jnp.bfloat16)

    for at in order:
        for k in range(2):
            load(at, k).start()
            exchange(at, k).start()
    gains = [
        remote(gain_ref, wide_gains.at[step], wide_send.at[step], wide_got.at[step], device)
        for step, device in enumerate(wides)
    ]
    for copy in gains:
        copy.start()

    def pair_up(at):
        for k in range(2):
            load(at, k).wait()
            exchange(at, k).wait_recv()
        add(own.at[at], other.at[at], 4 * rows)
        for k in range(2):
            half(at, k).start()

    def turn(at):
        for k in range(2):
            half(at, k).wait_recv()
            add(half_block(at, near[1 - k], k), halves.at[at, k], half_rows)
        for k in range(2):
            whole(at, k).start()

    def settle(at):
        for k in range(2):
            whole(at, k).wait_recv()
        target = block(at, narrow)

        @pl.loop(0, rows // 64)
        def _(i):
            piece = pl.ds(pl.multiple_of(i * 64, 64), 64)
            target[piece, :] = (
                target[piece, :].astype(f32)
                + wholes[at, 0, piece, :].astype(f32)
                + wholes[at, 1, piece, :].astype(f32)
            ).astype(jnp.bfloat16)

        @pl.when(at > chip)
        def _():
            @pl.when(chip > 0)
            def _():
                to_right(at).wait_recv()
                add(target, from_left.at[at], rows)

            to_right(at).start()

        @pl.when(at < chip)
        def _():
            @pl.when(chip < 3)
            def _():
                to_left(at).wait_recv()
                add(target, from_right.at[at], rows)

            to_left(at).start()

    pair_up(order[0])
    pair_up(order[1])
    turn(order[0])
    pair_up(order[2])
    turn(order[1])
    settle(order[0])
    pair_up(order[3])
    turn(order[2])
    settle(order[1])
    for copy in gains:
        copy.wait()
    total = gain_ref[...]
    for step in range(7):
        total = total + wide_gains[step]
    mid_gain[...] = total
    gains = [
        remote(mid_gain, narrow_gains.at[step], narrow_send.at[step], narrow_got.at[step], device)
        for step, device in enumerate(narrows)
    ]
    for copy in gains:
        copy.start()
    turn(order[3])
    settle(order[2])
    settle(order[3])
    target = block(chip, narrow)

    @pl.when(chip > 0)
    def _():
        to_right(chip).wait_recv()
        add(target, from_left.at[chip], rows)

    @pl.when(chip < 3)
    def _():
        to_left(chip).wait_recv()
        add(target, from_right.at[chip], rows)

    lanes = pl.ds(split - 128, 128)
    for i in range(rows // 128):
        piece = pl.ds(pl.multiple_of(narrow * rows + i * 128, 128), 128)
        here = pl.ds(i * 128, 128)
        query_sum[here, :] = own[chip, piece, pl.ds(0, split - 128)].astype(f32)
        output_sum[:, here] = own[chip, piece, pl.ds(split, out_ref.shape[2])].astype(f32).T
        low[here, :] = own[chip, piece, lanes]

    spread_ref[wide] = low[...]

    def spread(step):
        return remote(
            low, spread_ref.at[wide], spread_send.at[step - 1], spread_got.at[step - 1],
            (narrow, (wide + 2 * step) % 8),
        )

    def arrival(step):
        target = spread_ref.at[(wide + 8 - 2 * step) % 8]
        return remote(target, target, spread_send.at[step - 1], spread_got.at[step - 1], twin)

    def pass_on(step):
        piece = spread_ref.at[(wide + 8 - 2 * step) % 8]
        return remote(piece, piece, pass_send.at[step], pass_got.at[step], twin)

    def passed(step):
        piece = spread_ref.at[(2 * chip + 1 - core + 8 - 2 * step) % 8]
        return remote(piece, piece, pass_send.at[step], pass_got.at[step], twin)

    for step in (1, 2, 3):
        spread(step).start()
    pass_on(0).start()
    for copy in gains:
        copy.wait()
    for step in range(3):
        total = total + narrow_gains[step]
    gain_sum_ref[...] = total
    for step in (1, 2, 3):
        arrival(step).wait_recv()
        pass_on(step).start()
    for step in range(4):
        passed(step).wait_recv()
        pass_on(step).wait_send()
    for step in (1, 2, 3):
        spread(step).wait_send()
    first = low_lanes(rows)
    for at in range(4):
        even = spread_ref[2 * at].astype(f32)
        odd = spread_ref[2 * at + 1].astype(f32)
        here = pl.ds(at * 128, 128)
        key_sum[:, here] = jnp.where(first, even, pltpu.roll(odd, 64, 1))
        value_sum[:, here] = jnp.where(first, pltpu.roll(even, 64, 1), odd)
    for at in range(4):
        for k in range(2):
            exchange(at, k).wait_send()
            half(at, k).wait_send()
            whole(at, k).wait_send()

        @pl.when(at != chip)
        def _():
            to_right(at).wait_send()


def sum_weights(input_wgrad, output_wgrad, gains, key_heads):
    narrow_count = lax.axis_size("narrow")
    wide_count = lax.axis_size("wide")
    split = input_wgrad.shape[2]
    if narrow_count != 4 or wide_count != 8 or key_heads != 8:
        total = jnp.concatenate([input_wgrad, output_wgrad], axis=2)
        total = lax.psum_scatter(total, "narrow", scatter_dimension=1, tiled=True)
        total = lax.psum_scatter(total, "wide", scatter_dimension=0)
        spread = lax.all_gather(total[:, split - 128 : split], "wide", axis=0)
        spread = spread.reshape(key_heads, wide_count // key_heads, -1, 2, 64)
        spread = jnp.sum(spread.astype(jnp.float32), axis=1).transpose(2, 1, 0, 3)
        spread = spread.reshape(2, -1, key_heads * 64)
        gains = jnp.sum(lax.all_gather(gains, ("narrow", "wide"), axis=0), axis=0)
        total = total.astype(jnp.float32)
        return total[:, : split - 128], total[:, split:].T, spread[0], spread[1], gains
    low = jnp.bfloat16
    rows = input_wgrad.shape[1] // 4
    columns = split + output_wgrad.shape[2]
    size = gains.size
    gain_rows = -(-size // 1024) * 8
    flat = jnp.pad(gains.reshape(-1), (0, gain_rows * 128 - size)).reshape(gain_rows, 128)
    dma = pltpu.SemaphoreType.DMA
    vmem = pltpu.VMEM
    *sums, flat = pl.pallas_call(
        scatter_kernel,
        out_shape=[
            jax.ShapeDtypeStruct((rows, split - 128), jnp.float32),
            jax.ShapeDtypeStruct((columns - split, rows), jnp.float32),
            jax.ShapeDtypeStruct((rows, 512), jnp.float32),
            jax.ShapeDtypeStruct((rows, 512), jnp.float32),
            jax.ShapeDtypeStruct(flat.shape, jnp.float32),
        ],
        in_specs=[
            pl.BlockSpec(memory_space=pl.ANY),
            pl.BlockSpec(memory_space=pl.ANY),
            pl.BlockSpec(memory_space=vmem),
        ],
        out_specs=[pl.BlockSpec(memory_space=vmem)] * 5,
        scratch_shapes=[
            vmem((4, 4 * rows, columns), low),
            vmem((4, 4 * rows, columns), low),
            vmem((4, 2, rows // 2, columns), low),
            vmem((4, 2, rows, columns), low),
            vmem((4, rows, columns), low),
            vmem((4, rows, columns), low),
            vmem((8, rows, 128), low),
            vmem((rows, 128), low),
            vmem((7, gain_rows, 128), jnp.float32),
            vmem((gain_rows, 128), jnp.float32),
            vmem((3, gain_rows, 128), jnp.float32),
            dma((4, 2)), dma((4, 2)), dma((4, 2)), dma((4, 2)), dma((4, 2)), dma((4, 2)),
            dma((4, 2)), dma((4,)), dma((4,)), dma((4,)), dma((3,)), dma((3,)), dma((4,)),
            dma((4,)), dma((7,)), dma((7,)), dma((3,)), dma((3,)),
        ],
        compiler_params=pltpu.CompilerParams(
            collective_id=3, has_side_effects=True, vmem_limit_bytes=52 << 20
        ),
        cost_estimate=pl.CostEstimate(flops=0, bytes_accessed=1 << 20, transcendentals=0),
        name="sum_weights",
    )(input_wgrad, output_wgrad, flat)
    return *sums, flat.reshape(-1)[:size].reshape(gains.shape)


def tell_all():
    narrow = lax.axis_index("narrow")
    wide = lax.axis_index("wide")
    barrier = pltpu.get_barrier_semaphore()
    for step in range(1, 8):
        pl.semaphore_signal(
            barrier, inc=1, device_id=(narrow, (wide + step) % 8),
            device_id_type=pl.DeviceIdType.MESH,
        )
    for step in range(1, 4):
        pl.semaphore_signal(
            barrier, inc=1, device_id=((narrow + step) % 4, wide),
            device_id_type=pl.DeviceIdType.MESH,
        )
    pl.semaphore_wait(barrier, 10)


def attend_swap_kernel(
    heads, src_ref, up_ref, down_ref, packed_ref, o_ref, s_ref, out_ref, up_all, down_all,
    kk_ref, va_ref, vb_ref, acc_ref, low_ref,
    own_sem, send_sem, got_sem, out_send, out_got, ffn_own, ffn_send, ffn_got,
):
    narrow, wide, chip, core = place()
    block = src_ref.shape[1]
    base = 4 * (chip // 2)
    away = 4 - base
    low = low_lanes(block)
    columns = down_ref.shape[1]
    tell_all()

    def ffn_slot(k, who):
        if k:
            return down_all.at[:, pl.ds(pl.multiple_of(who * columns, columns), columns)]
        return up_all.at[who]

    def ffn(k, step):
        return remote(
            (up_ref, down_ref)[k], ffn_slot(k, narrow), ffn_send.at[k, step],
            ffn_got.at[k, step], ((narrow + step) % 4, wide),
        )

    def ffn_arrival(k, step):
        target = ffn_slot(k, (narrow + 4 - step) % 4)
        return remote(
            target, target, ffn_send.at[k, step], ffn_got.at[k, step], ((narrow + step) % 4, wide)
        )

    def send(to):
        return remote(
            src_ref.at[to], packed_ref.at[wide], send_sem.at[to], got_sem.at[wide], (narrow, to)
        )

    def arrival(at):
        target = packed_ref.at[at]
        return remote(target, target, send_sem.at[at], got_sem.at[at], (narrow, at))

    def send_out(to):
        return remote(
            low_ref.at[to], out_ref.at[wide], out_send.at[to], out_got.at[wide], (narrow, to)
        )

    own = pltpu.make_async_copy(src_ref.at[wide], packed_ref.at[wide], own_sem)
    own.start()
    for step in range(1, 8):
        send((wide + step) % 8).start()
    keep = [
        pltpu.make_async_copy((up_ref, down_ref)[k], ffn_slot(k, narrow), ffn_own.at[k])
        for k in range(2)
    ]
    for k in (1, 0):
        keep[k].start()
        for step in range(1, 4):
            ffn(k, step).start()

    def prepare(j):
        rows = pl.ds(pl.multiple_of(j * block, block), block)
        kv = packed_ref[j, :, pl.ds(heads * 64, 128)]
        vk = jnp.concatenate([kv[:, 64:], kv[:, :64]], axis=1)
        one = jnp.ones_like(kv)
        kk_ref[rows, :] = jnp.where(low, kv, vk)
        va_ref[rows, :] = jnp.where(low, vk, one)
        vb_ref[rows, :] = jnp.where(low, one, kv)

    def await_blocks(start):
        @pl.loop(start, start + 4)
        def _(j):
            @pl.when(j != wide)
            def _():
                arrival(j).wait_recv()

            prepare(j)

    causal = lax.broadcasted_iota(jnp.int32, (block, block), 0) >= lax.broadcasted_iota(
        jnp.int32, (block, block), 1
    )

    def pairs(i, first, stop, diagonal):
        for pair in range(heads // 2):
            both = packed_ref[i, :, pl.ds(pair * 128, 128)]
            zero = jnp.zeros_like(both)
            sides = (jnp.where(low, both, zero), jnp.where(low, zero, both))

            def step(j, masked, fresh):
                keys = pl.ds(pl.multiple_of(j * block, block), block)
                kk = kk_ref[keys, :]
                for side in range(2):
                    weights = jnp.exp2(nt(sides[side], kk))
                    if masked:
                        weights = jnp.where(causal, weights, 0.0)
                    part = nn(weights.astype(jnp.bfloat16), (va_ref, vb_ref)[side][keys, :])
                    if fresh:
                        acc_ref[i, pair * 2 + side] = part
                    else:
                        acc_ref[i, pair * 2 + side] += part

            if diagonal:
                step(i, True, True)

            @pl.loop(first, stop)
            def _(j):
                step(j, False, False)

    def finish(i):
        rows = pl.ds(pl.multiple_of(i * block, block), block)
        for pair in range(heads // 2):
            lanes = pl.ds(pair * 128, 128)
            first, second = acc_ref[i, pair * 2], acc_ref[i, pair * 2 + 1]
            summed = jnp.where(low, first, second)
            sums = jnp.where(low, second, first)
            sums = jnp.concatenate([sums[:, 64:], sums[:, :64]], axis=1)
            result = summed / sums
            o_ref[rows, lanes] = result
            s_ref[rows, lanes] = sums
            low_ref[i, :, lanes] = result.astype(jnp.bfloat16)

        @pl.when(i != wide)
        def _():
            send_out(i).start()

        @pl.when(i == wide)
        def _():
            out_ref[i] = low_ref[i]

    own.wait()
    await_blocks(base)

    @pl.loop(base, base + 4)
    def _(i):
        pairs(i, base, i, True)

        @pl.when(base == 0)
        def _():
            finish(i)

    await_blocks(away)

    @pl.loop(away, away + 4)
    def _(i):
        pairs(i, 0, i, True)
        finish(i)

    @pl.when(base > 0)
    def _():
        @pl.loop(4, 8)
        def _(i):
            pairs(i, 0, 4, False)
            finish(i)

    for step in range(1, 8):
        to = (wide + step) % 8
        target = out_ref.at[to]
        remote(target, target, out_send.at[to], out_got.at[to], (narrow, to)).wait_recv()
        send_out(to).wait_send()
        send(to).wait_send()
    for k in range(2):
        keep[k].wait()
        for step in range(1, 4):
            ffn_arrival(k, step).wait_recv()
            ffn(k, step).wait_send()


def attend_swap(src, up, down, heads):
    if lax.axis_size("narrow") != 4 or lax.axis_size("wide") != 8:
        packed = swap(src)
        flat = packed.reshape(-1, src.shape[2])
        attended, weight_sums, attended_low = attend(flat, heads)
        attended_low = swap(attended_low.reshape(src.shape[0], -1, heads * 64))
        up_all = lax.all_gather(up, "narrow", axis=0, tiled=True)
        down_all = lax.all_gather(down, "narrow", axis=1, tiled=True)
        return packed, attended, weight_sums, attended_low, up_all, down_all
    count, block, lanes = src.shape
    total = count * block
    dma = pltpu.SemaphoreType.DMA
    vmem = pltpu.VMEM
    cost = heads * total * total // 2
    *results, up_all, down_all = pl.pallas_call(
        functools.partial(attend_swap_kernel, heads),
        out_shape=[
            jax.ShapeDtypeStruct(src.shape, jnp.bfloat16),
            jax.ShapeDtypeStruct((total, heads * 64), jnp.float32),
            jax.ShapeDtypeStruct((total, heads * 64), jnp.float32),
            jax.ShapeDtypeStruct((count, block, heads * 64), jnp.bfloat16),
            jax.ShapeDtypeStruct((4,) + up.shape, jnp.bfloat16),
            jax.ShapeDtypeStruct((down.shape[0], 4 * down.shape[1]), jnp.bfloat16),
        ],
        in_specs=[pl.BlockSpec(memory_space=pl.ANY)] * 3,
        out_specs=[pl.BlockSpec(memory_space=vmem)] * 4 + [pl.BlockSpec(memory_space=pl.ANY)] * 2,
        scratch_shapes=[vmem((total, 128), jnp.bfloat16)] * 3
        + [
            vmem((count, heads, block, 128), jnp.float32),
            vmem((count, block, heads * 64), jnp.bfloat16),
            dma, dma((8,)), dma((8,)), dma((8,)), dma((8,)), dma((2,)), dma((2, 4)), dma((2, 4)),
        ],
        compiler_params=pltpu.CompilerParams(
            collective_id=4, has_side_effects=True, vmem_limit_bytes=52 << 20
        ),
        cost_estimate=pl.CostEstimate(
            flops=8 * cost * 256, bytes_accessed=12 * src.size, transcendentals=cost
        ),
        name="attend_swap",
    )(src, up, down)
    return *results, up_all.reshape(-1, up.shape[1]), down_all


def back_swap_kernel(
    heads, packed_ref, g_ref, o_ref, s_ref, gate_ref, up_ref, down_ref,
    dq_out, dkv_out, gate_out, up_out, down_out,
    grad_ref, scaled_ref, dots_ref, dq_ref, dkv_ref, kk_ref, vv_ref, ka_ref, kb_ref,
    low_q, low_kv, own_sem, send_sem, got_sem, q_send, q_got, kv_send, kv_got,
    ffn_own, ffn_send, ffn_got,
):
    narrow, wide, chip, core = place()
    count, block, _ = packed_ref.shape
    base = 4 * (chip // 2)
    away = 4 - base
    low = low_lanes(block)
    rows_out = gate_out.shape[1]
    columns = down_out.shape[2]
    tell_all()

    def share(k, who):
        if k == 2:
            return down_ref.at[:, pl.ds(pl.multiple_of(who * columns, columns), columns)]
        return (gate_ref, up_ref)[k].at[pl.ds(pl.multiple_of(who * rows_out, rows_out), rows_out), :]

    def ffn(k, step):
        to = (narrow + step) % 4
        return remote(
            share(k, to), (gate_out, up_out, down_out)[k].at[step], ffn_send.at[k, step],
            ffn_got.at[k, step], (to, wide),
        )

    def send(to):
        return remote(
            g_ref.at[to], grad_ref.at[wide], send_sem.at[to], got_sem.at[wide], (narrow, to)
        )

    def send_q(to):
        return remote(low_q.at[to], dq_out.at[wide], q_send.at[to], q_got.at[wide], (narrow, to))

    def send_kv(to):
        return remote(
            low_kv.at[to], dkv_out.at[wide], kv_send.at[to], kv_got.at[wide], (narrow, to)
        )

    own = pltpu.make_async_copy(g_ref.at[wide], grad_ref.at[wide], own_sem)
    own.start()
    for step in range(1, 8):
        send((wide + step) % 8).start()
    keep = [
        pltpu.make_async_copy(
            share(k, narrow), (gate_out, up_out, down_out)[k].at[0], ffn_own.at[k]
        )
        for k in range(3)
    ]
    for k in range(3):
        keep[k].start()
        for step in range(1, 4):
            ffn(k, step).start()

    @pl.loop(0, count)
    def _(j):
        rows = pl.ds(pl.multiple_of(j * block, block), block)
        kv = packed_ref[j, :, pl.ds(heads * 64, 128)]
        vk = jnp.concatenate([kv[:, 64:], kv[:, :64]], axis=1)
        zero = jnp.zeros_like(kv)
        kk_ref[rows, :] = jnp.where(low, kv, vk)
        vv_ref[rows, :] = jnp.where(low, vk, kv)
        ka_ref[rows, :] = jnp.where(low, kv, zero)
        kb_ref[rows, :] = jnp.where(low, zero, vk)
        dkv_ref[0, rows, :] = jnp.zeros((block, 128), jnp.float32)
        dkv_ref[1, rows, :] = jnp.zeros((block, 128), jnp.float32)

    causal = lax.broadcasted_iota(jnp.int32, (block, block), 0) <= lax.broadcasted_iota(
        jnp.int32, (block, block), 1
    )
    first_lanes = lax.broadcasted_iota(jnp.int32, (8, 128), 1) < 64
    picks = (
        jnp.where(first_lanes, 1.0, 0.0).astype(jnp.bfloat16),
        jnp.where(first_lanes, 0.0, 1.0).astype(jnp.bfloat16),
    )

    def rows_back(i):
        rows = pl.ds(pl.multiple_of(i * block, block), block)
        for pair in range(heads // 2):
            lanes = pl.ds(pair * 128, 128)
            grad = grad_ref[i, :, lanes].astype(jnp.float32) / s_ref[rows, lanes]
            scaled_ref[...] = grad.astype(jnp.bfloat16)
            product = grad * o_ref[rows, lanes]
            high = product.astype(jnp.bfloat16)
            rest = (product - high.astype(jnp.float32)).astype(jnp.bfloat16)
            for side in range(2):
                dots_ref[side] = nt(picks[side], high) + nt(picks[side], rest)
            qboth = packed_ref[i, :, lanes]
            gboth = scaled_ref[...]
            zero = jnp.zeros_like(qboth)
            qs = (jnp.where(low, qboth, zero), jnp.where(low, zero, qboth))
            gs = (jnp.where(low, gboth, zero), jnp.where(low, zero, gboth))

            def step(j, diagonal):
                keys = pl.ds(pl.multiple_of(j * block, block), block)
                kk = kk_ref[keys, :]
                vv = vv_ref[keys, :]
                for side in range(2):
                    weights = jnp.exp2(nt(kk, qs[side]))
                    if diagonal:
                        weights = jnp.where(causal, weights, 0.0)
                    dots = dots_ref[side, pl.ds(0, 1), :]
                    grads = (weights * (nt(vv, gs[side]) - dots)).astype(jnp.bfloat16)
                    dkv_ref[1, keys, :] += nn(weights.astype(jnp.bfloat16), gs[side])
                    dkv_ref[0, keys, :] += nn(grads, qs[side])
                    part = tn(grads, (ka_ref, kb_ref)[side][keys, :])
                    if diagonal and side == 0:
                        dq_ref[...] = part
                    else:
                        dq_ref[...] += part

            step(i, True)

            @pl.loop(0, i)
            def _(j):
                step(j, False)

            low_q[i, :, lanes] = (dq_ref[...] * 0.125).astype(jnp.bfloat16)

        @pl.when(i != wide)
        def _():
            send_q(i).start()

        @pl.when(i == wide)
        def _():
            dq_out[i] = low_q[i]

    def keys_back(j):
        rows = pl.ds(pl.multiple_of(j * block, block), block)
        keys = dkv_ref[0, rows, :] * (1.0 / LOG2E)
        values = dkv_ref[1, rows, :]
        keys = keys + jnp.concatenate([keys[:, 64:], keys[:, :64]], axis=1)
        values = values + jnp.concatenate([values[:, 64:], values[:, :64]], axis=1)
        low_kv[j] = jnp.where(low, keys, values).astype(jnp.bfloat16)

        @pl.when(j != wide)
        def _():
            send_kv(j).start()

        @pl.when(j == wide)
        def _():
            dkv_out[j] = low_kv[j]

    own.wait()

    @pl.loop(0, 4)
    def _(k):
        i = base + 3 - k

        @pl.when(i != wide)
        def _():
            target = grad_ref.at[i]
            remote(target, target, send_sem.at[i], got_sem.at[i], (narrow, i)).wait_recv()

        rows_back(i)

        @pl.when(base > 0)
        def _():
            keys_back(i)

    @pl.loop(0, 4)
    def _(k):
        i = away + 3 - k
        target = grad_ref.at[i]
        remote(target, target, send_sem.at[i], got_sem.at[i], (narrow, i)).wait_recv()
        rows_back(i)
        keys_back(i)

    @pl.when(base == 0)
    def _():
        @pl.loop(0, 4)
        def _(k):
            keys_back(3 - k)

    for step in range(1, 8):
        to = (wide + step) % 8
        target = dq_out.at[to]
        remote(target, target, q_send.at[to], q_got.at[to], (narrow, to)).wait_recv()
        target = dkv_out.at[to]
        remote(target, target, kv_send.at[to], kv_got.at[to], (narrow, to)).wait_recv()
        send(to).wait_send()
        send_q(to).wait_send()
        send_kv(to).wait_send()
    for k in range(3):
        keep[k].wait()
        for step in range(1, 4):
            ffn(k, step).wait()


def back_swap(packed, grad, attended, weight_sums, gate, up, down, heads):
    count, block, lanes = packed.shape
    split = heads * 64
    if lax.axis_size("narrow") != 4 or lax.axis_size("wide") != 8:
        head_grad = swap(grad).reshape(-1, split).astype(jnp.float32) / weight_sums
        dots = jnp.sum((head_grad * attended).reshape(-1, heads, 64), axis=-1).T
        result = attend_back(
            packed.reshape(-1, lanes), head_grad.astype(jnp.bfloat16), dots, heads
        )
        result = swap(result.reshape(packed.shape))
        return (
            result[:, :, :split],
            result[:, :, split:],
            lax.psum_scatter(gate, "narrow", scatter_dimension=0, tiled=True)[None],
            lax.psum_scatter(up, "narrow", scatter_dimension=0, tiled=True)[None],
            lax.psum_scatter(down, "narrow", scatter_dimension=1, tiled=True)[None],
        )
    total = count * block
    dma = pltpu.SemaphoreType.DMA
    vmem = pltpu.VMEM
    low = jnp.bfloat16
    cost = heads * total * total // 2
    return pl.pallas_call(
        functools.partial(back_swap_kernel, heads),
        out_shape=[
            jax.ShapeDtypeStruct((count, block, split), low),
            jax.ShapeDtypeStruct((count, block, 128), low),
            jax.ShapeDtypeStruct((4, gate.shape[0] // 4, gate.shape[1]), low),
            jax.ShapeDtypeStruct((4, up.shape[0] // 4, up.shape[1]), low),
            jax.ShapeDtypeStruct((4, down.shape[0], down.shape[1] // 4), low),
        ],
        in_specs=[
            pl.BlockSpec(memory_space=vmem),
            pl.BlockSpec(memory_space=pl.ANY),
            pl.BlockSpec(memory_space=vmem),
            pl.BlockSpec(memory_space=vmem),
        ]
        + [pl.BlockSpec(memory_space=pl.ANY)] * 3,
        out_specs=[pl.BlockSpec(memory_space=vmem)] * 2 + [pl.BlockSpec(memory_space=pl.ANY)] * 3,
        scratch_shapes=[
            vmem((count, block, split), low),
            vmem((block, 128), low),
            vmem((2, 8, block), jnp.float32),
            vmem((block, 128), jnp.float32),
            vmem((2, total, 128), jnp.float32),
        ]
        + [vmem((total, 128), low)] * 4
        + [
            vmem((count, block, split), low),
            vmem((count, block, 128), low),
            dma, dma((8,)), dma((8,)), dma((8,)), dma((8,)), dma((8,)), dma((8,)),
            dma((3,)), dma((3, 4)), dma((3, 4)),
        ],
        compiler_params=pltpu.CompilerParams(
            collective_id=5, has_side_effects=True, vmem_limit_bytes=52 << 20
        ),
        cost_estimate=pl.CostEstimate(
            flops=12 * cost * 256, bytes_accessed=12 * packed.size, transcendentals=cost
        ),
        name="back_swap",
    )(packed, grad, attended, weight_sums, gate, up, down)


def swap_halves(values):
    lane = lax.broadcasted_iota(jnp.int32, values.shape, 1)
    return jnp.where(lane % 64 < 32, pltpu.roll(values, 96, 1), pltpu.roll(values, 32, 1))


def head_mean(values):
    row = lax.broadcasted_iota(jnp.int32, (128, 128), 0) < 64
    lane = lax.broadcasted_iota(jnp.int32, (128, 128), 1) < 64
    same = jnp.logical_or(
        jnp.logical_and(row, lane),
        jnp.logical_and(jnp.logical_not(row), jnp.logical_not(lane)),
    )
    spread = jnp.where(same, 1.0 / 64.0, 0.0).astype(jnp.bfloat16)
    high = values.astype(jnp.bfloat16)
    rest = (values - high.astype(jnp.float32)).astype(jnp.bfloat16)
    return nn(high, spread) + nn(rest, spread)


def project_kernel(pairs, rows_ref, weight_ref, cos_ref, sin_ref, gain_ref, src_ref, raw_ref):
    low = low_lanes(rows_ref.shape[0])
    raw_ref[0] = nn(rows_ref[...], weight_ref[0])
    for pair in range(pairs + 1):
        lanes = pl.ds(pair * 128, 128)
        raw = raw_ref[0, :, lanes]
        which = 0 if pair < pairs else 1
        scaled = raw * lax.rsqrt(head_mean(raw * raw) + EPSILON) * gain_ref[which : which + 1, :]
        turned = scaled * cos_ref[...] + swap_halves(scaled) * sin_ref[...]
        if pair < pairs:
            result = turned * (0.125 * LOG2E)
        else:
            result = jnp.where(low, turned, raw)
        src_ref[0, :, lanes] = result.astype(jnp.bfloat16)


def project(rows, weights, cosine, sine_part, gains, heads):
    count, width, _ = weights.shape
    length = rows.shape[0]
    lanes = heads * 64 + 128
    whole = lambda g: (0, 0)
    group = lambda g: (g, 0, 0)
    return pl.pallas_call(
        functools.partial(project_kernel, heads // 2),
        grid=(count,),
        out_shape=[
            jax.ShapeDtypeStruct((count, length, lanes), jnp.bfloat16),
            jax.ShapeDtypeStruct((count, length, lanes), jnp.float32),
        ],
        in_specs=[
            pl.BlockSpec((length, width), whole),
            pl.BlockSpec((1, width, lanes), group),
            pl.BlockSpec((length, 128), whole),
            pl.BlockSpec((length, 128), whole),
            pl.BlockSpec((2, 128), whole),
        ],
        out_specs=[pl.BlockSpec((1, length, lanes), group)] * 2,
        compiler_params=pltpu.CompilerParams(vmem_limit_bytes=48 << 20),
        cost_estimate=pl.CostEstimate(
            flops=2 * count * length * width * lanes,
            bytes_accessed=2 * count * width * lanes + 8 * count * length * lanes,
            transcendentals=0,
        ),
        name="project",
    )(rows, weights, cosine, sine_part, gains)


def project_back_kernel(
    pairs, dq_ref, dkv_ref, raw_ref, cos_ref, sin_ref, gain_ref, rows_ref, weight_ref,
    branch_ref, att_ref, in_ref, out_ref, back_ref, gain_out, low_ref, rows_turned, branch_turned,
):
    length, width = rows_ref.shape
    low = low_lanes(length)
    step = 512

    @pl.when(pl.program_id(0) == 0)
    def _():
        back_ref[...] = jnp.zeros_like(back_ref)
        gain_out[...] = jnp.zeros_like(gain_out)

        @pl.loop(0, width // step)
        def _(i):
            piece = pl.ds(pl.multiple_of(i * step, step), step)
            rows_turned[piece, :] = rows_ref[:, piece].T
            branch_turned[piece, :] = branch_ref[:, piece].T

    for pair in range(pairs + 1):
        lanes = pl.ds(pair * 128, 128)
        last = pair == pairs
        which = 1 if last else 0
        turned = (dkv_ref[0] if last else dq_ref[0, :, lanes]).astype(jnp.float32)
        raw = raw_ref[0, :, lanes]
        inverse = lax.rsqrt(head_mean(raw * raw) + EPSILON)
        unit = raw * inverse
        scaled = turned * cos_ref[...] + swap_halves(turned * sin_ref[...])
        part = jnp.sum(scaled * unit, axis=0, keepdims=True)
        scaled = scaled * gain_ref[which : which + 1, :]
        result = inverse * (scaled - unit * inverse * head_mean(scaled * raw))
        if last:
            result = jnp.where(low, result, turned)
        gain_out[which : which + 1, :] += part
        low_ref[:, lanes] = result.astype(jnp.bfloat16)

    @pl.loop(0, width // step)
    def _(i):
        piece = pl.ds(pl.multiple_of(i * step, step), step)
        in_ref[0, piece, :] = nn(rows_turned[piece, :], low_ref[...]).astype(jnp.bfloat16)
        out_ref[0, piece, :] = nn(branch_turned[piece, :], att_ref[0]).astype(jnp.bfloat16)
        back_ref[:, piece] += nt(low_ref[...], weight_ref[0, piece, :])


def project_back(dq, dkv, raw, cosine, sine_part, gains, rows, weights, branch, attended, heads):
    count, length, lanes = raw.shape
    width = rows.shape[1]
    split = heads * 64
    low = jnp.bfloat16
    whole = lambda g: (0, 0)
    group = lambda g: (g, 0, 0)
    return pl.pallas_call(
        functools.partial(project_back_kernel, heads // 2),
        grid=(count,),
        out_shape=[
            jax.ShapeDtypeStruct((count, width, lanes), low),
            jax.ShapeDtypeStruct((count, width, split), low),
            jax.ShapeDtypeStruct((length, width), jnp.float32),
            jax.ShapeDtypeStruct((8, 128), jnp.float32),
        ],
        in_specs=[
            pl.BlockSpec((1, length, split), group),
            pl.BlockSpec((1, length, 128), group),
            pl.BlockSpec((1, length, lanes), group),
            pl.BlockSpec((length, 128), whole),
            pl.BlockSpec((length, 128), whole),
            pl.BlockSpec((2, 128), whole),
            pl.BlockSpec((length, width), whole),
            pl.BlockSpec((1, width, lanes), group),
            pl.BlockSpec((length, width), whole),
            pl.BlockSpec((1, length, split), group),
        ],
        out_specs=[
            pl.BlockSpec((1, width, lanes), group),
            pl.BlockSpec((1, width, split), group),
            pl.BlockSpec((length, width), whole),
            pl.BlockSpec((8, 128), whole),
        ],
        scratch_shapes=[
            pltpu.VMEM((length, lanes), low),
            pltpu.VMEM((width, length), low),
            pltpu.VMEM((width, length), low),
        ],
        compiler_params=pltpu.CompilerParams(vmem_limit_bytes=48 << 20),
        cost_estimate=pl.CostEstimate(
            flops=2 * count * length * width * (2 * lanes + split),
            bytes_accessed=count * width * (4 * lanes + 2 * split) + 8 * count * length * lanes,
            transcendentals=0,
        ),
        name="project_back",
    )(dq, dkv, raw, cosine, sine_part, gains, rows, weights, branch, attended)


def shards(
    tokens_in,
    out_grad,
    positions,
    query_weight,
    query_first,
    query_second,
    key_weight,
    key_first,
    key_second,
    value_weight,
    value_first,
    value_second,
    output_weight,
    output_first,
    output_second,
    gate_weight,
    gate_first,
    gate_second,
    up_weight,
    up_first,
    up_second,
    down_weight,
    down_first,
    down_second,
    norm_gains,
    norm_first,
    norm_second,
    head_gains,
    head_first,
    head_second,
):
    wide_count = lax.axis_size("wide")
    wide_rank = lax.axis_index("wide")
    narrow_count = lax.axis_size("narrow")
    head_dim = head_gains.shape[1]
    key_heads = key_weight.shape[1] // head_dim
    local_heads = query_weight.shape[1] // head_dim
    shard_rows, model_width = tokens_in.shape
    copies = wide_count // key_heads
    key_slot = wide_rank // copies
    key_own = lax.dynamic_slice_in_dim(key_weight, key_slot * head_dim, head_dim, 1)
    value_own = lax.dynamic_slice_in_dim(value_weight, key_slot * head_dim, head_dim, 1)
    query_columns = query_weight.shape[1]
    att_own = jnp.concatenate([query_weight, key_own, value_own, output_weight.T], axis=1)
    half_rows = shard_rows // 2
    grad_halves = [
        lax.all_gather(out_grad[:half_rows], "wide", axis=0, tiled=True),
        lax.all_gather(out_grad[half_rows:], "wide", axis=0, tiled=True),
    ]
    att_full, gate_own = lax.optimization_barrier(
        (gather_weights(att_own.astype(jnp.bfloat16)), gate_weight.astype(jnp.bfloat16))
    )
    gate_local = lax.all_gather(gate_own, "narrow", axis=0, tiled=True)
    group_columns = query_columns + 2 * head_dim
    output_full = att_full[:, :, group_columns:]
    inverse = jnp.power(ROTARY_BASE, -2.0 * jnp.arange(head_dim // 2, dtype=jnp.float32) / head_dim)
    own_positions = lax.dynamic_slice_in_dim(positions, wide_rank * shard_rows, shard_rows, 0)
    angles = own_positions.astype(jnp.float32)[:, None] * inverse[None, :]
    cosine = jnp.cos(angles)
    sine_part = jnp.sin(angles)
    cosine = jnp.concatenate([cosine] * 4, axis=1)
    sine_part = jnp.concatenate([-sine_part, sine_part] * 2, axis=1)
    lane_gains = jnp.concatenate([head_gains, head_gains], axis=1)
    residual = tokens_in.astype(jnp.float32)
    normed_in, norm_in_back = jax.vjp(rms_scale, residual, norm_gains[0])
    rows_in = normed_in.astype(jnp.bfloat16)
    packed, input_raw = project(rows_in, att_full, cosine, sine_part, lane_gains, local_heads)
    packed, grad_halves = lax.optimization_barrier((packed, grad_halves))
    packed, attended, weight_sums, attended_low, up_local, down_local = attend_swap(
        packed, up_weight.astype(jnp.bfloat16), down_weight.astype(jnp.bfloat16), local_heads
    )
    attended_low, gate_local = lax.optimization_barrier((attended_low, gate_local))
    branch = jnp.einsum("gth,gdh->td", attended_low, output_full, preferred_element_type=jnp.float32)
    middle = residual + branch
    normed_mid, norm_mid_back = jax.vjp(rms_scale, middle, norm_gains[1])
    mid_low = normed_mid.astype(jnp.bfloat16)
    down_wgrad = gate_wgrad = up_wgrad = 0.0
    block_parts = []
    mid_sums = []
    rows_halves = [gather_rows(mid_low[:half_rows]), gather_rows(mid_low[half_rows:])]
    hidden_grads = [dot_back(rows, down_local).astype(jnp.bfloat16) for rows in grad_halves]
    rows_halves[0], hidden_grads = lax.optimization_barrier((rows_halves[0], hidden_grads))
    for rows_mid, grad_rows, hidden_grad in zip(rows_halves, grad_halves, hidden_grads):
        gate_pre = dot_last(rows_mid, gate_local)
        up_pre = dot_last(rows_mid, up_local)
        hidden, hidden_back = jax.vjp(
            lambda gate_in, up_in: jax.nn.silu(gate_in) * up_in, gate_pre, up_pre
        )
        hidden_low = hidden.astype(jnp.bfloat16)
        gate_grad, up_grad = hidden_back(hidden_grad.astype(jnp.float32))
        gate_grad = gate_grad.astype(jnp.bfloat16)
        up_grad = up_grad.astype(jnp.bfloat16)
        mid_sums.append(sum_back(((gate_grad, gate_local), (up_grad, up_local))))
        pieces = [hidden_low]
        if not block_parts:
            blocks = hidden_low.reshape(wide_count, half_rows, -1)
            quarter = half_rows // 2
            pieces = [
                blocks[:, :quarter].reshape(wide_count * quarter, -1),
                blocks[:, quarter:].reshape(wide_count * quarter, -1),
            ]
        for piece in pieces:
            block_parts.append(dot_last(piece, down_local).astype(jnp.bfloat16))
        down_wgrad = down_wgrad + dot_first(hidden_low, grad_rows)
        gate_wgrad = gate_wgrad + dot_first(rows_mid, gate_grad)
        up_wgrad = up_wgrad + dot_first(rows_mid, up_grad)
    down_wgrad = down_wgrad.astype(jnp.bfloat16)
    gate_wgrad = gate_wgrad.astype(jnp.bfloat16)
    up_wgrad = up_wgrad.astype(jnp.bfloat16)
    mid_sums, gate_wgrad, up_wgrad, down_wgrad, block_parts = lax.optimization_barrier(
        (mid_sums, gate_wgrad, up_wgrad, down_wgrad, block_parts)
    )
    mid_back = jnp.concatenate(mid_sums, axis=0)
    middle_part, mid_gain_grad = norm_mid_back(mid_back)
    middle_grad = out_grad.astype(jnp.float32) + middle_part
    branch_grad = middle_grad.astype(jnp.bfloat16)
    attended_grad = jnp.einsum(
        "td,gdh->gth", branch_grad, output_full, preferred_element_type=jnp.float32
    ).astype(jnp.bfloat16)
    attended_grad, first_part = lax.optimization_barrier((attended_grad, block_parts[0]))
    first_sum = lax.psum_scatter(first_part, "wide", scatter_dimension=0, tiled=True)
    query_rot_grad, key_value_grad, gate_shares, up_shares, down_shares = back_swap(
        packed, attended_grad, attended, weight_sums, gate_wgrad, up_wgrad, down_wgrad, local_heads
    )
    query_rot_grad, first_sum, second_part, third_part = lax.optimization_barrier(
        (query_rot_grad, first_sum, block_parts[1], block_parts[2])
    )
    second_sum = lax.psum_scatter(second_part, "wide", scatter_dimension=0, tiled=True)
    third_sum = lax.psum_scatter(third_part, "wide", scatter_dimension=0, tiled=True)
    input_wgrad, output_wgrad, input_back, head_sums = project_back(
        query_rot_grad, key_value_grad, input_raw, cosine, sine_part, lane_gains, rows_in,
        att_full, branch_grad, attended_low, local_heads,
    )
    input_part, in_gain_grad = norm_in_back(input_back)
    input_grad = middle_grad + input_part
    gain_stack = jnp.stack([in_gain_grad, mid_gain_grad])
    head_stack = jnp.stack(
        [head_sums[0, :head_dim] + head_sums[0, head_dim:], head_sums[1, :head_dim]]
    )
    query_total, output_total, key_total, value_total, gains = sum_weights(
        input_wgrad,
        output_wgrad,
        jnp.concatenate([gain_stack, head_stack], axis=1),
        key_heads,
    )
    query_total, second_sum, third_sum = lax.optimization_barrier(
        (query_total, second_sum, third_sum)
    )
    block_sum = jnp.concatenate([first_sum, second_sum, third_sum], axis=0).astype(jnp.float32)
    block_out = (middle + block_sum).astype(jnp.bfloat16)
    gain_total = gains[:, :model_width]
    head_total = gains[:, model_width:]
    gate_total, up_total, down_total = (
        jnp.sum(gate_shares.astype(jnp.float32), axis=0),
        jnp.sum(up_shares.astype(jnp.float32), axis=0),
        jnp.sum(down_shares.astype(jnp.float32), axis=0),
    )
    wide_rate = D ** (-0.5)
    query_new = adam_update(
        query_weight, query_first, query_second, query_total, wide_rate, WEIGHT_DECAY
    )
    key_new = adam_update(key_weight, key_first, key_second, key_total, wide_rate, WEIGHT_DECAY)
    value_new = adam_update(
        value_weight, value_first, value_second, value_total, wide_rate, WEIGHT_DECAY
    )
    output_new = adam_update(
        output_weight, output_first, output_second, output_total, O_FAN ** (-0.5), WEIGHT_DECAY
    )
    gate_new = adam_update(
        gate_weight, gate_first, gate_second, gate_total, wide_rate, WEIGHT_DECAY
    )
    up_new = adam_update(up_weight, up_first, up_second, up_total, wide_rate, WEIGHT_DECAY)
    down_new = adam_update(
        down_weight, down_first, down_second, down_total, FF ** (-0.5), WEIGHT_DECAY
    )
    norm_new = adam_update(norm_gains, norm_first, norm_second, gain_total, GAIN_RATE, 0.0)
    head_new = adam_update(head_gains, head_first, head_second, head_total, GAIN_RATE, 0.0)
    return (
        block_out,
        input_grad,
        query_new[0],
        query_new[1],
        query_new[2],
        key_new[0],
        key_new[1],
        key_new[2],
        value_new[0],
        value_new[1],
        value_new[2],
        output_new[0],
        output_new[1],
        output_new[2],
        gate_new[0],
        gate_new[1],
        gate_new[2],
        up_new[0],
        up_new[1],
        up_new[2],
        down_new[0],
        down_new[1],
        down_new[2],
        norm_new[0],
        norm_new[1],
        norm_new[2],
        head_new[0],
        head_new[1],
        head_new[2],
    )


def solution(mesh):
    return jax.shard_map(
        shards,
        mesh=mesh,
        in_specs=(
            P(("narrow", "wide"), None),
            P(("narrow", "wide"), None),
            P("narrow"),
            P("narrow", "wide"),
            P("narrow", "wide"),
            P("narrow", "wide"),
            P("narrow", None),
            P("narrow", None),
            P("narrow", None),
            P("narrow", None),
            P("narrow", None),
            P("narrow", None),
            P("wide", "narrow"),
            P("wide", "narrow"),
            P("wide", "narrow"),
            P("narrow", "wide"),
            P("narrow", "wide"),
            P("narrow", "wide"),
            P("narrow", "wide"),
            P("narrow", "wide"),
            P("narrow", "wide"),
            P("wide", "narrow"),
            P("wide", "narrow"),
            P("wide", "narrow"),
            P(),
            P(),
            P(),
            P(),
            P(),
            P(),
        ),
        out_specs=(
            P(("narrow", "wide"), None),
            P(("narrow", "wide"), None),
            P("narrow", "wide"),
            P("narrow", "wide"),
            P("narrow", "wide"),
            P("narrow", None),
            P("narrow", None),
            P("narrow", None),
            P("narrow", None),
            P("narrow", None),
            P("narrow", None),
            P("wide", "narrow"),
            P("wide", "narrow"),
            P("wide", "narrow"),
            P("narrow", "wide"),
            P("narrow", "wide"),
            P("narrow", "wide"),
            P("narrow", "wide"),
            P("narrow", "wide"),
            P("narrow", "wide"),
            P("wide", "narrow"),
            P("wide", "narrow"),
            P("wide", "narrow"),
            P(),
            P(),
            P(),
            P(),
            P(),
            P(),
        ),
        check_vma=False,
    )
```
